32 devices in a mesh: ctx: 8 (over z, y), fsdp: 4 (over x, core).
Axes of the slice: x: 2, y: 2, z: 4, core: 2. Of those that a mesh axis runs over, the one named last changes fastest.
Arguments:
- tokens: bfloat16 [4, 2048, 1536], P('fsdp', 'ctx'), may hold values from -6 to 6
- lengths: int32 [4, 6], P('fsdp'), may hold values from 1 to 1024, as said below
- deal: int32 [4, 8], P('fsdp'), may hold values from 0 to 7, as said below
- loss_mask: int32 [4, 2048], P('fsdp', 'ctx'), may hold values from 0 to 1, as said below
- teacher: bfloat16 [4, 2048, 1536], P('fsdp', 'ctx'), may hold values from -18 to 18
- out_grad: bfloat16 [4, 2048, 1536], P('fsdp', 'ctx'), may hold values from -6 to 6
- attn_gain: bfloat16 [1536], P(('ctx', 'fsdp')), may hold values from 0.5 to 1.5
- w_query: bfloat16 [1536, 1536], P(('ctx', 'fsdp')), may hold values from -0.15625 to 0.15625
- w_key: bfloat16 [1536, 768], P(('ctx', 'fsdp')), may hold values from -0.15625 to 0.15625
- w_value: bfloat16 [1536, 768], P(('ctx', 'fsdp')), may hold values from -0.15625 to 0.15625
- w_out: bfloat16 [1536, 1536], P(('ctx', 'fsdp')), may hold values from -1.25 to 1.25
- ffn_gain: bfloat16 [1536], P(('ctx', 'fsdp')), may hold values from 0.5 to 1.5
- w_gate: bfloat16 [1536, 4096], P(('ctx', 'fsdp')), may hold values from -0.15625 to 0.15625
- w_up: bfloat16 [1536, 4096], P(('ctx', 'fsdp')), may hold values from -0.15625 to 0.15625
- w_down: bfloat16 [4096, 1536], P(('ctx', 'fsdp')), may hold values from -0.09375 to 0.09375
Outputs:
- output: bfloat16 [4, 2048, 1536], P('fsdp', 'ctx')
- loss: float32 [], replicated
- input_grad: float32 [4, 2048, 1536], P('fsdp', 'ctx')
- attn_gain_grad: float32 [1536], P(('ctx', 'fsdp'))
- w_query_grad: float32 [1536, 1536], P(('ctx', 'fsdp'))
- w_key_grad: float32 [1536, 768], P(('ctx', 'fsdp'))
- w_value_grad: float32 [1536, 768], P(('ctx', 'fsdp'))
- w_out_grad: float32 [1536, 1536], P(('ctx', 'fsdp'))
- ffn_gain_grad: float32 [1536], P(('ctx', 'fsdp'))
- w_gate_grad: float32 [1536, 4096], P(('ctx', 'fsdp'))
- w_up_grad: float32 [1536, 4096], P(('ctx', 'fsdp'))
- w_down_grad: float32 [4096, 1536], P(('ctx', 'fsdp'))
The draws below stay inside these ranges and needn't reach their ends.
Inputs may be any that keep to these rules, and one draw needn't show every extreme that they name: `lengths`: the first sequence of every pack has exactly 1024 tokens; the others have 1 or more; they sum to less than 2048, the rest of the pack being padding at its end. `deal`: each row is a permutation of the ctx indices. `loss_mask`: the token at pack position 0 has a 1.
All inputs are finite; a program needn't handle non-finite values.
Results may differ from the reference program's by a relative error of at most 0.02.
Values may be sent and summed in bfloat16 or wider, within the bound.
A program may use at most 384 MiB of HBM per device.

```python
import jax
import jax.numpy as jnp
from jax import lax

D = 1536
HEADS = 16
KV = 8
HD = 96
FF = 4096
NSEQ = 6
QW = 1536
KW = 768
TOK_DEV = 256
PACK = 2048
N_CTX = 8
N_FSDP = 4


def dealing(key):
    keys = jax.random.split(key, N_FSDP)
    return jax.vmap(lambda sub: jax.random.permutation(sub, N_CTX))(keys).astype(jnp.int32)


def draw_deal(key, part):
    return dealing(key)


def draw_loss_mask(key, part):
    dealt = dealing(key)
    key = jax.random.fold_in(key, 23)
    bits = jax.random.randint(key, (N_FSDP, PACK), 0, 4)
    marks = (bits > 0).astype(jnp.int32)
    owner = jnp.repeat(dealt, TOK_DEV, axis=1)
    start = (jnp.arange(PACK, dtype=jnp.int32) % TOK_DEV == 0)[None, :]
    forced = ((owner == 0) & start).astype(jnp.int32)
    return jnp.maximum(marks, forced)


def draw_lengths(key, part):
    key = jax.random.fold_in(key, 11)
    half = PACK // 2

    def single(sub):
        cuts = jnp.sort(jax.random.permutation(sub, half - 1)[:NSEQ - 1] + 1).astype(jnp.int32)
        edges = jnp.concatenate([jnp.zeros((1,), jnp.int32), cuts])
        others = edges[1:] - edges[:-1]
        return jnp.concatenate([jnp.full((1,), half, jnp.int32), others])
    return jax.vmap(single)(jax.random.split(key, N_FSDP)).astype(jnp.int32)


def draw_teacher(key, part):
    key = jax.random.fold_in(key, 31)
    rise = jnp.arange(PACK, dtype=jnp.float32) / max(PACK - 1, 1)
    climb = jnp.arange(N_FSDP, dtype=jnp.float32) / max(N_FSDP - 1, 1)
    across = 3.0 ** climb
    base = jnp.clip(jax.random.normal(key, (N_FSDP, PACK, D), jnp.float32), -6.0, 6.0)
    factor = 0.1 * 10.0 ** rise
    return (base * factor[None, :, None] * across[:, None, None]).astype(jnp.bfloat16)


def steps_of(own_key, extent, shards, smallest, high):
    def one(position, shards_of):
        steps = jax.random.uniform(jax.random.fold_in(jax.random.fold_in(own_key, 6), position), (shards_of,), jnp.float32, smallest / len(shards), high / len(shards))
        return jnp.repeat(jnp.exp(steps), extent[position] // shards_of).reshape((-1,) + (1,) * (len(extent) - position - 1))

    gain = one(*shards[0])
    for cut in shards[1:]:
        gain = gain * one(*cut)
    return gain


def scatter_about(rng, dims, spread, limit, cuts=(), kind=jnp.bfloat16):
    values = spread * jax.random.normal(rng, dims, jnp.float32)
    if cuts:
        values = values * steps_of(rng, dims, cuts, -0.22, 0.18)
    return jnp.clip(values, -limit, limit).astype(kind)


def setup_inputs(seed: int = 0) -> dict:
    key_list = jax.random.split(jax.random.key(seed), 16)
    tokens = scatter_about(key_list[0], (N_FSDP, PACK, D), 1.0, 6.0, ((0, 4), (1, 8)))
    lengths = draw_lengths(jax.random.fold_in(key_list[15], 71), 0)
    deal = draw_deal(jax.random.fold_in(key_list[15], 71), 0)
    loss_mask = draw_loss_mask(jax.random.fold_in(key_list[15], 71), 0)
    teacher = draw_teacher(jax.random.fold_in(key_list[15], 71), 0)
    out_grad = scatter_about(key_list[5], (N_FSDP, PACK, D), 1.0, 6.0, ((0, 4), (1, 8)))
    attn_gain = jnp.clip(1.0 + 0.1 * jax.random.normal(key_list[6], (D,), jnp.float32), 0.5, 1.5).astype(jnp.bfloat16)
    w_query = scatter_about(key_list[7], (D, QW), D ** -0.5, 0.15625, ((0, 32),))
    w_key = scatter_about(key_list[8], (D, KW), D ** -0.5, 0.15625, ((0, 32),))
    w_value = scatter_about(key_list[9], (D, KW), D ** -0.5, 0.15625, ((0, 32),))
    w_out = scatter_about(key_list[10], (QW, D), (QW // 64) ** -0.5, 1.25, ((0, 32),))
    ffn_gain = jnp.clip(1.0 + 0.1 * jax.random.normal(key_list[11], (D,), jnp.float32), 0.5, 1.5).astype(jnp.bfloat16)
    w_gate = scatter_about(key_list[12], (D, FF), D ** -0.5, 0.15625, ((0, 32),))
    w_up = scatter_about(key_list[13], (D, FF), D ** -0.5, 0.15625, ((0, 32),))
    w_down = scatter_about(key_list[14], (FF, D), FF ** -0.5, 0.09375, ((0, 32),))
    return dict(tokens=tokens, lengths=lengths, deal=deal, loss_mask=loss_mask, teacher=teacher, out_grad=out_grad, attn_gain=attn_gain, w_query=w_query, w_key=w_key, w_value=w_value, w_out=w_out, ffn_gain=ffn_gain, w_gate=w_gate, w_up=w_up, w_down=w_down)


@jax.custom_vjp
def low(v):
    return lax.optimization_barrier(v.astype(jnp.bfloat16)).astype(jnp.float32)

@jax.custom_vjp
def low_back(v):
    return v

def low_keep(v):
    return (low(v), None)

def low_pass(kept, grad):
    return (grad,)

def back_keep(v):
    return (v, None)

def back_low(kept, grad):
    return (low(grad),)
low.defvjp(low_keep, low_pass)
low_back.defvjp(back_keep, back_low)
rope_base = 100000.0
epsilon = 1e-05
masked_score = -1e+30

def precise(left, right):
    return jnp.dot(left, right, precision=lax.Precision.HIGHEST, preferred_element_type=jnp.float32)

def pack_places(deal_row):
    half_block = TOK_DEV // 2
    dealt = jnp.arange(PACK, dtype=jnp.int32)
    local = dealt % TOK_DEV
    first = jnp.repeat(deal_row, TOK_DEV).astype(jnp.int32)
    block = jnp.where(local < half_block, first, 2 * N_CTX - 1 - first)
    return (block * half_block + local % half_block).astype(jnp.int32)

def segments(places, lengths_row):
    ends = jnp.cumsum(lengths_row).astype(jnp.int32)
    after = (places[:, None] >= ends[None, :]).astype(jnp.int32)
    seg_row = lax.optimization_barrier(jnp.sum(after, 1)).astype(jnp.int32)
    inseq_row = (places - lax.optimization_barrier(jnp.sum(after * lengths_row[None, :], 1))).astype(jnp.int32)
    return (seg_row, inseq_row)

def rms_scale(values):
    return lax.rsqrt(lax.optimization_barrier(jnp.mean(values * values, -1, keepdims=True)) + epsilon)

def rotary_tables(inseq_row):
    freq = rope_base ** (-(jnp.arange(HD // 2, dtype=jnp.float32) * 2.0 / HD))
    angle = inseq_row.astype(jnp.float32)[:, None] * freq[None, :]
    return (jnp.cos(angle)[:, None, :], jnp.sin(angle)[:, None, :])

def rotary(values, cosine, sine):
    half = values.shape[-1] // 2
    first = values[..., :half]
    second = values[..., half:]
    return jnp.concatenate([first * cosine - second * sine, second * cosine + first * sine], -1)

def attend(queries, keys, values, seg_row):
    block_rows = min(512, PACK)
    places = jnp.arange(PACK, dtype=jnp.int32)
    query_blocks = queries.reshape(PACK // block_rows, block_rows, KV, HEADS // KV, HD)

    def block(item):
        query_block, place_block, seg_block = item
        raw = jnp.einsum('qcgd,kcd->cgqk', query_block, keys, precision=lax.Precision.HIGHEST) * HD ** (-0.5)
        score = low_back(raw)
        same = (seg_block[:, None] == seg_row[None, :]) & (seg_block[:, None] < NSEQ)
        allowed = same & (places[None, :] <= place_block[:, None]) | (places[None, :] == place_block[:, None])
        prob = low(jax.nn.softmax(jnp.where(allowed, score, masked_score), axis=-1))
        weighted = jnp.einsum('cgqk,kcd->qcgd', prob, values, precision=lax.Precision.HIGHEST)
        return weighted.reshape(block_rows, HEADS * HD)
    items = (query_blocks, places.reshape(-1, block_rows), seg_row.reshape(-1, block_rows))
    return lax.map(jax.checkpoint(block), items).reshape(PACK, HEADS * HD)

def layer(rows, seg_row, inseq_row, gain_one, query_w, key_w, value_w, out_w, gain_two, gate_w, up_w, down_w):
    count = rows.shape[0]
    cosine, sine = rotary_tables(inseq_row)
    normed_low = low(rows * rms_scale(rows) * gain_one)
    query_pre = low_back(precise(normed_low, query_w)).reshape(count, HEADS, HD)
    key_pre = low_back(precise(normed_low, key_w)).reshape(count, KV, HD)
    values = low(low_back(precise(normed_low, value_w))).reshape(count, KV, HD)
    queries = low(rotary(query_pre, cosine, sine)).reshape(count, KV, HEADS // KV, HD)
    keys = low(rotary(key_pre, cosine, sine))
    attended = attend(queries, keys, values, seg_row)
    hidden = rows + low_back(precise(low(low_back(attended)), out_w))
    ffn_low = low(hidden * rms_scale(hidden) * gain_two)
    gate = low_back(precise(ffn_low, gate_w))
    up = low_back(precise(ffn_low, up_w))
    mixed = low(jax.nn.silu(gate) * up)
    return hidden + low_back(precise(mixed, down_w))

def reference(tokens, lengths, deal, loss_mask, teacher, out_grad, attn_gain, w_query, w_key, w_value, w_out, ffn_gain, w_gate, w_up, w_down):
    places = jax.vmap(pack_places)(deal)
    order = jnp.argsort(places, axis=1).astype(jnp.int32)

    def to_pack(array):
        return jnp.take_along_axis(array.astype(jnp.float32), order[:, :, None], 1)
    inputs = to_pack(tokens)
    target = to_pack(teacher)
    cotangent = to_pack(out_grad)
    mask_pack = jnp.take_along_axis(loss_mask, order, 1)
    linear = jnp.arange(PACK, dtype=jnp.int32)
    seg_all, inseq_all = jax.vmap(lambda row: segments(linear, row))(lengths)
    valid = (mask_pack * (seg_all < NSEQ)).astype(jnp.float32)
    count = jnp.sum(valid)
    params = (attn_gain.astype(jnp.float32), w_query.astype(jnp.float32), w_key.astype(jnp.float32), w_value.astype(jnp.float32), w_out.astype(jnp.float32), ffn_gain.astype(jnp.float32), w_gate.astype(jnp.float32), w_up.astype(jnp.float32), w_down.astype(jnp.float32))

    def forward(inputs, params):

        def one(item):
            rows, seg_row, inseq_row = item
            return layer(rows, seg_row, inseq_row, *params)
        result = lax.map(one, (inputs, seg_all, inseq_all))
        differ = result - target
        loss = jnp.sum(valid[:, :, None] * differ * differ) / (count * D)
        return (result, loss)
    (result, loss), pullback = jax.vjp(forward, inputs, params)
    input_grad, grads = pullback((cotangent, jnp.ones((), jnp.float32)))

    def to_dealt(array):
        return jnp.take_along_axis(array, places[:, :, None], 1)
    return (to_dealt(result).astype(jnp.bfloat16), loss, to_dealt(input_grad), grads[0], grads[1], grads[2], grads[3], grads[4], grads[5], grads[6], grads[7], grads[8])
```

```python
import functools

import jax
import jax.numpy as jnp
from jax import lax
from jax.experimental import pallas as pl
from jax.experimental.pallas import tpu as pltpu
from jax.sharding import PartitionSpec as P

HEADS = 16
KV = 8
HD = 96
NSEQ = 6


rope_base = 100000.0
epsilon = 1e-05
masked_score = -1e30


def shifted(value, axis, by):
    size = lax.axis_size(axis)
    return lax.ppermute(value, axis, [(i, (i + by) % size) for i in range(size)])


def rms_scale(values):
    return lax.rsqrt(jnp.mean(values * values, -1, keepdims=True) + epsilon)


def rotary_tables(inseq):
    freq = rope_base ** (-(jnp.arange(HD // 2, dtype=jnp.float32) * 2.0 / HD))
    angle = inseq.astype(jnp.float32)[:, None] * freq[None, :]
    return (jnp.cos(angle)[:, None, :], jnp.sin(angle)[:, None, :])


def rotary(values, cosine, sine):
    half = values.shape[-1] // 2
    first = values[..., :half]
    second = values[..., half:]
    return jnp.concatenate([first * cosine - second * sine, second * cosine + first * sine], -1)


def rotary_back(grads, cosine, sine):
    half = grads.shape[-1] // 2
    first = grads[..., :half]
    second = grads[..., half:]
    return jnp.concatenate([first * cosine + second * sine, second * cosine - first * sine], -1)


def transposed(left, right):
    return lax.dot_general(
        left, right, (((0,), (0,)), ((), ())), preferred_element_type=jnp.float32
    )


def against(left, right):
    return lax.dot_general(
        left, right, (((1,), (1,)), ((), ())), preferred_element_type=jnp.float32
    )


def permitted(query_place, query_seg, key_place, key_seg):
    same = (query_seg[:, None] == key_seg[None, :]) & (query_seg[:, None] < NSEQ)
    return same & (key_place[None, :] <= query_place[:, None]) | (
        key_place[None, :] == query_place[:, None]
    )


def ring_per_device(
    tokens,
    lengths,
    deal,
    loss_mask,
    teacher,
    out_grad,
    attn_gain,
    w_query,
    w_key,
    w_value,
    w_out,
    ffn_gain,
    w_gate,
    w_up,
    w_down,
):
    count_ctx = lax.axis_size("ctx")
    myself = lax.axis_index("ctx")
    tok_rows = tokens.shape[1]
    width = tokens.shape[2]
    half_block = tok_rows // 2
    groups = HEADS // KV
    scale = HD ** (-0.5)
    gain_one, query_w, key_w, value_w, out_w = (
        lax.all_gather(attn_gain, ("ctx", "fsdp"), axis=0, tiled=True),
        lax.all_gather(w_query, ("ctx", "fsdp"), axis=0, tiled=True),
        lax.all_gather(w_key, ("ctx", "fsdp"), axis=0, tiled=True),
        lax.all_gather(w_value, ("ctx", "fsdp"), axis=0, tiled=True),
        lax.all_gather(w_out, ("ctx", "fsdp"), axis=0, tiled=True),
    )
    gain_two, gate_w, up_w, down_w = (
        lax.all_gather(ffn_gain, ("ctx", "fsdp"), axis=0, tiled=True),
        lax.all_gather(w_gate, ("ctx", "fsdp"), axis=0, tiled=True),
        lax.all_gather(w_up, ("ctx", "fsdp"), axis=0, tiled=True),
        lax.all_gather(w_down, ("ctx", "fsdp"), axis=0, tiled=True),
    )
    dealt = jnp.arange(count_ctx * tok_rows, dtype=jnp.int32)
    local = dealt % tok_rows
    first = jnp.repeat(deal[0], tok_rows)
    block = jnp.where(local < half_block, first, 2 * count_ctx - 1 - first)
    places = block * half_block + local % half_block
    ends = jnp.cumsum(lengths[0])
    after = (places[:, None] >= ends[None, :]).astype(jnp.int32)
    seg_all = jnp.sum(after, 1)
    inseq_all = places - jnp.sum(after * lengths[0][None, :], 1)
    own_place = lax.dynamic_slice_in_dim(places, myself * tok_rows, tok_rows)
    own_seg = lax.dynamic_slice_in_dim(seg_all, myself * tok_rows, tok_rows)
    own_inseq = lax.dynamic_slice_in_dim(inseq_all, myself * tok_rows, tok_rows)
    cosine, sine = rotary_tables(own_inseq)
    inputs = tokens[0].astype(jnp.float32)
    scale_one = rms_scale(inputs)
    normed_one = inputs * scale_one
    gain_first = gain_one.astype(jnp.float32)
    normed_low = (normed_one * gain_first).astype(jnp.bfloat16)
    query_pre = jnp.dot(normed_low, query_w, preferred_element_type=jnp.float32).reshape(
        tok_rows, HEADS, HD
    )
    key_pre = jnp.dot(normed_low, key_w, preferred_element_type=jnp.float32).reshape(
        tok_rows, KV, HD
    )
    value_low = jnp.dot(normed_low, value_w, preferred_element_type=jnp.float32).astype(
        jnp.bfloat16
    )
    queries = rotary(query_pre, cosine, sine).astype(jnp.bfloat16).reshape(tok_rows, KV, groups, HD)
    keys = rotary(key_pre, cosine, sine).astype(jnp.bfloat16).reshape(tok_rows, KV * HD)

    def logits(key_block):
        return (
            jnp.einsum(
                "qcgd,kcd->cgqk",
                queries,
                key_block.reshape(-1, KV, HD),
                preferred_element_type=jnp.float32,
            )
            * scale
        )

    key_block = lax.all_gather(keys, "ctx", axis=0, tiled=True)
    value_block = lax.all_gather(value_low, "ctx", axis=0, tiled=True)
    allowed = permitted(own_place, own_seg, places, seg_all)
    top = jnp.full((KV, groups, tok_rows, 1), masked_score, jnp.float32)
    score = jnp.where(allowed, logits(key_block), masked_score)
    new_top = jnp.maximum(top, jnp.max(score, -1, keepdims=True))
    weight = jnp.where(allowed, jnp.exp(score - new_top), 0.0)
    summed = jnp.einsum(
        "cgqk,kcd->cgqd",
        weight.astype(jnp.bfloat16),
        value_block.reshape(-1, KV, HD),
        preferred_element_type=jnp.float32,
    )
    summed, top, total = (summed, new_top, jnp.sum(weight, -1, keepdims=True))
    attended = summed / total
    log_total = top + jnp.log(total)
    attended_low = (
        jnp.transpose(attended, (2, 0, 1, 3)).reshape(tok_rows, HEADS * HD).astype(jnp.bfloat16)
    )
    hidden = inputs + jnp.dot(attended_low, out_w, preferred_element_type=jnp.float32)
    scale_two = rms_scale(hidden)
    normed_two = hidden * scale_two
    gain_second = gain_two.astype(jnp.float32)
    ffn_low = (normed_two * gain_second).astype(jnp.bfloat16)
    gate = jnp.dot(ffn_low, gate_w, preferred_element_type=jnp.float32)
    up = jnp.dot(ffn_low, up_w, preferred_element_type=jnp.float32)
    sigmoid = jax.nn.sigmoid(gate)
    activated = gate * sigmoid
    mixed_low = (activated * up).astype(jnp.bfloat16)
    result = hidden + jnp.dot(mixed_low, down_w, preferred_element_type=jnp.float32)
    target = teacher[0].astype(jnp.float32)
    valid = (loss_mask[0] * (own_seg < NSEQ)).astype(jnp.float32)[:, None]
    differ = result - target
    square_sum, valid_count = lax.psum(
        (jnp.sum(valid * differ * differ), jnp.sum(valid)), ("ctx", "fsdp")
    )
    loss = square_sum / (valid_count * width)
    out_total = out_grad[0].astype(jnp.float32) + 2.0 * valid * differ / (valid_count * width)
    out_low = out_total.astype(jnp.bfloat16)
    down_grad = transposed(mixed_low, out_low)
    mixed_grad = against(out_low, down_w)
    silu_slope = sigmoid * (1.0 + gate * (1.0 - sigmoid))
    gate_low = (mixed_grad * up * silu_slope).astype(jnp.bfloat16)
    up_low = (mixed_grad * activated).astype(jnp.bfloat16)
    gate_grad = transposed(ffn_low, gate_low)
    up_grad = transposed(ffn_low, up_low)
    normed_grad = against(gate_low, gate_w) + against(up_low, up_w)
    gain_two_grad = jnp.sum(normed_grad * normed_two, 0)
    scaled_two = normed_grad * gain_second
    hidden_grad = out_total + scale_two * (
        scaled_two - normed_two * jnp.mean(scaled_two * normed_two, -1, keepdims=True)
    )
    ffn_final = (
        lax.psum_scatter(gain_two_grad, ("ctx", "fsdp"), scatter_dimension=0, tiled=True),
        lax.psum_scatter(gate_grad, ("ctx", "fsdp"), scatter_dimension=0, tiled=True),
        lax.psum_scatter(up_grad, ("ctx", "fsdp"), scatter_dimension=0, tiled=True),
        lax.psum_scatter(down_grad, ("ctx", "fsdp"), scatter_dimension=0, tiled=True),
    )
    branch_low = hidden_grad.astype(jnp.bfloat16)
    out_w_grad = transposed(attended_low, branch_low)
    attended_grad = against(branch_low, out_w).astype(jnp.bfloat16)
    grad_heads = jnp.transpose(attended_grad.reshape(tok_rows, KV, groups, HD), (1, 2, 0, 3))
    delta = jnp.sum(grad_heads.astype(jnp.float32) * attended, -1, keepdims=True)

    def cycle_step(step, state):
        key_block, value_block, key_acc, value_acc, query_acc = state
        source = (myself - step) % count_ctx
        allowed = permitted(
            own_place,
            own_seg,
            lax.dynamic_slice_in_dim(places, source * tok_rows, tok_rows),
            lax.dynamic_slice_in_dim(seg_all, source * tok_rows, tok_rows),
        )
        current_key = key_block
        current_value = value_block
        keys_three = current_key.reshape(tok_rows, KV, HD)
        values_three = current_value.reshape(tok_rows, KV, HD)
        prob = jnp.where(allowed, jnp.exp(logits(current_key) - log_total), 0.0)
        prob_grad = jnp.einsum(
            "cgqd,kcd->cgqk", grad_heads, values_three, preferred_element_type=jnp.float32
        )
        score_low = (prob * (prob_grad - delta)).astype(jnp.bfloat16)
        query_add = (
            jnp.einsum("cgqk,kcd->cgqd", score_low, keys_three, preferred_element_type=jnp.float32)
            * scale
        )
        key_add = (
            jnp.einsum(
                "cgqk,qcgd->kcd", score_low, queries, preferred_element_type=jnp.float32
            ).reshape(tok_rows, KV * HD)
            * scale
        )
        value_add = jnp.einsum(
            "cgqk,cgqd->kcd",
            prob.astype(jnp.bfloat16),
            grad_heads,
            preferred_element_type=jnp.float32,
        ).reshape(tok_rows, KV * HD)
        key_block, value_block = shifted((key_block, value_block), "ctx", 1)
        key_acc, value_acc = (
            shifted((key_acc + key_add).astype(jnp.bfloat16), "ctx", 1).astype(jnp.float32),
            shifted((value_acc + value_add).astype(jnp.bfloat16), "ctx", 1).astype(jnp.float32),
        )
        return (key_block, value_block, key_acc, value_acc, query_acc + query_add)

    cycle_start = (
        keys,
        value_low,
        jnp.zeros((tok_rows, KV * HD), jnp.float32),
        jnp.zeros((tok_rows, KV * HD), jnp.float32),
        jnp.zeros((KV, groups, tok_rows, HD), jnp.float32),
    )
    cycle_end = lax.fori_loop(0, count_ctx, cycle_step, cycle_start)
    key_acc = cycle_end[2]
    value_acc = cycle_end[3]
    query_acc = cycle_end[4]
    query_grad = jnp.transpose(query_acc, (2, 0, 1, 3)).reshape(tok_rows, HEADS, HD)
    query_low = (
        rotary_back(query_grad, cosine, sine).reshape(tok_rows, HEADS * HD).astype(jnp.bfloat16)
    )
    key_low = (
        rotary_back(key_acc.reshape(tok_rows, KV, HD), cosine, sine)
        .reshape(tok_rows, KV * HD)
        .astype(jnp.bfloat16)
    )
    value_grad_low = value_acc.astype(jnp.bfloat16)
    query_w_grad = transposed(normed_low, query_low)
    key_w_grad = transposed(normed_low, key_low)
    value_w_grad = transposed(normed_low, value_grad_low)
    normed_one_grad = (
        against(query_low, query_w) + against(key_low, key_w) + against(value_grad_low, value_w)
    )
    gain_one_grad = jnp.sum(normed_one_grad * normed_one, 0)
    scaled_one = normed_one_grad * gain_first
    input_grad = hidden_grad + scale_one * (
        scaled_one - normed_one * jnp.mean(scaled_one * normed_one, -1, keepdims=True)
    )
    attn_final = (
        lax.psum_scatter(gain_one_grad, ("ctx", "fsdp"), scatter_dimension=0, tiled=True),
        lax.psum_scatter(query_w_grad, ("ctx", "fsdp"), scatter_dimension=0, tiled=True),
        lax.psum_scatter(key_w_grad, ("ctx", "fsdp"), scatter_dimension=0, tiled=True),
        lax.psum_scatter(value_w_grad, ("ctx", "fsdp"), scatter_dimension=0, tiled=True),
        lax.psum_scatter(out_w_grad, ("ctx", "fsdp"), scatter_dimension=0, tiled=True),
    )
    return (
        result.astype(jnp.bfloat16)[None],
        loss,
        input_grad[None],
        attn_final[0],
        attn_final[1],
        attn_final[2],
        attn_final[3],
        attn_final[4],
        ffn_final[0],
        ffn_final[1],
        ffn_final[2],
        ffn_final[3],
    )


MESH = pl.DeviceIdType.MESH
ROWS_Y = 2
PLANE = 8
LANES = 128
VMEM_LIMIT = 60 * 2**20


def coordinates():
    ctx = lax.axis_index("ctx")
    fsdp = lax.axis_index("fsdp")
    return ctx // 2, ctx % 2, fsdp // 2, fsdp % 2


def device(z, y, x, c):
    return (z * 2 + y, x * 2 + c)


def greet(devices):
    barrier = pltpu.get_barrier_semaphore()
    for other in devices:
        pl.semaphore_signal(barrier, inc=1, device_id=other, device_id_type=MESH)
    pl.semaphore_wait(barrier, len(devices))


def remote(src, dst, send, recv, target):
    return pltpu.make_async_remote_copy(
        src_ref=src,
        dst_ref=dst,
        send_sem=send,
        recv_sem=recv,
        device_id=target,
        device_id_type=MESH,
    )


def exchange_kernel(group, count, x_ref, o_ref, send, recv, here):
    z, y, x, c = coordinates()
    if group == "ctx":
        me = z * 2 + y
        to_device = lambda i: (i, x * 2 + c)
    else:
        me = y * 4 + x * 2 + c
        to_device = lambda i: (z * 2 + i // 4, i % 4)
    others = [lax.rem(me + k, count) for k in range(1, count)]
    greet([to_device(i) for i in others])
    copies = [
        remote(x_ref.at[i], o_ref.at[me], send.at[k], recv.at[k], to_device(i))
        for k, i in enumerate(others)
    ]
    for copy in copies:
        copy.start()
    own = pltpu.make_async_copy(x_ref.at[me], o_ref.at[me], here)
    own.start()
    own.wait()
    for copy in copies:
        copy.wait()


def exchange(values, group, identity, name):
    count = values.shape[0]
    return pl.pallas_call(
        functools.partial(exchange_kernel, group, count),
        out_shape=jax.ShapeDtypeStruct(values.shape, values.dtype),
        in_specs=[pl.BlockSpec(memory_space=pl.ANY)],
        out_specs=pl.BlockSpec(memory_space=pl.ANY),
        scratch_shapes=[
            pltpu.SemaphoreType.DMA((count - 1,)),
            pltpu.SemaphoreType.DMA((count - 1,)),
            pltpu.SemaphoreType.DMA,
        ],
        compiler_params=pltpu.CompilerParams(collective_id=identity),
        name=name,
    )(values)


def column_cut(width):
    tiles = width // LANES
    return (tiles + 1) // 2 * LANES


def gather_kernel(lines, x_ref, o_ref, send, recv, here):
    z, y, x, c = coordinates()
    width = x_ref.shape[1]
    cut = column_cut(width)
    first, second = pl.ds(0, cut), pl.ds(cut, width - cut)
    side, over, sibling = device(z, y, 1 - x, c), device(z, 1 - y, x, c), device(z, y, x, 1 - c)
    above, below = device(z + 1, y, x, c), device(z - 1, y, x, c)
    greet([side, over, sibling] + [device(lax.rem(z + k, lines), y, x, c) for k in range(1, lines)])
    slot = lambda zz, yy, xx, cc: (zz * 2 + yy) * 4 + xx * 2 + cc
    mine = pltpu.make_async_copy(x_ref, o_ref.at[slot(z, y, x, c)], here)
    mine.start()

    def item(sign, s):
        index = 0 if s == 0 else (2 * s - 1 if sign < 0 else 2 * s)
        zz = z + sign * s
        at = lambda yy, xx, cc: o_ref.at[slot(zz, yy, xx, cc)]
        own = x_ref if s == 0 else at(y, x, c)
        make = lambda kind, src, dst, to: remote(
            src, dst, send.at[index, kind], recv.at[index, kind], to
        )
        same = lambda kind, ref, to: make(kind, ref, ref, to)
        corner_at = lambda columns: at(1 - y, 1 - x, c).at[:, columns]
        return dict(
            side=lambda: make(1, own, at(y, x, c), side),
            over=lambda: make(2, own, at(y, x, c), over),
            side_on=lambda: same(3, at(y, 1 - x, c).at[:, first], over),
            over_on=lambda: same(4, at(1 - y, x, c).at[:, second], side),
            core=lambda: make(5, own, at(y, x, c), sibling),
            core_side=lambda: same(6, at(y, 1 - x, c), sibling),
            core_over=lambda: same(7, at(1 - y, x, c), sibling),
            core_first=lambda: same(8, corner_at(first), sibling),
            core_second=lambda: same(9, corner_at(second), sibling),
        )

    def along(sign, s):
        index = 2 * s - 1 if sign < 0 else 2 * s
        zz = z + sign * (s - 1)
        src = x_ref if s == 1 else o_ref.at[slot(zz, y, x, c)]
        return remote(
            src, o_ref.at[slot(zz, y, x, c)], send.at[index, 0], recv.at[index, 0], above if sign < 0 else below
        )

    def sends_along(sign, s):
        if sign < 0:
            return (z - (s - 1) >= 0) & (z + 1 < lines)
        return (z + (s - 1) < lines) & (z - 1 >= 0)

    def present(sign, s):
        return z - s >= 0 if sign < 0 else z + s < lines

    arrivals = [(-1, 0)] + [(sign, s) for s in range(1, lines) for sign in (-1, 1)]

    def begin(sign, s):
        copies = item(sign, s)
        if s > 0:
            along(sign, s).wait_recv()
        for way in ((-1, 1) if s == 0 else (sign,)):
            if s + 1 < lines:
                @pl.when(sends_along(way, s + 1))
                def _():
                    along(way, s + 1).start()
        copies["side"]().start()
        copies["over"]().start()
        copies["core"]().start()

    def pass_on(sign, s):
        copies = item(sign, s)
        copies["side"]().wait_recv()
        copies["side_on"]().start()
        copies["core_side"]().start()
        copies["over"]().wait_recv()
        copies["over_on"]().start()
        copies["core_over"]().start()

    def corner(sign, s):
        copies = item(sign, s)
        copies["side_on"]().wait_recv()
        copies["core_first"]().start()
        copies["over_on"]().wait_recv()
        copies["core_second"]().start()

    def finish(sign, s):
        copies = item(sign, s)
        for kind in ("core", "core_side", "core_over", "core_first", "core_second"):
            copies[kind]().wait()
        for kind in ("side", "over", "side_on", "over_on"):
            copies[kind]().wait_send()

    def where(sign, s, step):
        if s == 0:
            step(sign, s)
        else:
            pl.when(present(sign, s))(functools.partial(step, sign, s))

    waves = [[(-1, 0)]] + [[(-1, s), (1, s)] for s in range(1, lines)]
    for number in range(len(waves) + 2):
        for stage, lag in ((begin, 0), (pass_on, 1), (corner, 2)):
            if 0 <= number - lag < len(waves):
                for sign, s in waves[number - lag]:
                    where(sign, s, stage)
    for sign, s in arrivals:
        where(sign, s, finish)
    for s in range(1, lines):
        for sign in (-1, 1):
            @pl.when(sends_along(sign, s))
            def _():
                along(sign, s).wait_send()
    mine.wait()


def gather_everywhere(rows, lines, identity, name):
    return pl.pallas_call(
        functools.partial(gather_kernel, lines),
        out_shape=jax.ShapeDtypeStruct((lines * PLANE,) + rows.shape, rows.dtype),
        in_specs=[pl.BlockSpec(memory_space=pl.ANY)],
        out_specs=pl.BlockSpec(memory_space=pl.ANY),
        scratch_shapes=[
            pltpu.SemaphoreType.DMA((2 * lines - 1, 10)),
            pltpu.SemaphoreType.DMA((2 * lines - 1, 10)),
            pltpu.SemaphoreType.DMA,
        ],
        compiler_params=pltpu.CompilerParams(collective_id=identity),
        name=name,
    )(rows)


def plane_gather_kernel(x_ref, o_ref, send, recv, here):
    z, y, x, c = coordinates()
    width = x_ref.shape[1]
    cut = column_cut(width)
    first, second = pl.ds(0, cut), pl.ds(cut, width - cut)
    side, over, sibling = device(z, y, 1 - x, c), device(z, 1 - y, x, c), device(z, y, x, 1 - c)
    greet([side, over, sibling])
    at = lambda yy, xx: o_ref.at[yy * 4 + xx * 2 + c]
    make = lambda kind, src, dst, to: remote(src, dst, send.at[kind], recv.at[kind], to)
    same = lambda kind, ref, to: make(kind, ref, ref, to)
    to_side = make(0, x_ref, at(y, x), side)
    to_over = make(1, x_ref, at(y, x), over)
    to_core = make(2, x_ref, at(y, x), sibling)
    mine = pltpu.make_async_copy(x_ref, at(y, x), here)
    to_side.start()
    to_over.start()
    to_core.start()
    mine.start()
    side_on = same(3, at(y, 1 - x).at[:, first], over)
    over_on = same(4, at(1 - y, x).at[:, second], side)
    core_side = same(5, at(y, 1 - x), sibling)
    core_over = same(6, at(1 - y, x), sibling)
    core_first = same(7, at(1 - y, 1 - x).at[:, first], sibling)
    core_second = same(8, at(1 - y, 1 - x).at[:, second], sibling)
    to_side.wait_recv()
    side_on.start()
    core_side.start()
    to_over.wait_recv()
    over_on.start()
    core_over.start()
    side_on.wait_recv()
    core_first.start()
    over_on.wait_recv()
    core_second.start()
    for copy in (to_core, core_side, core_over, core_first, core_second):
        copy.wait()
    for copy in (to_side, to_over, side_on, over_on):
        copy.wait_send()
    mine.wait()


def plane_gather(rows, identity, name):
    return pl.pallas_call(
        plane_gather_kernel,
        out_shape=jax.ShapeDtypeStruct((PLANE,) + rows.shape, rows.dtype),
        in_specs=[pl.BlockSpec(memory_space=pl.ANY)],
        out_specs=pl.BlockSpec(memory_space=pl.ANY),
        scratch_shapes=[
            pltpu.SemaphoreType.DMA((9,)),
            pltpu.SemaphoreType.DMA((9,)),
            pltpu.SemaphoreType.DMA,
        ],
        compiler_params=pltpu.CompilerParams(collective_id=identity),
        name=name,
    )(rows)


def reduce_kernel(parts, lines, p_ref, o_ref, held, corner_a, corner_b, from_side, from_over, along, send, recv):
    z, y, x, c = coordinates()
    rows, width = held.shape[2], held.shape[3]
    cut = column_cut(width)
    first, second = pl.ds(0, cut), pl.ds(cut, width - cut)
    side, over, sibling = device(z, y, 1 - x, c), device(z, 1 - y, x, c), device(z, y, x, 1 - c)
    neighbours = [side, over, sibling]
    if lines:
        neighbours += [device(lax.rem(z + k, lines), y, x, c) for k in range(1, lines)]
    greet(neighbours)

    def given(part, yy, xx, cc):
        member = yy * 4 + xx * 2 + cc
        if lines:
            return p_ref.at[lax.rem(z + part + 1, lines), member]
        return p_ref.at[member, pl.ds(part * rows, rows)]

    def make(part, kind, src, dst, to):
        return remote(src, dst, send.at[part, kind], recv.at[part, kind], to)

    lane = lambda part, yy, xx: held.at[part, yy * 2 + xx]

    def over_core(part):
        return [
            make(part, yy * 2 + xx, given(part, yy, xx, 1 - c), lane(part, yy, xx), sibling)
            for yy in range(2)
            for xx in range(2)
        ]

    def to_corner(part):
        return (
            make(part, 4, lane(part, 1 - y, 1 - x).at[:, first], corner_a.at[part], over),
            make(part, 5, lane(part, 1 - y, 1 - x).at[:, second], corner_b.at[part], side),
        )

    def to_neighbour(part, way):
        columns = (first, second)[way % 2]
        if way < 2:
            return make(part, 6 + way, lane(part, y, 1 - x).at[:, columns], from_side.at[part, :, columns], side)
        return make(part, 6 + way, lane(part, 1 - y, x).at[:, columns], from_over.at[part, :, columns], over)

    def along_z(part):
        to = lax.rem(z + part + 1, lines)
        return make(part, 10, lane(part, y, x), along.at[part], device(to, y, x, c))

    step = 16

    def add_core(part):
        for copy in over_core(part):
            copy.wait_recv()
        for yy, xx in ((1 - y, 1 - x), (y, 1 - x), (1 - y, x), (y, x)):
            mine, other = given(part, yy, xx, c), lane(part, yy, xx)

            def body(i, carry):
                at = pl.ds(pl.multiple_of(i * step, step), step)
                total = mine[at, :].astype(jnp.float32) + other[at, :].astype(jnp.float32)
                other[at, :] = total.astype(other.dtype)
                return carry

            lax.fori_loop(0, rows // step, body, 0)
        for copy in to_corner(part):
            copy.start()
        to_neighbour(part, 1).start()
        to_neighbour(part, 2).start()

    def add_corner(part):
        copies = to_corner(part)
        pairs = (
            (copies[0], lane(part, y, 1 - x), corner_a.at[part], first),
            (copies[1], lane(part, 1 - y, x), corner_b.at[part], second),
        )
        for copy, mine, other, columns in pairs:
            copy.wait_recv()

            def body(i, carry):
                at = pl.ds(pl.multiple_of(i * step, step), step)
                total = mine[at, columns].astype(jnp.float32) + other[at, :].astype(jnp.float32)
                mine[at, columns] = total.astype(mine.dtype)
                return carry

            lax.fori_loop(0, rows // step, body, 0)
        to_neighbour(part, 0).start()
        to_neighbour(part, 3).start()

    def add_neighbours(part):
        for way in range(4):
            to_neighbour(part, way).wait_recv()
        last = not lines or part == parts - 1
        mine = lane(part, y, x)

        def body(i, carry):
            at = pl.ds(pl.multiple_of(i * step, step), step)
            total = mine[at, :].astype(jnp.float32) + from_side[part, at, :].astype(jnp.float32)
            total += from_over[part, at, :].astype(jnp.float32)
            if last:
                low = 0 if lines else part * rows
                o_ref[pl.ds(pl.multiple_of(low + i * step, step), step), :] = total.astype(o_ref.dtype)
            else:
                mine[at, :] = total.astype(mine.dtype)
            return carry

        lax.fori_loop(0, rows // step, body, 0)
        if not last:
            along_z(part).start()

    for part in range(parts):
        for copy in over_core(part):
            copy.start()
    for number in range(parts + 2):
        for stage, lag in ((add_core, 0), (add_corner, 1), (add_neighbours, 2)):
            if 0 <= number - lag < parts:
                stage(number - lag)
    if lines:
        for part in range(parts - 1):
            along_z(part).wait_recv()

        def body(i, carry):
            at = pl.ds(pl.multiple_of(i * step, step), step)
            total = o_ref[at, :]
            for part in range(parts - 1):
                total += along[part, at, :].astype(jnp.float32)
            o_ref[at, :] = total
            return carry

        lax.fori_loop(0, rows // step, body, 0)
        for part in range(parts - 1):
            along_z(part).wait_send()
    for part in range(parts):
        for copy in (*over_core(part), *to_corner(part), *(to_neighbour(part, way) for way in range(4))):
            copy.wait_send()


def reduced(values, lines, parts, identity, name):
    rows, width = values.shape[-2:]
    out_rows = rows
    if lines:
        parts = lines
    else:
        rows = rows // parts
    cut = column_cut(width)
    low = values.dtype
    return pl.pallas_call(
        functools.partial(reduce_kernel, parts, lines),
        out_shape=jax.ShapeDtypeStruct((out_rows, width), jnp.float32),
        in_specs=[pl.BlockSpec(memory_space=pltpu.VMEM)],
        out_specs=pl.BlockSpec(memory_space=pltpu.VMEM),
        scratch_shapes=[
            pltpu.VMEM((parts, 4, rows, width), low),
            pltpu.VMEM((parts, rows, cut), low),
            pltpu.VMEM((parts, rows, width - cut), low),
            pltpu.VMEM((parts, rows, width), low),
            pltpu.VMEM((parts, rows, width), low),
            pltpu.VMEM((max(lines - 1, 1), rows, width if lines else LANES), low),
            pltpu.SemaphoreType.DMA((parts, 11)),
            pltpu.SemaphoreType.DMA((parts, 11)),
        ],
        compiler_params=pltpu.CompilerParams(collective_id=identity, vmem_limit_bytes=VMEM_LIMIT),
        name=name,
    )(values)


def attend_kernel(scale, q_ref, k_ref, v_ref, low_ref, high_ref, place_ref, o_ref, p_ref):
    keys = k_ref[...].reshape(-1, HD)
    values = v_ref[...].reshape(-1, HD)
    rows = low_ref.shape[-2]
    place = place_ref[0]
    allowed = (place >= low_ref[0]) & (place <= high_ref[0])
    for group in range(q_ref.shape[0]):
        queries = q_ref[group].reshape(rows, HD)
        score = against(queries, keys) * scale
        score = jnp.where(allowed, score, masked_score)
        top = jnp.max(score, -1, keepdims=True)
        weight = jnp.exp(score - top)
        total = jnp.sum(weight, -1, keepdims=True)
        low = (weight * (1.0 / total)).astype(jnp.bfloat16)
        p_ref[group, 0, 0] = low
        out = jnp.dot(low, values, preferred_element_type=jnp.float32)
        o_ref[group] = out.astype(jnp.bfloat16).reshape(o_ref.shape[1:])


def attend_back_kernel(scale, q_ref, k_ref, v_ref, p_ref, do_ref, dq_ref, dk_ref, dv_ref, dk_sum, dv_sum):
    block = pl.program_id(1)
    keys = k_ref[...].reshape(-1, HD)
    values = v_ref[...].reshape(-1, HD)
    rows = p_ref.shape[-2]

    @pl.when(block == 0)
    def _():
        dk_sum[...] = jnp.zeros_like(dk_sum)
        dv_sum[...] = jnp.zeros_like(dv_sum)

    for group in range(q_ref.shape[0]):
        queries = q_ref[group].reshape(rows, HD)
        grads = do_ref[group].reshape(rows, HD)
        low = p_ref[group, 0, 0]
        prob = low.astype(jnp.float32)
        prob_grad = against(grads, values)
        delta = jnp.sum(prob * prob_grad, -1, keepdims=True)
        score_low = (prob * (prob_grad - delta)).astype(jnp.bfloat16)
        dq = jnp.dot(score_low, keys, preferred_element_type=jnp.float32) * scale
        dq_ref[group] = dq.reshape(dq_ref.shape[1:])
        dk_sum[...] += transposed(score_low, queries)
        dv_sum[...] += transposed(low, grads)

    @pl.when(block == pl.num_programs(1) - 1)
    def _():
        dk_ref[...] = (dk_sum[...] * scale).reshape(dk_ref.shape)
        dv_ref[...] = dv_sum[...].reshape(dv_ref.shape)


def plane_per_device(lines, *arrays):
    (
        tokens,
        lengths,
        deal,
        loss_mask,
        teacher,
        out_grad,
        attn_gain,
        w_query,
        w_key,
        w_value,
        w_out,
        ffn_gain,
        w_gate,
        w_up,
        w_down,
    ) = arrays
    count_ctx = lax.axis_size("ctx")
    devices = lines * PLANE
    myself = lax.axis_index("ctx")
    number = myself * lax.axis_size("fsdp") + lax.axis_index("fsdp")
    tok_rows, width = tokens.shape[1:]
    half_block = tok_rows // 2
    groups = HEADS // KV
    scale = HD ** (-0.5)
    weight_rows = w_query.shape[0]
    hidden_units = w_gate.shape[1]
    down_rows = w_down.shape[0]
    share = hidden_units // PLANE
    low = jnp.bfloat16
    z_lines = [[zz * 2 + yy for zz in range(lines)] for yy in range(2)]

    dealt = jnp.arange(count_ctx * tok_rows, dtype=jnp.int32)
    local = dealt % tok_rows
    first = jnp.repeat(deal[0], tok_rows)
    block = jnp.where(local < half_block, first, 2 * count_ctx - 1 - first)
    places = block * half_block + local % half_block
    ends = jnp.cumsum(lengths[0])
    after = (places[:, None] >= ends[None, :]).astype(jnp.int32)
    seg_all = jnp.sum(after, 1)
    start_all = jnp.sum(after * lengths[0][None, :], 1)
    own = lambda array: lax.dynamic_slice_in_dim(array, myself * tok_rows, tok_rows)
    own_seg = own(seg_all)
    cosine, sine = rotary_tables(own(places) - own(start_all))
    valid = (loss_mask[0] * (own_seg < NSEQ)).astype(jnp.float32)

    split_units = lambda w: jnp.transpose(
        w.reshape(weight_rows, lines, PLANE, down_rows), (2, 0, 1, 3)
    ).reshape(PLANE, weight_rows, share)
    gate_up = jnp.concatenate([split_units(w_gate), split_units(w_up)], -1)
    gate_up = exchange(gate_up, "plane", 1, "gate_up_share").reshape(PLANE * weight_rows, 2 * share)
    gate_up_w = lax.all_gather(gate_up, "ctx", axis=0, tiled=True, axis_index_groups=z_lines)
    down_w = lax.all_gather(w_down, "ctx", axis=0, tiled=True, axis_index_groups=z_lines)

    by_head = lambda w, heads: w.reshape(weight_rows, KV, heads * HD)
    qkv_rows = jnp.concatenate([by_head(w_query, groups), by_head(w_key, 1), by_head(w_value, 1)], -1)
    head_cols = (groups + 2) * HD
    qkv_cols = KV * head_cols
    extras = jnp.concatenate(
        [
            attn_gain[:, None],
            ffn_gain[:, None],
            jnp.broadcast_to(jnp.sum(valid).astype(low), (weight_rows, 1)),
            jnp.zeros((weight_rows, LANES - 3), low),
        ],
        -1,
    )
    attn_rows = jnp.concatenate([qkv_rows.reshape(weight_rows, qkv_cols), w_out, extras], -1)
    attn_all = gather_everywhere(attn_rows, lines, 2, "gather_weights")
    extras_all = attn_all[:, :, qkv_cols + width :]
    attn_all = attn_all.reshape(devices * weight_rows, -1)
    qkv_w = attn_all[:, :qkv_cols]
    out_w = attn_all[:, qkv_cols : qkv_cols + width]
    gain_first = extras_all[:, :, 0].reshape(-1).astype(jnp.float32)
    gain_second = extras_all[:, :, 1].reshape(-1).astype(jnp.float32)
    valid_count = jnp.sum(extras_all[:, 0, 2].astype(jnp.float32))

    inputs = tokens[0].astype(jnp.float32)
    scale_one = rms_scale(inputs)
    normed_one = inputs * scale_one
    normed_low = (normed_one * gain_first).astype(low)
    ones, zeros = jnp.ones_like(cosine), jnp.zeros_like(sine)
    cos_four = jnp.concatenate([cosine] * (groups + 1) + [ones], 1)[:, None]
    sin_four = jnp.concatenate([sine] * (groups + 1) + [zeros], 1)[:, None]
    qkv = jnp.dot(normed_low, qkv_w, preferred_element_type=jnp.float32)
    qkv = rotary(qkv.reshape(tok_rows, KV, groups + 2, HD), cos_four, sin_four).astype(low)
    qkv = jnp.transpose(qkv.reshape(tok_rows, KV, head_cols), (1, 0, 2))
    qkv = exchange(qkv, "ctx", 3, "heads_out")
    qkv = qkv.reshape(count_ctx, 2, half_block, groups + 2, HD)
    qkv = jnp.transpose(qkv, (3, 0, 1, 2, 4))
    queries, keys, values = qkv[:groups], qkv[groups], qkv[groups + 1]

    half = count_ctx * half_block
    per_half = lambda array: jnp.transpose(array.reshape(count_ctx, 2, half_block), (1, 0, 2)).reshape(2, half)
    place_half = per_half(places)
    low_half = jnp.where(per_half(seg_all) < NSEQ, per_half(start_all), place_half)
    blocks = 4
    sources = count_ctx // blocks
    rows = sources * half_block
    q_spec = pl.BlockSpec((groups, sources, 1, half_block, HD), lambda h, b: (0, b, h, 0, 0))
    k_spec = pl.BlockSpec((count_ctx, 1, half_block, HD), lambda h, b: (0, h, 0, 0))
    column_spec = pl.BlockSpec((1, rows, 1), lambda h, b: (h, b, 0))
    p_spec = pl.BlockSpec((groups, 1, 1, rows, half), lambda h, b: (0, h, b, 0, 0))
    attended, probs = pl.pallas_call(
        functools.partial(attend_kernel, scale),
        grid=(2, blocks),
        in_specs=[
            q_spec,
            k_spec,
            k_spec,
            column_spec,
            column_spec,
            pl.BlockSpec((1, 1, half), lambda h, b: (h, 0, 0)),
        ],
        out_specs=[q_spec, p_spec],
        out_shape=[
            jax.ShapeDtypeStruct(queries.shape, low),
            jax.ShapeDtypeStruct((groups, 2, blocks, rows, half), low),
        ],
        compiler_params=pltpu.CompilerParams(vmem_limit_bytes=VMEM_LIMIT),
        name="attend",
    )(queries, keys, values, low_half[:, :, None], place_half[:, :, None], place_half[:, None, :])
    to_rows = lambda array: jnp.transpose(array.reshape(groups, count_ctx, tok_rows, HD), (1, 2, 0, 3)).reshape(
        count_ctx, tok_rows, groups * HD
    )
    from_heads = lambda array: jnp.transpose(array, (1, 0, 2)).reshape(tok_rows, width)
    attended_low = from_heads(exchange(to_rows(attended), "ctx", 4, "heads_back"))

    hidden = inputs + jnp.dot(attended_low, out_w, preferred_element_type=jnp.float32)
    scale_two = rms_scale(hidden)
    normed_two = hidden * scale_two
    ffn_low = plane_gather((normed_two * gain_second).astype(low), 5, "gather_tokens").reshape(-1, width)
    both = jnp.dot(ffn_low, gate_up_w, preferred_element_type=jnp.float32)
    gate, up = both[:, :share], both[:, share:]
    sigmoid = jax.nn.sigmoid(gate)
    activated = gate * sigmoid
    mixed_low = (activated * up).astype(low)
    result = jnp.dot(mixed_low, down_w, preferred_element_type=jnp.float32).astype(low)
    result = hidden + reduced(result.reshape(PLANE, tok_rows, width), 0, 4, 6, "reduce_result")
    differ = result - teacher[0].astype(jnp.float32)
    square_sum = jnp.sum(valid[:, None] * differ * differ)
    out_total = out_grad[0].astype(jnp.float32) + 2.0 * valid[:, None] * differ / (valid_count * width)

    out_low = plane_gather(out_total.astype(low), 7, "gather_grads").reshape(-1, width)
    down_grad = transposed(mixed_low, out_low).astype(low)
    mixed_grad = against(out_low, down_w)
    silu_slope = sigmoid * (1.0 + gate * (1.0 - sigmoid))
    both_low = jnp.concatenate(
        [(mixed_grad * up * silu_slope).astype(low), (mixed_grad * activated).astype(low)], -1
    )
    both_grad = transposed(ffn_low, both_low).astype(low)
    normed_grad = against(both_low, gate_up_w).astype(low)
    down_final = lax.psum_scatter(
        down_grad, "ctx", scatter_dimension=0, tiled=True, axis_index_groups=z_lines
    ).astype(jnp.float32)
    both_final = lax.psum_scatter(both_grad, "ctx", scatter_dimension=0, tiled=True, axis_index_groups=z_lines)
    normed_grad = reduced(normed_grad.reshape(PLANE, tok_rows, width), 0, 4, 8, "reduce_grads")
    gain_two_grad = jnp.sum(normed_grad * normed_two, 0)
    scaled_two = normed_grad * gain_second
    hidden_grad = out_total + scale_two * (
        scaled_two - normed_two * jnp.mean(scaled_two * normed_two, -1, keepdims=True)
    )

    branch_low = hidden_grad.astype(low)
    out_w_grad = transposed(attended_low, branch_low)
    attended_grad = against(branch_low, out_w).astype(low)
    to_heads = lambda array: jnp.transpose(array.reshape(tok_rows, KV, -1), (1, 0, 2))
    attended_grad = exchange(to_heads(attended_grad), "ctx", 9, "grads_out")
    attended_grad = jnp.transpose(
        attended_grad.reshape(count_ctx, 2, half_block, groups, HD), (3, 0, 1, 2, 4)
    )
    query_grad, key_grad, value_grad = pl.pallas_call(
        functools.partial(attend_back_kernel, scale),
        grid=(2, blocks),
        in_specs=[q_spec, k_spec, k_spec, p_spec, q_spec],
        out_specs=[q_spec, k_spec, k_spec],
        out_shape=[
            jax.ShapeDtypeStruct(queries.shape, jnp.float32),
            jax.ShapeDtypeStruct(keys.shape, jnp.float32),
            jax.ShapeDtypeStruct(keys.shape, jnp.float32),
        ],
        scratch_shapes=[pltpu.VMEM((half, HD), jnp.float32)] * 2,
        compiler_params=pltpu.CompilerParams(vmem_limit_bytes=VMEM_LIMIT),
        name="attend_back",
    )(queries, keys, values, probs, attended_grad)
    qkv_grad = jnp.concatenate([query_grad, key_grad[None], value_grad[None]], 0)
    qkv_grad = jnp.transpose(qkv_grad.reshape(groups + 2, count_ctx, tok_rows, HD), (1, 2, 0, 3))
    qkv_grad = exchange(qkv_grad.astype(low).reshape(count_ctx, tok_rows, head_cols), "ctx", 10, "grads_back")
    qkv_grad = jnp.transpose(qkv_grad, (1, 0, 2)).reshape(tok_rows, KV, groups + 2, HD)
    qkv_grad = rotary_back(qkv_grad.astype(jnp.float32), cos_four, sin_four)
    qkv_grad = qkv_grad.astype(low).reshape(tok_rows, qkv_cols)
    normed_one_grad = against(qkv_grad, qkv_w)
    qkv_w_grad = transposed(normed_low, qkv_grad)
    gain_one_grad = jnp.sum(normed_one_grad * normed_one, 0)
    scaled_one = normed_one_grad * gain_first
    input_grad = hidden_grad + scale_one * (
        scaled_one - normed_one * jnp.mean(scaled_one * normed_one, -1, keepdims=True)
    )

    top = square_sum.astype(low)
    rest = square_sum - top.astype(jnp.float32)
    middle = rest.astype(low)
    bottom = (rest - middle.astype(jnp.float32)).astype(low)
    terms = jnp.where(jnp.arange(devices) == number, jnp.stack([top, middle, bottom])[:, None], jnp.zeros((), low))
    terms = jnp.broadcast_to(terms.reshape(1, -1), (width, 3 * devices))
    pad = jnp.zeros((width, LANES - 2 - 3 * devices), low)
    attn_grads = jnp.concatenate(
        [
            qkv_w_grad.astype(low),
            out_w_grad.astype(low),
            gain_one_grad.astype(low)[:, None],
            gain_two_grad.astype(low)[:, None],
            terms,
            pad,
        ],
        -1,
    )
    final = reduced(attn_grads.reshape(lines, PLANE, weight_rows, -1), lines, lines, 11, "reduce_weights")
    qkv_final = final[:, :qkv_cols].reshape(weight_rows, KV, head_cols)
    cuts = (groups * HD, (groups + 1) * HD)
    pieces = [qkv_final[..., : cuts[0]], qkv_final[..., cuts[0] : cuts[1]], qkv_final[..., cuts[1] :]]
    query_final, key_final, value_final = [piece.reshape(weight_rows, -1) for piece in pieces]
    out_final = final[:, qkv_cols : qkv_cols + width]
    tail = final[:, qkv_cols + width :]
    loss = jnp.sum(tail[0, 2 : 2 + 3 * devices]) / (valid_count * width)

    both_final = exchange(both_final.reshape(PLANE, weight_rows, 2 * share), "plane", 12, "gate_up_grads")
    both_final = both_final.reshape(PLANE, weight_rows, 2, lines, down_rows).astype(jnp.float32)
    gate_final, up_final = [
        jnp.transpose(both_final[:, :, i], (1, 2, 0, 3)).reshape(weight_rows, hidden_units) for i in range(2)
    ]
    return (
        result.astype(low)[None],
        loss,
        input_grad[None],
        tail[:, 0],
        query_final,
        key_final,
        value_final,
        out_final,
        tail[:, 1],
        gate_final,
        up_final,
        down_final,
    )


def suits_planes(mesh):
    sizes = dict(mesh.shape)
    return sizes["fsdp"] == 4 and sizes["ctx"] == KV


def solution(mesh):
    placed = (
        P("fsdp", "ctx", None),
        P("fsdp", None),
        P("fsdp", None),
        P("fsdp", "ctx"),
        P("fsdp", "ctx", None),
        P("fsdp", "ctx", None),
        P(("ctx", "fsdp")),
        P(("ctx", "fsdp"), None),
        P(("ctx", "fsdp"), None),
        P(("ctx", "fsdp"), None),
        P(("ctx", "fsdp"), None),
        P(("ctx", "fsdp")),
        P(("ctx", "fsdp"), None),
        P(("ctx", "fsdp"), None),
        P(("ctx", "fsdp"), None),
    )
    if suits_planes(mesh):
        per_device = functools.partial(plane_per_device, mesh.shape["ctx"] // ROWS_Y)
    else:
        per_device = ring_per_device
    return jax.shard_map(
        per_device,
        mesh=mesh,
        in_specs=placed,
        out_specs=(
            P("fsdp", "ctx", None),
            P(),
            P("fsdp", "ctx", None),
            P(("ctx", "fsdp")),
            P(("ctx", "fsdp"), None),
            P(("ctx", "fsdp"), None),
            P(("ctx", "fsdp"), None),
            P(("ctx", "fsdp"), None),
            P(("ctx", "fsdp")),
            P(("ctx", "fsdp"), None),
            P(("ctx", "fsdp"), None),
            P(("ctx", "fsdp"), None),
        ),
        check_vma=False,
    )
```

```python
import functools

import jax
import jax.numpy as jnp
from jax import lax
from jax.experimental import pallas as pl
from jax.experimental.pallas import tpu as pltpu
from jax.sharding import PartitionSpec as P

HEADS = 16
KV = 8
HD = 96
NSEQ = 6


rope_base = 100000.0
epsilon = 1e-05
masked_score = -1e30


def shifted(value, axis, by):
    size = lax.axis_size(axis)
    return lax.ppermute(value, axis, [(i, (i + by) % size) for i in range(size)])


def rms_scale(values):
    return lax.rsqrt(jnp.mean(values * values, -1, keepdims=True) + epsilon)


def rotary_tables(inseq):
    freq = rope_base ** (-(jnp.arange(HD // 2, dtype=jnp.float32) * 2.0 / HD))
    angle = inseq.astype(jnp.float32)[:, None] * freq[None, :]
    return (jnp.cos(angle)[:, None, :], jnp.sin(angle)[:, None, :])


def rotary(values, cosine, sine):
    half = values.shape[-1] // 2
    first = values[..., :half]
    second = values[..., half:]
    return jnp.concatenate([first * cosine - second * sine, second * cosine + first * sine], -1)


def rotary_back(grads, cosine, sine):
    half = grads.shape[-1] // 2
    first = grads[..., :half]
    second = grads[..., half:]
    return jnp.concatenate([first * cosine + second * sine, second * cosine - first * sine], -1)


def transposed(left, right):
    return lax.dot_general(
        left, right, (((0,), (0,)), ((), ())), preferred_element_type=jnp.float32
    )


def against(left, right):
    return lax.dot_general(
        left, right, (((1,), (1,)), ((), ())), preferred_element_type=jnp.float32
    )


def permitted(query_place, query_seg, key_place, key_seg):
    same = (query_seg[:, None] == key_seg[None, :]) & (query_seg[:, None] < NSEQ)
    return same & (key_place[None, :] <= query_place[:, None]) | (
        key_place[None, :] == query_place[:, None]
    )


def ring_per_device(
    tokens,
    lengths,
    deal,
    loss_mask,
    teacher,
    out_grad,
    attn_gain,
    w_query,
    w_key,
    w_value,
    w_out,
    ffn_gain,
    w_gate,
    w_up,
    w_down,
):
    count_ctx = lax.axis_size("ctx")
    myself = lax.axis_index("ctx")
    tok_rows = tokens.shape[1]
    width = tokens.shape[2]
    half_block = tok_rows // 2
    groups = HEADS // KV
    scale = HD ** (-0.5)
    gain_one, query_w, key_w, value_w, out_w = (
        lax.all_gather(attn_gain, ("ctx", "fsdp"), axis=0, tiled=True),
        lax.all_gather(w_query, ("ctx", "fsdp"), axis=0, tiled=True),
        lax.all_gather(w_key, ("ctx", "fsdp"), axis=0, tiled=True),
        lax.all_gather(w_value, ("ctx", "fsdp"), axis=0, tiled=True),
        lax.all_gather(w_out, ("ctx", "fsdp"), axis=0, tiled=True),
    )
    gain_two, gate_w, up_w, down_w = (
        lax.all_gather(ffn_gain, ("ctx", "fsdp"), axis=0, tiled=True),
        lax.all_gather(w_gate, ("ctx", "fsdp"), axis=0, tiled=True),
        lax.all_gather(w_up, ("ctx", "fsdp"), axis=0, tiled=True),
        lax.all_gather(w_down, ("ctx", "fsdp"), axis=0, tiled=True),
    )
    dealt = jnp.arange(count_ctx * tok_rows, dtype=jnp.int32)
    local = dealt % tok_rows
    first = jnp.repeat(deal[0], tok_rows)
    block = jnp.where(local < half_block, first, 2 * count_ctx - 1 - first)
    places = block * half_block + local % half_block
    ends = jnp.cumsum(lengths[0])
    after = (places[:, None] >= ends[None, :]).astype(jnp.int32)
    seg_all = jnp.sum(after, 1)
    inseq_all = places - jnp.sum(after * lengths[0][None, :], 1)
    own_place = lax.dynamic_slice_in_dim(places, myself * tok_rows, tok_rows)
    own_seg = lax.dynamic_slice_in_dim(seg_all, myself * tok_rows, tok_rows)
    own_inseq = lax.dynamic_slice_in_dim(inseq_all, myself * tok_rows, tok_rows)
    cosine, sine = rotary_tables(own_inseq)
    inputs = tokens[0].astype(jnp.float32)
    scale_one = rms_scale(inputs)
    normed_one = inputs * scale_one
    gain_first = gain_one.astype(jnp.float32)
    normed_low = (normed_one * gain_first).astype(jnp.bfloat16)
    query_pre = jnp.dot(normed_low, query_w, preferred_element_type=jnp.float32).reshape(
        tok_rows, HEADS, HD
    )
    key_pre = jnp.dot(normed_low, key_w, preferred_element_type=jnp.float32).reshape(
        tok_rows, KV, HD
    )
    value_low = jnp.dot(normed_low, value_w, preferred_element_type=jnp.float32).astype(
        jnp.bfloat16
    )
    queries = rotary(query_pre, cosine, sine).astype(jnp.bfloat16).reshape(tok_rows, KV, groups, HD)
    keys = rotary(key_pre, cosine, sine).astype(jnp.bfloat16).reshape(tok_rows, KV * HD)

    def logits(key_block):
        return (
            jnp.einsum(
                "qcgd,kcd->cgqk",
                queries,
                key_block.reshape(-1, KV, HD),
                preferred_element_type=jnp.float32,
            )
            * scale
        )

    key_block = lax.all_gather(keys, "ctx", axis=0, tiled=True)
    value_block = lax.all_gather(value_low, "ctx", axis=0, tiled=True)
    allowed = permitted(own_place, own_seg, places, seg_all)
    top = jnp.full((KV, groups, tok_rows, 1), masked_score, jnp.float32)
    score = jnp.where(allowed, logits(key_block), masked_score)
    new_top = jnp.maximum(top, jnp.max(score, -1, keepdims=True))
    weight = jnp.where(allowed, jnp.exp(score - new_top), 0.0)
    summed = jnp.einsum(
        "cgqk,kcd->cgqd",
        weight.astype(jnp.bfloat16),
        value_block.reshape(-1, KV, HD),
        preferred_element_type=jnp.float32,
    )
    summed, top, total = (summed, new_top, jnp.sum(weight, -1, keepdims=True))
    attended = summed / total
    log_total = top + jnp.log(total)
    attended_low = (
        jnp.transpose(attended, (2, 0, 1, 3)).reshape(tok_rows, HEADS * HD).astype(jnp.bfloat16)
    )
    hidden = inputs + jnp.dot(attended_low, out_w, preferred_element_type=jnp.float32)
    scale_two = rms_scale(hidden)
    normed_two = hidden * scale_two
    gain_second = gain_two.astype(jnp.float32)
    ffn_low = (normed_two * gain_second).astype(jnp.bfloat16)
    gate = jnp.dot(ffn_low, gate_w, preferred_element_type=jnp.float32)
    up = jnp.dot(ffn_low, up_w, preferred_element_type=jnp.float32)
    sigmoid = jax.nn.sigmoid(gate)
    activated = gate * sigmoid
    mixed_low = (activated * up).astype(jnp.bfloat16)
    result = hidden + jnp.dot(mixed_low, down_w, preferred_element_type=jnp.float32)
    target = teacher[0].astype(jnp.float32)
    valid = (loss_mask[0] * (own_seg < NSEQ)).astype(jnp.float32)[:, None]
    differ = result - target
    square_sum, valid_count = lax.psum(
        (jnp.sum(valid * differ * differ), jnp.sum(valid)), ("ctx", "fsdp")
    )
    loss = square_sum / (valid_count * width)
    out_total = out_grad[0].astype(jnp.float32) + 2.0 * valid * differ / (valid_count * width)
    out_low = out_total.astype(jnp.bfloat16)
    down_grad = transposed(mixed_low, out_low)
    mixed_grad = against(out_low, down_w)
    silu_slope = sigmoid * (1.0 + gate * (1.0 - sigmoid))
    gate_low = (mixed_grad * up * silu_slope).astype(jnp.bfloat16)
    up_low = (mixed_grad * activated).astype(jnp.bfloat16)
    gate_grad = transposed(ffn_low, gate_low)
    up_grad = transposed(ffn_low, up_low)
    normed_grad = against(gate_low, gate_w) + against(up_low, up_w)
    gain_two_grad = jnp.sum(normed_grad * normed_two, 0)
    scaled_two = normed_grad * gain_second
    hidden_grad = out_total + scale_two * (
        scaled_two - normed_two * jnp.mean(scaled_two * normed_two, -1, keepdims=True)
    )
    ffn_final = (
        lax.psum_scatter(gain_two_grad, ("ctx", "fsdp"), scatter_dimension=0, tiled=True),
        lax.psum_scatter(gate_grad, ("ctx", "fsdp"), scatter_dimension=0, tiled=True),
        lax.psum_scatter(up_grad, ("ctx", "fsdp"), scatter_dimension=0, tiled=True),
        lax.psum_scatter(down_grad, ("ctx", "fsdp"), scatter_dimension=0, tiled=True),
    )
    branch_low = hidden_grad.astype(jnp.bfloat16)
    out_w_grad = transposed(attended_low, branch_low)
    attended_grad = against(branch_low, out_w).astype(jnp.bfloat16)
    grad_heads = jnp.transpose(attended_grad.reshape(tok_rows, KV, groups, HD), (1, 2, 0, 3))
    delta = jnp.sum(grad_heads.astype(jnp.float32) * attended, -1, keepdims=True)

    def cycle_step(step, state):
        key_block, value_block, key_acc, value_acc, query_acc = state
        source = (myself - step) % count_ctx
        allowed = permitted(
            own_place,
            own_seg,
            lax.dynamic_slice_in_dim(places, source * tok_rows, tok_rows),
            lax.dynamic_slice_in_dim(seg_all, source * tok_rows, tok_rows),
        )
        current_key = key_block
        current_value = value_block
        keys_three = current_key.reshape(tok_rows, KV, HD)
        values_three = current_value.reshape(tok_rows, KV, HD)
        prob = jnp.where(allowed, jnp.exp(logits(current_key) - log_total), 0.0)
        prob_grad = jnp.einsum(
            "cgqd,kcd->cgqk", grad_heads, values_three, preferred_element_type=jnp.float32
        )
        score_low = (prob * (prob_grad - delta)).astype(jnp.bfloat16)
        query_add = (
            jnp.einsum("cgqk,kcd->cgqd", score_low, keys_three, preferred_element_type=jnp.float32)
            * scale
        )
        key_add = (
            jnp.einsum(
                "cgqk,qcgd->kcd", score_low, queries, preferred_element_type=jnp.float32
            ).reshape(tok_rows, KV * HD)
            * scale
        )
        value_add = jnp.einsum(
            "cgqk,cgqd->kcd",
            prob.astype(jnp.bfloat16),
            grad_heads,
            preferred_element_type=jnp.float32,
        ).reshape(tok_rows, KV * HD)
        key_block, value_block = shifted((key_block, value_block), "ctx", 1)
        key_acc, value_acc = (
            shifted((key_acc + key_add).astype(jnp.bfloat16), "ctx", 1).astype(jnp.float32),
            shifted((value_acc + value_add).astype(jnp.bfloat16), "ctx", 1).astype(jnp.float32),
        )
        return (key_block, value_block, key_acc, value_acc, query_acc + query_add)

    cycle_start = (
        keys,
        value_low,
        jnp.zeros((tok_rows, KV * HD), jnp.float32),
        jnp.zeros((tok_rows, KV * HD), jnp.float32),
        jnp.zeros((KV, groups, tok_rows, HD), jnp.float32),
    )
    cycle_end = lax.fori_loop(0, count_ctx, cycle_step, cycle_start)
    key_acc = cycle_end[2]
    value_acc = cycle_end[3]
    query_acc = cycle_end[4]
    query_grad = jnp.transpose(query_acc, (2, 0, 1, 3)).reshape(tok_rows, HEADS, HD)
    query_low = (
        rotary_back(query_grad, cosine, sine).reshape(tok_rows, HEADS * HD).astype(jnp.bfloat16)
    )
    key_low = (
        rotary_back(key_acc.reshape(tok_rows, KV, HD), cosine, sine)
        .reshape(tok_rows, KV * HD)
        .astype(jnp.bfloat16)
    )
    value_grad_low = value_acc.astype(jnp.bfloat16)
    query_w_grad = transposed(normed_low, query_low)
    key_w_grad = transposed(normed_low, key_low)
    value_w_grad = transposed(normed_low, value_grad_low)
    normed_one_grad = (
        against(query_low, query_w) + against(key_low, key_w) + against(value_grad_low, value_w)
    )
    gain_one_grad = jnp.sum(normed_one_grad * normed_one, 0)
    scaled_one = normed_one_grad * gain_first
    input_grad = hidden_grad + scale_one * (
        scaled_one - normed_one * jnp.mean(scaled_one * normed_one, -1, keepdims=True)
    )
    attn_final = (
        lax.psum_scatter(gain_one_grad, ("ctx", "fsdp"), scatter_dimension=0, tiled=True),
        lax.psum_scatter(query_w_grad, ("ctx", "fsdp"), scatter_dimension=0, tiled=True),
        lax.psum_scatter(key_w_grad, ("ctx", "fsdp"), scatter_dimension=0, tiled=True),
        lax.psum_scatter(value_w_grad, ("ctx", "fsdp"), scatter_dimension=0, tiled=True),
        lax.psum_scatter(out_w_grad, ("ctx", "fsdp"), scatter_dimension=0, tiled=True),
    )
    return (
        result.astype(jnp.bfloat16)[None],
        loss,
        input_grad[None],
        attn_final[0],
        attn_final[1],
        attn_final[2],
        attn_final[3],
        attn_final[4],
        ffn_final[0],
        ffn_final[1],
        ffn_final[2],
        ffn_final[3],
    )


MESH = pl.DeviceIdType.MESH
ROWS_Y = 2
PLANE = 8
LANES = 128
VMEM_LIMIT = 60 * 2**20


def coordinates():
    ctx = lax.axis_index("ctx")
    fsdp = lax.axis_index("fsdp")
    return ctx // 2, ctx % 2, fsdp // 2, fsdp % 2


def device(z, y, x, c):
    return (z * 2 + y, x * 2 + c)


def greet(devices):
    barrier = pltpu.get_barrier_semaphore()
    for other in devices:
        pl.semaphore_signal(barrier, inc=1, device_id=other, device_id_type=MESH)
    pl.semaphore_wait(barrier, len(devices))


def remote(src, dst, send, recv, target):
    return pltpu.make_async_remote_copy(
        src_ref=src,
        dst_ref=dst,
        send_sem=send,
        recv_sem=recv,
        device_id=target,
        device_id_type=MESH,
    )


def exchange_kernel(group, count, x_ref, o_ref, send, recv, here):
    z, y, x, c = coordinates()
    if group == "ctx":
        me = z * 2 + y
        to_device = lambda i: (i, x * 2 + c)
    else:
        me = y * 4 + x * 2 + c
        to_device = lambda i: (z * 2 + i // 4, i % 4)
    others = [lax.rem(me + k, count) for k in range(1, count)]
    greet([to_device(i) for i in others])
    copies = [
        remote(x_ref.at[i], o_ref.at[me], send.at[k], recv.at[k], to_device(i))
        for k, i in enumerate(others)
    ]
    for copy in copies:
        copy.start()
    own = pltpu.make_async_copy(x_ref.at[me], o_ref.at[me], here)
    own.start()
    own.wait()
    for copy in copies:
        copy.wait()


def exchange(values, group, identity, name):
    count = values.shape[0]
    return pl.pallas_call(
        functools.partial(exchange_kernel, group, count),
        out_shape=jax.ShapeDtypeStruct(values.shape, values.dtype),
        in_specs=[pl.BlockSpec(memory_space=pl.ANY)],
        out_specs=pl.BlockSpec(memory_space=pl.ANY),
        scratch_shapes=[
            pltpu.SemaphoreType.DMA((count - 1,)),
            pltpu.SemaphoreType.DMA((count - 1,)),
            pltpu.SemaphoreType.DMA,
        ],
        compiler_params=pltpu.CompilerParams(collective_id=identity),
        name=name,
    )(values)


def column_cut(width):
    tiles = width // LANES
    return (tiles + 1) // 2 * LANES


def gather_kernel(lines, x_ref, o_ref, send, recv, here):
    z, y, x, c = coordinates()
    width = x_ref.shape[1]
    cut = column_cut(width)
    first, second = pl.ds(0, cut), pl.ds(cut, width - cut)
    side, over, sibling = device(z, y, 1 - x, c), device(z, 1 - y, x, c), device(z, y, x, 1 - c)
    above, below = device(z + 1, y, x, c), device(z - 1, y, x, c)
    greet([side, over, sibling] + [device(lax.rem(z + k, lines), y, x, c) for k in range(1, lines)])
    slot = lambda zz, yy, xx, cc: (zz * 2 + yy) * 4 + xx * 2 + cc
    mine = pltpu.make_async_copy(x_ref, o_ref.at[slot(z, y, x, c)], here)
    mine.start()

    def item(sign, s):
        index = 0 if s == 0 else (2 * s - 1 if sign < 0 else 2 * s)
        zz = z + sign * s
        at = lambda yy, xx, cc: o_ref.at[slot(zz, yy, xx, cc)]
        own = x_ref if s == 0 else at(y, x, c)
        make = lambda kind, src, dst, to: remote(
            src, dst, send.at[index, kind], recv.at[index, kind], to
        )
        same = lambda kind, ref, to: make(kind, ref, ref, to)
        corner_at = lambda columns: at(1 - y, 1 - x, c).at[:, columns]
        return dict(
            side=lambda: make(1, own, at(y, x, c), side),
            over=lambda: make(2, own, at(y, x, c), over),
            side_on=lambda: same(3, at(y, 1 - x, c).at[:, first], over),
            over_on=lambda: same(4, at(1 - y, x, c).at[:, second], side),
            core=lambda: make(5, own, at(y, x, c), sibling),
            core_side=lambda: same(6, at(y, 1 - x, c), sibling),
            core_over=lambda: same(7, at(1 - y, x, c), sibling),
            core_first=lambda: same(8, corner_at(first), sibling),
            core_second=lambda: same(9, corner_at(second), sibling),
        )

    def along(sign, s):
        index = 2 * s - 1 if sign < 0 else 2 * s
        zz = z + sign * (s - 1)
        src = x_ref if s == 1 else o_ref.at[slot(zz, y, x, c)]
        return remote(
            src, o_ref.at[slot(zz, y, x, c)], send.at[index, 0], recv.at[index, 0], above if sign < 0 else below
        )

    def sends_along(sign, s):
        if sign < 0:
            return (z - (s - 1) >= 0) & (z + 1 < lines)
        return (z + (s - 1) < lines) & (z - 1 >= 0)

    def present(sign, s):
        return z - s >= 0 if sign < 0 else z + s < lines

    arrivals = [(-1, 0)] + [(sign, s) for s in range(1, lines) for sign in (-1, 1)]

    def begin(sign, s):
        copies = item(sign, s)
        if s > 0:
            along(sign, s).wait_recv()
        for way in ((-1, 1) if s == 0 else (sign,)):
            if s + 1 < lines:
                @pl.when(sends_along(way, s + 1))
                def _():
                    along(way, s + 1).start()
        copies["side"]().start()
        copies["over"]().start()
        copies["core"]().start()

    def pass_on(sign, s):
        copies = item(sign, s)
        copies["side"]().wait_recv()
        copies["side_on"]().start()
        copies["core_side"]().start()
        copies["over"]().wait_recv()
        copies["over_on"]().start()
        copies["core_over"]().start()

    def corner(sign, s):
        copies = item(sign, s)
        copies["side_on"]().wait_recv()
        copies["core_first"]().start()
        copies["over_on"]().wait_recv()
        copies["core_second"]().start()

    def finish(sign, s):
        copies = item(sign, s)
        for kind in ("core", "core_side", "core_over", "core_first", "core_second"):
            copies[kind]().wait()
        for kind in ("side", "over", "side_on", "over_on"):
            copies[kind]().wait_send()

    def where(sign, s, step):
        if s == 0:
            step(sign, s)
        else:
            pl.when(present(sign, s))(functools.partial(step, sign, s))

    waves = [[(-1, 0)]] + [[(-1, s), (1, s)] for s in range(1, lines)]
    for number in range(len(waves) + 2):
        for stage, lag in ((begin, 0), (pass_on, 1), (corner, 2)):
            if 0 <= number - lag < len(waves):
                for sign, s in waves[number - lag]:
                    where(sign, s, stage)
    for sign, s in arrivals:
        where(sign, s, finish)
    for s in range(1, lines):
        for sign in (-1, 1):
            @pl.when(sends_along(sign, s))
            def _():
                along(sign, s).wait_send()
    mine.wait()


def gather_everywhere(rows, lines, identity, name):
    return pl.pallas_call(
        functools.partial(gather_kernel, lines),
        out_shape=jax.ShapeDtypeStruct((lines * PLANE,) + rows.shape, rows.dtype),
        in_specs=[pl.BlockSpec(memory_space=pl.ANY)],
        out_specs=pl.BlockSpec(memory_space=pl.ANY),
        scratch_shapes=[
            pltpu.SemaphoreType.DMA((2 * lines - 1, 10)),
            pltpu.SemaphoreType.DMA((2 * lines - 1, 10)),
            pltpu.SemaphoreType.DMA,
        ],
        compiler_params=pltpu.CompilerParams(collective_id=identity),
        name=name,
    )(rows)


def reduce_kernel(parts, lines, p_ref, o_ref, held, corner_a, corner_b, from_side, from_over, along, send, recv):
    z, y, x, c = coordinates()
    rows, width = held.shape[2], held.shape[3]
    cut = column_cut(width)
    first, second = pl.ds(0, cut), pl.ds(cut, width - cut)
    side, over, sibling = device(z, y, 1 - x, c), device(z, 1 - y, x, c), device(z, y, x, 1 - c)
    neighbours = [side, over, sibling]
    if lines:
        neighbours += [device(lax.rem(z + k, lines), y, x, c) for k in range(1, lines)]
    greet(neighbours)

    def given(part, yy, xx, cc):
        member = yy * 4 + xx * 2 + cc
        if lines:
            return p_ref.at[lax.rem(z + part + 1, lines), member]
        return p_ref.at[member, pl.ds(part * rows, rows)]

    def make(part, kind, src, dst, to):
        return remote(src, dst, send.at[part, kind], recv.at[part, kind], to)

    lane = lambda part, yy, xx: held.at[part, yy * 2 + xx]

    def over_core(part):
        return [
            make(part, yy * 2 + xx, given(part, yy, xx, 1 - c), lane(part, yy, xx), sibling)
            for yy in range(2)
            for xx in range(2)
        ]

    def to_corner(part):
        return (
            make(part, 4, lane(part, 1 - y, 1 - x).at[:, first], corner_a.at[part], over),
            make(part, 5, lane(part, 1 - y, 1 - x).at[:, second], corner_b.at[part], side),
        )

    def to_neighbour(part, way):
        columns = (first, second)[way % 2]
        if way < 2:
            return make(part, 6 + way, lane(part, y, 1 - x).at[:, columns], from_side.at[part, :, columns], side)
        return make(part, 6 + way, lane(part, 1 - y, x).at[:, columns], from_over.at[part, :, columns], over)

    def along_z(part):
        to = lax.rem(z + part + 1, lines)
        return make(part, 10, lane(part, y, x), along.at[part], device(to, y, x, c))

    step = 16

    def add_core(part):
        for copy in over_core(part):
            copy.wait_recv()
        for yy, xx in ((1 - y, 1 - x), (y, 1 - x), (1 - y, x), (y, x)):
            mine, other = given(part, yy, xx, c), lane(part, yy, xx)

            def body(i, carry):
                at = pl.ds(pl.multiple_of(i * step, step), step)
                total = mine[at, :].astype(jnp.float32) + other[at, :].astype(jnp.float32)
                other[at, :] = total.astype(other.dtype)
                return carry

            lax.fori_loop(0, rows // step, body, 0)
        for copy in to_corner(part):
            copy.start()
        to_neighbour(part, 1).start()
        to_neighbour(part, 2).start()

    def add_corner(part):
        copies = to_corner(part)
        pairs = (
            (copies[0], lane(part, y, 1 - x), corner_a.at[part], first),
            (copies[1], lane(part, 1 - y, x), corner_b.at[part], second),
        )
        for copy, mine, other, columns in pairs:
            copy.wait_recv()

            def body(i, carry):
                at = pl.ds(pl.multiple_of(i * step, step), step)
                total = mine[at, columns].astype(jnp.float32) + other[at, :].astype(jnp.float32)
                mine[at, columns] = total.astype(mine.dtype)
                return carry

            lax.fori_loop(0, rows // step, body, 0)
        to_neighbour(part, 0).start()
        to_neighbour(part, 3).start()

    def add_neighbours(part):
        for way in range(4):
            to_neighbour(part, way).wait_recv()
        last = not lines or part == parts - 1
        mine = lane(part, y, x)

        def body(i, carry):
            at = pl.ds(pl.multiple_of(i * step, step), step)
            total = mine[at, :].astype(jnp.float32) + from_side[part, at, :].astype(jnp.float32)
            total += from_over[part, at, :].astype(jnp.float32)
            if last:
                low = 0 if lines else part * rows
                o_ref[pl.ds(pl.multiple_of(low + i * step, step), step), :] = total.astype(o_ref.dtype)
            else:
                mine[at, :] = total.astype(mine.dtype)
            return carry

        lax.fori_loop(0, rows // step, body, 0)
        if not last:
            along_z(part).start()

    for part in range(parts):
        for copy in over_core(part):
            copy.start()
    for number in range(parts + 2):
        for stage, lag in ((add_core, 0), (add_corner, 1), (add_neighbours, 2)):
            if 0 <= number - lag < parts:
                stage(number - lag)
    if lines:
        for part in range(parts - 1):
            along_z(part).wait_recv()

        def body(i, carry):
            at = pl.ds(pl.multiple_of(i * step, step), step)
            total = o_ref[at, :]
            for part in range(parts - 1):
                total += along[part, at, :].astype(jnp.float32)
            o_ref[at, :] = total
            return carry

        lax.fori_loop(0, rows // step, body, 0)
        for part in range(parts - 1):
            along_z(part).wait_send()
    for part in range(parts):
        for copy in (*over_core(part), *to_corner(part), *(to_neighbour(part, way) for way in range(4))):
            copy.wait_send()


def reduced(values, lines, parts, identity, name):
    rows, width = values.shape[-2:]
    out_rows = rows
    if lines:
        parts = lines
    else:
        rows = rows // parts
    cut = column_cut(width)
    low = values.dtype
    return pl.pallas_call(
        functools.partial(reduce_kernel, parts, lines),
        out_shape=jax.ShapeDtypeStruct((out_rows, width), jnp.float32),
        in_specs=[pl.BlockSpec(memory_space=pltpu.VMEM)],
        out_specs=pl.BlockSpec(memory_space=pltpu.VMEM),
        scratch_shapes=[
            pltpu.VMEM((parts, 4, rows, width), low),
            pltpu.VMEM((parts, rows, cut), low),
            pltpu.VMEM((parts, rows, width - cut), low),
            pltpu.VMEM((parts, rows, width), low),
            pltpu.VMEM((parts, rows, width), low),
            pltpu.VMEM((max(lines - 1, 1), rows, width if lines else LANES), low),
            pltpu.SemaphoreType.DMA((parts, 11)),
            pltpu.SemaphoreType.DMA((parts, 11)),
        ],
        compiler_params=pltpu.CompilerParams(collective_id=identity, vmem_limit_bytes=VMEM_LIMIT),
        name=name,
    )(values)


def halves(width):
    cut = column_cut(width)
    return pl.ds(0, cut), pl.ds(cut, width - cut)


def gather_steps(place, whole, send, recv):
    z, y, x, c = place
    side, over, sibling = device(z, y, 1 - x, c), device(z, 1 - y, x, c), device(z, y, x, 1 - c)
    first, second = halves(whole.shape[-1])
    at = lambda yy, xx: whole.at[yy * 4 + xx * 2 + c]
    own, next_x, next_y, corner = at(y, x), at(y, 1 - x), at(1 - y, x), at(1 - y, 1 - x)
    table = (
        (own.at[:, first], side),
        (own.at[:, second], side),
        (own.at[:, first], over),
        (own.at[:, second], over),
        (own, sibling),
        (next_x.at[:, first], over),
        (next_y.at[:, second], side),
        (next_x.at[:, first], sibling),
        (next_x.at[:, second], sibling),
        (next_y.at[:, first], sibling),
        (next_y.at[:, second], sibling),
        (corner.at[:, first], sibling),
        (corner.at[:, second], sibling),
    )

    def copy(kind):
        ref, to = table[kind]
        return remote(ref, ref, send.at[kind], recv.at[kind], to)

    return copy


GATHER_KINDS = 13
REDUCE_KINDS = 10


def reduce_steps(place, partial, held, corner_a, corner_b, from_side, from_over, send, recv):
    z, y, x, c = place
    side, over, sibling = device(z, y, 1 - x, c), device(z, 1 - y, x, c), device(z, y, x, 1 - c)
    first, second = halves(held.shape[-1])
    lane = lambda yy, xx: held.at[yy * 2 + xx]
    next_x, next_y, corner = lane(y, 1 - x), lane(1 - y, x), lane(1 - y, 1 - x)

    def to_core(yy, xx):
        kind = yy * 2 + xx
        src = partial.at[yy * 4 + xx * 2 + 1 - c]
        return remote(src, lane(yy, xx), send.at[kind], recv.at[kind], sibling)

    table = (
        (corner.at[:, first], corner_a, over),
        (corner.at[:, second], corner_b, side),
        (next_x.at[:, first], from_side.at[:, first], side),
        (next_x.at[:, second], from_side.at[:, second], side),
        (next_y.at[:, first], from_over.at[:, first], over),
        (next_y.at[:, second], from_over.at[:, second], over),
    )

    def copy(kind):
        src, dst, to = table[kind]
        return remote(src, dst, send.at[4 + kind], recv.at[4 + kind], to)

    return to_core, copy


def add_rows(target, other, columns=None, step=32):
    def body(i, carry):
        at = pl.ds(pl.multiple_of(i * step, step), step)
        mine = target[at, :] if columns is None else target[at, columns]
        total = (mine.astype(jnp.float32) + other[at, :].astype(jnp.float32)).astype(target.dtype)
        if columns is None:
            target[at, :] = total
        else:
            target[at, columns] = total
        return carry

    lax.fori_loop(0, other.shape[0] // step, body, 0)


def feed_forward_kernel(
    attended, out_w, tokens, teacher, out_grad, valid, gain, norm, gate_up_w, down_w,
    result, square, hidden_grad, branch, attended_grad, gain_grad, down_grad, both_grad,
    normed_all, kept, mixed, grads_all, partial, held, corner_a, corner_b, from_side, from_over, hidden, total_grad, scales,
    gather_send, gather_recv, reduce_send, reduce_recv,
):
    place = coordinates()
    z, y, x, c = place
    greet([device(z, y, 1 - x, c), device(z, 1 - y, x, c), device(z, y, x, 1 - c)])
    rows, width = tokens.shape
    share = down_w.shape[0]
    step = 64
    steps = rows // step
    first, second = halves(width)
    mine = y * 4 + x * 2 + c
    chips = ((y, x), (y, 1 - x), (1 - y, x), (1 - y, 1 - x))

    def by_rows(body):
        def run(i, carry):
            body(pl.ds(pl.multiple_of(i * step, step), step))
            return carry

        lax.fori_loop(0, steps, run, 0)

    hidden[...] = tokens[...].astype(jnp.float32) + jnp.dot(
        attended[...], out_w[...], preferred_element_type=jnp.float32
    )

    def norm_rows(at):
        values = hidden[at, :]
        scale = rms_scale(values)
        scales[at, :] = scale
        normed_all[mine, at, :] = (values * scale * gain[...]).astype(normed_all.dtype)

    by_rows(norm_rows)

    def gathered(phase, whole, compute):
        copy = gather_steps(place, whole, gather_send.at[phase], gather_recv.at[phase])
        to_core, pass_on = reduce_steps(
            place, partial, held, corner_a, corner_b, from_side, from_over, reduce_send.at[phase], reduce_recv.at[phase]
        )
        for kind in (0, 3, 4, 1, 2):
            copy(kind).start()

        def wave(yy, xx):
            lax.fori_loop(0, 2, lambda cc, carry: compute(yy * 4 + xx * 2 + cc, carry), 0)
            to_core(yy, xx).start()

        def join(yy, xx):
            to_core(yy, xx).wait_recv()
            add_rows(held.at[yy * 2 + xx], partial.at[yy * 4 + xx * 2 + c])

        copy(4).wait_recv()
        wave(*chips[0])
        copy(0).wait_recv()
        copy(5).start()
        copy(7).start()
        copy(3).wait_recv()
        copy(6).start()
        copy(10).start()
        copy(1).wait_recv()
        copy(8).start()
        copy(2).wait_recv()
        copy(9).start()
        copy(7).wait_recv()
        copy(8).wait_recv()
        wave(*chips[1])
        copy(5).wait_recv()
        copy(11).start()
        copy(6).wait_recv()
        copy(12).start()
        copy(9).wait_recv()
        copy(10).wait_recv()
        wave(*chips[2])
        join(*chips[1])
        pass_on(3).start()
        copy(11).wait_recv()
        copy(12).wait_recv()
        wave(*chips[3])
        join(*chips[2])
        pass_on(4).start()
        join(*chips[3])
        pass_on(0).start()
        pass_on(1).start()
        join(*chips[0])
        for kind in range(GATHER_KINDS):
            copy(kind).wait_send()
        return to_core, pass_on

    def reduced_rest(to_core, pass_on):
        pass_on(0).wait_recv()
        add_rows(held.at[y * 2 + 1 - x], corner_a, first)
        pass_on(2).start()
        pass_on(1).wait_recv()
        add_rows(held.at[(1 - y) * 2 + x], corner_b, second)
        pass_on(5).start()
        for kind in (2, 3, 4, 5):
            pass_on(kind).wait_recv()
        for kind in range(6):
            pass_on(kind).wait_send()
        for yy, xx in chips:
            to_core(yy, xx).wait_send()

    def summed(at):
        total = held[y * 2 + x, at, :].astype(jnp.float32) + from_side[at, :].astype(jnp.float32)
        return total + from_over[at, :].astype(jnp.float32)

    def forward(member, carry):
        both = jnp.dot(normed_all[member], gate_up_w[...], preferred_element_type=jnp.float32)
        gate, up = both[:, :share], both[:, share:]
        sigmoid = 1.0 / (1.0 + jnp.exp(-gate))
        activated = gate * sigmoid
        kept[member, :, :share] = (up * (sigmoid + activated * (1.0 - sigmoid))).astype(kept.dtype)
        kept[member, :, share:] = activated.astype(kept.dtype)
        low = (activated * up).astype(mixed.dtype)
        mixed[member] = low
        partial[member] = jnp.dot(low, down_w[...], preferred_element_type=jnp.float32).astype(partial.dtype)
        return carry

    reduced_rest(*gathered(0, normed_all, forward))

    def result_rows(at):
        values = hidden[at, :] + summed(at)
        result[at, :] = values.astype(result.dtype)
        differ = values - teacher[at, :].astype(jnp.float32)
        weighed = valid[at, :] * differ
        square[at, :] = jnp.sum(weighed * differ, -1, keepdims=True)
        total = out_grad[at, :].astype(jnp.float32) + weighed * norm[...]
        total_grad[at, :] = total
        grads_all[mine, at, :] = total.astype(grads_all.dtype)

    by_rows(result_rows)

    def backward(member, carry):
        mixed_grad = against(grads_all[member], down_w[...])
        low_gate = (mixed_grad * kept[member, :, :share].astype(jnp.float32)).astype(kept.dtype)
        low_up = (mixed_grad * kept[member, :, share:].astype(jnp.float32)).astype(kept.dtype)
        kept[member, :, :share] = low_gate
        kept[member, :, share:] = low_up
        partial[member] = against(kept[member], gate_up_w[...]).astype(partial.dtype)
        return carry

    rest = gathered(1, grads_all, backward)
    tokens_all = normed_all.shape[0] * rows
    block = 256

    def down_block(i, carry):
        at = pl.ds(pl.multiple_of(i * block, block), block)
        left = mixed[:, :, at].reshape(tokens_all, block)
        down_grad[at, :] = transposed(left, grads_all[...].reshape(tokens_all, width)).astype(down_grad.dtype)
        return carry

    def both_block(i, carry):
        at = pl.ds(pl.multiple_of(i * block, block), block)
        left = normed_all[:, :, at].reshape(tokens_all, block)
        both_grad[at, :] = transposed(left, kept[...].reshape(tokens_all, 2 * share)).astype(both_grad.dtype)
        return carry

    lax.fori_loop(0, share // block, down_block, 0)
    lax.fori_loop(0, width // block, both_block, 0)
    reduced_rest(*rest)

    gain_grad[...] = jnp.zeros_like(gain_grad)

    def grad_rows(at):
        grads = summed(at)
        normed = hidden[at, :] * scales[at, :]
        gain_grad[...] += jnp.sum(grads * normed, 0, keepdims=True)
        scaled = grads * gain[...]
        values = total_grad[at, :] + scales[at, :] * (scaled - normed * jnp.mean(scaled * normed, -1, keepdims=True))
        hidden_grad[at, :] = values
        branch[at, :] = values.astype(branch.dtype)

    by_rows(grad_rows)
    attended_grad[...] = against(branch[...], out_w[...]).astype(attended_grad.dtype)


def feed_forward(attended, out_w, tokens, teacher, out_grad, valid, gain, norm, gate_up_w, down_w, identity):
    rows, width = tokens.shape
    share = down_w.shape[0]
    low = tokens.dtype
    shape = jax.ShapeDtypeStruct
    vmem = pl.BlockSpec(memory_space=pltpu.VMEM)
    cut = column_cut(width)
    return pl.pallas_call(
        feed_forward_kernel,
        out_shape=[
            shape((rows, width), low),
            shape((rows, 1), jnp.float32),
            shape((rows, width), jnp.float32),
            shape((rows, width), low),
            shape((rows, width), low),
            shape((1, width), jnp.float32),
            shape((share, width), low),
            shape((width, 2 * share), low),
        ],
        in_specs=[vmem] * 10,
        out_specs=[vmem] * 8,
        scratch_shapes=[
            pltpu.VMEM((PLANE, rows, width), low),
            pltpu.VMEM((PLANE, rows, 2 * share), low),
            pltpu.VMEM((PLANE, rows, share), low),
            pltpu.VMEM((PLANE, rows, width), low),
            pltpu.VMEM((PLANE, rows, width), low),
            pltpu.VMEM((4, rows, width), low),
            pltpu.VMEM((rows, cut), low),
            pltpu.VMEM((rows, width - cut), low),
            pltpu.VMEM((rows, width), low),
            pltpu.VMEM((rows, width), low),
            pltpu.VMEM((rows, width), jnp.float32),
            pltpu.VMEM((rows, width), jnp.float32),
            pltpu.VMEM((rows, 1), jnp.float32),
            pltpu.SemaphoreType.DMA((2, GATHER_KINDS)),
            pltpu.SemaphoreType.DMA((2, GATHER_KINDS)),
            pltpu.SemaphoreType.DMA((2, REDUCE_KINDS)),
            pltpu.SemaphoreType.DMA((2, REDUCE_KINDS)),
        ],
        compiler_params=pltpu.CompilerParams(collective_id=identity, vmem_limit_bytes=VMEM_LIMIT),
        cost_estimate=pl.CostEstimate(flops=40 * PLANE * rows * width * share // 2, bytes_accessed=30 * 2**20, transcendentals=0),
        name="feed_forward",
    )(attended, out_w, tokens, teacher, out_grad, valid, gain, norm, gate_up_w, down_w)


def attend_kernel(scale, q_ref, k_ref, v_ref, low_ref, high_ref, place_ref, o_ref, p_ref):
    keys = k_ref[...].reshape(-1, HD)
    values = v_ref[...].reshape(-1, HD)
    rows = low_ref.shape[-2]
    place = place_ref[0]
    allowed = (place >= low_ref[0]) & (place <= high_ref[0])
    for group in range(q_ref.shape[0]):
        queries = q_ref[group].reshape(rows, HD)
        score = against(queries, keys) * scale
        score = jnp.where(allowed, score, masked_score)
        top = jnp.max(score, -1, keepdims=True)
        weight = jnp.exp(score - top)
        total = jnp.sum(weight, -1, keepdims=True)
        low = (weight * (1.0 / total)).astype(jnp.bfloat16)
        p_ref[group, 0, 0] = low
        out = jnp.dot(low, values, preferred_element_type=jnp.float32)
        o_ref[group] = out.astype(jnp.bfloat16).reshape(o_ref.shape[1:])


def attend_back_kernel(scale, q_ref, k_ref, v_ref, p_ref, do_ref, dq_ref, dk_ref, dv_ref, dk_sum, dv_sum):
    block = pl.program_id(1)
    keys = k_ref[...].reshape(-1, HD)
    values = v_ref[...].reshape(-1, HD)
    rows = p_ref.shape[-2]

    @pl.when(block == 0)
    def _():
        dk_sum[...] = jnp.zeros_like(dk_sum)
        dv_sum[...] = jnp.zeros_like(dv_sum)

    for group in range(q_ref.shape[0]):
        queries = q_ref[group].reshape(rows, HD)
        grads = do_ref[group].reshape(rows, HD)
        low = p_ref[group, 0, 0]
        prob = low.astype(jnp.float32)
        prob_grad = against(grads, values)
        delta = jnp.sum(prob * prob_grad, -1, keepdims=True)
        score_low = (prob * (prob_grad - delta)).astype(jnp.bfloat16)
        dq = jnp.dot(score_low, keys, preferred_element_type=jnp.float32) * scale
        dq_ref[group] = dq.reshape(dq_ref.shape[1:])
        dk_sum[...] += transposed(score_low, queries)
        dv_sum[...] += transposed(low, grads)

    @pl.when(block == pl.num_programs(1) - 1)
    def _():
        dk_ref[...] = (dk_sum[...] * scale).reshape(dk_ref.shape)
        dv_ref[...] = dv_sum[...].reshape(dv_ref.shape)


def plane_per_device(lines, *arrays):
    (
        tokens,
        lengths,
        deal,
        loss_mask,
        teacher,
        out_grad,
        attn_gain,
        w_query,
        w_key,
        w_value,
        w_out,
        ffn_gain,
        w_gate,
        w_up,
        w_down,
    ) = arrays
    count_ctx = lax.axis_size("ctx")
    devices = lines * PLANE
    myself = lax.axis_index("ctx")
    number = myself * lax.axis_size("fsdp") + lax.axis_index("fsdp")
    tok_rows, width = tokens.shape[1:]
    half_block = tok_rows // 2
    groups = HEADS // KV
    scale = HD ** (-0.5)
    weight_rows = w_query.shape[0]
    hidden_units = w_gate.shape[1]
    down_rows = w_down.shape[0]
    share = hidden_units // PLANE
    low = jnp.bfloat16
    z_lines = [[zz * 2 + yy for zz in range(lines)] for yy in range(2)]

    dealt = jnp.arange(count_ctx * tok_rows, dtype=jnp.int32)
    local = dealt % tok_rows
    first = jnp.repeat(deal[0], tok_rows)
    block = jnp.where(local < half_block, first, 2 * count_ctx - 1 - first)
    places = block * half_block + local % half_block
    ends = jnp.cumsum(lengths[0])
    after = (places[:, None] >= ends[None, :]).astype(jnp.int32)
    seg_all = jnp.sum(after, 1)
    start_all = jnp.sum(after * lengths[0][None, :], 1)
    own = lambda array: lax.dynamic_slice_in_dim(array, myself * tok_rows, tok_rows)
    own_seg = own(seg_all)
    cosine, sine = rotary_tables(own(places) - own(start_all))
    valid = (loss_mask[0] * (own_seg < NSEQ)).astype(jnp.float32)

    split_units = lambda w: jnp.transpose(
        w.reshape(weight_rows, lines, PLANE, down_rows), (2, 0, 1, 3)
    ).reshape(PLANE, weight_rows, share)
    gate_up = jnp.concatenate([split_units(w_gate), split_units(w_up)], -1)
    gate_up = exchange(gate_up, "plane", 1, "gate_up_share").reshape(PLANE * weight_rows, 2 * share)
    gate_up_w = lax.all_gather(gate_up, "ctx", axis=0, tiled=True, axis_index_groups=z_lines)
    down_w = lax.all_gather(w_down, "ctx", axis=0, tiled=True, axis_index_groups=z_lines)

    by_head = lambda w, heads: w.reshape(weight_rows, KV, heads * HD)
    qkv_rows = jnp.concatenate([by_head(w_query, groups), by_head(w_key, 1), by_head(w_value, 1)], -1)
    head_cols = (groups + 2) * HD
    qkv_cols = KV * head_cols
    extras = jnp.concatenate(
        [
            attn_gain[:, None],
            ffn_gain[:, None],
            jnp.broadcast_to(jnp.sum(valid).astype(low), (weight_rows, 1)),
            jnp.zeros((weight_rows, LANES - 3), low),
        ],
        -1,
    )
    attn_rows = jnp.concatenate([qkv_rows.reshape(weight_rows, qkv_cols), w_out, extras], -1)
    attn_all = gather_everywhere(attn_rows, lines, 2, "gather_weights")
    extras_all = attn_all[:, :, qkv_cols + width :]
    attn_all = attn_all.reshape(devices * weight_rows, -1)
    qkv_w = attn_all[:, :qkv_cols]
    out_w = attn_all[:, qkv_cols : qkv_cols + width]
    gain_first = extras_all[:, :, 0].reshape(-1).astype(jnp.float32)
    gain_second = extras_all[:, :, 1].reshape(-1).astype(jnp.float32)
    valid_count = jnp.sum(extras_all[:, 0, 2].astype(jnp.float32))

    inputs = tokens[0].astype(jnp.float32)
    scale_one = rms_scale(inputs)
    normed_one = inputs * scale_one
    normed_low = (normed_one * gain_first).astype(low)
    ones, zeros = jnp.ones_like(cosine), jnp.zeros_like(sine)
    cos_four = jnp.concatenate([cosine] * (groups + 1) + [ones], 1)[:, None]
    sin_four = jnp.concatenate([sine] * (groups + 1) + [zeros], 1)[:, None]
    qkv = jnp.dot(normed_low, qkv_w, preferred_element_type=jnp.float32)
    qkv = rotary(qkv.reshape(tok_rows, KV, groups + 2, HD), cos_four, sin_four).astype(low)
    qkv = jnp.transpose(qkv.reshape(tok_rows, KV, head_cols), (1, 0, 2))
    qkv = exchange(qkv, "ctx", 3, "heads_out")
    qkv = qkv.reshape(count_ctx, 2, half_block, groups + 2, HD)
    qkv = jnp.transpose(qkv, (3, 0, 1, 2, 4))
    queries, keys, values = qkv[:groups], qkv[groups], qkv[groups + 1]

    half = count_ctx * half_block
    per_half = lambda array: jnp.transpose(array.reshape(count_ctx, 2, half_block), (1, 0, 2)).reshape(2, half)
    place_half = per_half(places)
    low_half = jnp.where(per_half(seg_all) < NSEQ, per_half(start_all), place_half)
    blocks = 4
    sources = count_ctx // blocks
    rows = sources * half_block
    q_spec = pl.BlockSpec((groups, sources, 1, half_block, HD), lambda h, b: (0, b, h, 0, 0))
    k_spec = pl.BlockSpec((count_ctx, 1, half_block, HD), lambda h, b: (0, h, 0, 0))
    column_spec = pl.BlockSpec((1, rows, 1), lambda h, b: (h, b, 0))
    p_spec = pl.BlockSpec((groups, 1, 1, rows, half), lambda h, b: (0, h, b, 0, 0))
    attended, probs = pl.pallas_call(
        functools.partial(attend_kernel, scale),
        grid=(2, blocks),
        in_specs=[
            q_spec,
            k_spec,
            k_spec,
            column_spec,
            column_spec,
            pl.BlockSpec((1, 1, half), lambda h, b: (h, 0, 0)),
        ],
        out_specs=[q_spec, p_spec],
        out_shape=[
            jax.ShapeDtypeStruct(queries.shape, low),
            jax.ShapeDtypeStruct((groups, 2, blocks, rows, half), low),
        ],
        compiler_params=pltpu.CompilerParams(vmem_limit_bytes=VMEM_LIMIT),
        name="attend",
    )(queries, keys, values, low_half[:, :, None], place_half[:, :, None], place_half[:, None, :])
    to_rows = lambda array: jnp.transpose(array.reshape(groups, count_ctx, tok_rows, HD), (1, 2, 0, 3)).reshape(
        count_ctx, tok_rows, groups * HD
    )
    from_heads = lambda array: jnp.transpose(array, (1, 0, 2)).reshape(tok_rows, width)
    attended_low = from_heads(exchange(to_rows(attended), "ctx", 4, "heads_back"))

    inputs_low = tokens[0]
    result, square, hidden_grad, branch_low, attended_grad, gain_two_grad, down_grad, both_grad = feed_forward(
        attended_low,
        out_w,
        inputs_low,
        teacher[0],
        out_grad[0],
        valid[:, None],
        gain_second[None],
        (2.0 / (valid_count * width)).reshape(1, 1),
        gate_up_w,
        down_w,
        5,
    )
    square_sum = jnp.sum(square)
    gain_two_grad = gain_two_grad[0]
    down_final = lax.psum_scatter(
        down_grad, "ctx", scatter_dimension=0, tiled=True, axis_index_groups=z_lines
    ).astype(jnp.float32)
    both_final = lax.psum_scatter(both_grad, "ctx", scatter_dimension=0, tiled=True, axis_index_groups=z_lines)

    out_w_grad = transposed(attended_low, branch_low)
    to_heads = lambda array: jnp.transpose(array.reshape(tok_rows, KV, -1), (1, 0, 2))
    attended_grad = exchange(to_heads(attended_grad), "ctx", 9, "grads_out")
    attended_grad = jnp.transpose(
        attended_grad.reshape(count_ctx, 2, half_block, groups, HD), (3, 0, 1, 2, 4)
    )
    query_grad, key_grad, value_grad = pl.pallas_call(
        functools.partial(attend_back_kernel, scale),
        grid=(2, blocks),
        in_specs=[q_spec, k_spec, k_spec, p_spec, q_spec],
        out_specs=[q_spec, k_spec, k_spec],
        out_shape=[
            jax.ShapeDtypeStruct(queries.shape, jnp.float32),
            jax.ShapeDtypeStruct(keys.shape, jnp.float32),
            jax.ShapeDtypeStruct(keys.shape, jnp.float32),
        ],
        scratch_shapes=[pltpu.VMEM((half, HD), jnp.float32)] * 2,
        compiler_params=pltpu.CompilerParams(vmem_limit_bytes=VMEM_LIMIT),
        name="attend_back",
    )(queries, keys, values, probs, attended_grad)
    qkv_grad = jnp.concatenate([query_grad, key_grad[None], value_grad[None]], 0)
    qkv_grad = jnp.transpose(qkv_grad.reshape(groups + 2, count_ctx, tok_rows, HD), (1, 2, 0, 3))
    qkv_grad = exchange(qkv_grad.astype(low).reshape(count_ctx, tok_rows, head_cols), "ctx", 10, "grads_back")
    qkv_grad = jnp.transpose(qkv_grad, (1, 0, 2)).reshape(tok_rows, KV, groups + 2, HD)
    qkv_grad = rotary_back(qkv_grad.astype(jnp.float32), cos_four, sin_four)
    qkv_grad = qkv_grad.astype(low).reshape(tok_rows, qkv_cols)
    normed_one_grad = against(qkv_grad, qkv_w)
    qkv_w_grad = transposed(normed_low, qkv_grad)
    gain_one_grad = jnp.sum(normed_one_grad * normed_one, 0)
    scaled_one = normed_one_grad * gain_first
    input_grad = hidden_grad + scale_one * (
        scaled_one - normed_one * jnp.mean(scaled_one * normed_one, -1, keepdims=True)
    )

    top = square_sum.astype(low)
    rest = square_sum - top.astype(jnp.float32)
    middle = rest.astype(low)
    bottom = (rest - middle.astype(jnp.float32)).astype(low)
    terms = jnp.where(jnp.arange(devices) == number, jnp.stack([top, middle, bottom])[:, None], jnp.zeros((), low))
    terms = jnp.broadcast_to(terms.reshape(1, -1), (width, 3 * devices))
    pad = jnp.zeros((width, LANES - 2 - 3 * devices), low)
    attn_grads = jnp.concatenate(
        [
            qkv_w_grad.astype(low),
            out_w_grad.astype(low),
            gain_one_grad.astype(low)[:, None],
            gain_two_grad.astype(low)[:, None],
            terms,
            pad,
        ],
        -1,
    )
    final = reduced(attn_grads.reshape(lines, PLANE, weight_rows, -1), lines, lines, 11, "reduce_weights")
    qkv_final = final[:, :qkv_cols].reshape(weight_rows, KV, head_cols)
    cuts = (groups * HD, (groups + 1) * HD)
    pieces = [qkv_final[..., : cuts[0]], qkv_final[..., cuts[0] : cuts[1]], qkv_final[..., cuts[1] :]]
    query_final, key_final, value_final = [piece.reshape(weight_rows, -1) for piece in pieces]
    out_final = final[:, qkv_cols : qkv_cols + width]
    tail = final[:, qkv_cols + width :]
    loss = jnp.sum(tail[0, 2 : 2 + 3 * devices]) / (valid_count * width)

    both_final = exchange(both_final.reshape(PLANE, weight_rows, 2 * share), "plane", 12, "gate_up_grads")
    both_final = both_final.reshape(PLANE, weight_rows, 2, lines, down_rows).astype(jnp.float32)
    gate_final, up_final = [
        jnp.transpose(both_final[:, :, i], (1, 2, 0, 3)).reshape(weight_rows, hidden_units) for i in range(2)
    ]
    return (
        result[None],
        loss,
        input_grad[None],
        tail[:, 0],
        query_final,
        key_final,
        value_final,
        out_final,
        tail[:, 1],
        gate_final,
        up_final,
        down_final,
    )


def suits_planes(mesh):
    sizes = dict(mesh.shape)
    return sizes["fsdp"] == 4 and sizes["ctx"] == KV


def solution(mesh):
    placed = (
        P("fsdp", "ctx", None),
        P("fsdp", None),
        P("fsdp", None),
        P("fsdp", "ctx"),
        P("fsdp", "ctx", None),
        P("fsdp", "ctx", None),
        P(("ctx", "fsdp")),
        P(("ctx", "fsdp"), None),
        P(("ctx", "fsdp"), None),
        P(("ctx", "fsdp"), None),
        P(("ctx", "fsdp"), None),
        P(("ctx", "fsdp")),
        P(("ctx", "fsdp"), None),
        P(("ctx", "fsdp"), None),
        P(("ctx", "fsdp"), None),
    )
    if suits_planes(mesh):
        per_device = functools.partial(plane_per_device, mesh.shape["ctx"] // ROWS_Y)
    else:
        per_device = ring_per_device
    return jax.shard_map(
        per_device,
        mesh=mesh,
        in_specs=placed,
        out_specs=(
            P("fsdp", "ctx", None),
            P(),
            P("fsdp", "ctx", None),
            P(("ctx", "fsdp")),
            P(("ctx", "fsdp"), None),
            P(("ctx", "fsdp"), None),
            P(("ctx", "fsdp"), None),
            P(("ctx", "fsdp"), None),
            P(("ctx", "fsdp")),
            P(("ctx", "fsdp"), None),
            P(("ctx", "fsdp"), None),
            P(("ctx", "fsdp"), None),
        ),
        check_vma=False,
    )
```

```python
import functools

import jax
import jax.numpy as jnp
from jax import lax
from jax.experimental import pallas as pl
from jax.experimental.pallas import tpu as pltpu
from jax.sharding import PartitionSpec as P

HEADS = 16
KV = 8
HD = 96
NSEQ = 6


rope_base = 100000.0
epsilon = 1e-05
masked_score = -1e30


def shifted(value, axis, by):
    size = lax.axis_size(axis)
    return lax.ppermute(value, axis, [(i, (i + by) % size) for i in range(size)])


def rms_scale(values):
    return lax.rsqrt(jnp.mean(values * values, -1, keepdims=True) + epsilon)


def rotary_tables(inseq):
    freq = rope_base ** (-(jnp.arange(HD // 2, dtype=jnp.float32) * 2.0 / HD))
    angle = inseq.astype(jnp.float32)[:, None] * freq[None, :]
    return (jnp.cos(angle)[:, None, :], jnp.sin(angle)[:, None, :])


def rotary(values, cosine, sine):
    half = values.shape[-1] // 2
    first = values[..., :half]
    second = values[..., half:]
    return jnp.concatenate([first * cosine - second * sine, second * cosine + first * sine], -1)


def rotary_back(grads, cosine, sine):
    half = grads.shape[-1] // 2
    first = grads[..., :half]
    second = grads[..., half:]
    return jnp.concatenate([first * cosine + second * sine, second * cosine - first * sine], -1)


def transposed(left, right):
    return lax.dot_general(
        left, right, (((0,), (0,)), ((), ())), preferred_element_type=jnp.float32
    )


def against(left, right):
    return lax.dot_general(
        left, right, (((1,), (1,)), ((), ())), preferred_element_type=jnp.float32
    )


def permitted(query_place, query_seg, key_place, key_seg):
    same = (query_seg[:, None] == key_seg[None, :]) & (query_seg[:, None] < NSEQ)
    return same & (key_place[None, :] <= query_place[:, None]) | (
        key_place[None, :] == query_place[:, None]
    )


def ring_per_device(
    tokens,
    lengths,
    deal,
    loss_mask,
    teacher,
    out_grad,
    attn_gain,
    w_query,
    w_key,
    w_value,
    w_out,
    ffn_gain,
    w_gate,
    w_up,
    w_down,
):
    count_ctx = lax.axis_size("ctx")
    myself = lax.axis_index("ctx")
    tok_rows = tokens.shape[1]
    width = tokens.shape[2]
    half_block = tok_rows // 2
    groups = HEADS // KV
    scale = HD ** (-0.5)
    gain_one, query_w, key_w, value_w, out_w = (
        lax.all_gather(attn_gain, ("ctx", "fsdp"), axis=0, tiled=True),
        lax.all_gather(w_query, ("ctx", "fsdp"), axis=0, tiled=True),
        lax.all_gather(w_key, ("ctx", "fsdp"), axis=0, tiled=True),
        lax.all_gather(w_value, ("ctx", "fsdp"), axis=0, tiled=True),
        lax.all_gather(w_out, ("ctx", "fsdp"), axis=0, tiled=True),
    )
    gain_two, gate_w, up_w, down_w = (
        lax.all_gather(ffn_gain, ("ctx", "fsdp"), axis=0, tiled=True),
        lax.all_gather(w_gate, ("ctx", "fsdp"), axis=0, tiled=True),
        lax.all_gather(w_up, ("ctx", "fsdp"), axis=0, tiled=True),
        lax.all_gather(w_down, ("ctx", "fsdp"), axis=0, tiled=True),
    )
    dealt = jnp.arange(count_ctx * tok_rows, dtype=jnp.int32)
    local = dealt % tok_rows
    first = jnp.repeat(deal[0], tok_rows)
    block = jnp.where(local < half_block, first, 2 * count_ctx - 1 - first)
    places = block * half_block + local % half_block
    ends = jnp.cumsum(lengths[0])
    after = (places[:, None] >= ends[None, :]).astype(jnp.int32)
    seg_all = jnp.sum(after, 1)
    inseq_all = places - jnp.sum(after * lengths[0][None, :], 1)
    own_place = lax.dynamic_slice_in_dim(places, myself * tok_rows, tok_rows)
    own_seg = lax.dynamic_slice_in_dim(seg_all, myself * tok_rows, tok_rows)
    own_inseq = lax.dynamic_slice_in_dim(inseq_all, myself * tok_rows, tok_rows)
    cosine, sine = rotary_tables(own_inseq)
    inputs = tokens[0].astype(jnp.float32)
    scale_one = rms_scale(inputs)
    normed_one = inputs * scale_one
    gain_first = gain_one.astype(jnp.float32)
    normed_low = (normed_one * gain_first).astype(jnp.bfloat16)
    query_pre = jnp.dot(normed_low, query_w, preferred_element_type=jnp.float32).reshape(
        tok_rows, HEADS, HD
    )
    key_pre = jnp.dot(normed_low, key_w, preferred_element_type=jnp.float32).reshape(
        tok_rows, KV, HD
    )
    value_low = jnp.dot(normed_low, value_w, preferred_element_type=jnp.float32).astype(
        jnp.bfloat16
    )
    queries = rotary(query_pre, cosine, sine).astype(jnp.bfloat16).reshape(tok_rows, KV, groups, HD)
    keys = rotary(key_pre, cosine, sine).astype(jnp.bfloat16).reshape(tok_rows, KV * HD)

    def logits(key_block):
        return (
            jnp.einsum(
                "qcgd,kcd->cgqk",
                queries,
                key_block.reshape(-1, KV, HD),
                preferred_element_type=jnp.float32,
            )
            * scale
        )

    key_block = lax.all_gather(keys, "ctx", axis=0, tiled=True)
    value_block = lax.all_gather(value_low, "ctx", axis=0, tiled=True)
    allowed = permitted(own_place, own_seg, places, seg_all)
    top = jnp.full((KV, groups, tok_rows, 1), masked_score, jnp.float32)
    score = jnp.where(allowed, logits(key_block), masked_score)
    new_top = jnp.maximum(top, jnp.max(score, -1, keepdims=True))
    weight = jnp.where(allowed, jnp.exp(score - new_top), 0.0)
    summed = jnp.einsum(
        "cgqk,kcd->cgqd",
        weight.astype(jnp.bfloat16),
        value_block.reshape(-1, KV, HD),
        preferred_element_type=jnp.float32,
    )
    summed, top, total = (summed, new_top, jnp.sum(weight, -1, keepdims=True))
    attended = summed / total
    log_total = top + jnp.log(total)
    attended_low = (
        jnp.transpose(attended, (2, 0, 1, 3)).reshape(tok_rows, HEADS * HD).astype(jnp.bfloat16)
    )
    hidden = inputs + jnp.dot(attended_low, out_w, preferred_element_type=jnp.float32)
    scale_two = rms_scale(hidden)
    normed_two = hidden * scale_two
    gain_second = gain_two.astype(jnp.float32)
    ffn_low = (normed_two * gain_second).astype(jnp.bfloat16)
    gate = jnp.dot(ffn_low, gate_w, preferred_element_type=jnp.float32)
    up = jnp.dot(ffn_low, up_w, preferred_element_type=jnp.float32)
    sigmoid = jax.nn.sigmoid(gate)
    activated = gate * sigmoid
    mixed_low = (activated * up).astype(jnp.bfloat16)
    result = hidden + jnp.dot(mixed_low, down_w, preferred_element_type=jnp.float32)
    target = teacher[0].astype(jnp.float32)
    valid = (loss_mask[0] * (own_seg < NSEQ)).astype(jnp.float32)[:, None]
    differ = result - target
    square_sum, valid_count = lax.psum(
        (jnp.sum(valid * differ * differ), jnp.sum(valid)), ("ctx", "fsdp")
    )
    loss = square_sum / (valid_count * width)
    out_total = out_grad[0].astype(jnp.float32) + 2.0 * valid * differ / (valid_count * width)
    out_low = out_total.astype(jnp.bfloat16)
    down_grad = transposed(mixed_low, out_low)
    mixed_grad = against(out_low, down_w)
    silu_slope = sigmoid * (1.0 + gate * (1.0 - sigmoid))
    gate_low = (mixed_grad * up * silu_slope).astype(jnp.bfloat16)
    up_low = (mixed_grad * activated).astype(jnp.bfloat16)
    gate_grad = transposed(ffn_low, gate_low)
    up_grad = transposed(ffn_low, up_low)
    normed_grad = against(gate_low, gate_w) + against(up_low, up_w)
    gain_two_grad = jnp.sum(normed_grad * normed_two, 0)
    scaled_two = normed_grad * gain_second
    hidden_grad = out_total + scale_two * (
        scaled_two - normed_two * jnp.mean(scaled_two * normed_two, -1, keepdims=True)
    )
    ffn_final = (
        lax.psum_scatter(gain_two_grad, ("ctx", "fsdp"), scatter_dimension=0, tiled=True),
        lax.psum_scatter(gate_grad, ("ctx", "fsdp"), scatter_dimension=0, tiled=True),
        lax.psum_scatter(up_grad, ("ctx", "fsdp"), scatter_dimension=0, tiled=True),
        lax.psum_scatter(down_grad, ("ctx", "fsdp"), scatter_dimension=0, tiled=True),
    )
    branch_low = hidden_grad.astype(jnp.bfloat16)
    out_w_grad = transposed(attended_low, branch_low)
    attended_grad = against(branch_low, out_w).astype(jnp.bfloat16)
    grad_heads = jnp.transpose(attended_grad.reshape(tok_rows, KV, groups, HD), (1, 2, 0, 3))
    delta = jnp.sum(grad_heads.astype(jnp.float32) * attended, -1, keepdims=True)

    def cycle_step(step, state):
        key_block, value_block, key_acc, value_acc, query_acc = state
        source = (myself - step) % count_ctx
        allowed = permitted(
            own_place,
            own_seg,
            lax.dynamic_slice_in_dim(places, source * tok_rows, tok_rows),
            lax.dynamic_slice_in_dim(seg_all, source * tok_rows, tok_rows),
        )
        current_key = key_block
        current_value = value_block
        keys_three = current_key.reshape(tok_rows, KV, HD)
        values_three = current_value.reshape(tok_rows, KV, HD)
        prob = jnp.where(allowed, jnp.exp(logits(current_key) - log_total), 0.0)
        prob_grad = jnp.einsum(
            "cgqd,kcd->cgqk", grad_heads, values_three, preferred_element_type=jnp.float32
        )
        score_low = (prob * (prob_grad - delta)).astype(jnp.bfloat16)
        query_add = (
            jnp.einsum("cgqk,kcd->cgqd", score_low, keys_three, preferred_element_type=jnp.float32)
            * scale
        )
        key_add = (
            jnp.einsum(
                "cgqk,qcgd->kcd", score_low, queries, preferred_element_type=jnp.float32
            ).reshape(tok_rows, KV * HD)
            * scale
        )
        value_add = jnp.einsum(
            "cgqk,cgqd->kcd",
            prob.astype(jnp.bfloat16),
            grad_heads,
            preferred_element_type=jnp.float32,
        ).reshape(tok_rows, KV * HD)
        key_block, value_block = shifted((key_block, value_block), "ctx", 1)
        key_acc, value_acc = (
            shifted((key_acc + key_add).astype(jnp.bfloat16), "ctx", 1).astype(jnp.float32),
            shifted((value_acc + value_add).astype(jnp.bfloat16), "ctx", 1).astype(jnp.float32),
        )
        return (key_block, value_block, key_acc, value_acc, query_acc + query_add)

    cycle_start = (
        keys,
        value_low,
        jnp.zeros((tok_rows, KV * HD), jnp.float32),
        jnp.zeros((tok_rows, KV * HD), jnp.float32),
        jnp.zeros((KV, groups, tok_rows, HD), jnp.float32),
    )
    cycle_end = lax.fori_loop(0, count_ctx, cycle_step, cycle_start)
    key_acc = cycle_end[2]
    value_acc = cycle_end[3]
    query_acc = cycle_end[4]
    query_grad = jnp.transpose(query_acc, (2, 0, 1, 3)).reshape(tok_rows, HEADS, HD)
    query_low = (
        rotary_back(query_grad, cosine, sine).reshape(tok_rows, HEADS * HD).astype(jnp.bfloat16)
    )
    key_low = (
        rotary_back(key_acc.reshape(tok_rows, KV, HD), cosine, sine)
        .reshape(tok_rows, KV * HD)
        .astype(jnp.bfloat16)
    )
    value_grad_low = value_acc.astype(jnp.bfloat16)
    query_w_grad = transposed(normed_low, query_low)
    key_w_grad = transposed(normed_low, key_low)
    value_w_grad = transposed(normed_low, value_grad_low)
    normed_one_grad = (
        against(query_low, query_w) + against(key_low, key_w) + against(value_grad_low, value_w)
    )
    gain_one_grad = jnp.sum(normed_one_grad * normed_one, 0)
    scaled_one = normed_one_grad * gain_first
    input_grad = hidden_grad + scale_one * (
        scaled_one - normed_one * jnp.mean(scaled_one * normed_one, -1, keepdims=True)
    )
    attn_final = (
        lax.psum_scatter(gain_one_grad, ("ctx", "fsdp"), scatter_dimension=0, tiled=True),
        lax.psum_scatter(query_w_grad, ("ctx", "fsdp"), scatter_dimension=0, tiled=True),
        lax.psum_scatter(key_w_grad, ("ctx", "fsdp"), scatter_dimension=0, tiled=True),
        lax.psum_scatter(value_w_grad, ("ctx", "fsdp"), scatter_dimension=0, tiled=True),
        lax.psum_scatter(out_w_grad, ("ctx", "fsdp"), scatter_dimension=0, tiled=True),
    )
    return (
        result.astype(jnp.bfloat16)[None],
        loss,
        input_grad[None],
        attn_final[0],
        attn_final[1],
        attn_final[2],
        attn_final[3],
        attn_final[4],
        ffn_final[0],
        ffn_final[1],
        ffn_final[2],
        ffn_final[3],
    )


MESH = pl.DeviceIdType.MESH
ROWS_Y = 2
PLANE = 8
LANES = 128
VMEM_LIMIT = 60 * 2**20


def coordinates():
    ctx = lax.axis_index("ctx")
    fsdp = lax.axis_index("fsdp")
    return ctx // 2, ctx % 2, fsdp // 2, fsdp % 2


def device(z, y, x, c):
    return (z * 2 + y, x * 2 + c)


def greet(devices):
    barrier = pltpu.get_barrier_semaphore()
    for other in devices:
        pl.semaphore_signal(barrier, inc=1, device_id=other, device_id_type=MESH)
    pl.semaphore_wait(barrier, len(devices))


def remote(src, dst, send, recv, target):
    return pltpu.make_async_remote_copy(
        src_ref=src,
        dst_ref=dst,
        send_sem=send,
        recv_sem=recv,
        device_id=target,
        device_id_type=MESH,
    )


def exchange_kernel(group, count, x_ref, o_ref, send, recv, here):
    z, y, x, c = coordinates()
    if group == "ctx":
        me = z * 2 + y
        to_device = lambda i: (i, x * 2 + c)
    else:
        me = y * 4 + x * 2 + c
        to_device = lambda i: (z * 2 + i // 4, i % 4)
    others = [lax.rem(me + k, count) for k in range(1, count)]
    greet([to_device(i) for i in others])
    copies = [
        remote(x_ref.at[i], o_ref.at[me], send.at[k], recv.at[k], to_device(i))
        for k, i in enumerate(others)
    ]
    for copy in copies:
        copy.start()
    own = pltpu.make_async_copy(x_ref.at[me], o_ref.at[me], here)
    own.start()
    own.wait()
    for copy in copies:
        copy.wait()


def exchange(values, group, identity, name):
    count = values.shape[0]
    return pl.pallas_call(
        functools.partial(exchange_kernel, group, count),
        out_shape=jax.ShapeDtypeStruct(values.shape, values.dtype),
        in_specs=[pl.BlockSpec(memory_space=pl.ANY)],
        out_specs=pl.BlockSpec(memory_space=pl.ANY),
        scratch_shapes=[
            pltpu.SemaphoreType.DMA((count - 1,)),
            pltpu.SemaphoreType.DMA((count - 1,)),
            pltpu.SemaphoreType.DMA,
        ],
        compiler_params=pltpu.CompilerParams(collective_id=identity),
        name=name,
    )(values)


def column_cut(width):
    tiles = width // LANES
    return (tiles + 1) // 2 * LANES


def gather_kernel(lines, x_ref, o_ref, send, recv, here):
    z, y, x, c = coordinates()
    width = x_ref.shape[1]
    cut = column_cut(width)
    first, second = pl.ds(0, cut), pl.ds(cut, width - cut)
    side, over, sibling = device(z, y, 1 - x, c), device(z, 1 - y, x, c), device(z, y, x, 1 - c)
    above, below = device(z + 1, y, x, c), device(z - 1, y, x, c)
    greet([side, over, sibling] + [device(lax.rem(z + k, lines), y, x, c) for k in range(1, lines)])
    slot = lambda zz, yy, xx, cc: (zz * 2 + yy) * 4 + xx * 2 + cc
    mine = pltpu.make_async_copy(x_ref, o_ref.at[slot(z, y, x, c)], here)
    mine.start()

    def item(sign, s):
        index = 0 if s == 0 else (2 * s - 1 if sign < 0 else 2 * s)
        zz = z + sign * s
        at = lambda yy, xx, cc: o_ref.at[slot(zz, yy, xx, cc)]
        own = x_ref if s == 0 else at(y, x, c)
        make = lambda kind, src, dst, to: remote(
            src, dst, send.at[index, kind], recv.at[index, kind], to
        )
        same = lambda kind, ref, to: make(kind, ref, ref, to)
        corner_at = lambda columns: at(1 - y, 1 - x, c).at[:, columns]
        return dict(
            side=lambda: make(1, own, at(y, x, c), side),
            over=lambda: make(2, own, at(y, x, c), over),
            side_on=lambda: same(3, at(y, 1 - x, c).at[:, first], over),
            over_on=lambda: same(4, at(1 - y, x, c).at[:, second], side),
            core=lambda: make(5, own, at(y, x, c), sibling),
            core_side=lambda: same(6, at(y, 1 - x, c), sibling),
            core_over=lambda: same(7, at(1 - y, x, c), sibling),
            core_first=lambda: same(8, corner_at(first), sibling),
            core_second=lambda: same(9, corner_at(second), sibling),
        )

    def along(sign, s):
        index = 2 * s - 1 if sign < 0 else 2 * s
        zz = z + sign * (s - 1)
        src = x_ref if s == 1 else o_ref.at[slot(zz, y, x, c)]
        return remote(
            src, o_ref.at[slot(zz, y, x, c)], send.at[index, 0], recv.at[index, 0], above if sign < 0 else below
        )

    def sends_along(sign, s):
        if sign < 0:
            return (z - (s - 1) >= 0) & (z + 1 < lines)
        return (z + (s - 1) < lines) & (z - 1 >= 0)

    def present(sign, s):
        return z - s >= 0 if sign < 0 else z + s < lines

    arrivals = [(-1, 0)] + [(sign, s) for s in range(1, lines) for sign in (-1, 1)]

    def begin(sign, s):
        copies = item(sign, s)
        if s > 0:
            along(sign, s).wait_recv()
        for way in ((-1, 1) if s == 0 else (sign,)):
            if s + 1 < lines:
                @pl.when(sends_along(way, s + 1))
                def _():
                    along(way, s + 1).start()
        copies["side"]().start()
        copies["over"]().start()
        copies["core"]().start()

    def pass_on(sign, s):
        copies = item(sign, s)
        copies["side"]().wait_recv()
        copies["side_on"]().start()
        copies["core_side"]().start()
        copies["over"]().wait_recv()
        copies["over_on"]().start()
        copies["core_over"]().start()

    def corner(sign, s):
        copies = item(sign, s)
        copies["side_on"]().wait_recv()
        copies["core_first"]().start()
        copies["over_on"]().wait_recv()
        copies["core_second"]().start()

    def finish(sign, s):
        copies = item(sign, s)
        for kind in ("core", "core_side", "core_over", "core_first", "core_second"):
            copies[kind]().wait()
        for kind in ("side", "over", "side_on", "over_on"):
            copies[kind]().wait_send()

    def where(sign, s, step):
        if s == 0:
            step(sign, s)
        else:
            pl.when(present(sign, s))(functools.partial(step, sign, s))

    waves = [[(-1, 0)]] + [[(-1, s), (1, s)] for s in range(1, lines)]
    for number in range(len(waves) + 2):
        for stage, lag in ((begin, 0), (pass_on, 1), (corner, 2)):
            if 0 <= number - lag < len(waves):
                for sign, s in waves[number - lag]:
                    where(sign, s, stage)
    for sign, s in arrivals:
        where(sign, s, finish)
    for s in range(1, lines):
        for sign in (-1, 1):
            @pl.when(sends_along(sign, s))
            def _():
                along(sign, s).wait_send()
    mine.wait()


def gather_everywhere(rows, lines, identity, name):
    return pl.pallas_call(
        functools.partial(gather_kernel, lines),
        out_shape=jax.ShapeDtypeStruct((lines * PLANE,) + rows.shape, rows.dtype),
        in_specs=[pl.BlockSpec(memory_space=pl.ANY)],
        out_specs=pl.BlockSpec(memory_space=pl.ANY),
        scratch_shapes=[
            pltpu.SemaphoreType.DMA((2 * lines - 1, 10)),
            pltpu.SemaphoreType.DMA((2 * lines - 1, 10)),
            pltpu.SemaphoreType.DMA,
        ],
        compiler_params=pltpu.CompilerParams(collective_id=identity),
        name=name,
    )(rows)


def reduce_kernel(parts, lines, prepare, between, p_ref, o_ref, held, corner_a, corner_b, from_side, from_over, along, send, recv):
    z, y, x, c = coordinates()
    rows, width = held.shape[2], held.shape[3]
    cut = column_cut(width)
    first, second = pl.ds(0, cut), pl.ds(cut, width - cut)
    side, over, sibling = device(z, y, 1 - x, c), device(z, 1 - y, x, c), device(z, y, x, 1 - c)
    greet([side, over, sibling] + [device(lax.rem(z + k, lines), y, x, c) for k in range(1, lines)])

    def given(part, yy, xx, cc):
        member = yy * 4 + xx * 2 + cc
        return p_ref.at[lax.rem(z + part + 1, lines), member]

    def make(part, kind, src, dst, to):
        return remote(src, dst, send.at[part, kind], recv.at[part, kind], to)

    lane = lambda part, yy, xx: held.at[part, yy * 2 + xx]

    def over_core(part):
        return [
            make(part, yy * 2 + xx, given(part, yy, xx, 1 - c), lane(part, yy, xx), sibling)
            for yy in range(2)
            for xx in range(2)
        ]

    def to_corner(part):
        return (
            make(part, 4, lane(part, 1 - y, 1 - x).at[:, first], corner_a.at[part], over),
            make(part, 5, lane(part, 1 - y, 1 - x).at[:, second], corner_b.at[part], side),
        )

    def to_neighbour(part, way):
        columns = (first, second)[way % 2]
        if way < 2:
            return make(part, 6 + way, lane(part, y, 1 - x).at[:, columns], from_side.at[part, :, columns], side)
        return make(part, 6 + way, lane(part, 1 - y, x).at[:, columns], from_over.at[part, :, columns], over)

    def along_z(part):
        to = lax.rem(z + part + 1, lines)
        return make(part, 10, lane(part, y, x), along.at[part], device(to, y, x, c))

    step = 16

    def add_core(part):
        for copy in over_core(part):
            copy.wait_recv()
        for yy, xx in ((1 - y, 1 - x), (y, 1 - x), (1 - y, x), (y, x)):
            mine, other = given(part, yy, xx, c), lane(part, yy, xx)

            def body(i, carry):
                at = pl.ds(pl.multiple_of(i * step, step), step)
                total = mine[at, :].astype(jnp.float32) + other[at, :].astype(jnp.float32)
                other[at, :] = total.astype(other.dtype)
                return carry

            lax.fori_loop(0, rows // step, body, 0)
        for copy in to_corner(part):
            copy.start()
        to_neighbour(part, 1).start()
        to_neighbour(part, 2).start()

    def add_corner(part):
        copies = to_corner(part)
        pairs = (
            (copies[0], lane(part, y, 1 - x), corner_a.at[part], first),
            (copies[1], lane(part, 1 - y, x), corner_b.at[part], second),
        )
        for copy, mine, other, columns in pairs:
            copy.wait_recv()

            def body(i, carry):
                at = pl.ds(pl.multiple_of(i * step, step), step)
                total = mine[at, columns].astype(jnp.float32) + other[at, :].astype(jnp.float32)
                mine[at, columns] = total.astype(mine.dtype)
                return carry

            lax.fori_loop(0, rows // step, body, 0)
        to_neighbour(part, 0).start()
        to_neighbour(part, 3).start()

    def add_neighbours(part):
        for way in range(4):
            to_neighbour(part, way).wait_recv()
        last = part == parts - 1
        mine = lane(part, y, x)

        def body(i, carry):
            at = pl.ds(pl.multiple_of(i * step, step), step)
            total = mine[at, :].astype(jnp.float32) + from_side[part, at, :].astype(jnp.float32)
            total += from_over[part, at, :].astype(jnp.float32)
            if last:
                o_ref[at, :] = total
            else:
                mine[at, :] = total.astype(mine.dtype)
            return carry

        lax.fori_loop(0, rows // step, body, 0)
        if not last:
            along_z(part).start()

    def ready(part):
        prepare(lax.rem(z + part + 1, lines))
        for copy in over_core(part):
            copy.start()

    stages = (ready, add_core, add_corner, add_neighbours)
    for number in range(parts + len(stages) - 1):
        if number == parts:
            between()
        for lag, stage in enumerate(stages):
            if 0 <= number - lag < parts:
                stage(number - lag)
    for part in range(parts - 1):
        along_z(part).wait_recv()

    def body(i, carry):
        at = pl.ds(pl.multiple_of(i * step, step), step)
        total = o_ref[at, :]
        for part in range(parts - 1):
            total += along[part, at, :].astype(jnp.float32)
        o_ref[at, :] = total
        return carry

    lax.fori_loop(0, rows // step, body, 0)
    for part in range(parts - 1):
        along_z(part).wait_send()
    for part in range(parts):
        for copy in (*over_core(part), *to_corner(part), *(to_neighbour(part, way) for way in range(4))):
            copy.wait_send()


def halves(width):
    cut = column_cut(width)
    return pl.ds(0, cut), pl.ds(cut, width - cut)


def gather_steps(place, whole, send, recv):
    z, y, x, c = place
    side, over, sibling = device(z, y, 1 - x, c), device(z, 1 - y, x, c), device(z, y, x, 1 - c)
    first, second = halves(whole.shape[-1])
    at = lambda yy, xx: whole.at[yy * 4 + xx * 2 + c]
    own, next_x, next_y, corner = at(y, x), at(y, 1 - x), at(1 - y, x), at(1 - y, 1 - x)
    table = (
        (own.at[:, first], side),
        (own.at[:, second], side),
        (own.at[:, first], over),
        (own.at[:, second], over),
        (own, sibling),
        (next_x.at[:, first], over),
        (next_y.at[:, second], side),
        (next_x.at[:, first], sibling),
        (next_x.at[:, second], sibling),
        (next_y.at[:, first], sibling),
        (next_y.at[:, second], sibling),
        (corner.at[:, first], sibling),
        (corner.at[:, second], sibling),
    )

    def copy(kind):
        ref, to = table[kind]
        return remote(ref, ref, send.at[kind], recv.at[kind], to)

    return copy


GATHER_KINDS = 13
REDUCE_KINDS = 10


def reduce_steps(place, partial, held, corner_a, corner_b, from_side, from_over, send, recv):
    z, y, x, c = place
    side, over, sibling = device(z, y, 1 - x, c), device(z, 1 - y, x, c), device(z, y, x, 1 - c)
    first, second = halves(held.shape[-1])
    lane = lambda yy, xx: held.at[yy * 2 + xx]
    next_x, next_y, corner = lane(y, 1 - x), lane(1 - y, x), lane(1 - y, 1 - x)

    def to_core(yy, xx):
        kind = yy * 2 + xx
        src = partial.at[yy * 4 + xx * 2 + 1 - c]
        return remote(src, lane(yy, xx), send.at[kind], recv.at[kind], sibling)

    table = (
        (corner.at[:, first], corner_a, over),
        (corner.at[:, second], corner_b, side),
        (next_x.at[:, first], from_side.at[:, first], side),
        (next_x.at[:, second], from_side.at[:, second], side),
        (next_y.at[:, first], from_over.at[:, first], over),
        (next_y.at[:, second], from_over.at[:, second], over),
    )

    def copy(kind):
        src, dst, to = table[kind]
        return remote(src, dst, send.at[4 + kind], recv.at[4 + kind], to)

    return to_core, copy


def add_rows(target, other, columns=None, step=32):
    def body(i, carry):
        at = pl.ds(pl.multiple_of(i * step, step), step)
        mine = target[at, :] if columns is None else target[at, columns]
        total = (mine.astype(jnp.float32) + other[at, :].astype(jnp.float32)).astype(target.dtype)
        if columns is None:
            target[at, :] = total
        else:
            target[at, columns] = total
        return carry

    lax.fori_loop(0, other.shape[0] // step, body, 0)


def feed_forward_kernel(
    weights, attended, tokens, teacher, out_grad, valid, gain, norm, gate_up_w, down_w,
    result, square, hidden_grad, branch, attended_grad, gain_terms, down_grad, both_grad,
    out_w, normed_all, kept, mixed, grads_all, partial, held, corner_a, corner_b, from_side, from_over, hidden, total_grad, scales,
    out_sem, gather_send, gather_recv, reduce_send, reduce_recv,
):
    place = coordinates()
    z, y, x, c = place
    width = tokens.shape[1]
    load = pltpu.make_async_copy(weights.at[:, pl.ds(weights.shape[1] - LANES - width, width)], out_w, out_sem)
    load.start()
    greet([device(z, y, 1 - x, c), device(z, 1 - y, x, c), device(z, y, x, 1 - c)])
    rows = tokens.shape[0]
    share = down_w.shape[0]
    first, second = halves(width)
    mine = y * 4 + x * 2 + c
    chips = ((y, x), (y, 1 - x), (1 - y, x), (1 - y, 1 - x))

    load.wait()
    hidden[...] = tokens[...].astype(jnp.float32) + jnp.dot(
        attended[...], out_w[...], preferred_element_type=jnp.float32
    )

    def norm_rows(at):
        values = hidden[at, :]
        scale = rms_scale(values)
        scales[at, :] = scale
        normed_all[mine, at, :] = (values * scale * gain[...]).astype(normed_all.dtype)

    by_rows(rows, norm_rows)

    def gathered(phase, whole, compute):
        copy = gather_steps(place, whole, gather_send.at[phase], gather_recv.at[phase])
        to_core, pass_on = reduce_steps(
            place, partial, held, corner_a, corner_b, from_side, from_over, reduce_send.at[phase], reduce_recv.at[phase]
        )
        for kind in (0, 3, 4, 1, 2):
            copy(kind).start()

        def wave(yy, xx):
            lax.fori_loop(0, 2, lambda cc, carry: compute(yy * 4 + xx * 2 + cc, carry), 0)
            to_core(yy, xx).start()

        def join(yy, xx):
            to_core(yy, xx).wait_recv()
            add_rows(held.at[yy * 2 + xx], partial.at[yy * 4 + xx * 2 + c])

        copy(4).wait_recv()
        wave(*chips[0])
        copy(0).wait_recv()
        copy(5).start()
        copy(7).start()
        copy(3).wait_recv()
        copy(6).start()
        copy(10).start()
        copy(1).wait_recv()
        copy(8).start()
        copy(2).wait_recv()
        copy(9).start()
        copy(7).wait_recv()
        copy(8).wait_recv()
        wave(*chips[1])
        copy(5).wait_recv()
        copy(11).start()
        copy(6).wait_recv()
        copy(12).start()
        copy(9).wait_recv()
        copy(10).wait_recv()
        wave(*chips[2])
        join(*chips[1])
        pass_on(3).start()
        copy(11).wait_recv()
        copy(12).wait_recv()
        wave(*chips[3])
        join(*chips[2])
        pass_on(4).start()
        join(*chips[3])
        pass_on(0).start()
        pass_on(1).start()
        join(*chips[0])
        for kind in range(GATHER_KINDS):
            copy(kind).wait_send()
        return to_core, pass_on

    def reduced_rest(to_core, pass_on):
        pass_on(0).wait_recv()
        add_rows(held.at[y * 2 + 1 - x], corner_a, first)
        pass_on(2).start()
        pass_on(1).wait_recv()
        add_rows(held.at[(1 - y) * 2 + x], corner_b, second)
        pass_on(5).start()
        for kind in (2, 3, 4, 5):
            pass_on(kind).wait_recv()
        for kind in range(6):
            pass_on(kind).wait_send()
        for yy, xx in chips:
            to_core(yy, xx).wait_send()

    def summed(at):
        total = held[y * 2 + x, at, :].astype(jnp.float32) + from_side[at, :].astype(jnp.float32)
        return total + from_over[at, :].astype(jnp.float32)

    def forward(member, carry):
        both = jnp.dot(normed_all[member], gate_up_w[...], preferred_element_type=jnp.float32)
        gate, up = both[:, :share], both[:, share:]
        sigmoid = 1.0 / (1.0 + jnp.exp(-gate))
        activated = gate * sigmoid
        kept[member, :, :share] = (up * (sigmoid + activated * (1.0 - sigmoid))).astype(kept.dtype)
        kept[member, :, share:] = activated.astype(kept.dtype)
        low = (activated * up).astype(mixed.dtype)
        mixed[member] = low
        partial[member] = jnp.dot(low, down_w[...], preferred_element_type=jnp.float32).astype(partial.dtype)
        return carry

    reduced_rest(*gathered(0, normed_all, forward))

    def result_rows(at):
        values = hidden[at, :] + summed(at)
        result[at, :] = values.astype(result.dtype)
        differ = values - teacher[at, :].astype(jnp.float32)
        weighed = valid[at, :] * differ
        square[at, :] = jnp.sum(weighed * differ, -1, keepdims=True)
        total = out_grad[at, :].astype(jnp.float32) + weighed * norm[...]
        total_grad[at, :] = total
        grads_all[mine, at, :] = total.astype(grads_all.dtype)

    by_rows(rows, result_rows)

    def backward(member, carry):
        mixed_grad = against(grads_all[member], down_w[...])
        low_gate = (mixed_grad * kept[member, :, :share].astype(jnp.float32)).astype(kept.dtype)
        low_up = (mixed_grad * kept[member, :, share:].astype(jnp.float32)).astype(kept.dtype)
        kept[member, :, :share] = low_gate
        kept[member, :, share:] = low_up
        partial[member] = against(kept[member], gate_up_w[...]).astype(partial.dtype)
        return carry

    rest = gathered(1, grads_all, backward)
    tokens_all = normed_all.shape[0] * rows
    block = 256

    def down_block(i, carry):
        at = pl.ds(pl.multiple_of(i * block, block), block)
        left = mixed[:, :, at].reshape(tokens_all, block)
        down_grad[at, :] = transposed(left, grads_all[...].reshape(tokens_all, width)).astype(down_grad.dtype)
        return carry

    def both_block(i, carry):
        at = pl.ds(pl.multiple_of(i * block, block), block)
        left = normed_all[:, :, at].reshape(tokens_all, block)
        both_grad[at, :] = transposed(left, kept[...].reshape(tokens_all, 2 * share)).astype(both_grad.dtype)
        return carry

    lax.fori_loop(0, share // block, down_block, 0)
    lax.fori_loop(0, width // block, both_block, 0)
    reduced_rest(*rest)

    def grad_rows(at):
        grads = summed(at)
        normed = hidden[at, :] * scales[at, :]
        gain_terms[at, :] = (grads * normed).astype(gain_terms.dtype)
        scaled = grads * gain[...]
        values = total_grad[at, :] + scales[at, :] * (scaled - normed * jnp.mean(scaled * normed, -1, keepdims=True))
        hidden_grad[at, :] = values
        branch[at, :] = values.astype(branch.dtype)

    by_rows(rows, grad_rows)
    attended_grad[...] = against(branch[...], out_w[...]).astype(attended_grad.dtype)


def feed_forward(weights, attended, tokens, teacher, out_grad, valid, gain, norm, gate_up_w, down_w, identity):
    rows, width = tokens.shape
    share = down_w.shape[0]
    low = tokens.dtype
    shape = jax.ShapeDtypeStruct
    vmem = pl.BlockSpec(memory_space=pltpu.VMEM)
    cut = column_cut(width)
    return pl.pallas_call(
        feed_forward_kernel,
        out_shape=[
            shape((rows, width), low),
            shape((rows, 1), jnp.float32),
            shape((rows, width), jnp.float32),
            shape((rows, width), low),
            shape((rows, width), low),
            shape((rows, width), low),
            shape((share, width), low),
            shape((width, 2 * share), low),
        ],
        in_specs=[pl.BlockSpec(memory_space=pl.ANY)] + [vmem] * 9,
        out_specs=[vmem] * 8,
        scratch_shapes=[
            pltpu.VMEM((width, width), low),
            pltpu.VMEM((PLANE, rows, width), low),
            pltpu.VMEM((PLANE, rows, 2 * share), low),
            pltpu.VMEM((PLANE, rows, share), low),
            pltpu.VMEM((PLANE, rows, width), low),
            pltpu.VMEM((PLANE, rows, width), low),
            pltpu.VMEM((4, rows, width), low),
            pltpu.VMEM((rows, cut), low),
            pltpu.VMEM((rows, width - cut), low),
            pltpu.VMEM((rows, width), low),
            pltpu.VMEM((rows, width), low),
            pltpu.VMEM((rows, width), jnp.float32),
            pltpu.VMEM((rows, width), jnp.float32),
            pltpu.VMEM((rows, 1), jnp.float32),
            pltpu.SemaphoreType.DMA,
            pltpu.SemaphoreType.DMA((2, GATHER_KINDS)),
            pltpu.SemaphoreType.DMA((2, GATHER_KINDS)),
            pltpu.SemaphoreType.DMA((2, REDUCE_KINDS)),
            pltpu.SemaphoreType.DMA((2, REDUCE_KINDS)),
        ],
        compiler_params=pltpu.CompilerParams(collective_id=identity, vmem_limit_bytes=VMEM_LIMIT),
        cost_estimate=pl.CostEstimate(flops=40 * PLANE * rows * width * share // 2, bytes_accessed=30 * 2**20, transcendentals=0),
        name="feed_forward",
    )(weights, attended, tokens, teacher, out_grad, valid, gain, norm, gate_up_w, down_w)


HEAD_TILES = 3
ROW_STEP = 64


def by_rows(rows, body, step=ROW_STEP):
    def run(i, carry):
        body(pl.ds(pl.multiple_of(i * step, step), step))
        return carry

    lax.fori_loop(0, rows // step, run, 0)


def lanes_of(values):
    return lax.broadcasted_iota(jnp.int32, values.shape, len(values.shape) - 1)


def turned(tile, cosine, sine_low, sine_high):
    half = HD // 2
    return (
        tile * cosine + pltpu.roll(tile, LANES - half, 1) * sine_low + pltpu.roll(tile, half, 1) * sine_high
    )


def packed_pair(first, second, even):
    lane = lanes_of(first)
    moved = pltpu.roll(second, HD, 1)
    full_even = jnp.where(lane < HD, first, moved)
    full_odd = jnp.where(lane < 32, pltpu.roll(first, 64, 1), pltpu.roll(second, 32, 1))
    return jnp.where(even, full_even, full_odd), jnp.where(even, moved, first)


def unpacked_pair(full, part, even):
    lane = lanes_of(full)
    zero = jnp.zeros_like(full)
    first_even = jnp.where(lane < HD, full, zero)
    second_even = jnp.where(lane < 32, pltpu.roll(full, 32, 1), jnp.where(lane < HD, pltpu.roll(part, 32, 1), zero))
    first_odd = jnp.where(lane < 64, part, jnp.where(lane < HD, pltpu.roll(full, 64, 1), zero))
    second_odd = jnp.where(lane < HD, pltpu.roll(full, HD, 1), zero)
    return jnp.where(even, first_even, first_odd), jnp.where(even, second_even, second_odd)


def keys_and_values(qkv, keys, values, count, rows):
    def body(src, carry):
        block = qkv[src].astype(jnp.float32)
        tiles = [block[:, i * LANES : (i + 1) * LANES] for i in range(HEAD_TILES)]
        lane = lanes_of(tiles[0])
        key = jnp.where(lane < HD, tiles[2], 0.0)
        value = jnp.where(lane < 64, pltpu.roll(tiles[1], 64, 1), pltpu.roll(tiles[2], HD, 1))
        value = jnp.where(lane < 32, pltpu.roll(tiles[0], 32, 1), value)
        value = jnp.where(lane < HD, value, 0.0)
        at = pl.ds(pl.multiple_of(src * rows, rows), rows)
        for half in range(2):
            keys[half, at, :] = key[half * rows : (half + 1) * rows].astype(keys.dtype)
            values[half, at, :] = value[half * rows : (half + 1) * rows].astype(values.dtype)
        return carry

    lax.fori_loop(0, count, body, 0)


def attend_kernel(
    scale, weights, tokens, gain, cosine, sine_low, sine_high, lowest, place_column, place_row,
    attended, normed, qkv_out, probs,
    w, sent, qkv, keys, values, prob_blocks, o_sent, o_came,
    w_sem, send, recv, o_send, o_recv, p_sem, q_sem,
):
    z, y, x, c = coordinates()
    count = sent.shape[0]
    me = z * 2 + y
    even = y == 0
    rows, width = tokens.shape
    half_rows = rows // 2
    head_cols = HEAD_TILES * LANES
    to_device = lambda i: (i, x * 2 + c)
    peer = lambda k: lax.rem(me + k, count)

    def load(k):
        at = pl.ds(pl.multiple_of(peer(k) * head_cols, LANES), head_cols)
        return pltpu.make_async_copy(weights.at[:, at], w.at[peer(k)], w_sem.at[k])

    for k in range(1, count + 1):
        load(k).start()
    greet([to_device(peer(k)) for k in range(1, count)])

    def norm_rows(at):
        values_at = tokens[at, :].astype(jnp.float32)
        normed[at, :] = (values_at * rms_scale(values_at) * gain[...]).astype(normed.dtype)

    by_rows(rows, norm_rows)

    def out(k):
        return remote(sent.at[peer(k)], qkv.at[me], send.at[k], recv.at[k], to_device(peer(k)))

    def project(k, carry):
        i = peer(k)
        load(k).wait()
        both = jnp.dot(normed[...], w[i], preferred_element_type=jnp.float32)
        for tile in range(HEAD_TILES):
            at = slice(tile * LANES, (tile + 1) * LANES)
            sent[i, :, at] = turned(both[:, at], cosine[...], sine_low[...], sine_high[...]).astype(sent.dtype)

        @pl.when(k < count)
        def _():
            out(k).start()

        return carry

    lax.fori_loop(1, count + 1, project, 0)
    qkv[me] = sent[me]

    def arrive(k, carry):
        out(k).wait_recv()
        return carry

    lax.fori_loop(1, count, arrive, 0)
    keep_qkv = pltpu.make_async_copy(qkv, qkv_out, q_sem)
    keep_qkv.start()
    keys_and_values(qkv, keys, values, count, half_rows)

    def back(k):
        return remote(o_sent.at[peer(k)], o_came.at[me], o_send.at[k], o_recv.at[k], to_device(peer(k)))

    def keep(src, half):
        return pltpu.make_async_copy(prob_blocks.at[src, half], probs.at[src, half], p_sem.at[src, half])

    def attend(k, carry):
        src = peer(k)
        halves_out = []
        for half in range(2):
            at = pl.ds(half * half_rows, half_rows)
            queries = jnp.concatenate([qkv[src, at, :LANES], qkv[src, at, LANES : 2 * LANES]], 0)
            score = against(queries, keys[half]) * scale
            in_pack = pl.ds(pl.multiple_of(src * rows + half * half_rows, half_rows), half_rows)
            place = place_row[half]
            allowed = (place >= lowest[in_pack, :]) & (place <= place_column[in_pack, :])
            allowed = jnp.concatenate([allowed, allowed], 0)
            score = jnp.where(allowed, score, masked_score)
            top = jnp.max(score, -1, keepdims=True)
            weight = jnp.exp(score - top)
            total = jnp.sum(weight, -1, keepdims=True)
            low = (weight * (1.0 / total)).astype(prob_blocks.dtype)
            prob_blocks[src, half] = low
            keep(src, half).start()
            summed = jnp.dot(low, values[half], preferred_element_type=jnp.float32)
            full, part = packed_pair(summed[:half_rows], summed[half_rows:], even)
            o_sent[src, at, :] = full.astype(o_sent.dtype)
            halves_out.append(part)
        lane = lanes_of(halves_out[0])
        part = jnp.where(lane < 64, halves_out[0], pltpu.roll(halves_out[1], 64, 1))
        o_sent[src, pl.ds(rows, half_rows), :] = part.astype(o_sent.dtype)

        @pl.when(k < count)
        def _():
            back(k).start()

        return carry

    lax.fori_loop(1, count + 1, attend, 0)
    o_came[me] = o_sent[me]

    def return_arrive(k, carry):
        back(k).wait_recv()
        return carry

    lax.fori_loop(1, count, return_arrive, 0)
    for pair in range(count // 2):
        at = pair * head_cols
        attended[:, at : at + LANES] = o_came[2 * pair, :rows, :]
        attended[:, at + 2 * LANES : at + 3 * LANES] = o_came[2 * pair + 1, :rows, :]
        one = o_came[2 * pair, rows:, :].astype(jnp.float32)
        two = o_came[2 * pair + 1, rows:, :].astype(jnp.float32)
        lane = lanes_of(one)
        middle = slice(at + LANES, at + 2 * LANES)
        attended[:half_rows, middle] = jnp.where(lane < 64, one, pltpu.roll(two, 64, 1)).astype(attended.dtype)
        attended[half_rows:, middle] = jnp.where(lane < 64, pltpu.roll(one, 64, 1), two).astype(attended.dtype)

    def drain(k, carry):
        out(k).wait_send()
        back(k).wait_send()
        return carry

    lax.fori_loop(1, count, drain, 0)

    def drain_probs(src, carry):
        keep(src, 0).wait()
        keep(src, 1).wait()
        return carry

    lax.fori_loop(0, count, drain_probs, 0)
    keep_qkv.wait()


def attend(scale, weights, tokens, gain, tables, lowest, place_column, place_row, count, identity):
    rows, width = tokens.shape
    half_rows = rows // 2
    half = count * half_rows
    head_cols = HEAD_TILES * LANES
    low = tokens.dtype
    shape = jax.ShapeDtypeStruct
    vmem, anywhere = pl.BlockSpec(memory_space=pltpu.VMEM), pl.BlockSpec(memory_space=pl.ANY)
    dma = pltpu.SemaphoreType.DMA
    return pl.pallas_call(
        functools.partial(attend_kernel, scale),
        out_shape=[
            shape((rows, width), low),
            shape((rows, width), low),
            shape((count, rows, head_cols), low),
            shape((count, 2, rows, half), low),
        ],
        in_specs=[anywhere] + [vmem] * 8,
        out_specs=[vmem, vmem, anywhere, anywhere],
        scratch_shapes=[
            pltpu.VMEM((count, width, head_cols), low),
            pltpu.VMEM((count, rows, head_cols), low),
            pltpu.VMEM((count, rows, head_cols), low),
            pltpu.VMEM((2, half, LANES), low),
            pltpu.VMEM((2, half, LANES), low),
            pltpu.VMEM((count, 2, rows, half), low),
            pltpu.VMEM((count, rows + half_rows, LANES), low),
            pltpu.VMEM((count, rows + half_rows, LANES), low),
            dma((count + 1,)),
            dma((count,)),
            dma((count,)),
            dma((count,)),
            dma((count,)),
            dma((count, 2)),
            dma,
        ],
        compiler_params=pltpu.CompilerParams(collective_id=identity, vmem_limit_bytes=VMEM_LIMIT),
        name="attend",
    )(weights, tokens, gain, *tables, lowest, place_column, place_row)


def attend_back_kernel(
    scale, attended_grad, qkv, probs, cosine, sine_low, sine_high, qkv_grad,
    sent, came, keys, values, prob_blocks, dk_sum, dv_sum, back_sent, back_came,
    send, recv, back_send, back_recv, p_sem,
):
    z, y, x, c = coordinates()
    count = sent.shape[0]
    me = z * 2 + y
    even = y == 0
    rows, width = attended_grad.shape
    half_rows = rows // 2
    head_cols = HEAD_TILES * LANES
    to_device = lambda i: (i, x * 2 + c)
    peer = lambda k: lax.rem(me + k, count)
    source = lambda k: lax.rem(me + count - k, count)

    def load(src, half):
        return pltpu.make_async_copy(probs.at[src, half], prob_blocks.at[src, half], p_sem.at[src, half])

    def load_start(k, carry):
        load(source(k), 0).start()
        load(source(k), 1).start()
        return carry

    lax.fori_loop(0, count, load_start, 0)
    greet([to_device(peer(k)) for k in range(1, count)])
    for pair in range(count // 2):
        at = pair * head_cols
        sent[2 * pair, :rows, :] = attended_grad[:, at : at + LANES]
        sent[2 * pair + 1, :rows, :] = attended_grad[:, at + 2 * LANES : at + 3 * LANES]
        middle = attended_grad[:, at + LANES : at + 2 * LANES].astype(jnp.float32)
        one, two = middle[:half_rows], middle[half_rows:]
        lane = lanes_of(one)
        sent[2 * pair, rows:, :] = jnp.where(lane < 64, one, pltpu.roll(two, 64, 1)).astype(sent.dtype)
        sent[2 * pair + 1, rows:, :] = jnp.where(lane < 64, pltpu.roll(one, 64, 1), two).astype(sent.dtype)

    def out(k):
        return remote(sent.at[peer(k)], came.at[me], send.at[k], recv.at[k], to_device(peer(k)))

    def begin(k, carry):
        out(k).start()
        return carry

    lax.fori_loop(1, count, begin, 0)
    came[me] = sent[me]
    keys_and_values(qkv, keys, values, count, half_rows)
    dk_sum[...] = jnp.zeros_like(dk_sum)
    dv_sum[...] = jnp.zeros_like(dv_sum)

    def grads(k, carry):
        src = source(k)

        @pl.when(k > 0)
        def _():
            out(k).wait_recv()

        for half in range(2):
            at = pl.ds(half * half_rows, half_rows)
            full = came[src, at, :].astype(jnp.float32)
            part = came[src, pl.ds(rows, half_rows), :].astype(jnp.float32)
            if half:
                part = pltpu.roll(part, 64, 1)
            pair = jnp.concatenate(unpacked_pair(full, part, even), 0).astype(came.dtype)
            queries = jnp.concatenate([qkv[src, at, :LANES], qkv[src, at, LANES : 2 * LANES]], 0)
            load(src, half).wait()
            low = prob_blocks[src, half]
            prob = low.astype(jnp.float32)
            prob_grad = against(pair, values[half])
            delta = jnp.sum(prob * prob_grad, -1, keepdims=True)
            score_low = (prob * (prob_grad - delta)).astype(low.dtype)
            dq = jnp.dot(score_low, keys[half], preferred_element_type=jnp.float32) * scale
            back_sent[src, at, :LANES] = dq[:half_rows].astype(back_sent.dtype)
            back_sent[src, at, LANES : 2 * LANES] = dq[half_rows:].astype(back_sent.dtype)
            dk_sum[half] += transposed(score_low, queries)
            dv_sum[half] += transposed(low, pair)
        return carry

    lax.fori_loop(0, count, grads, 0)

    def back(k):
        return remote(back_sent.at[peer(k)], back_came.at[me], back_send.at[k], back_recv.at[k], to_device(peer(k)))

    def finish(k, carry):
        src = peer(k)
        in_half = pl.ds(pl.multiple_of(src * half_rows, half_rows), half_rows)
        for half in range(2):
            at = pl.ds(half * half_rows, half_rows)
            dk = dk_sum[half, in_half, :] * scale
            dv = dv_sum[half, in_half, :]
            lane = lanes_of(dk)
            for tile in range(HEAD_TILES):
                columns = slice(tile * LANES, (tile + 1) * LANES)
                head = dk if tile == 2 else back_sent[src, at, columns].astype(jnp.float32)
                third = pltpu.roll(dv, HD - 32 * tile, 1)
                back_sent[src, at, columns] = jnp.where(lane < HD, head, third).astype(back_sent.dtype)

        @pl.when(k < count)
        def _():
            back(k).start()

        return carry

    lax.fori_loop(1, count + 1, finish, 0)
    back_came[me] = back_sent[me]

    def turn_back(k, carry):
        src = source(k)

        @pl.when(k > 0)
        def _():
            back(k).wait_recv()

        for tile in range(HEAD_TILES):
            columns = slice(tile * LANES, (tile + 1) * LANES)
            values_at = back_came[src, :, columns].astype(jnp.float32)
            turned_at = turned(values_at, cosine[...], -sine_low[...], -sine_high[...])
            at = pl.ds(pl.multiple_of(src * head_cols + tile * LANES, LANES), LANES)
            qkv_grad[:, at] = turned_at.astype(qkv_grad.dtype)
        return carry

    lax.fori_loop(0, count, turn_back, 0)

    def drain(k, carry):
        out(k).wait_send()
        back(k).wait_send()
        return carry

    lax.fori_loop(1, count, drain, 0)


def attend_back(scale, attended_grad, qkv, probs, tables, identity):
    rows, width = attended_grad.shape
    count, _, head_cols = qkv.shape
    half = probs.shape[-1]
    half_rows = rows // 2
    low = attended_grad.dtype
    vmem, anywhere = pl.BlockSpec(memory_space=pltpu.VMEM), pl.BlockSpec(memory_space=pl.ANY)
    dma = pltpu.SemaphoreType.DMA
    return pl.pallas_call(
        functools.partial(attend_back_kernel, scale),
        out_shape=jax.ShapeDtypeStruct((rows, count * head_cols), low),
        in_specs=[vmem, vmem, anywhere] + [vmem] * 3,
        out_specs=vmem,
        scratch_shapes=[
            pltpu.VMEM((count, rows + half_rows, LANES), low),
            pltpu.VMEM((count, rows + half_rows, LANES), low),
            pltpu.VMEM((2, half, LANES), low),
            pltpu.VMEM((2, half, LANES), low),
            pltpu.VMEM((count, 2, rows, half), low),
            pltpu.VMEM((2, half, LANES), jnp.float32),
            pltpu.VMEM((2, half, LANES), jnp.float32),
            pltpu.VMEM((count, rows, head_cols), low),
            pltpu.VMEM((count, rows, head_cols), low),
            dma((count,)),
            dma((count,)),
            dma((count,)),
            dma((count,)),
            dma((count, 2)),
        ],
        compiler_params=pltpu.CompilerParams(collective_id=identity, vmem_limit_bytes=VMEM_LIMIT),
        name="attend_back",
    )(attended_grad, qkv, probs, *tables)


def finish_kernel(
    weights, normed, qkv_grad, attended, branch, hidden_grad, tokens, gain, ffn_terms, loss_terms,
    input_grad, final,
    w, normed_grad, terms, p, held, corner_a, corner_b, from_side, from_over, along, w_sem, send, recv,
):
    lines = p.shape[0]
    rows, width = tokens.shape
    qkv_cols = qkv_grad.shape[1]
    low = normed.dtype
    members, share = p.shape[1:3]
    load = pltpu.make_async_copy(weights.at[:, pl.ds(0, qkv_cols)], w, w_sem)
    load.start()
    load.wait()
    normed_grad[...] = against(qkv_grad[...], w[...])

    def gain_rows(at):
        values = tokens[at, :].astype(jnp.float32)
        terms[at, :] = (normed_grad[at, :] * (values * rms_scale(values))).astype(low)

    by_rows(rows, gain_rows)
    lane = lax.broadcasted_iota(jnp.int32, (rows, LANES), 1)
    pick = lambda i: jnp.where(lane == i, 1.0, 0.0).astype(low)

    def prepare(block):
        at = pl.ds(pl.multiple_of(block * members * share, LANES), members * share)
        store = lambda start, value: p.__setitem__(
            (block, slice(None), slice(None), slice(start, start + value.shape[1])),
            value.astype(low).reshape(members, share, value.shape[1]),
        )
        left = normed[:, at]
        chunk = qkv_cols // 2
        for start in range(0, qkv_cols, chunk):
            store(start, transposed(left, qkv_grad[:, start : start + chunk]))
        store(qkv_cols, transposed(attended[:, at], branch[...]))
        extra = transposed(terms[:, at], pick(0)) + transposed(ffn_terms[:, at], pick(1))
        store(qkv_cols + width, extra + loss_terms[...])

    def between():
        def grad_rows(at):
            values = tokens[at, :].astype(jnp.float32)
            scale = rms_scale(values)
            unit = values * scale
            scaled = normed_grad[at, :] * gain[...]
            input_grad[at, :] = hidden_grad[at, :] + scale * (
                scaled - unit * jnp.mean(scaled * unit, -1, keepdims=True)
            )

        by_rows(rows, grad_rows)

    reduce_kernel(
        lines, lines, prepare, between, p, final, held, corner_a, corner_b, from_side, from_over, along, send, recv
    )


def finish(lines, weights, normed, qkv_grad, attended, branch, hidden_grad, tokens, gain, ffn_terms, loss_terms, identity):
    rows, width = tokens.shape
    qkv_cols = qkv_grad.shape[1]
    share = weights.shape[0] // (lines * PLANE)
    columns = weights.shape[1]
    cut = column_cut(columns)
    low = tokens.dtype
    vmem, anywhere = pl.BlockSpec(memory_space=pltpu.VMEM), pl.BlockSpec(memory_space=pl.ANY)
    dma = pltpu.SemaphoreType.DMA
    return pl.pallas_call(
        finish_kernel,
        out_shape=[
            jax.ShapeDtypeStruct((rows, width), jnp.float32),
            jax.ShapeDtypeStruct((share, columns), jnp.float32),
        ],
        in_specs=[anywhere] + [vmem] * 9,
        out_specs=[vmem, vmem],
        scratch_shapes=[
            pltpu.VMEM((width, qkv_cols), low),
            pltpu.VMEM((rows, width), jnp.float32),
            pltpu.VMEM((rows, width), low),
            pltpu.VMEM((lines, PLANE, share, columns), low),
            pltpu.VMEM((lines, 4, share, columns), low),
            pltpu.VMEM((lines, share, cut), low),
            pltpu.VMEM((lines, share, columns - cut), low),
            pltpu.VMEM((lines, share, columns), low),
            pltpu.VMEM((lines, share, columns), low),
            pltpu.VMEM((lines - 1, share, columns), low),
            dma,
            dma((lines, 11)),
            dma((lines, 11)),
        ],
        compiler_params=pltpu.CompilerParams(collective_id=identity, vmem_limit_bytes=VMEM_LIMIT),
        name="finish",
    )(weights, normed, qkv_grad, attended, branch, hidden_grad, tokens, gain, ffn_terms, loss_terms)


def plane_per_device(lines, *arrays):
    (
        tokens,
        lengths,
        deal,
        loss_mask,
        teacher,
        out_grad,
        attn_gain,
        w_query,
        w_key,
        w_value,
        w_out,
        ffn_gain,
        w_gate,
        w_up,
        w_down,
    ) = arrays
    count_ctx = lax.axis_size("ctx")
    devices = lines * PLANE
    myself = lax.axis_index("ctx")
    number = myself * lax.axis_size("fsdp") + lax.axis_index("fsdp")
    tok_rows, width = tokens.shape[1:]
    half_block = tok_rows // 2
    groups = HEADS // KV
    scale = HD ** (-0.5)
    weight_rows = w_query.shape[0]
    hidden_units = w_gate.shape[1]
    down_rows = w_down.shape[0]
    share = hidden_units // PLANE
    low = jnp.bfloat16
    z_lines = [[zz * 2 + yy for zz in range(lines)] for yy in range(2)]

    dealt = jnp.arange(count_ctx * tok_rows, dtype=jnp.int32)
    local = dealt % tok_rows
    first = jnp.repeat(deal[0], tok_rows)
    block = jnp.where(local < half_block, first, 2 * count_ctx - 1 - first)
    places = block * half_block + local % half_block
    ends = jnp.cumsum(lengths[0])
    after = (places[:, None] >= ends[None, :]).astype(jnp.int32)
    seg_all = jnp.sum(after, 1)
    start_all = jnp.sum(after * lengths[0][None, :], 1)
    own = lambda array: lax.dynamic_slice_in_dim(array, myself * tok_rows, tok_rows)
    own_seg = own(seg_all)
    cosine, sine = [table[:, 0] for table in rotary_tables(own(places) - own(start_all))]
    blank = jnp.zeros_like(sine)
    others = jnp.zeros((tok_rows, LANES - HD), jnp.float32)
    tables = [
        jnp.concatenate(parts, -1)
        for parts in ((cosine, cosine, others + 1.0), (-sine, blank, others), (blank, sine, others))
    ]
    valid = (loss_mask[0] * (own_seg < NSEQ)).astype(jnp.float32)

    split_units = lambda w: jnp.transpose(
        w.reshape(weight_rows, lines, PLANE, down_rows), (2, 0, 1, 3)
    ).reshape(PLANE, weight_rows, share)
    gate_up = jnp.concatenate([split_units(w_gate), split_units(w_up)], -1)
    gate_up = exchange(gate_up, "plane", 1, "gate_up_share").reshape(PLANE * weight_rows, 2 * share)
    gate_up_w = lax.all_gather(gate_up, "ctx", axis=0, tiled=True, axis_index_groups=z_lines)
    down_w = lax.all_gather(w_down, "ctx", axis=0, tiled=True, axis_index_groups=z_lines)

    heads = lambda w, count: w.reshape(weight_rows, KV, count, -1)
    qk_rows = jnp.concatenate([heads(w_query, groups), heads(w_key, 1)], 2)
    head_cols = HEAD_TILES * LANES
    qkv_cols = KV * head_cols
    qkv_rows = jnp.concatenate([qk_rows, heads(w_value, HEAD_TILES)], -1)
    extras = jnp.concatenate(
        [
            attn_gain[:, None],
            ffn_gain[:, None],
            jnp.broadcast_to(jnp.sum(valid).astype(low), (weight_rows, 1)),
            jnp.zeros((weight_rows, LANES - 3), low),
        ],
        -1,
    )
    attn_rows = jnp.concatenate([qkv_rows.reshape(weight_rows, qkv_cols), w_out, extras], -1)
    attn_all = gather_everywhere(attn_rows, lines, 2, "gather_weights")
    extras_all = attn_all[:, :, qkv_cols + width :]
    attn_all = attn_all.reshape(devices * weight_rows, -1)
    gain_first = extras_all[:, :, 0].reshape(-1).astype(jnp.float32)
    gain_second = extras_all[:, :, 1].reshape(-1).astype(jnp.float32)
    valid_count = jnp.sum(extras_all[:, 0, 2].astype(jnp.float32))

    half = count_ctx * half_block
    low_all = jnp.where(seg_all < NSEQ, start_all, places)
    place_row = jnp.transpose(places.reshape(count_ctx, 2, half_block), (1, 0, 2)).reshape(2, 1, half)
    attended_low, normed_low, qkv, probs = attend(
        scale, attn_all, tokens[0], gain_first[None], tables, low_all[:, None], places[:, None], place_row, count_ctx, 3
    )

    result, square, hidden_grad, branch_low, attended_grad, ffn_terms, down_grad, both_grad = feed_forward(
        attn_all,
        attended_low,
        tokens[0],
        teacher[0],
        out_grad[0],
        valid[:, None],
        gain_second[None],
        (2.0 / (valid_count * width)).reshape(1, 1),
        gate_up_w,
        down_w,
        5,
    )
    square_sum = jnp.sum(square)
    down_final = lax.psum_scatter(
        down_grad, "ctx", scatter_dimension=0, tiled=True, axis_index_groups=z_lines
    ).astype(jnp.float32)
    both_final = lax.psum_scatter(both_grad, "ctx", scatter_dimension=0, tiled=True, axis_index_groups=z_lines)

    qkv_grad = attend_back(scale, attended_grad, qkv, probs, tables, 9)

    top = square_sum.astype(low)
    rest = square_sum - top.astype(jnp.float32)
    middle = rest.astype(low)
    bottom = (rest - middle.astype(jnp.float32)).astype(low)
    terms = jnp.where(jnp.arange(devices) == number, jnp.stack([top, middle, bottom])[:, None], jnp.zeros((), low))
    terms = jnp.concatenate([jnp.zeros((2,), low), terms.reshape(-1), jnp.zeros((LANES - 2 - 3 * devices,), low)])
    input_grad, final = finish(
        lines,
        attn_all,
        normed_low,
        qkv_grad,
        attended_low,
        branch_low,
        hidden_grad,
        tokens[0],
        gain_first[None],
        ffn_terms,
        terms.astype(jnp.float32)[None],
        11,
    )
    qkv_final = final[:, :qkv_cols].reshape(weight_rows, KV, HEAD_TILES, LANES)
    pieces = [qkv_final[:, :, :groups, :HD], qkv_final[:, :, groups, :HD], qkv_final[..., HD:]]
    query_final, key_final, value_final = [piece.reshape(weight_rows, -1) for piece in pieces]
    out_final = final[:, qkv_cols : qkv_cols + width]
    tail = final[:, qkv_cols + width :]
    loss = jnp.sum(tail[0, 2 : 2 + 3 * devices]) / (valid_count * width)

    both_final = exchange(both_final.reshape(PLANE, weight_rows, 2 * share), "plane", 12, "gate_up_grads")
    both_final = both_final.reshape(PLANE, weight_rows, 2, lines, down_rows).astype(jnp.float32)
    gate_final, up_final = [
        jnp.transpose(both_final[:, :, i], (1, 2, 0, 3)).reshape(weight_rows, hidden_units) for i in range(2)
    ]
    return (
        result[None],
        loss,
        input_grad[None],
        tail[:, 0],
        query_final,
        key_final,
        value_final,
        out_final,
        tail[:, 1],
        gate_final,
        up_final,
        down_final,
    )


def suits_planes(mesh):
    sizes = dict(mesh.shape)
    return sizes["fsdp"] == 4 and sizes["ctx"] == KV


def solution(mesh):
    placed = (
        P("fsdp", "ctx", None),
        P("fsdp", None),
        P("fsdp", None),
        P("fsdp", "ctx"),
        P("fsdp", "ctx", None),
        P("fsdp", "ctx", None),
        P(("ctx", "fsdp")),
        P(("ctx", "fsdp"), None),
        P(("ctx", "fsdp"), None),
        P(("ctx", "fsdp"), None),
        P(("ctx", "fsdp"), None),
        P(("ctx", "fsdp")),
        P(("ctx", "fsdp"), None),
        P(("ctx", "fsdp"), None),
        P(("ctx", "fsdp"), None),
    )
    if suits_planes(mesh):
        per_device = functools.partial(plane_per_device, mesh.shape["ctx"] // ROWS_Y)
    else:
        per_device = ring_per_device
    return jax.shard_map(
        per_device,
        mesh=mesh,
        in_specs=placed,
        out_specs=(
            P("fsdp", "ctx", None),
            P(),
            P("fsdp", "ctx", None),
            P(("ctx", "fsdp")),
            P(("ctx", "fsdp"), None),
            P(("ctx", "fsdp"), None),
            P(("ctx", "fsdp"), None),
            P(("ctx", "fsdp"), None),
            P(("ctx", "fsdp")),
            P(("ctx", "fsdp"), None),
            P(("ctx", "fsdp"), None),
            P(("ctx", "fsdp"), None),
        ),
        check_vma=False,
    )
```

```python
import functools

import jax
import jax.numpy as jnp
from jax import lax
from jax.experimental import pallas as pl
from jax.experimental.pallas import tpu as pltpu
from jax.sharding import PartitionSpec as P

HEADS = 16
KV = 8
HD = 96
NSEQ = 6


rope_base = 100000.0
epsilon = 1e-05
masked_score = -1e30


def shifted(value, axis, by):
    size = lax.axis_size(axis)
    return lax.ppermute(value, axis, [(i, (i + by) % size) for i in range(size)])


def rms_scale(values):
    return lax.rsqrt(jnp.mean(values * values, -1, keepdims=True) + epsilon)


def rotary_tables(inseq):
    freq = rope_base ** (-(jnp.arange(HD // 2, dtype=jnp.float32) * 2.0 / HD))
    angle = inseq.astype(jnp.float32)[:, None] * freq[None, :]
    return (jnp.cos(angle)[:, None, :], jnp.sin(angle)[:, None, :])


def rotary(values, cosine, sine):
    half = values.shape[-1] // 2
    first = values[..., :half]
    second = values[..., half:]
    return jnp.concatenate([first * cosine - second * sine, second * cosine + first * sine], -1)


def rotary_back(grads, cosine, sine):
    half = grads.shape[-1] // 2
    first = grads[..., :half]
    second = grads[..., half:]
    return jnp.concatenate([first * cosine + second * sine, second * cosine - first * sine], -1)


def transposed(left, right):
    return lax.dot_general(
        left, right, (((0,), (0,)), ((), ())), preferred_element_type=jnp.float32
    )


def against(left, right):
    return lax.dot_general(
        left, right, (((1,), (1,)), ((), ())), preferred_element_type=jnp.float32
    )


def permitted(query_place, query_seg, key_place, key_seg):
    same = (query_seg[:, None] == key_seg[None, :]) & (query_seg[:, None] < NSEQ)
    return same & (key_place[None, :] <= query_place[:, None]) | (
        key_place[None, :] == query_place[:, None]
    )


def ring_per_device(
    tokens,
    lengths,
    deal,
    loss_mask,
    teacher,
    out_grad,
    attn_gain,
    w_query,
    w_key,
    w_value,
    w_out,
    ffn_gain,
    w_gate,
    w_up,
    w_down,
):
    count_ctx = lax.axis_size("ctx")
    myself = lax.axis_index("ctx")
    tok_rows = tokens.shape[1]
    width = tokens.shape[2]
    half_block = tok_rows // 2
    groups = HEADS // KV
    scale = HD ** (-0.5)
    gain_one, query_w, key_w, value_w, out_w = (
        lax.all_gather(attn_gain, ("ctx", "fsdp"), axis=0, tiled=True),
        lax.all_gather(w_query, ("ctx", "fsdp"), axis=0, tiled=True),
        lax.all_gather(w_key, ("ctx", "fsdp"), axis=0, tiled=True),
        lax.all_gather(w_value, ("ctx", "fsdp"), axis=0, tiled=True),
        lax.all_gather(w_out, ("ctx", "fsdp"), axis=0, tiled=True),
    )
    gain_two, gate_w, up_w, down_w = (
        lax.all_gather(ffn_gain, ("ctx", "fsdp"), axis=0, tiled=True),
        lax.all_gather(w_gate, ("ctx", "fsdp"), axis=0, tiled=True),
        lax.all_gather(w_up, ("ctx", "fsdp"), axis=0, tiled=True),
        lax.all_gather(w_down, ("ctx", "fsdp"), axis=0, tiled=True),
    )
    dealt = jnp.arange(count_ctx * tok_rows, dtype=jnp.int32)
    local = dealt % tok_rows
    first = jnp.repeat(deal[0], tok_rows)
    block = jnp.where(local < half_block, first, 2 * count_ctx - 1 - first)
    places = block * half_block + local % half_block
    ends = jnp.cumsum(lengths[0])
    after = (places[:, None] >= ends[None, :]).astype(jnp.int32)
    seg_all = jnp.sum(after, 1)
    inseq_all = places - jnp.sum(after * lengths[0][None, :], 1)
    own_place = lax.dynamic_slice_in_dim(places, myself * tok_rows, tok_rows)
    own_seg = lax.dynamic_slice_in_dim(seg_all, myself * tok_rows, tok_rows)
    own_inseq = lax.dynamic_slice_in_dim(inseq_all, myself * tok_rows, tok_rows)
    cosine, sine = rotary_tables(own_inseq)
    inputs = tokens[0].astype(jnp.float32)
    scale_one = rms_scale(inputs)
    normed_one = inputs * scale_one
    gain_first = gain_one.astype(jnp.float32)
    normed_low = (normed_one * gain_first).astype(jnp.bfloat16)
    query_pre = jnp.dot(normed_low, query_w, preferred_element_type=jnp.float32).reshape(
        tok_rows, HEADS, HD
    )
    key_pre = jnp.dot(normed_low, key_w, preferred_element_type=jnp.float32).reshape(
        tok_rows, KV, HD
    )
    value_low = jnp.dot(normed_low, value_w, preferred_element_type=jnp.float32).astype(
        jnp.bfloat16
    )
    queries = rotary(query_pre, cosine, sine).astype(jnp.bfloat16).reshape(tok_rows, KV, groups, HD)
    keys = rotary(key_pre, cosine, sine).astype(jnp.bfloat16).reshape(tok_rows, KV * HD)

    def logits(key_block):
        return (
            jnp.einsum(
                "qcgd,kcd->cgqk",
                queries,
                key_block.reshape(-1, KV, HD),
                preferred_element_type=jnp.float32,
            )
            * scale
        )

    key_block = lax.all_gather(keys, "ctx", axis=0, tiled=True)
    value_block = lax.all_gather(value_low, "ctx", axis=0, tiled=True)
    allowed = permitted(own_place, own_seg, places, seg_all)
    top = jnp.full((KV, groups, tok_rows, 1), masked_score, jnp.float32)
    score = jnp.where(allowed, logits(key_block), masked_score)
    new_top = jnp.maximum(top, jnp.max(score, -1, keepdims=True))
    weight = jnp.where(allowed, jnp.exp(score - new_top), 0.0)
    summed = jnp.einsum(
        "cgqk,kcd->cgqd",
        weight.astype(jnp.bfloat16),
        value_block.reshape(-1, KV, HD),
        preferred_element_type=jnp.float32,
    )
    summed, top, total = (summed, new_top, jnp.sum(weight, -1, keepdims=True))
    attended = summed / total
    log_total = top + jnp.log(total)
    attended_low = (
        jnp.transpose(attended, (2, 0, 1, 3)).reshape(tok_rows, HEADS * HD).astype(jnp.bfloat16)
    )
    hidden = inputs + jnp.dot(attended_low, out_w, preferred_element_type=jnp.float32)
    scale_two = rms_scale(hidden)
    normed_two = hidden * scale_two
    gain_second = gain_two.astype(jnp.float32)
    ffn_low = (normed_two * gain_second).astype(jnp.bfloat16)
    gate = jnp.dot(ffn_low, gate_w, preferred_element_type=jnp.float32)
    up = jnp.dot(ffn_low, up_w, preferred_element_type=jnp.float32)
    sigmoid = jax.nn.sigmoid(gate)
    activated = gate * sigmoid
    mixed_low = (activated * up).astype(jnp.bfloat16)
    result = hidden + jnp.dot(mixed_low, down_w, preferred_element_type=jnp.float32)
    target = teacher[0].astype(jnp.float32)
    valid = (loss_mask[0] * (own_seg < NSEQ)).astype(jnp.float32)[:, None]
    differ = result - target
    square_sum, valid_count = lax.psum(
        (jnp.sum(valid * differ * differ), jnp.sum(valid)), ("ctx", "fsdp")
    )
    loss = square_sum / (valid_count * width)
    out_total = out_grad[0].astype(jnp.float32) + 2.0 * valid * differ / (valid_count * width)
    out_low = out_total.astype(jnp.bfloat16)
    down_grad = transposed(mixed_low, out_low)
    mixed_grad = against(out_low, down_w)
    silu_slope = sigmoid * (1.0 + gate * (1.0 - sigmoid))
    gate_low = (mixed_grad * up * silu_slope).astype(jnp.bfloat16)
    up_low = (mixed_grad * activated).astype(jnp.bfloat16)
    gate_grad = transposed(ffn_low, gate_low)
    up_grad = transposed(ffn_low, up_low)
    normed_grad = against(gate_low, gate_w) + against(up_low, up_w)
    gain_two_grad = jnp.sum(normed_grad * normed_two, 0)
    scaled_two = normed_grad * gain_second
    hidden_grad = out_total + scale_two * (
        scaled_two - normed_two * jnp.mean(scaled_two * normed_two, -1, keepdims=True)
    )
    ffn_final = (
        lax.psum_scatter(gain_two_grad, ("ctx", "fsdp"), scatter_dimension=0, tiled=True),
        lax.psum_scatter(gate_grad, ("ctx", "fsdp"), scatter_dimension=0, tiled=True),
        lax.psum_scatter(up_grad, ("ctx", "fsdp"), scatter_dimension=0, tiled=True),
        lax.psum_scatter(down_grad, ("ctx", "fsdp"), scatter_dimension=0, tiled=True),
    )
    branch_low = hidden_grad.astype(jnp.bfloat16)
    out_w_grad = transposed(attended_low, branch_low)
    attended_grad = against(branch_low, out_w).astype(jnp.bfloat16)
    grad_heads = jnp.transpose(attended_grad.reshape(tok_rows, KV, groups, HD), (1, 2, 0, 3))
    delta = jnp.sum(grad_heads.astype(jnp.float32) * attended, -1, keepdims=True)

    def cycle_step(step, state):
        key_block, value_block, key_acc, value_acc, query_acc = state
        source = (myself - step) % count_ctx
        allowed = permitted(
            own_place,
            own_seg,
            lax.dynamic_slice_in_dim(places, source * tok_rows, tok_rows),
            lax.dynamic_slice_in_dim(seg_all, source * tok_rows, tok_rows),
        )
        current_key = key_block
        current_value = value_block
        keys_three = current_key.reshape(tok_rows, KV, HD)
        values_three = current_value.reshape(tok_rows, KV, HD)
        prob = jnp.where(allowed, jnp.exp(logits(current_key) - log_total), 0.0)
        prob_grad = jnp.einsum(
            "cgqd,kcd->cgqk", grad_heads, values_three, preferred_element_type=jnp.float32
        )
        score_low = (prob * (prob_grad - delta)).astype(jnp.bfloat16)
        query_add = (
            jnp.einsum("cgqk,kcd->cgqd", score_low, keys_three, preferred_element_type=jnp.float32)
            * scale
        )
        key_add = (
            jnp.einsum(
                "cgqk,qcgd->kcd", score_low, queries, preferred_element_type=jnp.float32
            ).reshape(tok_rows, KV * HD)
            * scale
        )
        value_add = jnp.einsum(
            "cgqk,cgqd->kcd",
            prob.astype(jnp.bfloat16),
            grad_heads,
            preferred_element_type=jnp.float32,
        ).reshape(tok_rows, KV * HD)
        key_block, value_block = shifted((key_block, value_block), "ctx", 1)
        key_acc, value_acc = (
            shifted((key_acc + key_add).astype(jnp.bfloat16), "ctx", 1).astype(jnp.float32),
            shifted((value_acc + value_add).astype(jnp.bfloat16), "ctx", 1).astype(jnp.float32),
        )
        return (key_block, value_block, key_acc, value_acc, query_acc + query_add)

    cycle_start = (
        keys,
        value_low,
        jnp.zeros((tok_rows, KV * HD), jnp.float32),
        jnp.zeros((tok_rows, KV * HD), jnp.float32),
        jnp.zeros((KV, groups, tok_rows, HD), jnp.float32),
    )
    cycle_end = lax.fori_loop(0, count_ctx, cycle_step, cycle_start)
    key_acc = cycle_end[2]
    value_acc = cycle_end[3]
    query_acc = cycle_end[4]
    query_grad = jnp.transpose(query_acc, (2, 0, 1, 3)).reshape(tok_rows, HEADS, HD)
    query_low = (
        rotary_back(query_grad, cosine, sine).reshape(tok_rows, HEADS * HD).astype(jnp.bfloat16)
    )
    key_low = (
        rotary_back(key_acc.reshape(tok_rows, KV, HD), cosine, sine)
        .reshape(tok_rows, KV * HD)
        .astype(jnp.bfloat16)
    )
    value_grad_low = value_acc.astype(jnp.bfloat16)
    query_w_grad = transposed(normed_low, query_low)
    key_w_grad = transposed(normed_low, key_low)
    value_w_grad = transposed(normed_low, value_grad_low)
    normed_one_grad = (
        against(query_low, query_w) + against(key_low, key_w) + against(value_grad_low, value_w)
    )
    gain_one_grad = jnp.sum(normed_one_grad * normed_one, 0)
    scaled_one = normed_one_grad * gain_first
    input_grad = hidden_grad + scale_one * (
        scaled_one - normed_one * jnp.mean(scaled_one * normed_one, -1, keepdims=True)
    )
    attn_final = (
        lax.psum_scatter(gain_one_grad, ("ctx", "fsdp"), scatter_dimension=0, tiled=True),
        lax.psum_scatter(query_w_grad, ("ctx", "fsdp"), scatter_dimension=0, tiled=True),
        lax.psum_scatter(key_w_grad, ("ctx", "fsdp"), scatter_dimension=0, tiled=True),
        lax.psum_scatter(value_w_grad, ("ctx", "fsdp"), scatter_dimension=0, tiled=True),
        lax.psum_scatter(out_w_grad, ("ctx", "fsdp"), scatter_dimension=0, tiled=True),
    )
    return (
        result.astype(jnp.bfloat16)[None],
        loss,
        input_grad[None],
        attn_final[0],
        attn_final[1],
        attn_final[2],
        attn_final[3],
        attn_final[4],
        ffn_final[0],
        ffn_final[1],
        ffn_final[2],
        ffn_final[3],
    )


MESH = pl.DeviceIdType.MESH
ROWS_Y = 2
PLANE = 8
LANES = 128
VMEM_LIMIT = 60 * 2**20


def coordinates():
    ctx = lax.axis_index("ctx")
    fsdp = lax.axis_index("fsdp")
    return ctx // 2, ctx % 2, fsdp // 2, fsdp % 2


def device(z, y, x, c):
    return (z * 2 + y, x * 2 + c)


def greet(devices):
    barrier = pltpu.get_barrier_semaphore()
    for other in devices:
        pl.semaphore_signal(barrier, inc=1, device_id=other, device_id_type=MESH)
    pl.semaphore_wait(barrier, len(devices))


def remote(src, dst, send, recv, target):
    return pltpu.make_async_remote_copy(
        src_ref=src,
        dst_ref=dst,
        send_sem=send,
        recv_sem=recv,
        device_id=target,
        device_id_type=MESH,
    )


def line_gather(place, lines, x_ref, o_ref, send, recv, here=None):
    z, y, x, c = place
    mine = None if here is None else pltpu.make_async_copy(x_ref, o_ref.at[z], here)
    ways = ((0, -1, device(z + 1, y, x, c)), (1, 1, device(z - 1, y, x, c)))

    def along(way, sign, to, s):
        zz = z + sign * (s - 1)
        return remote(x_ref if s == 1 else o_ref.at[zz], o_ref.at[zz], send.at[way, s], recv.at[way, s], to)

    def sends(sign, s):
        if sign < 0:
            return (z - (s - 1) >= 0) & (z + 1 < lines)
        return (z + (s - 1) < lines) & (z - 1 >= 0)

    def present(sign, s):
        return z - s >= 0 if sign < 0 else z + s < lines

    def start(s):
        for way, sign, to in ways:
            pl.when(sends(sign, s))(lambda way=way, sign=sign, to=to: along(way, sign, to, s).start())

    def begin():
        if mine is not None:
            mine.start()
        start(1)

    def pass_on(s):
        for way, sign, to in ways:
            pl.when(present(sign, s))(lambda way=way, sign=sign, to=to: along(way, sign, to, s).wait_recv())
        if s + 1 < lines:
            start(s + 1)

    def last():
        for s in range(1, lines):
            for way, sign, to in ways:
                pl.when(sends(sign, s))(lambda way=way, sign=sign, to=to, s=s: along(way, sign, to, s).wait_send())
        if mine is not None:
            mine.wait()

    return begin, pass_on, last


def line_reduce(place, lines, parts, up, down, send, recv):
    z, y, x, c = place
    ways = ((0, up, device(z + 1, y, x, c)), (1, down, device(z - 1, y, x, c)))

    def copy(way, t, own):
        _, sums, to = ways[way]
        src = parts.at[t] if own else sums.at[t]
        return remote(src, sums.at[t], send.at[way, t], recv.at[way, t], to)

    def begin():
        @pl.when(z == 0)
        def _():
            for t in range(lines - 1, 0, -1):
                copy(0, t, True).start()

        @pl.when(z == lines - 1)
        def _():
            for t in range(lines - 1):
                copy(1, t, True).start()

    def add_on(way, t):
        copy(way, t, False).wait_recv()
        add_rows(ways[way][1].at[t], parts.at[t])
        copy(way, t, False).start()

    def hop(moment):
        for t in range(lines):
            for zz in range(1, lines - 1):
                if zz < t and zz + (lines - 1 - t) == moment:
                    pl.when(z == zz)(functools.partial(add_on, 0, t))
                if zz > t and (lines - 1 - zz) + t == moment:
                    pl.when(z == zz)(functools.partial(add_on, 1, t))

    def last(write):
        for way, first in ((0, 0), (1, lines - 1)):

            @pl.when(z != first)
            def _():
                copy(way, z, False).wait_recv()

        def body(at):
            from_below = jnp.where(z > 0, up[z, at, :].astype(jnp.float32), 0.0)
            from_above = jnp.where(z < lines - 1, down[z, at, :].astype(jnp.float32), 0.0)
            write(at, parts[z, at, :].astype(jnp.float32) + from_below + from_above)

        by_rows(parts.shape[1], body, 32)
        for zz in range(lines):

            @pl.when(z == zz)
            def _():
                for t in range(lines):
                    if t > zz:
                        copy(0, t, zz == 0).wait_send()
                    if t < zz:
                        copy(1, t, zz == lines - 1).wait_send()

    return begin, hop, last


def column_cut(width):
    tiles = width // LANES
    return (tiles + 1) // 2 * LANES


def gather_plan(lines, x_ref, o_ref, send, recv, here):
    z, y, x, c = coordinates()
    width = x_ref.shape[1]
    cut = column_cut(width)
    first, second = pl.ds(0, cut), pl.ds(cut, width - cut)
    side, over, sibling = device(z, y, 1 - x, c), device(z, 1 - y, x, c), device(z, y, x, 1 - c)
    above, below = device(z + 1, y, x, c), device(z - 1, y, x, c)
    slot = lambda zz, yy, xx, cc: (zz * 2 + yy) * 4 + xx * 2 + cc
    mine = pltpu.make_async_copy(x_ref, o_ref.at[slot(z, y, x, c)], here)

    def item(sign, s):
        index = 0 if s == 0 else (2 * s - 1 if sign < 0 else 2 * s)
        zz = z + sign * s
        at = lambda yy, xx, cc: o_ref.at[slot(zz, yy, xx, cc)]
        own = x_ref if s == 0 else at(y, x, c)
        make = lambda kind, src, dst, to: remote(
            src, dst, send.at[index, kind], recv.at[index, kind], to
        )
        same = lambda kind, ref, to: make(kind, ref, ref, to)
        corner_at = lambda columns: at(1 - y, 1 - x, c).at[:, columns]
        return dict(
            side=lambda: make(1, own, at(y, x, c), side),
            over=lambda: make(2, own, at(y, x, c), over),
            side_on=lambda: same(3, at(y, 1 - x, c).at[:, first], over),
            over_on=lambda: same(4, at(1 - y, x, c).at[:, second], side),
            core=lambda: make(5, own, at(y, x, c), sibling),
            core_side=lambda: same(6, at(y, 1 - x, c), sibling),
            core_over=lambda: same(7, at(1 - y, x, c), sibling),
            core_first=lambda: same(8, corner_at(first), sibling),
            core_second=lambda: same(9, corner_at(second), sibling),
        )

    def along(sign, s):
        index = 2 * s - 1 if sign < 0 else 2 * s
        zz = z + sign * (s - 1)
        src = x_ref if s == 1 else o_ref.at[slot(zz, y, x, c)]
        return remote(
            src, o_ref.at[slot(zz, y, x, c)], send.at[index, 0], recv.at[index, 0], above if sign < 0 else below
        )

    def sends_along(sign, s):
        if sign < 0:
            return (z - (s - 1) >= 0) & (z + 1 < lines)
        return (z + (s - 1) < lines) & (z - 1 >= 0)

    def present(sign, s):
        return z - s >= 0 if sign < 0 else z + s < lines

    arrivals = [(-1, 0)] + [(sign, s) for s in range(1, lines) for sign in (-1, 1)]

    def begin(sign, s):
        copies = item(sign, s)
        if s > 0:
            along(sign, s).wait_recv()
        for way in ((-1, 1) if s == 0 else (sign,)):
            if s + 1 < lines:
                @pl.when(sends_along(way, s + 1))
                def _():
                    along(way, s + 1).start()
        copies["side"]().start()
        copies["over"]().start()
        copies["core"]().start()

    def pass_on(sign, s):
        copies = item(sign, s)
        copies["side"]().wait_recv()
        copies["side_on"]().start()
        copies["core_side"]().start()
        copies["over"]().wait_recv()
        copies["over_on"]().start()
        copies["core_over"]().start()

    def corner(sign, s):
        copies = item(sign, s)
        copies["side_on"]().wait_recv()
        copies["core_first"]().start()
        copies["over_on"]().wait_recv()
        copies["core_second"]().start()

    def finish(sign, s):
        copies = item(sign, s)
        for kind in ("core", "core_side", "core_over", "core_first", "core_second"):
            copies[kind]().wait()
        for kind in ("side", "over", "side_on", "over_on"):
            copies[kind]().wait_send()

    def where(sign, s, step):
        if s == 0:
            step(sign, s)
        else:
            pl.when(present(sign, s))(functools.partial(step, sign, s))

    waves = [[(-1, 0)]] + [[(-1, s), (1, s)] for s in range(1, lines)]

    def run(number):
        if number == 0:
            mine.start()
        for stage, lag in ((begin, 0), (pass_on, 1), (corner, 2)):
            if 0 <= number - lag < len(waves):
                for sign, s in waves[number - lag]:
                    where(sign, s, stage)

    def last():
        for sign, s in arrivals:
            where(sign, s, finish)
        for s in range(1, lines):
            for sign in (-1, 1):
                pl.when(sends_along(sign, s))(lambda sign=sign, s=s: along(sign, s).wait_send())
        mine.wait()

    return [functools.partial(run, number) for number in range(len(waves) + 2)], last


def line_of(z, y, x, c, lines):
    return [device(lax.rem(z + k, lines), y, x, c) for k in range(1, lines)]


def gather_semaphores(lines):
    dma = pltpu.SemaphoreType.DMA
    return [dma((2 * lines - 1, 10)), dma((2 * lines - 1, 10)), dma]


def reduce_plan(lines, prepare, p_ref, o_ref, held, corner_a, corner_b, from_side, from_over, along, send, recv):
    z, y, x, c = coordinates()
    parts = lines
    rows, width = held.shape[2], held.shape[3]
    cut = column_cut(width)
    first, second = pl.ds(0, cut), pl.ds(cut, width - cut)
    side, over, sibling = device(z, y, 1 - x, c), device(z, 1 - y, x, c), device(z, y, x, 1 - c)
    def given(part, yy, xx, cc):
        member = yy * 4 + xx * 2 + cc
        return p_ref.at[lax.rem(z + part + 1, lines), member]

    def make(part, kind, src, dst, to):
        return remote(src, dst, send.at[part, kind], recv.at[part, kind], to)

    lane = lambda part, yy, xx: held.at[part, yy * 2 + xx]

    def over_core(part):
        return [
            make(part, yy * 2 + xx, given(part, yy, xx, 1 - c), lane(part, yy, xx), sibling)
            for yy in range(2)
            for xx in range(2)
        ]

    def to_corner(part):
        return (
            make(part, 4, lane(part, 1 - y, 1 - x).at[:, first], corner_a.at[part], over),
            make(part, 5, lane(part, 1 - y, 1 - x).at[:, second], corner_b.at[part], side),
        )

    def to_neighbour(part, way):
        columns = (first, second)[way % 2]
        if way < 2:
            return make(part, 6 + way, lane(part, y, 1 - x).at[:, columns], from_side.at[part, :, columns], side)
        return make(part, 6 + way, lane(part, 1 - y, x).at[:, columns], from_over.at[part, :, columns], over)

    def along_z(part):
        to = lax.rem(z + part + 1, lines)
        return make(part, 10, lane(part, y, x), along.at[part], device(to, y, x, c))

    step = 16

    def add_core(part):
        for copy in over_core(part):
            copy.wait_recv()
        for yy, xx in ((1 - y, 1 - x), (y, 1 - x), (1 - y, x), (y, x)):
            mine, other = given(part, yy, xx, c), lane(part, yy, xx)

            def body(i, carry):
                at = pl.ds(pl.multiple_of(i * step, step), step)
                total = mine[at, :].astype(jnp.float32) + other[at, :].astype(jnp.float32)
                other[at, :] = total.astype(other.dtype)
                return carry

            lax.fori_loop(0, rows // step, body, 0)
        for copy in to_corner(part):
            copy.start()
        to_neighbour(part, 1).start()
        to_neighbour(part, 2).start()

    def add_corner(part):
        copies = to_corner(part)
        pairs = (
            (copies[0], lane(part, y, 1 - x), corner_a.at[part], first),
            (copies[1], lane(part, 1 - y, x), corner_b.at[part], second),
        )
        for copy, mine, other, columns in pairs:
            copy.wait_recv()

            def body(i, carry):
                at = pl.ds(pl.multiple_of(i * step, step), step)
                total = mine[at, columns].astype(jnp.float32) + other[at, :].astype(jnp.float32)
                mine[at, columns] = total.astype(mine.dtype)
                return carry

            lax.fori_loop(0, rows // step, body, 0)
        to_neighbour(part, 0).start()
        to_neighbour(part, 3).start()

    def add_neighbours(part):
        for way in range(4):
            to_neighbour(part, way).wait_recv()
        last = part == parts - 1
        mine = lane(part, y, x)

        def body(i, carry):
            at = pl.ds(pl.multiple_of(i * step, step), step)
            total = mine[at, :].astype(jnp.float32) + from_side[part, at, :].astype(jnp.float32)
            total += from_over[part, at, :].astype(jnp.float32)
            if last:
                o_ref[at, :] = total
            else:
                mine[at, :] = total.astype(mine.dtype)
            return carry

        lax.fori_loop(0, rows // step, body, 0)
        if not last:
            along_z(part).start()

    def ready(part):
        prepare(lax.rem(z + part + 1, lines))
        for copy in over_core(part):
            copy.start()

    kinds = (ready, add_core, add_corner, add_neighbours)

    def run(number):
        for lag, kind in enumerate(kinds):
            if 0 <= number - lag < parts:
                kind(number - lag)

    def last():
        for part in range(parts - 1):
            along_z(part).wait_recv()

        def body(i, carry):
            at = pl.ds(pl.multiple_of(i * step, step), step)
            total = o_ref[at, :]
            for part in range(parts - 1):
                total += along[part, at, :].astype(jnp.float32)
            o_ref[at, :] = total
            return carry

        lax.fori_loop(0, rows // step, body, 0)
        for part in range(parts - 1):
            along_z(part).wait_send()
        for part in range(parts):
            for copy in (*over_core(part), *to_corner(part), *(to_neighbour(part, way) for way in range(4))):
                copy.wait_send()

    return [functools.partial(run, number) for number in range(parts + len(kinds) - 1)], last


def reduce_scratch(lines, share, columns, low):
    cut = column_cut(columns)
    return [
        pltpu.VMEM((lines, PLANE, share, columns), low),
        pltpu.VMEM((lines, 4, share, columns), low),
        pltpu.VMEM((lines, share, cut), low),
        pltpu.VMEM((lines, share, columns - cut), low),
        pltpu.VMEM((lines, share, columns), low),
        pltpu.VMEM((lines, share, columns), low),
        pltpu.VMEM((lines - 1, share, columns), low),
        pltpu.SemaphoreType.DMA((lines, 11)),
        pltpu.SemaphoreType.DMA((lines, 11)),
    ]


def store_terms(p, block, start, value):
    members, share = p.shape[1:3]
    width = value.shape[1]
    p[block, :, :, start : start + width] = value.astype(p.dtype).reshape(members, share, width)


def halves(width):
    cut = column_cut(width)
    return pl.ds(0, cut), pl.ds(cut, width - cut)


def gather_steps(place, whole, send, recv):
    z, y, x, c = place
    side, over, sibling = device(z, y, 1 - x, c), device(z, 1 - y, x, c), device(z, y, x, 1 - c)
    first, second = halves(whole.shape[-1])
    at = lambda yy, xx: whole.at[yy * 4 + xx * 2 + c]
    own, next_x, next_y, corner = at(y, x), at(y, 1 - x), at(1 - y, x), at(1 - y, 1 - x)
    table = (
        (own.at[:, first], side),
        (own.at[:, second], side),
        (own.at[:, first], over),
        (own.at[:, second], over),
        (own, sibling),
        (next_x.at[:, first], over),
        (next_y.at[:, second], side),
        (next_x.at[:, first], sibling),
        (next_x.at[:, second], sibling),
        (next_y.at[:, first], sibling),
        (next_y.at[:, second], sibling),
        (corner.at[:, first], sibling),
        (corner.at[:, second], sibling),
    )

    def copy(kind):
        ref, to = table[kind]
        return remote(ref, ref, send.at[kind], recv.at[kind], to)

    return copy


GATHER_KINDS = 13
REDUCE_KINDS = 10


def reduce_steps(place, partial, held, corner_a, corner_b, from_side, from_over, send, recv):
    z, y, x, c = place
    side, over, sibling = device(z, y, 1 - x, c), device(z, 1 - y, x, c), device(z, y, x, 1 - c)
    first, second = halves(held.shape[-1])
    lane = lambda yy, xx: held.at[yy * 2 + xx]
    next_x, next_y, corner = lane(y, 1 - x), lane(1 - y, x), lane(1 - y, 1 - x)

    def to_core(yy, xx):
        kind = yy * 2 + xx
        src = partial.at[yy * 4 + xx * 2 + 1 - c]
        return remote(src, lane(yy, xx), send.at[kind], recv.at[kind], sibling)

    table = (
        (corner.at[:, first], corner_a, over),
        (corner.at[:, second], corner_b, side),
        (next_x.at[:, first], from_side.at[:, first], side),
        (next_x.at[:, second], from_side.at[:, second], side),
        (next_y.at[:, first], from_over.at[:, first], over),
        (next_y.at[:, second], from_over.at[:, second], over),
    )

    def copy(kind):
        src, dst, to = table[kind]
        return remote(src, dst, send.at[4 + kind], recv.at[4 + kind], to)

    return to_core, copy


def add_rows(target, other, columns=None, step=32):
    def body(i, carry):
        at = pl.ds(pl.multiple_of(i * step, step), step)
        mine = target[at, :] if columns is None else target[at, columns]
        total = (mine.astype(jnp.float32) + other[at, :].astype(jnp.float32)).astype(target.dtype)
        if columns is None:
            target[at, :] = total
        else:
            target[at, columns] = total
        return carry

    lax.fori_loop(0, other.shape[0] // step, body, 0)


def feed_forward_kernel(
    out_rows, attended, tokens, teacher, out_grad, valid, gains, gate_up_w, down_rows,
    result, square, norm, hidden_grad, branch, attended_grad, down_final, both_grad,
    out_w, down_w, down_part, down_came, normed_all, kept, mixed, grads_all, partial, held, corner_a, corner_b, from_side, from_over, hidden, total_grad, scales, squares,
    out_sem, here, line_send, line_recv, down_send, down_recv, gather_send, gather_recv, reduce_send, reduce_recv,
):
    place = coordinates()
    z, y, x, c = place
    width = tokens.shape[1]
    load = pltpu.make_async_copy(out_rows, out_w, out_sem)
    load.start()
    lines, units = down_w.shape[:2]
    greet([device(z, y, 1 - x, c), device(z, 1 - y, x, c), device(z, y, x, 1 - c)] + line_of(z, y, x, c, lines))
    rows = tokens.shape[0]
    share = lines * units
    line_begin, line_pass, line_last = line_gather(place, lines, down_rows, down_w, line_send, line_recv, here)
    line_begin()
    first, second = halves(width)
    mine = y * 4 + x * 2 + c
    chips = ((y, x), (y, 1 - x), (1 - y, x), (1 - y, 1 - x))

    gain = gains[1:2, :]
    count = jnp.sum(gains[2:3, :], -1, keepdims=True) / (width // (lines * PLANE))
    norm[...] = 2.0 / (count * width)
    load.wait()
    hidden[...] = tokens[...].astype(jnp.float32) + jnp.dot(
        attended[...], out_w[...], preferred_element_type=jnp.float32
    )

    def norm_rows(at):
        values = hidden[at, :]
        scale = rms_scale(values)
        scales[at, :] = scale
        normed_all[mine, at, :] = (values * scale * gain[...]).astype(normed_all.dtype)

    by_rows(rows, norm_rows)

    def gathered(phase, whole, compute, late, beside):
        copy = gather_steps(place, whole, gather_send.at[phase], gather_recv.at[phase])
        to_core, pass_on = reduce_steps(
            place, partial, held, corner_a, corner_b, from_side, from_over, reduce_send.at[phase], reduce_recv.at[phase]
        )
        for kind in (0, 3, 4, 1, 2):
            copy(kind).start()

        def wave(yy, xx):
            lax.fori_loop(0, 2, lambda cc, carry: compute(yy * 4 + xx * 2 + cc, carry), 0)
            if late is None:
                to_core(yy, xx).start()

        def late_wave(yy, xx):
            if late is not None:
                lax.fori_loop(0, 2, lambda cc, carry: late(yy * 4 + xx * 2 + cc, carry), 0)
                to_core(yy, xx).start()

        def join(yy, xx):
            to_core(yy, xx).wait_recv()
            add_rows(held.at[yy * 2 + xx], partial.at[yy * 4 + xx * 2 + c])

        copy(4).wait_recv()
        wave(*chips[0])
        copy(0).wait_recv()
        copy(5).start()
        copy(7).start()
        copy(3).wait_recv()
        copy(6).start()
        copy(10).start()
        copy(1).wait_recv()
        copy(8).start()
        copy(2).wait_recv()
        copy(9).start()
        beside(1)
        copy(7).wait_recv()
        copy(8).wait_recv()
        wave(*chips[1])
        beside(2)
        copy(9).wait_recv()
        copy(10).wait_recv()
        wave(*chips[2])
        if late is None:
            join(*chips[1])
            pass_on(3).start()
        copy(5).wait_recv()
        copy(11).start()
        copy(6).wait_recv()
        copy(12).start()
        copy(11).wait_recv()
        copy(12).wait_recv()
        wave(*chips[3])
        beside(3)
        late_wave(*chips[1])
        late_wave(*chips[2])
        if late is not None:
            join(*chips[1])
            pass_on(3).start()
        late_wave(*chips[3])
        join(*chips[2])
        pass_on(4).start()
        late_wave(*chips[0])
        join(*chips[3])
        pass_on(0).start()
        pass_on(1).start()
        join(*chips[0])
        for kind in range(GATHER_KINDS):
            copy(kind).wait_send()
        return to_core, pass_on

    def reduced_rest(to_core, pass_on):
        pass_on(0).wait_recv()
        add_rows(held.at[y * 2 + 1 - x], corner_a, first)
        pass_on(2).start()
        pass_on(1).wait_recv()
        add_rows(held.at[(1 - y) * 2 + x], corner_b, second)
        pass_on(5).start()
        for kind in (2, 3, 4, 5):
            pass_on(kind).wait_recv()
        for kind in range(6):
            pass_on(kind).wait_send()
        for yy, xx in chips:
            to_core(yy, xx).wait_send()

    def summed(at):
        total = held[y * 2 + x, at, :].astype(jnp.float32) + from_side[at, :].astype(jnp.float32)
        return total + from_over[at, :].astype(jnp.float32)

    def forward(member, carry):
        both = jnp.dot(normed_all[member], gate_up_w[...], preferred_element_type=jnp.float32)
        gate, up = both[:, :share], both[:, share:]
        sigmoid = 1.0 / (1.0 + jnp.exp(-gate))
        activated = gate * sigmoid
        kept[member, :, :share] = (up * (sigmoid + activated * (1.0 - sigmoid))).astype(kept.dtype)
        kept[member, :, share:] = activated.astype(kept.dtype)
        low = (activated * up).astype(mixed.dtype)
        mixed[member] = low
        return carry

    def forward_down(member, carry):
        summed_units = jnp.dot(mixed[member], down_w[...].reshape(share, width), preferred_element_type=jnp.float32)
        partial[member] = summed_units.astype(partial.dtype)
        return carry

    def bring_down(moment):
        line_pass(moment)
        if moment == lines - 1:
            line_last()

    reduced_rest(*gathered(0, normed_all, forward, forward_down, bring_down))

    def result_rows(at):
        values = hidden[at, :] + summed(at)
        result[at, :] = values.astype(result.dtype)
        differ = values - teacher[at, :].astype(jnp.float32)
        weighed = valid[at, :] * differ
        squares[at, :] = jnp.sum(weighed * differ, -1, keepdims=True)
        total = out_grad[at, :].astype(jnp.float32) + weighed * norm[...]
        total_grad[at, :] = total
        grads_all[mine, at, :] = total.astype(grads_all.dtype)

    by_rows(rows, result_rows)
    square[...] = jnp.sum(squares[...], 0, keepdims=True)

    def backward(member, carry):
        mixed_grad = against(grads_all[member], down_w[...].reshape(share, width))
        low_gate = (mixed_grad * kept[member, :, :share].astype(jnp.float32)).astype(kept.dtype)
        low_up = (mixed_grad * kept[member, :, share:].astype(jnp.float32)).astype(kept.dtype)
        kept[member, :, :share] = low_gate
        kept[member, :, share:] = low_up
        partial[member] = against(kept[member], gate_up_w[...]).astype(partial.dtype)
        return carry

    rest = gathered(1, grads_all, backward, None, lambda moment: None)
    tokens_all = normed_all.shape[0] * rows
    block = 256

    def down_block(i, carry):
        at = pl.ds(pl.multiple_of(i * block, block), block)
        left = mixed[:, :, at].reshape(tokens_all, block)
        grads = transposed(left, grads_all[...].reshape(tokens_all, width)).astype(down_part.dtype)
        per = block // units
        down_part[pl.ds(i * per, per)] = grads.reshape(per, units, width)
        return carry

    def both_block(i, carry):
        at = pl.ds(pl.multiple_of(i * block, block), block)
        left = normed_all[:, :, at].reshape(tokens_all, block)
        both_grad[at, :] = transposed(left, kept[...].reshape(tokens_all, 2 * share)).astype(both_grad.dtype)
        return carry

    def down_out(k):
        to = lax.rem(z + k, lines)
        return remote(down_part.at[to], down_came.at[k - 1], down_send.at[k - 1], down_recv.at[k - 1], device(to, y, x, c))

    lax.fori_loop(0, share // block, down_block, 0)
    for k in range(1, lines):
        down_out(k).start()
    lax.fori_loop(0, width // block, both_block, 0)
    reduced_rest(*rest)

    def grad_rows(at):
        grads = summed(at)
        normed = hidden[at, :] * scales[at, :]
        scaled = grads * gain[...]
        values = total_grad[at, :] + scales[at, :] * (scaled - normed * jnp.mean(scaled * normed, -1, keepdims=True))
        hidden_grad[at, :] = values
        branch[at, :] = values.astype(branch.dtype)

    by_rows(rows, grad_rows)
    attended_grad[...] = against(branch[...], out_w[...]).astype(attended_grad.dtype)
    for k in range(1, lines):
        down_out(k).wait_recv()

    def down_sum(at):
        total = down_part[z, at, :].astype(jnp.float32)
        for k in range(1, lines):
            total += down_came[k - 1, at, :].astype(jnp.float32)
        down_final[at, :] = total

    by_rows(units, down_sum)
    for k in range(1, lines):
        down_out(k).wait_send()


def feed_forward(lines, out_rows, attended, tokens, teacher, out_grad, valid, gains, gate_up_w, down_rows, identity):
    rows, width = tokens.shape
    units = down_rows.shape[0]
    share = lines * units
    low = tokens.dtype
    shape = jax.ShapeDtypeStruct
    vmem, anywhere = pl.BlockSpec(memory_space=pltpu.VMEM), pl.BlockSpec(memory_space=pl.ANY)
    cut = column_cut(width)
    return pl.pallas_call(
        feed_forward_kernel,
        out_shape=[
            shape((rows, width), low),
            shape((1, 1), jnp.float32),
            shape((1, 1), jnp.float32),
            shape((rows, width), jnp.float32),
            shape((rows, width), low),
            shape((rows, width), low),
            shape((units, width), jnp.float32),
            shape((width, 2 * share), low),
        ],
        in_specs=[anywhere] + [vmem] * 7 + [anywhere],
        out_specs=[vmem] * 8,
        scratch_shapes=[
            pltpu.VMEM((width, width), low),
            pltpu.VMEM((lines, units, width), low),
            pltpu.VMEM((lines, units, width), low),
            pltpu.VMEM((lines - 1, units, width), low),
            pltpu.VMEM((PLANE, rows, width), low),
            pltpu.VMEM((PLANE, rows, 2 * share), low),
            pltpu.VMEM((PLANE, rows, share), low),
            pltpu.VMEM((PLANE, rows, width), low),
            pltpu.VMEM((PLANE, rows, width), low),
            pltpu.VMEM((4, rows, width), low),
            pltpu.VMEM((rows, cut), low),
            pltpu.VMEM((rows, width - cut), low),
            pltpu.VMEM((rows, width), low),
            pltpu.VMEM((rows, width), low),
            pltpu.VMEM((rows, width), jnp.float32),
            pltpu.VMEM((rows, width), jnp.float32),
            pltpu.VMEM((rows, 1), jnp.float32),
            pltpu.VMEM((rows, 1), jnp.float32),
            pltpu.SemaphoreType.DMA,
            pltpu.SemaphoreType.DMA,
            pltpu.SemaphoreType.DMA((2, lines)),
            pltpu.SemaphoreType.DMA((2, lines)),
            pltpu.SemaphoreType.DMA((lines - 1,)),
            pltpu.SemaphoreType.DMA((lines - 1,)),
            pltpu.SemaphoreType.DMA((2, GATHER_KINDS)),
            pltpu.SemaphoreType.DMA((2, GATHER_KINDS)),
            pltpu.SemaphoreType.DMA((2, REDUCE_KINDS)),
            pltpu.SemaphoreType.DMA((2, REDUCE_KINDS)),
        ],
        compiler_params=pltpu.CompilerParams(collective_id=identity, vmem_limit_bytes=VMEM_LIMIT),
        cost_estimate=pl.CostEstimate(flops=40 * PLANE * rows * width * share // 2, bytes_accessed=30 * 2**20, transcendentals=0),
        name="feed_forward",
    )(out_rows, attended, tokens, teacher, out_grad, valid, gains, gate_up_w, down_rows)


HEAD_TILES = 3
ROW_STEP = 64


def by_rows(rows, body, step=ROW_STEP):
    def run(i, carry):
        body(pl.ds(pl.multiple_of(i * step, step), step))
        return carry

    lax.fori_loop(0, rows // step, run, 0)


def lanes_of(values):
    return lax.broadcasted_iota(jnp.int32, values.shape, len(values.shape) - 1)


def turned(tile, cosine, sine):
    half = HD // 2
    partner = jnp.where(lanes_of(tile) < half, -pltpu.roll(tile, LANES - half, 1), pltpu.roll(tile, half, 1))
    return tile * cosine + partner * sine


def packed_pair(first, second, even):
    lane = lanes_of(first)
    moved = pltpu.roll(second, HD, 1)
    full_even = jnp.where(lane < HD, first, moved)
    full_odd = jnp.where(lane < 32, pltpu.roll(first, 64, 1), pltpu.roll(second, 32, 1))
    return jnp.where(even, full_even, full_odd), jnp.where(even, moved, first)


def unpacked_pair(full, part, even):
    lane = lanes_of(full)
    zero = jnp.zeros_like(full)
    first_even = jnp.where(lane < HD, full, zero)
    second_even = jnp.where(lane < 32, pltpu.roll(full, 32, 1), jnp.where(lane < HD, pltpu.roll(part, 32, 1), zero))
    first_odd = jnp.where(lane < 64, part, jnp.where(lane < HD, pltpu.roll(full, 64, 1), zero))
    second_odd = jnp.where(lane < HD, pltpu.roll(full, HD, 1), zero)
    return jnp.where(even, first_even, first_odd), jnp.where(even, second_even, second_odd)


def keys_and_values(qkv, keys, values, count, rows):
    def body(src, carry):
        block = qkv[src].astype(jnp.float32)
        tiles = [block[:, i * LANES : (i + 1) * LANES] for i in range(HEAD_TILES)]
        lane = lanes_of(tiles[0])
        key = jnp.where(lane < HD, tiles[2], 0.0)
        value = jnp.where(lane < 64, pltpu.roll(tiles[1], 64, 1), pltpu.roll(tiles[2], HD, 1))
        value = jnp.where(lane < 32, pltpu.roll(tiles[0], 32, 1), value)
        value = jnp.where(lane < HD, value, 0.0)
        at = pl.ds(pl.multiple_of(src * rows, rows), rows)
        for half in range(2):
            keys[half, at, :] = key[half * rows : (half + 1) * rows].astype(keys.dtype)
            values[half, at, :] = value[half * rows : (half + 1) * rows].astype(values.dtype)
        return carry

    lax.fori_loop(0, count, body, 0)


def segment_of(lengths, place):
    start, end = jnp.zeros_like(place), 0
    for length in [lengths[0, j] for j in range(NSEQ)]:
        end = end + length
        start = start + jnp.where(place >= end, length, 0)
    return start, end


def side_by_side(heads):
    full, part = packed_pair(heads[0], heads[1], True)
    full_odd, part_odd = packed_pair(heads[2], heads[3], False)
    middle = jnp.where(lanes_of(part) < 64, part, pltpu.roll(part_odd, 64, 1))
    return full, middle, full_odd


def apart(ref, group):
    start = group * HEAD_TILES * LANES
    tiles = [ref[:, start + i * LANES : start + (i + 1) * LANES].astype(jnp.float32) for i in range(HEAD_TILES)]
    return unpacked_pair(tiles[0], tiles[1], True) + unpacked_pair(tiles[2], pltpu.roll(tiles[1], 64, 1), False)


def arrange_rows(rows_in, w_query, w_key, w_value, gain_rows, count):
    share = rows_in.shape[0]
    groups = HEADS // KV
    queries = [head for group in range(HEADS // 4) for head in apart(w_query, group)]
    keys = [head for group in range(KV // 4) for head in apart(w_key, group)]
    values = [head for group in range(KV // 4) for head in apart(w_value, group)]
    lane = lanes_of(keys[0])
    for head in range(KV):
        for number, tile in enumerate(queries[head * groups : (head + 1) * groups] + [keys[head]]):
            third = pltpu.roll(values[head], HD - 32 * number, 1)
            start = (head * HEAD_TILES + number) * LANES
            rows_in[:, start : start + LANES] = jnp.where(lane < HD, tile, third).astype(rows_in.dtype)
    row = lax.broadcasted_iota(jnp.int32, (LANES, LANES), 0)
    columns = jnp.where(row == 0, gain_rows[0:1, :], jnp.where(row == 1, gain_rows[1:2, :], 0.0))
    columns = jnp.where(row == 2, count, columns)
    rows_in[:, KV * HEAD_TILES * LANES :] = jnp.transpose(columns)[:share, :].astype(rows_in.dtype)


def attend_kernel(
    scale, lines, w_query, w_key, w_value, w_gate, w_up, out_rows, gain_rows, freq, mask, deal, lengths, tokens,
    attended, normed, gains, cosine, sine, valid, weights, out_w, unit_w, qkv_out, probs,
    rows_in, unit_rows, w, place_row, sent, qkv, keys, values, prob_blocks, o_sent, o_came,
    send, recv, o_send, o_recv, p_sem, q_sem, w_sem, w_send, w_recv, w_here, g_send, g_recv, g_here,
    u_send, u_recv, u_here, l_send, l_recv,
):
    z, y, x, c = coordinates()
    count = sent.shape[0]
    me = z * 2 + y
    even = y == 0
    rows, width = tokens.shape
    half_rows = rows // 2
    head_cols = HEAD_TILES * LANES
    to_device = lambda i: (i, x * 2 + c)
    peer = lambda k: lax.rem(me + k, count)

    member = y * 4 + x * 2 + c
    in_plane = lambda i: (z * 2 + i // 4, i % 4)
    unit_peer = lambda k: lax.rem(member + k, PLANE)
    others = [device(z, yy, xx, cc) for yy, xx, cc in ((y, 1 - x, c), (y, x, 1 - c), (y, 1 - x, 1 - c))]
    others += [device(z, 1 - y, xx, cc) for xx, cc in ((1 - x, c), (x, 1 - c), (1 - x, 1 - c))]
    units = w_gate.shape[1] // (lines * PLANE)
    for i in range(PLANE):
        for zz in range(lines):
            start = (zz * PLANE + i) * units
            unit_rows[i, :, zz * units : (zz + 1) * units] = w_gate[:, start : start + units]
            unit_rows[i, :, (lines + zz) * units : (lines + zz + 1) * units] = w_up[:, start : start + units]
    greet([to_device(peer(k)) for k in range(1, count)] + others)

    def unit_out(k):
        i = unit_peer(k)
        return remote(unit_rows.at[i], unit_w.at[z, member], u_send.at[k], u_recv.at[k], in_plane(i))

    unit_own = pltpu.make_async_copy(unit_rows.at[member], unit_w.at[z, member], u_here)
    unit_own.start()
    stages, weights_last = gather_plan(lines, rows_in, w, w_send, w_recv, w_here)
    gather_stages, gather_last = gather_plan(lines, out_rows, out_w, g_send, g_recv, g_here)
    line_begin, line_pass, line_last = line_gather(
        (z, y, x, c), lines, unit_w.at[z], unit_w, l_send, l_recv
    )
    for k in range(1, PLANE):
        unit_out(k).start()
    first_block = deal[0, me]
    total = functools.reduce(lambda a, b: a + b, [lengths[0, j] for j in range(NSEQ)])
    token = lax.broadcasted_iota(jnp.int32, (1, rows), 1)
    in_pack = jnp.where(token < half_rows, first_block * half_rows, (2 * count - 2 - first_block) * half_rows) + token
    counted = jnp.where(in_pack < total, mask[...].astype(jnp.float32), 0.0)
    arrange_rows(rows_in, w_query, w_key, w_value, gain_rows, jnp.sum(counted, -1, keepdims=True))
    stages[0]()
    valid[...] = jnp.transpose(jnp.broadcast_to(counted, (LANES, rows)))[:, :1]
    token = lax.broadcasted_iota(jnp.int32, (rows, 1), 0)
    in_pack = jnp.where(token < half_rows, first_block * half_rows, (2 * count - 2 - first_block) * half_rows) + token
    angle = (in_pack - segment_of(lengths, in_pack)[0]).astype(jnp.float32) * freq[...]
    cosine[...] = jnp.cos(angle)
    sine[...] = jnp.sin(angle)
    unit_own.wait()
    for k in range(1, PLANE):
        unit_out(k).wait_recv()
    line_begin()
    for number, stage in enumerate(stages[1:]):
        stage()
        if number == lines - 1:
            line_pass(1)
    weights_last()
    keep_weights = pltpu.make_async_copy(w, weights, w_sem)
    keep_weights.start()

    def columns_of(start, size):
        return w[:, :, pl.ds(start, size)].reshape(width, size)

    extras = columns_of(count * head_cols, LANES)
    gains[...] = jnp.transpose(extras.astype(jnp.float32))[: gains.shape[0], :]
    gain = gains[0:1, :]

    def norm_rows(at):
        values_at = tokens[at, :].astype(jnp.float32)
        normed[at, :] = (values_at * rms_scale(values_at) * gain).astype(normed.dtype)

    by_rows(rows, norm_rows)

    def out(k):
        return remote(sent.at[peer(k)], qkv.at[me], send.at[k], recv.at[k], to_device(peer(k)))

    def project(k, carry):
        i = peer(k)
        columns = columns_of(pl.multiple_of(i * head_cols, LANES), head_cols)
        both = jnp.dot(normed[...], columns, preferred_element_type=jnp.float32)
        for tile in range(HEAD_TILES):
            at = slice(tile * LANES, (tile + 1) * LANES)
            sent[i, :, at] = turned(both[:, at], cosine[...], sine[...]).astype(sent.dtype)

        @pl.when(k < count)
        def _():
            out(k).start()

        return carry

    lax.fori_loop(1, count + 1, project, 0)
    gather_stages[0]()
    line_pass(2)
    qkv[me] = sent[me]
    for src in range(count):
        columns = slice(src * half_rows, (src + 1) * half_rows)
        steps = lax.broadcasted_iota(jnp.int32, (1, half_rows), 1)
        place_row[0, :, columns] = deal[0, src] * half_rows + steps
        place_row[1, :, columns] = (2 * count - 1 - deal[0, src]) * half_rows + steps

    def arrive(k, carry):
        out(k).wait_recv()
        return carry

    lax.fori_loop(1, count, arrive, 0)
    gather_stages[1]()
    keep_qkv = pltpu.make_async_copy(qkv, qkv_out, q_sem)
    keep_qkv.start()
    keys_and_values(qkv, keys, values, count, half_rows)

    def back(k):
        return remote(o_sent.at[peer(k)], o_came.at[me], o_send.at[k], o_recv.at[k], to_device(peer(k)))

    def keep(src, half):
        return pltpu.make_async_copy(prob_blocks.at[src, half], probs.at[src, half], p_sem.at[src, half])

    def attend(k, carry):
        src = peer(k)
        halves_out = []
        for half in range(2):
            at = pl.ds(half * half_rows, half_rows)
            queries = jnp.concatenate([qkv[src, at, :LANES], qkv[src, at, LANES : 2 * LANES]], 0)
            score = against(queries, keys[half]) * scale
            first = deal[0, src]
            block = first if half == 0 else 2 * count - 1 - first
            own = block * half_rows + lax.broadcasted_iota(jnp.int32, (half_rows, 1), 0)
            start, end = segment_of(lengths, own)
            lowest = jnp.where(own < end, start, own)
            place = place_row[half]
            allowed = (place >= lowest) & (place <= own)
            bias = jnp.where(allowed, 0.0, masked_score)
            score = score + jnp.concatenate([bias, bias], 0)
            top = jnp.max(score, -1, keepdims=True)
            weight = jnp.exp(score - top)
            total = jnp.sum(weight, -1, keepdims=True)
            low = (weight * (1.0 / total)).astype(prob_blocks.dtype)
            prob_blocks[src, half] = low
            keep(src, half).start()
            summed = jnp.dot(low, values[half], preferred_element_type=jnp.float32)
            full, part = packed_pair(summed[:half_rows], summed[half_rows:], even)
            o_sent[src, at, :] = full.astype(o_sent.dtype)
            halves_out.append(part)
        lane = lanes_of(halves_out[0])
        part = jnp.where(lane < 64, halves_out[0], pltpu.roll(halves_out[1], 64, 1))
        o_sent[src, pl.ds(rows, half_rows), :] = part.astype(o_sent.dtype)

        @pl.when(k < count)
        def _():
            back(k).start()

        for number in range(2, len(gather_stages)):
            pl.when(k == 2 * number - 2)(gather_stages[number])
        return carry

    lax.fori_loop(1, count + 1, attend, 0)
    o_came[me] = o_sent[me]

    def return_arrive(k, carry):
        back(k).wait_recv()
        return carry

    lax.fori_loop(1, count, return_arrive, 0)
    for pair in range(count // 2):
        at = pair * head_cols
        attended[:, at : at + LANES] = o_came[2 * pair, :rows, :]
        attended[:, at + 2 * LANES : at + 3 * LANES] = o_came[2 * pair + 1, :rows, :]
        one = o_came[2 * pair, rows:, :].astype(jnp.float32)
        two = o_came[2 * pair + 1, rows:, :].astype(jnp.float32)
        lane = lanes_of(one)
        middle = slice(at + LANES, at + 2 * LANES)
        attended[:half_rows, middle] = jnp.where(lane < 64, one, pltpu.roll(two, 64, 1)).astype(attended.dtype)
        attended[half_rows:, middle] = jnp.where(lane < 64, pltpu.roll(one, 64, 1), two).astype(attended.dtype)

    def drain(k, carry):
        out(k).wait_send()
        back(k).wait_send()
        return carry

    lax.fori_loop(1, count, drain, 0)

    def drain_probs(src, carry):
        keep(src, 0).wait()
        keep(src, 1).wait()
        return carry

    lax.fori_loop(0, count, drain_probs, 0)
    keep_qkv.wait()
    gather_last()
    for moment in range(3, lines):
        line_pass(moment)
    line_last()
    for k in range(1, PLANE):
        unit_out(k).wait_send()
    keep_weights.wait()


def attend(scale, lines, w_query, w_key, w_value, w_gate, w_up, out_rows, gain_rows, freq, mask, deal, lengths, tokens, identity):
    rows, width = tokens.shape
    share, units = out_rows.shape[0], w_gate.shape[1] // PLANE
    count = KV
    columns = count * HEAD_TILES * LANES + LANES
    half_rows = rows // 2
    half = count * half_rows
    head_cols = HEAD_TILES * LANES
    low = tokens.dtype
    shape = jax.ShapeDtypeStruct
    vmem, anywhere = pl.BlockSpec(memory_space=pltpu.VMEM), pl.BlockSpec(memory_space=pl.ANY)
    smem = pl.BlockSpec(memory_space=pltpu.SMEM)
    dma = pltpu.SemaphoreType.DMA
    return pl.pallas_call(
        functools.partial(attend_kernel, scale, lines),
        out_shape=[
            shape((rows, width), low),
            shape((rows, width), low),
            shape((8, width), jnp.float32),
            shape((rows, LANES), jnp.float32),
            shape((rows, LANES), jnp.float32),
            shape((rows, 1), jnp.float32),
            shape((lines * PLANE, share, columns), low),
            shape((lines * PLANE,) + out_rows.shape, low),
            shape((lines, PLANE, share, 2 * units), low),
            shape((count, rows, head_cols), low),
            shape((count, 2, rows, half), low),
        ],
        in_specs=[vmem] * 5 + [anywhere] + [vmem] * 3 + [smem, smem, vmem],
        out_specs=[vmem] * 6 + [anywhere] * 5,
        scratch_shapes=[
            pltpu.VMEM((share, columns), low),
            pltpu.VMEM((PLANE, share, 2 * units), low),
            pltpu.VMEM((lines * PLANE, share, columns), low),
            pltpu.VMEM((2, 1, half), jnp.int32),
            pltpu.VMEM((count, rows, head_cols), low),
            pltpu.VMEM((count, rows, head_cols), low),
            pltpu.VMEM((2, half, LANES), low),
            pltpu.VMEM((2, half, LANES), low),
            pltpu.VMEM((count, 2, rows, half), low),
            pltpu.VMEM((count, rows + half_rows, LANES), low),
            pltpu.VMEM((count, rows + half_rows, LANES), low),
            dma((count,)),
            dma((count,)),
            dma((count,)),
            dma((count,)),
            dma((count, 2)),
            dma,
            dma,
            *gather_semaphores(lines),
            *gather_semaphores(lines),
            dma((PLANE,)),
            dma((PLANE,)),
            dma,
            dma((2, lines)),
            dma((2, lines)),
        ],
        compiler_params=pltpu.CompilerParams(collective_id=identity, vmem_limit_bytes=VMEM_LIMIT),
        name="attend",
    )(w_query, w_key, w_value, w_gate, w_up, out_rows, gain_rows, freq, mask, deal, lengths, tokens)


def attend_back_kernel(
    scale, lines, attended_grad, qkv, probs, cosine, sine, attended, branch, both, qkv_grad, out_final, both_final,
    sent, came, keys, values, prob_blocks, dk_sum, dv_sum, back_sent, back_came,
    send, recv, back_send, back_recv, p_sem, up, down, l_send, l_recv, p, *reducing,
):
    z, y, x, c = coordinates()
    count = sent.shape[0]
    me = z * 2 + y
    even = y == 0
    rows, width = attended_grad.shape
    half_rows = rows // 2
    head_cols = HEAD_TILES * LANES
    to_device = lambda i: (i, x * 2 + c)
    peer = lambda k: lax.rem(me + k, count)
    source = lambda k: lax.rem(me + count - k, count)

    def load(src, half):
        return pltpu.make_async_copy(probs.at[src, half], prob_blocks.at[src, half], p_sem.at[src, half])

    def load_start(k, carry):
        load(source(k), 0).start()
        load(source(k), 1).start()
        return carry

    lax.fori_loop(0, count, load_start, 0)
    greet([to_device(peer(k)) for k in range(1, count)] + [device(z, y, 1 - x, c), device(z, y, x, 1 - c)])
    members, share = p.shape[1:3]

    def prepare(block):
        at = pl.ds(pl.multiple_of(block * members * share, LANES), members * share)
        store_terms(p, block, 0, transposed(attended[:, at], branch[...]))

    reduce_stages, reduce_last = reduce_plan(lines, prepare, p, out_final, *reducing)
    line_begin, line_hop, line_last = line_reduce((z, y, x, c), lines, both, up, down, l_send, l_recv)
    for pair in range(count // 2):
        at = pair * head_cols
        sent[2 * pair, :rows, :] = attended_grad[:, at : at + LANES]
        sent[2 * pair + 1, :rows, :] = attended_grad[:, at + 2 * LANES : at + 3 * LANES]
        middle = attended_grad[:, at + LANES : at + 2 * LANES].astype(jnp.float32)
        one, two = middle[:half_rows], middle[half_rows:]
        lane = lanes_of(one)
        sent[2 * pair, rows:, :] = jnp.where(lane < 64, one, pltpu.roll(two, 64, 1)).astype(sent.dtype)
        sent[2 * pair + 1, rows:, :] = jnp.where(lane < 64, pltpu.roll(one, 64, 1), two).astype(sent.dtype)

    def out(k):
        return remote(sent.at[peer(k)], came.at[me], send.at[k], recv.at[k], to_device(peer(k)))

    def begin(k, carry):
        out(k).start()
        return carry

    lax.fori_loop(1, count, begin, 0)
    reduce_stages[0]()
    came[me] = sent[me]
    keys_and_values(qkv, keys, values, count, half_rows)
    dk_sum[...] = jnp.zeros_like(dk_sum)
    dv_sum[...] = jnp.zeros_like(dv_sum)

    def grads(k, carry):
        src = source(k)

        @pl.when(k > 0)
        def _():
            out(k).wait_recv()

        for half in range(2):
            at = pl.ds(half * half_rows, half_rows)
            full = came[src, at, :].astype(jnp.float32)
            part = came[src, pl.ds(rows, half_rows), :].astype(jnp.float32)
            if half:
                part = pltpu.roll(part, 64, 1)
            pair = jnp.concatenate(unpacked_pair(full, part, even), 0).astype(came.dtype)
            queries = jnp.concatenate([qkv[src, at, :LANES], qkv[src, at, LANES : 2 * LANES]], 0)
            load(src, half).wait()
            low = prob_blocks[src, half]
            prob = low.astype(jnp.float32)
            prob_grad = against(pair, values[half])
            delta = jnp.sum(prob * prob_grad, -1, keepdims=True)
            score_low = (prob * (prob_grad - delta)).astype(low.dtype)
            dq = jnp.dot(score_low, keys[half], preferred_element_type=jnp.float32) * scale
            back_sent[src, at, :LANES] = dq[:half_rows].astype(back_sent.dtype)
            back_sent[src, at, LANES : 2 * LANES] = dq[half_rows:].astype(back_sent.dtype)
            dk_sum[half] += transposed(score_low, queries)
            dv_sum[half] += transposed(low, pair)
        pl.when(k == 2)(line_begin)
        for number in range(1, len(reduce_stages)):
            pl.when(k == number)(reduce_stages[number])
        return carry

    lax.fori_loop(0, count, grads, 0)

    def back(k):
        return remote(back_sent.at[peer(k)], back_came.at[me], back_send.at[k], back_recv.at[k], to_device(peer(k)))

    def finish(k, carry):
        src = peer(k)
        in_half = pl.ds(pl.multiple_of(src * half_rows, half_rows), half_rows)
        for half in range(2):
            at = pl.ds(half * half_rows, half_rows)
            dk = dk_sum[half, in_half, :] * scale
            dv = dv_sum[half, in_half, :]
            lane = lanes_of(dk)
            for tile in range(HEAD_TILES):
                columns = slice(tile * LANES, (tile + 1) * LANES)
                head = dk if tile == 2 else back_sent[src, at, columns].astype(jnp.float32)
                third = pltpu.roll(dv, HD - 32 * tile, 1)
                back_sent[src, at, columns] = jnp.where(lane < HD, head, third).astype(back_sent.dtype)

        @pl.when(k < count)
        def _():
            back(k).start()

        return carry

    lax.fori_loop(1, count + 1, finish, 0)
    for moment in range(1, lines - 1):
        line_hop(moment)
    reduce_last()
    back_came[me] = back_sent[me]

    def turn_back(k, carry):
        src = source(k)

        @pl.when(k > 0)
        def _():
            back(k).wait_recv()

        for tile in range(HEAD_TILES):
            columns = slice(tile * LANES, (tile + 1) * LANES)
            values_at = back_came[src, :, columns].astype(jnp.float32)
            turned_at = turned(values_at, cosine[...], -sine[...])
            at = pl.ds(pl.multiple_of(src * head_cols + tile * LANES, LANES), LANES)
            qkv_grad[:, at] = turned_at.astype(qkv_grad.dtype)
        return carry

    lax.fori_loop(0, count, turn_back, 0)

    def keep_sums(at, sums):
        both_final[at, :] = sums.astype(both_final.dtype)

    line_last(keep_sums)

    def drain(k, carry):
        out(k).wait_send()
        back(k).wait_send()
        return carry

    lax.fori_loop(1, count, drain, 0)


def attend_back(scale, lines, attended_grad, qkv, probs, tables, attended, branch, both, identity):
    rows, width = attended_grad.shape
    count, _, head_cols = qkv.shape
    half = probs.shape[-1]
    half_rows = rows // 2
    share = width // (lines * PLANE)
    low = attended_grad.dtype
    vmem, anywhere = pl.BlockSpec(memory_space=pltpu.VMEM), pl.BlockSpec(memory_space=pl.ANY)
    dma = pltpu.SemaphoreType.DMA
    return pl.pallas_call(
        functools.partial(attend_back_kernel, scale, lines),
        out_shape=[
            jax.ShapeDtypeStruct((rows, count * head_cols), low),
            jax.ShapeDtypeStruct((share, width), jnp.float32),
            jax.ShapeDtypeStruct(both.shape[1:], low),
        ],
        in_specs=[vmem, vmem, anywhere] + [vmem] * 5,
        out_specs=[vmem, vmem, vmem],
        scratch_shapes=[
            pltpu.VMEM((count, rows + half_rows, LANES), low),
            pltpu.VMEM((count, rows + half_rows, LANES), low),
            pltpu.VMEM((2, half, LANES), low),
            pltpu.VMEM((2, half, LANES), low),
            pltpu.VMEM((count, 2, rows, half), low),
            pltpu.VMEM((2, half, LANES), jnp.float32),
            pltpu.VMEM((2, half, LANES), jnp.float32),
            pltpu.VMEM((count, rows, head_cols), low),
            pltpu.VMEM((count, rows, head_cols), low),
            dma((count,)),
            dma((count,)),
            dma((count,)),
            dma((count,)),
            dma((count, 2)),
            pltpu.VMEM(both.shape, low),
            pltpu.VMEM(both.shape, low),
            dma((2, lines)),
            dma((2, lines)),
            *reduce_scratch(lines, share, width, low),
        ],
        compiler_params=pltpu.CompilerParams(collective_id=identity, vmem_limit_bytes=VMEM_LIMIT),
        name="attend_back",
    )(attended_grad, qkv, probs, *tables, attended, branch, both)


def finish_kernel(
    weights, normed, qkv_grad, hidden_grad, tokens, gains, square, norm, w_gate, w_up, both,
    input_grad, query_final, key_final, value_final, gate_final, up_final, gain_final, loss,
    w, own_rows, normed_grad, final, both_came, w_sem, own_sem, both_send, both_recv, here, p, *reducing,
):
    z, y, x, c = coordinates()
    lines, members, share = p.shape[:3]
    rows, width = tokens.shape
    qkv_cols = qkv_grad.shape[1]
    low = normed.dtype
    load = pltpu.make_async_copy(weights.at[:, pl.ds(0, qkv_cols)], w, w_sem)
    load.start()
    number = (z * 2 + y) * 4 + x * 2 + c
    own_at = pl.ds(pl.multiple_of(number * share, 16), share)
    load_own = pltpu.make_async_copy(weights.at[own_at, :], own_rows, own_sem)
    load_own.start()
    me = y * 4 + x * 2 + c
    peer = lambda k: lax.rem(me + k, members)
    member = lambda i: (z * 2 + i // 4, i % 4)
    greet([member(peer(k)) for k in range(1, members)] + line_of(z, y, x, c, lines))

    def both_out(k):
        return remote(both.at[peer(k)], both_came.at[me], both_send.at[k], both_recv.at[k], member(peer(k)))

    both_own = pltpu.make_async_copy(both.at[me], both_came.at[me], here)
    both_own.start()
    devices = lines * PLANE
    place = lax.broadcasted_iota(jnp.int32, (1, LANES), 1) - number
    rest = square[...]
    loss_terms = jnp.zeros((1, LANES), jnp.float32)
    for term in range(3):
        top = rest.astype(low).astype(jnp.float32)
        loss_terms = loss_terms + jnp.where(place == term * devices, top, 0.0)
        rest = rest - top

    def prepare(block):
        at = pl.ds(pl.multiple_of(block * members * share, LANES), members * share)
        left = normed[:, at]
        chunk = qkv_cols // 2
        for start in range(0, qkv_cols, chunk):
            store_terms(p, block, start, transposed(left, qkv_grad[:, start : start + chunk]))
        store_terms(p, block, qkv_cols, jnp.broadcast_to(loss_terms, (members * share, LANES)))

    stages, last = reduce_plan(lines, prepare, p, final, *reducing)

    def grad_rows(at):
        values = tokens[at, :].astype(jnp.float32)
        scale = rms_scale(values)
        unit = values * scale
        scaled = normed_grad[at, :] * gains[0:1, :]
        input_grad[at, :] = hidden_grad[at, :] + scale * (
            scaled - unit * jnp.mean(scaled * unit, -1, keepdims=True)
        )

    block = rows // lines
    for index, stage in enumerate(stages):
        if index == 2:
            for k in range(1, members):
                both_out(k).start()
            load.wait()
        stage()
        if 2 <= index < 2 + lines:
            at = slice((index - 2) * block, (index - 1) * block)
            normed_grad[at, :] = against(qkv_grad[at, :], w[...])
        if index == 2 + lines:
            by_rows(rows, grad_rows)
    both_own.wait()
    for k in range(1, members):
        both_out(k).wait_recv()
    units = both.shape[2] // (2 * lines)
    for i in range(members):
        for zz in range(lines):
            to = slice((zz * members + i) * units, (zz * members + i + 1) * units)
            gate_final[:, to] = both_came[i, :, zz * units : (zz + 1) * units].astype(jnp.float32)
            up_final[:, to] = both_came[i, :, (lines + zz) * units : (lines + zz + 1) * units].astype(jnp.float32)
    last()

    def tile(head, number):
        start = (head * HEAD_TILES + number) * LANES
        return final[:, start : start + LANES]

    def put(ref, group, heads):
        for number, value in enumerate(side_by_side(heads)):
            start = (group * HEAD_TILES + number) * LANES
            ref[:, start : start + LANES] = value

    for pair in range(KV // 2):
        put(query_final, pair, [tile(2 * pair + i, j) for i in range(2) for j in range(2)])
    for group in range(KV // 4):
        heads = [4 * group + i for i in range(4)]
        put(key_final, group, [tile(head, 2) for head in heads])
        parts = []
        for head in heads:
            thirds = [pltpu.roll(tile(head, number), 32 * (number + 1), 1) for number in range(HEAD_TILES)]
            in_tile = lanes_of(thirds[0])
            parts.append(jnp.where(in_tile < 32, thirds[0], jnp.where(in_tile < 64, thirds[1], thirds[2])))
        put(value_final, group, parts)

    load_own.wait()
    own_gains = own_rows[:, qkv_cols:].astype(jnp.float32)

    def product(grads, weights_of, width_of):
        sums = jnp.zeros((share, 1), jnp.float32)
        for start in range(0, width_of, 4 * LANES):
            at = slice(start, start + 4 * LANES)
            sums += jnp.sum(grads[:, at] * weights_of[:, at].astype(jnp.float32), -1, keepdims=True)
        return sums

    units_all = w_gate.shape[1]
    first_gain = product(final, own_rows, qkv_cols) / own_gains[:, 0:1]
    second_gain = product(gate_final, w_gate, units_all) + product(up_final, w_up, units_all)
    second_gain = second_gain / own_gains[:, 1:2]
    columns = lax.broadcasted_iota(jnp.int32, (share, LANES), 1)
    both_gains = jnp.where(columns == 0, first_gain, jnp.where(columns == 1, second_gain, 0.0))
    both_gains = jnp.concatenate([both_gains, jnp.zeros((LANES - share, LANES), jnp.float32)], 0)
    gain_final[...] = jnp.transpose(both_gains)[:8, :]
    tail = final[:, qkv_cols:]
    of_loss = lax.broadcasted_iota(jnp.int32, (1, LANES), 1) < 3 * devices
    loss[...] = jnp.sum(jnp.where(of_loss, tail[:1, :], 0.0), -1, keepdims=True) * (0.5 * norm[...])
    for k in range(1, members):
        both_out(k).wait_send()


def finish(lines, weights, normed, qkv_grad, hidden_grad, tokens, gains, square, norm, w_gate, w_up, both, identity):
    rows, width = tokens.shape
    qkv_cols = qkv_grad.shape[1]
    share = weights.shape[0] // (lines * PLANE)
    columns = weights.shape[1]
    units_all = PLANE * both.shape[2] // 2
    low = tokens.dtype
    vmem, anywhere = pl.BlockSpec(memory_space=pltpu.VMEM), pl.BlockSpec(memory_space=pl.ANY)
    dma = pltpu.SemaphoreType.DMA
    shapes = [
        (rows, width),
        (share, width),
        (share, KV * HD),
        (share, KV * HD),
        (share, units_all),
        (share, units_all),
        (8, LANES),
        (1, 1),
    ]
    return pl.pallas_call(
        finish_kernel,
        out_shape=[jax.ShapeDtypeStruct(shape, jnp.float32) for shape in shapes],
        in_specs=[anywhere] + [vmem] * 9 + [anywhere],
        out_specs=[vmem] * len(shapes),
        scratch_shapes=[
            pltpu.VMEM((width, qkv_cols), low),
            pltpu.VMEM((share, columns), low),
            pltpu.VMEM((rows, width), jnp.float32),
            pltpu.VMEM((share, columns), jnp.float32),
            pltpu.VMEM(both.shape, low),
            dma,
            dma,
            dma((PLANE,)),
            dma((PLANE,)),
            dma,
            *reduce_scratch(lines, share, columns, low),
        ],
        compiler_params=pltpu.CompilerParams(collective_id=identity, vmem_limit_bytes=VMEM_LIMIT),
        name="finish",
    )(weights, normed, qkv_grad, hidden_grad, tokens, gains, square, norm, w_gate, w_up, both)


def plane_per_device(lines, *arrays):
    (
        tokens,
        lengths,
        deal,
        loss_mask,
        teacher,
        out_grad,
        attn_gain,
        w_query,
        w_key,
        w_value,
        w_out,
        ffn_gain,
        w_gate,
        w_up,
        w_down,
    ) = arrays
    devices = lines * PLANE
    width = tokens.shape[2]
    weight_rows = w_query.shape[0]
    scale = HD ** (-0.5)
    gain_rows = jnp.zeros((8, LANES), jnp.float32)
    gain_rows = gain_rows.at[0, :weight_rows].set(attn_gain.astype(jnp.float32))
    gain_rows = gain_rows.at[1, :weight_rows].set(ffn_gain.astype(jnp.float32))
    freq = rope_base ** (-(jnp.arange(HD // 2, dtype=jnp.float32) * 2.0 / HD))
    freq = jnp.concatenate([freq, freq, jnp.zeros((LANES - HD,), jnp.float32)])[None]

    attended_low, normed_low, gains, cosine, sine, valid, attn_all, out_w, gate_up_w, qkv, probs = attend(
        scale,
        lines,
        w_query,
        w_key,
        w_value,
        w_gate,
        w_up,
        w_out,
        gain_rows,
        freq,
        loss_mask,
        deal,
        lengths,
        tokens[0],
        3,
    )
    attn_all = attn_all.reshape(devices * weight_rows, -1)
    gate_up_w = gate_up_w.reshape(devices * weight_rows, -1)

    result, square, norm, hidden_grad, branch_low, attended_grad, down_final, both_grad = feed_forward(
        lines,
        out_w.reshape(width, width),
        attended_low,
        tokens[0],
        teacher[0],
        out_grad[0],
        valid,
        gains,
        gate_up_w,
        w_down,
        5,
    )
    both_grad = both_grad.reshape(lines, PLANE * weight_rows, -1)
    qkv_grad, out_final, both_final = attend_back(
        scale, lines, attended_grad, qkv, probs, (cosine, sine), attended_low, branch_low, both_grad, 9
    )

    input_grad, query_final, key_final, value_final, gate_final, up_final, gain_final, loss = finish(
        lines,
        attn_all,
        normed_low,
        qkv_grad,
        hidden_grad,
        tokens[0],
        gains,
        square,
        norm,
        w_gate,
        w_up,
        both_final.reshape(PLANE, weight_rows, -1),
        11,
    )
    return (
        result[None],
        loss.reshape(()),
        input_grad[None],
        gain_final[0, :weight_rows],
        query_final,
        key_final,
        value_final,
        out_final,
        gain_final[1, :weight_rows],
        gate_final,
        up_final,
        down_final,
    )


def suits_planes(mesh):
    sizes = dict(mesh.shape)
    return sizes["fsdp"] == 4 and sizes["ctx"] == KV


def solution(mesh):
    placed = (
        P("fsdp", "ctx", None),
        P("fsdp", None),
        P("fsdp", None),
        P("fsdp", "ctx"),
        P("fsdp", "ctx", None),
        P("fsdp", "ctx", None),
        P(("ctx", "fsdp")),
        P(("ctx", "fsdp"), None),
        P(("ctx", "fsdp"), None),
        P(("ctx", "fsdp"), None),
        P(("ctx", "fsdp"), None),
        P(("ctx", "fsdp")),
        P(("ctx", "fsdp"), None),
        P(("ctx", "fsdp"), None),
        P(("ctx", "fsdp"), None),
    )
    if suits_planes(mesh):
        per_device = functools.partial(plane_per_device, mesh.shape["ctx"] // ROWS_Y)
    else:
        per_device = ring_per_device
    return jax.shard_map(
        per_device,
        mesh=mesh,
        in_specs=placed,
        out_specs=(
            P("fsdp", "ctx", None),
            P(),
            P("fsdp", "ctx", None),
            P(("ctx", "fsdp")),
            P(("ctx", "fsdp"), None),
            P(("ctx", "fsdp"), None),
            P(("ctx", "fsdp"), None),
            P(("ctx", "fsdp"), None),
            P(("ctx", "fsdp")),
            P(("ctx", "fsdp"), None),
            P(("ctx", "fsdp"), None),
            P(("ctx", "fsdp"), None),
        ),
        check_vma=False,
    )
```

```python
import functools

import jax
import jax.numpy as jnp
import numpy as np
from jax import lax
from jax.experimental import pallas as pl
from jax.experimental.pallas import tpu as pltpu
from jax.sharding import PartitionSpec as P

HEADS = 16
KV = 8
HD = 96
NSEQ = 6


rope_base = 100000.0
epsilon = 1e-05
masked_score = -1e30


def shifted(value, axis, by):
    size = lax.axis_size(axis)
    return lax.ppermute(value, axis, [(i, (i + by) % size) for i in range(size)])


def rms_scale(values):
    return lax.rsqrt(jnp.mean(values * values, -1, keepdims=True) + epsilon)


def rotary_tables(inseq):
    freq = rope_base ** (-(jnp.arange(HD // 2, dtype=jnp.float32) * 2.0 / HD))
    angle = inseq.astype(jnp.float32)[:, None] * freq[None, :]
    return (jnp.cos(angle)[:, None, :], jnp.sin(angle)[:, None, :])


def rotary(values, cosine, sine):
    half = values.shape[-1] // 2
    first = values[..., :half]
    second = values[..., half:]
    return jnp.concatenate([first * cosine - second * sine, second * cosine + first * sine], -1)


def rotary_back(grads, cosine, sine):
    half = grads.shape[-1] // 2
    first = grads[..., :half]
    second = grads[..., half:]
    return jnp.concatenate([first * cosine + second * sine, second * cosine - first * sine], -1)


def transposed(left, right):
    return lax.dot_general(
        left, right, (((0,), (0,)), ((), ())), preferred_element_type=jnp.float32
    )


def against(left, right):
    return lax.dot_general(
        left, right, (((1,), (1,)), ((), ())), preferred_element_type=jnp.float32
    )


def permitted(query_place, query_seg, key_place, key_seg):
    same = (query_seg[:, None] == key_seg[None, :]) & (query_seg[:, None] < NSEQ)
    return same & (key_place[None, :] <= query_place[:, None]) | (
        key_place[None, :] == query_place[:, None]
    )


def ring_per_device(
    tokens,
    lengths,
    deal,
    loss_mask,
    teacher,
    out_grad,
    attn_gain,
    w_query,
    w_key,
    w_value,
    w_out,
    ffn_gain,
    w_gate,
    w_up,
    w_down,
):
    count_ctx = lax.axis_size("ctx")
    myself = lax.axis_index("ctx")
    tok_rows = tokens.shape[1]
    width = tokens.shape[2]
    half_block = tok_rows // 2
    groups = HEADS // KV
    scale = HD ** (-0.5)
    gain_one, query_w, key_w, value_w, out_w = (
        lax.all_gather(attn_gain, ("ctx", "fsdp"), axis=0, tiled=True),
        lax.all_gather(w_query, ("ctx", "fsdp"), axis=0, tiled=True),
        lax.all_gather(w_key, ("ctx", "fsdp"), axis=0, tiled=True),
        lax.all_gather(w_value, ("ctx", "fsdp"), axis=0, tiled=True),
        lax.all_gather(w_out, ("ctx", "fsdp"), axis=0, tiled=True),
    )
    gain_two, gate_w, up_w, down_w = (
        lax.all_gather(ffn_gain, ("ctx", "fsdp"), axis=0, tiled=True),
        lax.all_gather(w_gate, ("ctx", "fsdp"), axis=0, tiled=True),
        lax.all_gather(w_up, ("ctx", "fsdp"), axis=0, tiled=True),
        lax.all_gather(w_down, ("ctx", "fsdp"), axis=0, tiled=True),
    )
    dealt = jnp.arange(count_ctx * tok_rows, dtype=jnp.int32)
    local = dealt % tok_rows
    first = jnp.repeat(deal[0], tok_rows)
    block = jnp.where(local < half_block, first, 2 * count_ctx - 1 - first)
    places = block * half_block + local % half_block
    ends = jnp.cumsum(lengths[0])
    after = (places[:, None] >= ends[None, :]).astype(jnp.int32)
    seg_all = jnp.sum(after, 1)
    inseq_all = places - jnp.sum(after * lengths[0][None, :], 1)
    own_place = lax.dynamic_slice_in_dim(places, myself * tok_rows, tok_rows)
    own_seg = lax.dynamic_slice_in_dim(seg_all, myself * tok_rows, tok_rows)
    own_inseq = lax.dynamic_slice_in_dim(inseq_all, myself * tok_rows, tok_rows)
    cosine, sine = rotary_tables(own_inseq)
    inputs = tokens[0].astype(jnp.float32)
    scale_one = rms_scale(inputs)
    normed_one = inputs * scale_one
    gain_first = gain_one.astype(jnp.float32)
    normed_low = (normed_one * gain_first).astype(jnp.bfloat16)
    query_pre = jnp.dot(normed_low, query_w, preferred_element_type=jnp.float32).reshape(
        tok_rows, HEADS, HD
    )
    key_pre = jnp.dot(normed_low, key_w, preferred_element_type=jnp.float32).reshape(
        tok_rows, KV, HD
    )
    value_low = jnp.dot(normed_low, value_w, preferred_element_type=jnp.float32).astype(
        jnp.bfloat16
    )
    queries = rotary(query_pre, cosine, sine).astype(jnp.bfloat16).reshape(tok_rows, KV, groups, HD)
    keys = rotary(key_pre, cosine, sine).astype(jnp.bfloat16).reshape(tok_rows, KV * HD)

    def logits(key_block):
        return (
            jnp.einsum(
                "qcgd,kcd->cgqk",
                queries,
                key_block.reshape(-1, KV, HD),
                preferred_element_type=jnp.float32,
            )
            * scale
        )

    key_block = lax.all_gather(keys, "ctx", axis=0, tiled=True)
    value_block = lax.all_gather(value_low, "ctx", axis=0, tiled=True)
    allowed = permitted(own_place, own_seg, places, seg_all)
    top = jnp.full((KV, groups, tok_rows, 1), masked_score, jnp.float32)
    score = jnp.where(allowed, logits(key_block), masked_score)
    new_top = jnp.maximum(top, jnp.max(score, -1, keepdims=True))
    weight = jnp.where(allowed, jnp.exp(score - new_top), 0.0)
    summed = jnp.einsum(
        "cgqk,kcd->cgqd",
        weight.astype(jnp.bfloat16),
        value_block.reshape(-1, KV, HD),
        preferred_element_type=jnp.float32,
    )
    summed, top, total = (summed, new_top, jnp.sum(weight, -1, keepdims=True))
    attended = summed / total
    log_total = top + jnp.log(total)
    attended_low = (
        jnp.transpose(attended, (2, 0, 1, 3)).reshape(tok_rows, HEADS * HD).astype(jnp.bfloat16)
    )
    hidden = inputs + jnp.dot(attended_low, out_w, preferred_element_type=jnp.float32)
    scale_two = rms_scale(hidden)
    normed_two = hidden * scale_two
    gain_second = gain_two.astype(jnp.float32)
    ffn_low = (normed_two * gain_second).astype(jnp.bfloat16)
    gate = jnp.dot(ffn_low, gate_w, preferred_element_type=jnp.float32)
    up = jnp.dot(ffn_low, up_w, preferred_element_type=jnp.float32)
    sigmoid = jax.nn.sigmoid(gate)
    activated = gate * sigmoid
    mixed_low = (activated * up).astype(jnp.bfloat16)
    result = hidden + jnp.dot(mixed_low, down_w, preferred_element_type=jnp.float32)
    target = teacher[0].astype(jnp.float32)
    valid = (loss_mask[0] * (own_seg < NSEQ)).astype(jnp.float32)[:, None]
    differ = result - target
    square_sum, valid_count = lax.psum(
        (jnp.sum(valid * differ * differ), jnp.sum(valid)), ("ctx", "fsdp")
    )
    loss = square_sum / (valid_count * width)
    out_total = out_grad[0].astype(jnp.float32) + 2.0 * valid * differ / (valid_count * width)
    out_low = out_total.astype(jnp.bfloat16)
    down_grad = transposed(mixed_low, out_low)
    mixed_grad = against(out_low, down_w)
    silu_slope = sigmoid * (1.0 + gate * (1.0 - sigmoid))
    gate_low = (mixed_grad * up * silu_slope).astype(jnp.bfloat16)
    up_low = (mixed_grad * activated).astype(jnp.bfloat16)
    gate_grad = transposed(ffn_low, gate_low)
    up_grad = transposed(ffn_low, up_low)
    normed_grad = against(gate_low, gate_w) + against(up_low, up_w)
    gain_two_grad = jnp.sum(normed_grad * normed_two, 0)
    scaled_two = normed_grad * gain_second
    hidden_grad = out_total + scale_two * (
        scaled_two - normed_two * jnp.mean(scaled_two * normed_two, -1, keepdims=True)
    )
    ffn_final = (
        lax.psum_scatter(gain_two_grad, ("ctx", "fsdp"), scatter_dimension=0, tiled=True),
        lax.psum_scatter(gate_grad, ("ctx", "fsdp"), scatter_dimension=0, tiled=True),
        lax.psum_scatter(up_grad, ("ctx", "fsdp"), scatter_dimension=0, tiled=True),
        lax.psum_scatter(down_grad, ("ctx", "fsdp"), scatter_dimension=0, tiled=True),
    )
    branch_low = hidden_grad.astype(jnp.bfloat16)
    out_w_grad = transposed(attended_low, branch_low)
    attended_grad = against(branch_low, out_w).astype(jnp.bfloat16)
    grad_heads = jnp.transpose(attended_grad.reshape(tok_rows, KV, groups, HD), (1, 2, 0, 3))
    delta = jnp.sum(grad_heads.astype(jnp.float32) * attended, -1, keepdims=True)

    def cycle_step(step, state):
        key_block, value_block, key_acc, value_acc, query_acc = state
        source = (myself - step) % count_ctx
        allowed = permitted(
            own_place,
            own_seg,
            lax.dynamic_slice_in_dim(places, source * tok_rows, tok_rows),
            lax.dynamic_slice_in_dim(seg_all, source * tok_rows, tok_rows),
        )
        current_key = key_block
        current_value = value_block
        keys_three = current_key.reshape(tok_rows, KV, HD)
        values_three = current_value.reshape(tok_rows, KV, HD)
        prob = jnp.where(allowed, jnp.exp(logits(current_key) - log_total), 0.0)
        prob_grad = jnp.einsum(
            "cgqd,kcd->cgqk", grad_heads, values_three, preferred_element_type=jnp.float32
        )
        score_low = (prob * (prob_grad - delta)).astype(jnp.bfloat16)
        query_add = (
            jnp.einsum("cgqk,kcd->cgqd", score_low, keys_three, preferred_element_type=jnp.float32)
            * scale
        )
        key_add = (
            jnp.einsum(
                "cgqk,qcgd->kcd", score_low, queries, preferred_element_type=jnp.float32
            ).reshape(tok_rows, KV * HD)
            * scale
        )
        value_add = jnp.einsum(
            "cgqk,cgqd->kcd",
            prob.astype(jnp.bfloat16),
            grad_heads,
            preferred_element_type=jnp.float32,
        ).reshape(tok_rows, KV * HD)
        key_block, value_block = shifted((key_block, value_block), "ctx", 1)
        key_acc, value_acc = (
            shifted((key_acc + key_add).astype(jnp.bfloat16), "ctx", 1).astype(jnp.float32),
            shifted((value_acc + value_add).astype(jnp.bfloat16), "ctx", 1).astype(jnp.float32),
        )
        return (key_block, value_block, key_acc, value_acc, query_acc + query_add)

    cycle_start = (
        keys,
        value_low,
        jnp.zeros((tok_rows, KV * HD), jnp.float32),
        jnp.zeros((tok_rows, KV * HD), jnp.float32),
        jnp.zeros((KV, groups, tok_rows, HD), jnp.float32),
    )
    cycle_end = lax.fori_loop(0, count_ctx, cycle_step, cycle_start)
    key_acc = cycle_end[2]
    value_acc = cycle_end[3]
    query_acc = cycle_end[4]
    query_grad = jnp.transpose(query_acc, (2, 0, 1, 3)).reshape(tok_rows, HEADS, HD)
    query_low = (
        rotary_back(query_grad, cosine, sine).reshape(tok_rows, HEADS * HD).astype(jnp.bfloat16)
    )
    key_low = (
        rotary_back(key_acc.reshape(tok_rows, KV, HD), cosine, sine)
        .reshape(tok_rows, KV * HD)
        .astype(jnp.bfloat16)
    )
    value_grad_low = value_acc.astype(jnp.bfloat16)
    query_w_grad = transposed(normed_low, query_low)
    key_w_grad = transposed(normed_low, key_low)
    value_w_grad = transposed(normed_low, value_grad_low)
    normed_one_grad = (
        against(query_low, query_w) + against(key_low, key_w) + against(value_grad_low, value_w)
    )
    gain_one_grad = jnp.sum(normed_one_grad * normed_one, 0)
    scaled_one = normed_one_grad * gain_first
    input_grad = hidden_grad + scale_one * (
        scaled_one - normed_one * jnp.mean(scaled_one * normed_one, -1, keepdims=True)
    )
    attn_final = (
        lax.psum_scatter(gain_one_grad, ("ctx", "fsdp"), scatter_dimension=0, tiled=True),
        lax.psum_scatter(query_w_grad, ("ctx", "fsdp"), scatter_dimension=0, tiled=True),
        lax.psum_scatter(key_w_grad, ("ctx", "fsdp"), scatter_dimension=0, tiled=True),
        lax.psum_scatter(value_w_grad, ("ctx", "fsdp"), scatter_dimension=0, tiled=True),
        lax.psum_scatter(out_w_grad, ("ctx", "fsdp"), scatter_dimension=0, tiled=True),
    )
    return (
        result.astype(jnp.bfloat16)[None],
        loss,
        input_grad[None],
        attn_final[0],
        attn_final[1],
        attn_final[2],
        attn_final[3],
        attn_final[4],
        ffn_final[0],
        ffn_final[1],
        ffn_final[2],
        ffn_final[3],
    )


MESH = pl.DeviceIdType.MESH
ROWS_Y = 2
PLANE = 8
LANES = 128
VMEM_LIMIT = 60 * 2**20


def coordinates():
    ctx = lax.axis_index("ctx")
    fsdp = lax.axis_index("fsdp")
    return ctx // 2, ctx % 2, fsdp // 2, fsdp % 2


def device(z, y, x, c):
    return (z * 2 + y, x * 2 + c)


def greet(devices):
    barrier = pltpu.get_barrier_semaphore()
    for other in devices:
        pl.semaphore_signal(barrier, inc=1, device_id=other, device_id_type=MESH)
    pl.semaphore_wait(barrier, len(devices))


def remote(src, dst, send, recv, target):
    return pltpu.make_async_remote_copy(
        src_ref=src,
        dst_ref=dst,
        send_sem=send,
        recv_sem=recv,
        device_id=target,
        device_id_type=MESH,
    )


def line_gather(place, lines, x_ref, o_ref, send, recv, here=None):
    z, y, x, c = place
    mine = None if here is None else pltpu.make_async_copy(x_ref, o_ref.at[z], here)
    ways = ((0, -1, device(z + 1, y, x, c)), (1, 1, device(z - 1, y, x, c)))

    def along(way, sign, to, s):
        zz = z + sign * (s - 1)
        return remote(x_ref if s == 1 else o_ref.at[zz], o_ref.at[zz], send.at[way, s], recv.at[way, s], to)

    def sends(sign, s):
        if sign < 0:
            return (z - (s - 1) >= 0) & (z + 1 < lines)
        return (z + (s - 1) < lines) & (z - 1 >= 0)

    def present(sign, s):
        return z - s >= 0 if sign < 0 else z + s < lines

    def start(s):
        for way, sign, to in ways:
            pl.when(sends(sign, s))(lambda way=way, sign=sign, to=to: along(way, sign, to, s).start())

    def begin():
        if mine is not None:
            mine.start()
        start(1)

    def pass_on(s):
        for way, sign, to in ways:
            pl.when(present(sign, s))(lambda way=way, sign=sign, to=to: along(way, sign, to, s).wait_recv())
        if s + 1 < lines:
            start(s + 1)

    def last():
        for s in range(1, lines):
            for way, sign, to in ways:
                pl.when(sends(sign, s))(lambda way=way, sign=sign, to=to, s=s: along(way, sign, to, s).wait_send())
        if mine is not None:
            mine.wait()

    return begin, pass_on, last


def line_reduce(place, lines, parts, up, down, send, recv):
    z, y, x, c = place
    ways = ((0, up, device(z + 1, y, x, c)), (1, down, device(z - 1, y, x, c)))

    def copy(way, t, own):
        _, sums, to = ways[way]
        src = parts.at[t] if own else sums.at[t]
        return remote(src, sums.at[t], send.at[way, t], recv.at[way, t], to)

    def begin():
        @pl.when(z == 0)
        def _():
            for t in range(lines - 1, 0, -1):
                copy(0, t, True).start()

        @pl.when(z == lines - 1)
        def _():
            for t in range(lines - 1):
                copy(1, t, True).start()

    def add_on(way, t):
        copy(way, t, False).wait_recv()
        add_rows(ways[way][1].at[t], parts.at[t])
        copy(way, t, False).start()

    def hop(moment):
        for t in range(lines):
            for zz in range(1, lines - 1):
                if zz < t and zz + (lines - 1 - t) == moment:
                    pl.when(z == zz)(functools.partial(add_on, 0, t))
                if zz > t and (lines - 1 - zz) + t == moment:
                    pl.when(z == zz)(functools.partial(add_on, 1, t))

    def last(write, step=32):
        for way, first in ((0, 0), (1, lines - 1)):

            @pl.when(z != first)
            def _():
                copy(way, z, False).wait_recv()

        def body(i, carry):
            at = pl.ds(pl.multiple_of(i * step, step), step)
            from_below = jnp.where(z > 0, up[z, at, :].astype(jnp.float32), 0.0)
            from_above = jnp.where(z < lines - 1, down[z, at, :].astype(jnp.float32), 0.0)
            write(i, parts[z, at, :].astype(jnp.float32) + from_below + from_above)
            return carry

        lax.fori_loop(0, parts.shape[1] // step, body, 0)
        for zz in range(lines):

            @pl.when(z == zz)
            def _():
                for t in range(lines):
                    if t > zz:
                        copy(0, t, zz == 0).wait_send()
                    if t < zz:
                        copy(1, t, zz == lines - 1).wait_send()

    return begin, hop, last


def column_cut(width):
    tiles = width // LANES
    return (tiles + 1) // 2 * LANES


def gather_plan(lines, x_ref, o_ref, send, recv, here):
    z, y, x, c = coordinates()
    width = x_ref.shape[1]
    cut = column_cut(width)
    first, second = pl.ds(0, cut), pl.ds(cut, width - cut)
    side, over, sibling = device(z, y, 1 - x, c), device(z, 1 - y, x, c), device(z, y, x, 1 - c)
    above, below = device(z + 1, y, x, c), device(z - 1, y, x, c)
    slot = lambda zz, yy, xx, cc: (zz * 2 + yy) * 4 + xx * 2 + cc
    mine = pltpu.make_async_copy(x_ref, o_ref.at[slot(z, y, x, c)], here)

    def item(sign, s):
        index = 0 if s == 0 else (2 * s - 1 if sign < 0 else 2 * s)
        zz = z + sign * s
        at = lambda yy, xx, cc: o_ref.at[slot(zz, yy, xx, cc)]
        own = x_ref if s == 0 else at(y, x, c)
        make = lambda kind, src, dst, to: remote(
            src, dst, send.at[index, kind], recv.at[index, kind], to
        )
        same = lambda kind, ref, to: make(kind, ref, ref, to)
        corner_at = lambda columns: at(1 - y, 1 - x, c).at[:, columns]
        return dict(
            side=lambda: make(1, own, at(y, x, c), side),
            over=lambda: make(2, own, at(y, x, c), over),
            side_on=lambda: same(3, at(y, 1 - x, c).at[:, first], over),
            over_on=lambda: same(4, at(1 - y, x, c).at[:, second], side),
            core=lambda: make(5, own, at(y, x, c), sibling),
            core_side=lambda: same(6, at(y, 1 - x, c), sibling),
            core_over=lambda: same(7, at(1 - y, x, c), sibling),
            core_first=lambda: same(8, corner_at(first), sibling),
            core_second=lambda: same(9, corner_at(second), sibling),
        )

    def along(sign, s):
        index = 2 * s - 1 if sign < 0 else 2 * s
        zz = z + sign * (s - 1)
        src = x_ref if s == 1 else o_ref.at[slot(zz, y, x, c)]
        return remote(
            src, o_ref.at[slot(zz, y, x, c)], send.at[index, 0], recv.at[index, 0], above if sign < 0 else below
        )

    def sends_along(sign, s):
        if sign < 0:
            return (z - (s - 1) >= 0) & (z + 1 < lines)
        return (z + (s - 1) < lines) & (z - 1 >= 0)

    def present(sign, s):
        return z - s >= 0 if sign < 0 else z + s < lines

    arrivals = [(-1, 0)] + [(sign, s) for s in range(1, lines) for sign in (-1, 1)]

    def begin(sign, s):
        copies = item(sign, s)
        if s > 0:
            along(sign, s).wait_recv()
        for way in ((-1, 1) if s == 0 else (sign,)):
            if s + 1 < lines:
                @pl.when(sends_along(way, s + 1))
                def _():
                    along(way, s + 1).start()
        copies["side"]().start()
        copies["over"]().start()
        copies["core"]().start()

    def pass_on(sign, s):
        copies = item(sign, s)
        copies["side"]().wait_recv()
        copies["side_on"]().start()
        copies["core_side"]().start()
        copies["over"]().wait_recv()
        copies["over_on"]().start()
        copies["core_over"]().start()

    def corner(sign, s):
        copies = item(sign, s)
        copies["side_on"]().wait_recv()
        copies["core_first"]().start()
        copies["over_on"]().wait_recv()
        copies["core_second"]().start()

    def finish(sign, s):
        copies = item(sign, s)
        for kind in ("core", "core_side", "core_over", "core_first", "core_second"):
            copies[kind]().wait()
        for kind in ("side", "over", "side_on", "over_on"):
            copies[kind]().wait_send()

    def where(sign, s, step):
        if s == 0:
            step(sign, s)
        else:
            pl.when(present(sign, s))(functools.partial(step, sign, s))

    waves = [[(-1, 0)]] + [[(-1, s), (1, s)] for s in range(1, lines)]

    def run(number):
        if number == 0:
            mine.start()
        for stage, lag in ((begin, 0), (pass_on, 1), (corner, 2)):
            if 0 <= number - lag < len(waves):
                for sign, s in waves[number - lag]:
                    where(sign, s, stage)

    def last():
        for sign, s in arrivals:
            where(sign, s, finish)
        for s in range(1, lines):
            for sign in (-1, 1):
                pl.when(sends_along(sign, s))(lambda sign=sign, s=s: along(sign, s).wait_send())
        mine.wait()

    return [functools.partial(run, number) for number in range(len(waves) + 2)], last


def line_of(z, y, x, c, lines):
    return [device(lax.rem(z + k, lines), y, x, c) for k in range(1, lines)]


def gather_semaphores(lines):
    dma = pltpu.SemaphoreType.DMA
    return [dma((2 * lines - 1, 10)), dma((2 * lines - 1, 10)), dma]


def reduce_plan(lines, prepare, p_ref, o_ref, held, corner_a, corner_b, from_side, from_over, along, send, recv):
    z, y, x, c = coordinates()
    parts = lines
    rows, width = held.shape[2], held.shape[3]
    cut = column_cut(width)
    first, second = pl.ds(0, cut), pl.ds(cut, width - cut)
    side, over, sibling = device(z, y, 1 - x, c), device(z, 1 - y, x, c), device(z, y, x, 1 - c)
    def given(part, yy, xx, cc):
        member = yy * 4 + xx * 2 + cc
        return p_ref.at[lax.rem(z + part + 1, lines), member]

    def make(part, kind, src, dst, to):
        return remote(src, dst, send.at[part, kind], recv.at[part, kind], to)

    lane = lambda part, yy, xx: held.at[part, yy * 2 + xx]

    def over_core(part):
        return [
            make(part, yy * 2 + xx, given(part, yy, xx, 1 - c), lane(part, yy, xx), sibling)
            for yy in range(2)
            for xx in range(2)
        ]

    def to_corner(part):
        return (
            make(part, 4, lane(part, 1 - y, 1 - x).at[:, first], corner_a.at[part], over),
            make(part, 5, lane(part, 1 - y, 1 - x).at[:, second], corner_b.at[part], side),
        )

    def to_neighbour(part, way):
        columns = (first, second)[way % 2]
        if way < 2:
            return make(part, 6 + way, lane(part, y, 1 - x).at[:, columns], from_side.at[part, :, columns], side)
        return make(part, 6 + way, lane(part, 1 - y, x).at[:, columns], from_over.at[part, :, columns], over)

    def along_z(part):
        to = lax.rem(z + part + 1, lines)
        return make(part, 10, lane(part, y, x), along.at[part], device(to, y, x, c))

    step = 16

    def add_core(part):
        for copy in over_core(part):
            copy.wait_recv()
        for yy, xx in ((1 - y, 1 - x), (y, 1 - x), (1 - y, x), (y, x)):
            mine, other = given(part, yy, xx, c), lane(part, yy, xx)

            def body(i, carry):
                at = pl.ds(pl.multiple_of(i * step, step), step)
                total = mine[at, :].astype(jnp.float32) + other[at, :].astype(jnp.float32)
                other[at, :] = total.astype(other.dtype)
                return carry

            lax.fori_loop(0, rows // step, body, 0)
        for copy in to_corner(part):
            copy.start()
        to_neighbour(part, 1).start()
        to_neighbour(part, 2).start()

    def add_corner(part):
        copies = to_corner(part)
        pairs = (
            (copies[0], lane(part, y, 1 - x), corner_a.at[part], first),
            (copies[1], lane(part, 1 - y, x), corner_b.at[part], second),
        )
        for copy, mine, other, columns in pairs:
            copy.wait_recv()

            def body(i, carry):
                at = pl.ds(pl.multiple_of(i * step, step), step)
                total = mine[at, columns].astype(jnp.float32) + other[at, :].astype(jnp.float32)
                mine[at, columns] = total.astype(mine.dtype)
                return carry

            lax.fori_loop(0, rows // step, body, 0)
        to_neighbour(part, 0).start()
        to_neighbour(part, 3).start()

    def add_neighbours(part):
        for way in range(4):
            to_neighbour(part, way).wait_recv()
        last = part == parts - 1
        mine = lane(part, y, x)

        def body(i, carry):
            at = pl.ds(pl.multiple_of(i * step, step), step)
            total = mine[at, :].astype(jnp.float32) + from_side[part, at, :].astype(jnp.float32)
            total += from_over[part, at, :].astype(jnp.float32)
            if last:
                o_ref[at, :] = total
            else:
                mine[at, :] = total.astype(mine.dtype)
            return carry

        lax.fori_loop(0, rows // step, body, 0)
        if not last:
            along_z(part).start()

    def ready(part):
        prepare(lax.rem(z + part + 1, lines))
        for copy in over_core(part):
            copy.start()

    kinds = (ready, add_core, add_corner, add_neighbours)

    def run(number):
        for lag, kind in enumerate(kinds):
            if 0 <= number - lag < parts:
                kind(number - lag)

    def last():
        for part in range(parts - 1):
            along_z(part).wait_recv()

        def body(i, carry):
            at = pl.ds(pl.multiple_of(i * step, step), step)
            total = o_ref[at, :]
            for part in range(parts - 1):
                total += along[part, at, :].astype(jnp.float32)
            o_ref[at, :] = total
            return carry

        lax.fori_loop(0, rows // step, body, 0)
        for part in range(parts - 1):
            along_z(part).wait_send()
        for part in range(parts):
            for copy in (*over_core(part), *to_corner(part), *(to_neighbour(part, way) for way in range(4))):
                copy.wait_send()

    return [functools.partial(run, number) for number in range(parts + len(kinds) - 1)], last


def reduce_scratch(lines, share, columns, low):
    cut = column_cut(columns)
    return [
        pltpu.VMEM((lines, PLANE, share, columns), low),
        pltpu.VMEM((lines, 4, share, columns), low),
        pltpu.VMEM((lines, share, cut), low),
        pltpu.VMEM((lines, share, columns - cut), low),
        pltpu.VMEM((lines, share, columns), low),
        pltpu.VMEM((lines, share, columns), low),
        pltpu.VMEM((lines - 1, share, columns), low),
        pltpu.SemaphoreType.DMA((lines, 11)),
        pltpu.SemaphoreType.DMA((lines, 11)),
    ]


def store_terms(p, block, start, value):
    members, share = p.shape[1:3]
    width = value.shape[1]
    p[block, :, :, start : start + width] = value.astype(p.dtype).reshape(members, share, width)


def halves(width):
    cut = column_cut(width)
    return pl.ds(0, cut), pl.ds(cut, width - cut)


def gather_steps(place, whole, send, recv):
    z, y, x, c = place
    side, over, sibling = device(z, y, 1 - x, c), device(z, 1 - y, x, c), device(z, y, x, 1 - c)
    first, second = halves(whole.shape[-1])
    at = lambda yy, xx: whole.at[yy * 4 + xx * 2 + c]
    own, next_x, next_y, corner = at(y, x), at(y, 1 - x), at(1 - y, x), at(1 - y, 1 - x)
    table = (
        (own.at[:, first], side),
        (own.at[:, second], side),
        (own.at[:, first], over),
        (own.at[:, second], over),
        (own, sibling),
        (next_x.at[:, first], over),
        (next_y.at[:, second], side),
        (next_x.at[:, first], sibling),
        (next_x.at[:, second], sibling),
        (next_y.at[:, first], sibling),
        (next_y.at[:, second], sibling),
        (corner.at[:, first], sibling),
        (corner.at[:, second], sibling),
    )

    def copy(kind):
        ref, to = table[kind]
        return remote(ref, ref, send.at[kind], recv.at[kind], to)

    return copy


GATHER_KINDS = 13
REDUCE_KINDS = 10


def reduce_steps(place, partial, held, corner_a, corner_b, from_side, from_over, send, recv):
    z, y, x, c = place
    side, over, sibling = device(z, y, 1 - x, c), device(z, 1 - y, x, c), device(z, y, x, 1 - c)
    first, second = halves(held.shape[-1])
    lane = lambda yy, xx: held.at[yy * 2 + xx]
    next_x, next_y, corner = lane(y, 1 - x), lane(1 - y, x), lane(1 - y, 1 - x)

    def to_core(yy, xx):
        kind = yy * 2 + xx
        src = partial.at[yy * 4 + xx * 2 + 1 - c]
        return remote(src, lane(yy, xx), send.at[kind], recv.at[kind], sibling)

    table = (
        (corner.at[:, first], corner_a, over),
        (corner.at[:, second], corner_b, side),
        (next_x.at[:, first], from_side.at[:, first], side),
        (next_x.at[:, second], from_side.at[:, second], side),
        (next_y.at[:, first], from_over.at[:, first], over),
        (next_y.at[:, second], from_over.at[:, second], over),
    )

    def copy(kind):
        src, dst, to = table[kind]
        return remote(src, dst, send.at[4 + kind], recv.at[4 + kind], to)

    return to_core, copy


def add_rows(target, other, columns=None, step=32):
    def body(i, carry):
        at = pl.ds(pl.multiple_of(i * step, step), step)
        mine = target[at, :] if columns is None else target[at, columns]
        total = (mine.astype(jnp.float32) + other[at, :].astype(jnp.float32)).astype(target.dtype)
        if columns is None:
            target[at, :] = total
        else:
            target[at, columns] = total
        return carry

    lax.fori_loop(0, other.shape[0] // step, body, 0)


def feed_forward_kernel(
    out_rows, attended, tokens, teacher_rows, out_grad_rows, valid, gains, gate_up_rows, down_rows,
    result, square, norm, hidden_grad, branch, attended_grad, down_final, gate_grad, up_grad,
    out_w, gate_up_w, teacher, out_grad, down_w, down_up, down_down, normed_all, kept, mixed, grads_all, partial, held, corner_a, corner_b, from_side, from_over, hidden, total_grad, scales, squares,
    load_sem, here, line_send, line_recv, down_send, down_recv, gather_send, gather_recv, reduce_send, reduce_recv,
):
    place = coordinates()
    z, y, x, c = place
    width = tokens.shape[1]
    pairs = ((out_rows, out_w), (gate_up_rows, gate_up_w), (teacher_rows, teacher), (out_grad_rows, out_grad))
    loads = [pltpu.make_async_copy(src, dst, load_sem.at[i]) for i, (src, dst) in enumerate(pairs)]
    for load in loads:
        load.start()
    lines, units = down_w.shape[:2]
    greet([device(z, y, 1 - x, c), device(z, 1 - y, x, c), device(z, y, x, 1 - c)] + line_of(z, y, x, c, lines))
    rows = tokens.shape[0]
    share = lines * units
    line_begin, line_pass, line_last = line_gather(place, lines, down_rows, down_w, line_send, line_recv, here)
    line_begin()
    first, second = halves(width)
    mine = y * 4 + x * 2 + c
    chips = ((y, x), (y, 1 - x), (1 - y, x), (1 - y, 1 - x))

    gain = gains[1:2, :]
    count = jnp.sum(gains[2:3, :], -1, keepdims=True) / (width // (lines * PLANE))
    norm[...] = 2.0 / (count * width)
    loads[0].wait()
    hidden[...] = tokens[...].astype(jnp.float32) + jnp.dot(
        attended[...], out_w[...], preferred_element_type=jnp.float32
    )

    def norm_rows(at):
        values = hidden[at, :]
        scale = rms_scale(values)
        scales[at, :] = scale
        normed_all[mine, at, :] = (values * scale * gain[...]).astype(normed_all.dtype)

    by_rows(rows, norm_rows)

    def gathered(phase, whole, compute, late, beside):
        copy = gather_steps(place, whole, gather_send.at[phase], gather_recv.at[phase])
        to_core, pass_on = reduce_steps(
            place, partial, held, corner_a, corner_b, from_side, from_over, reduce_send.at[phase], reduce_recv.at[phase]
        )
        for kind in (0, 3, 4, 1, 2):
            copy(kind).start()

        def wave(yy, xx):
            lax.fori_loop(0, 2, lambda cc, carry: compute(yy * 4 + xx * 2 + cc, carry), 0)
            if late is None:
                to_core(yy, xx).start()

        def late_wave(yy, xx):
            if late is not None:
                lax.fori_loop(0, 2, lambda cc, carry: late(yy * 4 + xx * 2 + cc, carry), 0)
                to_core(yy, xx).start()

        def join(yy, xx):
            to_core(yy, xx).wait_recv()
            add_rows(held.at[yy * 2 + xx], partial.at[yy * 4 + xx * 2 + c])

        copy(4).wait_recv()
        beside(0)
        wave(*chips[0])
        copy(0).wait_recv()
        copy(5).start()
        copy(7).start()
        copy(3).wait_recv()
        copy(6).start()
        copy(10).start()
        copy(1).wait_recv()
        copy(8).start()
        copy(2).wait_recv()
        copy(9).start()
        beside(1)
        copy(7).wait_recv()
        copy(8).wait_recv()
        wave(*chips[1])
        beside(2)
        copy(9).wait_recv()
        copy(10).wait_recv()
        wave(*chips[2])
        copy(5).wait_recv()
        copy(11).start()
        copy(6).wait_recv()
        copy(12).start()
        beside(3)
        late_wave(*chips[1])
        late_wave(*chips[2])
        join(*chips[1])
        pass_on(3).start()
        join(*chips[2])
        pass_on(4).start()
        copy(11).wait_recv()
        copy(12).wait_recv()
        wave(*chips[3])
        late_wave(*chips[3])
        late_wave(*chips[0])
        join(*chips[3])
        pass_on(0).start()
        pass_on(1).start()
        join(*chips[0])
        for kind in range(GATHER_KINDS):
            copy(kind).wait_send()
        return to_core, pass_on

    def reduced_corner(to_core, pass_on):
        pass_on(0).wait_recv()
        add_rows(held.at[y * 2 + 1 - x], corner_a, first)
        pass_on(2).start()
        pass_on(1).wait_recv()
        add_rows(held.at[(1 - y) * 2 + x], corner_b, second)
        pass_on(5).start()

    def reduced_rest(to_core, pass_on):
        for kind in (2, 3, 4, 5):
            pass_on(kind).wait_recv()
        for kind in range(6):
            pass_on(kind).wait_send()
        for yy, xx in chips:
            to_core(yy, xx).wait_send()

    def summed(at):
        total = held[y * 2 + x, at, :].astype(jnp.float32) + from_side[at, :].astype(jnp.float32)
        return total + from_over[at, :].astype(jnp.float32)

    def forward(member, carry):
        both = jnp.dot(normed_all[member], gate_up_w[...], preferred_element_type=jnp.float32)
        gate, up = both[:, :share], both[:, share:]
        sigmoid = 1.0 / (1.0 + jnp.exp(-gate))
        activated = gate * sigmoid
        kept[member, :, :share] = (up * (sigmoid + activated * (1.0 - sigmoid))).astype(kept.dtype)
        kept[member, :, share:] = activated.astype(kept.dtype)
        low = (activated * up).astype(mixed.dtype)
        mixed[member] = low
        return carry

    def forward_down(member, carry):
        summed_units = jnp.dot(mixed[member], down_w[...].reshape(share, width), preferred_element_type=jnp.float32)
        partial[member] = summed_units.astype(partial.dtype)
        return carry

    def bring_down(moment):
        if moment == 0:
            loads[1].wait()
            return
        line_pass(moment)
        if moment == lines - 1:
            line_last()

    rest = gathered(0, normed_all, forward, forward_down, bring_down)
    reduced_corner(*rest)
    loads[2].wait()
    loads[3].wait()
    reduced_rest(*rest)

    def result_rows(at):
        values = hidden[at, :] + summed(at)
        result[at, :] = values.astype(result.dtype)
        differ = values - teacher[at, :].astype(jnp.float32)
        weighed = valid[at, :] * differ
        squares[at, :] = jnp.sum(weighed * differ, -1, keepdims=True)
        total = out_grad[at, :].astype(jnp.float32) + weighed * norm[...]
        total_grad[at, :] = total
        grads_all[mine, at, :] = total.astype(grads_all.dtype)

    by_rows(rows, result_rows)
    square[...] = jnp.sum(squares[...], 0, keepdims=True)

    def backward(member, carry):
        mixed_grad = against(grads_all[member], down_w[...].reshape(share, width))
        low_gate = (mixed_grad * kept[member, :, :share].astype(jnp.float32)).astype(kept.dtype)
        low_up = (mixed_grad * kept[member, :, share:].astype(jnp.float32)).astype(kept.dtype)
        kept[member, :, :share] = low_gate
        kept[member, :, share:] = low_up
        partial[member] = against(kept[member], gate_up_w[...]).astype(partial.dtype)
        return carry

    rest = gathered(1, grads_all, backward, None, lambda moment: None)
    tokens_all = normed_all.shape[0] * rows
    block = 256

    def down_block(i, carry):
        at = pl.ds(pl.multiple_of(i * block, block), block)
        left = mixed[:, :, at].reshape(tokens_all, block)
        grads = transposed(left, grads_all[...].reshape(tokens_all, width)).astype(down_w.dtype)
        per = block // units
        down_w[pl.ds(i * per, per)] = grads.reshape(per, units, width)
        return carry

    def both_block(i, carry):
        at = pl.ds(pl.multiple_of(i * block, block), block)
        left = normed_all[:, :, at].reshape(tokens_all, block)
        both = transposed(left, kept[...].reshape(tokens_all, 2 * share)).astype(gate_grad.dtype)
        gate_grad[at, :] = both[:, :share]
        up_grad[at, :] = both[:, share:]
        return carry

    lax.fori_loop(0, share // block, down_block, 0)
    down_begin, down_hop, down_last = line_reduce(place, lines, down_w, down_up, down_down, down_send, down_recv)
    down_begin()
    blocks = width // block
    lax.fori_loop(0, blocks // 2, both_block, 0)
    reduced_corner(*rest)
    down_hop(1)
    lax.fori_loop(blocks // 2, blocks, both_block, 0)
    reduced_rest(*rest)
    for moment in range(2, lines - 1):
        down_hop(moment)

    def grad_rows(at):
        grads = summed(at)
        normed = hidden[at, :] * scales[at, :]
        scaled = grads * gain[...]
        values = total_grad[at, :] + scales[at, :] * (scaled - normed * jnp.mean(scaled * normed, -1, keepdims=True))
        hidden_grad[at, :] = values
        branch[at, :] = values.astype(branch.dtype)

    by_rows(rows, grad_rows)
    attended_grad[...] = against(branch[...], out_w[...]).astype(attended_grad.dtype)

    def keep_down(i, sums):
        down_final[pl.ds(pl.multiple_of(i * 32, 32), 32), :] = sums

    down_last(keep_down)


def feed_forward(lines, out_rows, attended, tokens, teacher, out_grad, valid, gains, gate_up_w, down_rows, identity):
    rows, width = tokens.shape
    units = down_rows.shape[0]
    share = lines * units
    low = tokens.dtype
    shape = jax.ShapeDtypeStruct
    vmem, anywhere = pl.BlockSpec(memory_space=pltpu.VMEM), pl.BlockSpec(memory_space=pl.ANY)
    cut = column_cut(width)
    return pl.pallas_call(
        feed_forward_kernel,
        out_shape=[
            shape((rows, width), low),
            shape((1, 1), jnp.float32),
            shape((1, 1), jnp.float32),
            shape((rows, width), jnp.float32),
            shape((rows, width), low),
            shape((rows, width), low),
            shape((units, width), jnp.float32),
            shape((width, share), low),
            shape((width, share), low),
        ],
        in_specs=[anywhere, vmem, vmem, anywhere, anywhere, vmem, vmem, anywhere, anywhere],
        out_specs=[vmem] * 9,
        scratch_shapes=[
            pltpu.VMEM((width, width), low),
            pltpu.VMEM((width, 2 * share), low),
            pltpu.VMEM((rows, width), low),
            pltpu.VMEM((rows, width), low),
            pltpu.VMEM((lines, units, width), low),
            pltpu.VMEM((lines, units, width), low),
            pltpu.VMEM((lines, units, width), low),
            pltpu.VMEM((PLANE, rows, width), low),
            pltpu.VMEM((PLANE, rows, 2 * share), low),
            pltpu.VMEM((PLANE, rows, share), low),
            pltpu.VMEM((PLANE, rows, width), low),
            pltpu.VMEM((PLANE, rows, width), low),
            pltpu.VMEM((4, rows, width), low),
            pltpu.VMEM((rows, cut), low),
            pltpu.VMEM((rows, width - cut), low),
            pltpu.VMEM((rows, width), low),
            pltpu.VMEM((rows, width), low),
            pltpu.VMEM((rows, width), jnp.float32),
            pltpu.VMEM((rows, width), jnp.float32),
            pltpu.VMEM((rows, 1), jnp.float32),
            pltpu.VMEM((rows, 1), jnp.float32),
            pltpu.SemaphoreType.DMA((4,)),
            pltpu.SemaphoreType.DMA,
            pltpu.SemaphoreType.DMA((2, lines)),
            pltpu.SemaphoreType.DMA((2, lines)),
            pltpu.SemaphoreType.DMA((2, lines)),
            pltpu.SemaphoreType.DMA((2, lines)),
            pltpu.SemaphoreType.DMA((2, GATHER_KINDS)),
            pltpu.SemaphoreType.DMA((2, GATHER_KINDS)),
            pltpu.SemaphoreType.DMA((2, REDUCE_KINDS)),
            pltpu.SemaphoreType.DMA((2, REDUCE_KINDS)),
        ],
        compiler_params=pltpu.CompilerParams(collective_id=identity, vmem_limit_bytes=VMEM_LIMIT),
        cost_estimate=pl.CostEstimate(flops=40 * PLANE * rows * width * share // 2, bytes_accessed=30 * 2**20, transcendentals=0),
        name="feed_forward",
    )(out_rows, attended, tokens, teacher, out_grad, valid, gains, gate_up_w, down_rows)


HEAD_TILES = 3
ROW_STEP = 64


def by_rows(rows, body, step=ROW_STEP):
    def run(i, carry):
        body(pl.ds(pl.multiple_of(i * step, step), step))
        return carry

    lax.fori_loop(0, rows // step, run, 0)


def lanes_of(values):
    return lax.broadcasted_iota(jnp.int32, values.shape, len(values.shape) - 1)


def turned(tile, cosine, sine):
    half = HD // 2
    partner = jnp.where(lanes_of(tile) < half, -pltpu.roll(tile, LANES - half, 1), pltpu.roll(tile, half, 1))
    return tile * cosine + partner * sine


def packed_pair(first, second, even):
    lane = lanes_of(first)
    moved = pltpu.roll(second, HD, 1)
    full_even = jnp.where(lane < HD, first, moved)
    full_odd = jnp.where(lane < 32, pltpu.roll(first, 64, 1), pltpu.roll(second, 32, 1))
    return jnp.where(even, full_even, full_odd), jnp.where(even, moved, first)


def unpacked_pair(full, part, even):
    lane = lanes_of(full)
    zero = jnp.zeros_like(full)
    first_even = jnp.where(lane < HD, full, zero)
    second_even = jnp.where(lane < 32, pltpu.roll(full, 32, 1), jnp.where(lane < HD, pltpu.roll(part, 32, 1), zero))
    first_odd = jnp.where(lane < 64, part, jnp.where(lane < HD, pltpu.roll(full, 64, 1), zero))
    second_odd = jnp.where(lane < HD, pltpu.roll(full, HD, 1), zero)
    return jnp.where(even, first_even, first_odd), jnp.where(even, second_even, second_odd)


def keys_and_values(qkv, keys, values, count, rows):
    def body(src, carry):
        block = qkv[src].astype(jnp.float32)
        tiles = [block[:, i * LANES : (i + 1) * LANES] for i in range(HEAD_TILES)]
        lane = lanes_of(tiles[0])
        key = jnp.where(lane < HD, tiles[2], 0.0)
        value = jnp.where(lane < 64, pltpu.roll(tiles[1], 64, 1), pltpu.roll(tiles[2], HD, 1))
        value = jnp.where(lane < 32, pltpu.roll(tiles[0], 32, 1), value)
        value = jnp.where(lane < HD, value, 0.0)
        at = pl.ds(pl.multiple_of(src * rows, rows), rows)
        for half in range(2):
            keys[half, at, :] = key[half * rows : (half + 1) * rows].astype(keys.dtype)
            values[half, at, :] = value[half * rows : (half + 1) * rows].astype(values.dtype)
        return carry

    lax.fori_loop(0, count, body, 0)


def segment_of(lengths, place):
    start, end = jnp.zeros_like(place), 0
    for length in [lengths[0, j] for j in range(NSEQ)]:
        end = end + length
        start = start + jnp.where(place >= end, length, 0)
    return start, end


def side_by_side(heads):
    full, part = packed_pair(heads[0], heads[1], True)
    full_odd, part_odd = packed_pair(heads[2], heads[3], False)
    middle = jnp.where(lanes_of(part) < 64, part, pltpu.roll(part_odd, 64, 1))
    return full, middle, full_odd


def apart(ref, group):
    start = group * HEAD_TILES * LANES
    tiles = [ref[:, start + i * LANES : start + (i + 1) * LANES].astype(jnp.float32) for i in range(HEAD_TILES)]
    return unpacked_pair(tiles[0], tiles[1], True) + unpacked_pair(tiles[2], pltpu.roll(tiles[1], 64, 1), False)


def arrange_rows(rows_in, w_query, w_key, w_value, gain_rows, count):
    share = rows_in.shape[0]
    groups = HEADS // KV
    queries = [head for group in range(HEADS // 4) for head in apart(w_query, group)]
    keys = [head for group in range(KV // 4) for head in apart(w_key, group)]
    values = [head for group in range(KV // 4) for head in apart(w_value, group)]
    lane = lanes_of(keys[0])
    for head in range(KV):
        for number, tile in enumerate(queries[head * groups : (head + 1) * groups] + [keys[head]]):
            third = pltpu.roll(values[head], HD - 32 * number, 1)
            start = (head * HEAD_TILES + number) * LANES
            rows_in[:, start : start + LANES] = jnp.where(lane < HD, tile, third).astype(rows_in.dtype)
    row = lax.broadcasted_iota(jnp.int32, (LANES, LANES), 0)
    columns = jnp.where(row == 0, gain_rows[0:1, :], jnp.where(row == 1, gain_rows[1:2, :], 0.0))
    columns = jnp.where(row == 2, count, columns)
    rows_in[:, KV * HEAD_TILES * LANES :] = jnp.transpose(columns)[:share, :].astype(rows_in.dtype)


def attend_kernel(
    scale, lines, w_query, w_key, w_value, w_gate, w_up, out_rows, gain_rows, freq, mask, deal, lengths, tokens,
    attended, normed, gains, cosine, sine, valid, weights, out_w, unit_w, qkv_out, probs,
    rows_in, unit_rows, w, place_row, sent, qkv, keys, values, prob_blocks, o_sent, o_came,
    send, recv, o_send, o_recv, p_sem, q_sem, w_sem, w_send, w_recv, w_here, g_send, g_recv, g_here,
    u_send, u_recv, u_here, l_send, l_recv,
):
    z, y, x, c = coordinates()
    count = sent.shape[0]
    me = z * 2 + y
    even = y == 0
    rows, width = tokens.shape
    half_rows = rows // 2
    head_cols = HEAD_TILES * LANES
    to_device = lambda i: (i, x * 2 + c)
    peer = lambda k: lax.rem(me + k, count)

    member = y * 4 + x * 2 + c
    in_plane = lambda i: (z * 2 + i // 4, i % 4)
    unit_peer = lambda k: lax.rem(member + k, PLANE)
    others = [device(z, yy, xx, cc) for yy, xx, cc in ((y, 1 - x, c), (y, x, 1 - c), (y, 1 - x, 1 - c))]
    others += [device(z, 1 - y, xx, cc) for xx, cc in ((1 - x, c), (x, 1 - c), (1 - x, 1 - c))]
    units = w_gate.shape[1] // (lines * PLANE)
    for i in range(PLANE):
        for zz in range(lines):
            start = (zz * PLANE + i) * units
            unit_rows[i, :, zz * units : (zz + 1) * units] = w_gate[:, start : start + units]
            unit_rows[i, :, (lines + zz) * units : (lines + zz + 1) * units] = w_up[:, start : start + units]
    greet([to_device(peer(k)) for k in range(1, count)] + others)

    def unit_out(k):
        i = unit_peer(k)
        return remote(unit_rows.at[i], unit_w.at[z, member], u_send.at[k], u_recv.at[k], in_plane(i))

    unit_own = pltpu.make_async_copy(unit_rows.at[member], unit_w.at[z, member], u_here)
    unit_own.start()
    stages, weights_last = gather_plan(lines, rows_in, w, w_send, w_recv, w_here)
    gather_stages, gather_last = gather_plan(lines, out_rows, out_w, g_send, g_recv, g_here)
    line_begin, line_pass, line_last = line_gather(
        (z, y, x, c), lines, unit_w.at[z], unit_w, l_send, l_recv
    )
    for k in range(1, PLANE):
        unit_out(k).start()
    first_block = deal[0, me]
    total = functools.reduce(lambda a, b: a + b, [lengths[0, j] for j in range(NSEQ)])
    token = lax.broadcasted_iota(jnp.int32, (1, rows), 1)
    in_pack = jnp.where(token < half_rows, first_block * half_rows, (2 * count - 2 - first_block) * half_rows) + token
    counted = jnp.where(in_pack < total, mask[...].astype(jnp.float32), 0.0)
    arrange_rows(rows_in, w_query, w_key, w_value, gain_rows, jnp.sum(counted, -1, keepdims=True))
    stages[0]()
    valid[...] = jnp.transpose(jnp.broadcast_to(counted, (LANES, rows)))[:, :1]
    token = lax.broadcasted_iota(jnp.int32, (rows, 1), 0)
    in_pack = jnp.where(token < half_rows, first_block * half_rows, (2 * count - 2 - first_block) * half_rows) + token
    angle = (in_pack - segment_of(lengths, in_pack)[0]).astype(jnp.float32) * freq[...]
    cosine[...] = jnp.cos(angle)
    sine[...] = jnp.sin(angle)
    unit_own.wait()
    for k in range(1, PLANE):
        unit_out(k).wait_recv()
    line_begin()
    for number, stage in enumerate(stages[1:]):
        stage()
        if number == lines - 1:
            line_pass(1)
    weights_last()
    keep_weights = pltpu.make_async_copy(w, weights, w_sem)
    keep_weights.start()

    def columns_of(start, size):
        return w[:, :, pl.ds(start, size)].reshape(width, size)

    extras = columns_of(count * head_cols, LANES)
    gains[...] = jnp.transpose(extras.astype(jnp.float32))[: gains.shape[0], :]
    gain = gains[0:1, :]

    def norm_rows(at):
        values_at = tokens[at, :].astype(jnp.float32)
        normed[at, :] = (values_at * rms_scale(values_at) * gain).astype(normed.dtype)

    by_rows(rows, norm_rows)

    def out(k):
        return remote(sent.at[peer(k)], qkv.at[me], send.at[k], recv.at[k], to_device(peer(k)))

    def project(k, carry):
        i = peer(k)
        columns = columns_of(pl.multiple_of(i * head_cols, LANES), head_cols)
        both = jnp.dot(normed[...], columns, preferred_element_type=jnp.float32)
        for tile in range(HEAD_TILES):
            at = slice(tile * LANES, (tile + 1) * LANES)
            sent[i, :, at] = turned(both[:, at], cosine[...], sine[...]).astype(sent.dtype)

        @pl.when(k < count)
        def _():
            out(k).start()

        return carry

    lax.fori_loop(1, count + 1, project, 0)
    gather_stages[0]()
    line_pass(2)
    qkv[me] = sent[me]
    for src in range(count):
        columns = slice(src * half_rows, (src + 1) * half_rows)
        steps = lax.broadcasted_iota(jnp.int32, (1, half_rows), 1)
        place_row[0, :, columns] = deal[0, src] * half_rows + steps
        place_row[1, :, columns] = (2 * count - 1 - deal[0, src]) * half_rows + steps

    def arrive(k, carry):
        out(k).wait_recv()
        return carry

    lax.fori_loop(1, count, arrive, 0)
    gather_stages[1]()
    keep_qkv = pltpu.make_async_copy(qkv, qkv_out, q_sem)
    keep_qkv.start()
    keys_and_values(qkv, keys, values, count, half_rows)

    def back(k):
        return remote(o_sent.at[peer(k)], o_came.at[me], o_send.at[k], o_recv.at[k], to_device(peer(k)))

    def keep(src, half):
        return pltpu.make_async_copy(prob_blocks.at[src, half], probs.at[src, half], p_sem.at[src, half])

    def attend(k, carry):
        src = peer(k)
        halves_out = []
        for half in range(2):
            at = pl.ds(half * half_rows, half_rows)
            queries = jnp.concatenate([qkv[src, at, :LANES], qkv[src, at, LANES : 2 * LANES]], 0)
            score = against(queries, keys[half]) * scale
            first = deal[0, src]
            block = first if half == 0 else 2 * count - 1 - first
            own = block * half_rows + lax.broadcasted_iota(jnp.int32, (half_rows, 1), 0)
            start, end = segment_of(lengths, own)
            lowest = jnp.where(own < end, start, own)
            place = place_row[half]
            allowed = (place >= lowest) & (place <= own)
            bias = jnp.where(allowed, 0.0, masked_score)
            score = score + jnp.concatenate([bias, bias], 0)
            top = jnp.max(score, -1, keepdims=True)
            weight = jnp.exp(score - top)
            total = jnp.sum(weight, -1, keepdims=True)
            low = (weight * (1.0 / total)).astype(prob_blocks.dtype)
            prob_blocks[src, half] = low
            keep(src, half).start()
            summed = jnp.dot(low, values[half], preferred_element_type=jnp.float32)
            full, part = packed_pair(summed[:half_rows], summed[half_rows:], even)
            o_sent[src, at, :] = full.astype(o_sent.dtype)
            halves_out.append(part)
        lane = lanes_of(halves_out[0])
        part = jnp.where(lane < 64, halves_out[0], pltpu.roll(halves_out[1], 64, 1))
        o_sent[src, pl.ds(rows, half_rows), :] = part.astype(o_sent.dtype)

        @pl.when(k < count)
        def _():
            back(k).start()

        for number in range(2, len(gather_stages)):
            pl.when(k == 2 * number - 2)(gather_stages[number])
        return carry

    lax.fori_loop(1, count + 1, attend, 0)
    o_came[me] = o_sent[me]

    def return_arrive(k, carry):
        back(k).wait_recv()
        return carry

    lax.fori_loop(1, count, return_arrive, 0)
    for pair in range(count // 2):
        at = pair * head_cols
        attended[:, at : at + LANES] = o_came[2 * pair, :rows, :]
        attended[:, at + 2 * LANES : at + 3 * LANES] = o_came[2 * pair + 1, :rows, :]
        one = o_came[2 * pair, rows:, :].astype(jnp.float32)
        two = o_came[2 * pair + 1, rows:, :].astype(jnp.float32)
        lane = lanes_of(one)
        middle = slice(at + LANES, at + 2 * LANES)
        attended[:half_rows, middle] = jnp.where(lane < 64, one, pltpu.roll(two, 64, 1)).astype(attended.dtype)
        attended[half_rows:, middle] = jnp.where(lane < 64, pltpu.roll(one, 64, 1), two).astype(attended.dtype)

    def drain(k, carry):
        out(k).wait_send()
        back(k).wait_send()
        return carry

    lax.fori_loop(1, count, drain, 0)

    def drain_probs(src, carry):
        keep(src, 0).wait()
        keep(src, 1).wait()
        return carry

    lax.fori_loop(0, count, drain_probs, 0)
    keep_qkv.wait()
    gather_last()
    for moment in range(3, lines):
        line_pass(moment)
    line_last()
    for k in range(1, PLANE):
        unit_out(k).wait_send()
    keep_weights.wait()


def attend(scale, lines, w_query, w_key, w_value, w_gate, w_up, out_rows, gain_rows, freq, mask, deal, lengths, tokens, identity):
    rows, width = tokens.shape
    share, units = out_rows.shape[0], w_gate.shape[1] // PLANE
    count = KV
    columns = count * HEAD_TILES * LANES + LANES
    half_rows = rows // 2
    half = count * half_rows
    head_cols = HEAD_TILES * LANES
    low = tokens.dtype
    shape = jax.ShapeDtypeStruct
    vmem, anywhere = pl.BlockSpec(memory_space=pltpu.VMEM), pl.BlockSpec(memory_space=pl.ANY)
    smem = pl.BlockSpec(memory_space=pltpu.SMEM)
    dma = pltpu.SemaphoreType.DMA
    return pl.pallas_call(
        functools.partial(attend_kernel, scale, lines),
        out_shape=[
            shape((rows, width), low),
            shape((rows, width), low),
            shape((8, width), jnp.float32),
            shape((rows, LANES), jnp.float32),
            shape((rows, LANES), jnp.float32),
            shape((rows, 1), jnp.float32),
            shape((lines * PLANE, share, columns), low),
            shape((lines * PLANE,) + out_rows.shape, low),
            shape((lines, PLANE, share, 2 * units), low),
            shape((count, rows, head_cols), low),
            shape((count, 2, rows, half), low),
        ],
        in_specs=[vmem] * 5 + [anywhere] + [vmem] * 3 + [smem, smem, vmem],
        out_specs=[vmem] * 6 + [anywhere] * 5,
        scratch_shapes=[
            pltpu.VMEM((share, columns), low),
            pltpu.VMEM((PLANE, share, 2 * units), low),
            pltpu.VMEM((lines * PLANE, share, columns), low),
            pltpu.VMEM((2, 1, half), jnp.int32),
            pltpu.VMEM((count, rows, head_cols), low),
            pltpu.VMEM((count, rows, head_cols), low),
            pltpu.VMEM((2, half, LANES), low),
            pltpu.VMEM((2, half, LANES), low),
            pltpu.VMEM((count, 2, rows, half), low),
            pltpu.VMEM((count, rows + half_rows, LANES), low),
            pltpu.VMEM((count, rows + half_rows, LANES), low),
            dma((count,)),
            dma((count,)),
            dma((count,)),
            dma((count,)),
            dma((count, 2)),
            dma,
            dma,
            *gather_semaphores(lines),
            *gather_semaphores(lines),
            dma((PLANE,)),
            dma((PLANE,)),
            dma,
            dma((2, lines)),
            dma((2, lines)),
        ],
        compiler_params=pltpu.CompilerParams(collective_id=identity, vmem_limit_bytes=VMEM_LIMIT),
        name="attend",
    )(w_query, w_key, w_value, w_gate, w_up, out_rows, gain_rows, freq, mask, deal, lengths, tokens)


def attend_back_kernel(
    scale, lines, attended_grad, qkv, probs, cosine, sine, attended, branch, gate_parts, qkv_grad, out_final, gate_sums,
    sent, came, keys, values, prob_blocks, dk_sum, dv_sum, back_sent, back_came,
    send, recv, back_send, back_recv, p_sem, up, down, l_send, l_recv, p, *reducing,
):
    z, y, x, c = coordinates()
    count = sent.shape[0]
    me = z * 2 + y
    even = y == 0
    rows, width = attended_grad.shape
    half_rows = rows // 2
    head_cols = HEAD_TILES * LANES
    to_device = lambda i: (i, x * 2 + c)
    peer = lambda k: lax.rem(me + k, count)
    source = lambda k: lax.rem(me + count - k, count)

    def load(src, half):
        return pltpu.make_async_copy(probs.at[src, half], prob_blocks.at[src, half], p_sem.at[src, half])

    def load_start(k, carry):
        load(source(k), 0).start()
        load(source(k), 1).start()
        return carry

    lax.fori_loop(0, count, load_start, 0)
    greet([to_device(peer(k)) for k in range(1, count)] + [device(z, y, 1 - x, c), device(z, y, x, 1 - c)])
    members, share = p.shape[1:3]

    def prepare(block):
        at = pl.ds(pl.multiple_of(block * members * share, LANES), members * share)
        store_terms(p, block, 0, transposed(attended[:, at], branch[...]))

    reduce_stages, reduce_last = reduce_plan(lines, prepare, p, out_final, *reducing)
    line_begin, line_hop, line_last = line_reduce((z, y, x, c), lines, gate_parts, up, down, l_send, l_recv)
    for pair in range(count // 2):
        at = pair * head_cols
        sent[2 * pair, :rows, :] = attended_grad[:, at : at + LANES]
        sent[2 * pair + 1, :rows, :] = attended_grad[:, at + 2 * LANES : at + 3 * LANES]
        middle = attended_grad[:, at + LANES : at + 2 * LANES].astype(jnp.float32)
        one, two = middle[:half_rows], middle[half_rows:]
        lane = lanes_of(one)
        sent[2 * pair, rows:, :] = jnp.where(lane < 64, one, pltpu.roll(two, 64, 1)).astype(sent.dtype)
        sent[2 * pair + 1, rows:, :] = jnp.where(lane < 64, pltpu.roll(one, 64, 1), two).astype(sent.dtype)

    def out(k):
        return remote(sent.at[peer(k)], came.at[me], send.at[k], recv.at[k], to_device(peer(k)))

    def begin(k, carry):
        out(k).start()
        return carry

    lax.fori_loop(1, count, begin, 0)
    reduce_stages[0]()
    came[me] = sent[me]
    keys_and_values(qkv, keys, values, count, half_rows)
    dk_sum[...] = jnp.zeros_like(dk_sum)
    dv_sum[...] = jnp.zeros_like(dv_sum)

    def grads(k, carry):
        src = source(k)

        @pl.when(k > 0)
        def _():
            out(k).wait_recv()

        for half in range(2):
            at = pl.ds(half * half_rows, half_rows)
            full = came[src, at, :].astype(jnp.float32)
            part = came[src, pl.ds(rows, half_rows), :].astype(jnp.float32)
            if half:
                part = pltpu.roll(part, 64, 1)
            pair = jnp.concatenate(unpacked_pair(full, part, even), 0).astype(came.dtype)
            queries = jnp.concatenate([qkv[src, at, :LANES], qkv[src, at, LANES : 2 * LANES]], 0)
            load(src, half).wait()
            low = prob_blocks[src, half]
            prob = low.astype(jnp.float32)
            prob_grad = against(pair, values[half])
            delta = jnp.sum(prob * prob_grad, -1, keepdims=True)
            score_low = (prob * (prob_grad - delta)).astype(low.dtype)
            dq = jnp.dot(score_low, keys[half], preferred_element_type=jnp.float32) * scale
            back_sent[src, at, :LANES] = dq[:half_rows].astype(back_sent.dtype)
            back_sent[src, at, LANES : 2 * LANES] = dq[half_rows:].astype(back_sent.dtype)
            dk_sum[half] += transposed(score_low, queries)
            dv_sum[half] += transposed(low, pair)
        pl.when(k == 2)(line_begin)
        for number in range(1, len(reduce_stages)):
            pl.when(k == number)(reduce_stages[number])
        return carry

    lax.fori_loop(0, count, grads, 0)

    def back(k):
        return remote(back_sent.at[peer(k)], back_came.at[me], back_send.at[k], back_recv.at[k], to_device(peer(k)))

    def finish(k, carry):
        src = peer(k)
        in_half = pl.ds(pl.multiple_of(src * half_rows, half_rows), half_rows)
        for half in range(2):
            at = pl.ds(half * half_rows, half_rows)
            dk = dk_sum[half, in_half, :] * scale
            dv = dv_sum[half, in_half, :]
            lane = lanes_of(dk)
            for tile in range(HEAD_TILES):
                columns = slice(tile * LANES, (tile + 1) * LANES)
                head = dk if tile == 2 else back_sent[src, at, columns].astype(jnp.float32)
                third = pltpu.roll(dv, HD - 32 * tile, 1)
                back_sent[src, at, columns] = jnp.where(lane < HD, head, third).astype(back_sent.dtype)

        @pl.when(k < count)
        def _():
            back(k).start()

        return carry

    lax.fori_loop(1, count + 1, finish, 0)
    for moment in range(1, lines - 1):
        line_hop(moment)
    reduce_last()
    back_came[me] = back_sent[me]

    def turn_back(k, carry):
        src = source(k)

        @pl.when(k > 0)
        def _():
            back(k).wait_recv()

        for tile in range(HEAD_TILES):
            columns = slice(tile * LANES, (tile + 1) * LANES)
            values_at = back_came[src, :, columns].astype(jnp.float32)
            turned_at = turned(values_at, cosine[...], -sine[...])
            at = pl.ds(pl.multiple_of(src * head_cols + tile * LANES, LANES), LANES)
            qkv_grad[:, at] = turned_at.astype(qkv_grad.dtype)
        return carry

    lax.fori_loop(0, count, turn_back, 0)

    def keep_sums(i, sums):
        gate_sums[i] = sums.astype(gate_sums.dtype)

    line_last(keep_sums, gate_sums.shape[1])

    def drain(k, carry):
        out(k).wait_send()
        back(k).wait_send()
        return carry

    lax.fori_loop(1, count, drain, 0)


def attend_back(scale, lines, attended_grad, qkv, probs, tables, attended, branch, gate_parts, identity):
    rows, width = attended_grad.shape
    count, _, head_cols = qkv.shape
    half = probs.shape[-1]
    half_rows = rows // 2
    share = width // (lines * PLANE)
    low = attended_grad.dtype
    vmem, anywhere = pl.BlockSpec(memory_space=pltpu.VMEM), pl.BlockSpec(memory_space=pl.ANY)
    dma = pltpu.SemaphoreType.DMA
    return pl.pallas_call(
        functools.partial(attend_back_kernel, scale, lines),
        out_shape=[
            jax.ShapeDtypeStruct((rows, count * head_cols), low),
            jax.ShapeDtypeStruct((share, width), jnp.float32),
            jax.ShapeDtypeStruct((PLANE, share, gate_parts.shape[2]), low),
        ],
        in_specs=[vmem, vmem, anywhere] + [vmem] * 5,
        out_specs=[vmem, vmem, vmem],
        scratch_shapes=[
            pltpu.VMEM((count, rows + half_rows, LANES), low),
            pltpu.VMEM((count, rows + half_rows, LANES), low),
            pltpu.VMEM((2, half, LANES), low),
            pltpu.VMEM((2, half, LANES), low),
            pltpu.VMEM((count, 2, rows, half), low),
            pltpu.VMEM((2, half, LANES), jnp.float32),
            pltpu.VMEM((2, half, LANES), jnp.float32),
            pltpu.VMEM((count, rows, head_cols), low),
            pltpu.VMEM((count, rows, head_cols), low),
            dma((count,)),
            dma((count,)),
            dma((count,)),
            dma((count,)),
            dma((count, 2)),
            pltpu.VMEM(gate_parts.shape, low),
            pltpu.VMEM(gate_parts.shape, low),
            dma((2, lines)),
            dma((2, lines)),
            *reduce_scratch(lines, share, width, low),
        ],
        compiler_params=pltpu.CompilerParams(collective_id=identity, vmem_limit_bytes=VMEM_LIMIT),
        name="attend_back",
    )(attended_grad, qkv, probs, *tables, attended, branch, gate_parts)


def finish_kernel(
    weights, normed, qkv_grad, hidden_grad, tokens, gains, square, norm, w_gate, w_up, gate_sums, up_parts,
    input_grad, query_final, key_final, value_final, gate_final, up_final, gain_final, loss,
    w, own_rows, normed_grad, final, up_sums, gate_came, up_came, line_up, line_down,
    w_sem, own_sem, gate_send, gate_recv, up_send, up_recv, here, l_send, l_recv, p, *reducing,
):
    z, y, x, c = coordinates()
    lines, members, share = p.shape[:3]
    rows, width = tokens.shape
    qkv_cols = qkv_grad.shape[1]
    low = normed.dtype
    load = pltpu.make_async_copy(weights.at[:, pl.ds(0, qkv_cols)], w, w_sem)
    load.start()
    number = (z * 2 + y) * 4 + x * 2 + c
    own_at = pl.ds(pl.multiple_of(number * share, 16), share)
    load_own = pltpu.make_async_copy(weights.at[own_at, :], own_rows, own_sem)
    load_own.start()
    me = y * 4 + x * 2 + c
    peer = lambda k: lax.rem(me + k, members)
    member = lambda i: (z * 2 + i // 4, i % 4)
    greet([member(peer(k)) for k in range(1, members)] + line_of(z, y, x, c, lines))

    def out(kind, k):
        src, came, send, recv = (
            (gate_sums, gate_came, gate_send, gate_recv),
            (up_sums, up_came, up_send, up_recv),
        )[kind]
        return remote(src.at[peer(k)], came.at[me], send.at[k], recv.at[k], member(peer(k)))

    gate_own = pltpu.make_async_copy(gate_sums.at[me], gate_came.at[me], here)
    gate_own.start()
    line_begin, line_hop, line_last = line_reduce((z, y, x, c), lines, up_parts, line_up, line_down, l_send, l_recv)
    line_begin()

    def keep_up(i, sums):
        up_sums[i] = sums.astype(up_sums.dtype)

    devices = lines * PLANE
    place = lax.broadcasted_iota(jnp.int32, (1, LANES), 1) - number
    rest = square[...]
    loss_terms = jnp.zeros((1, LANES), jnp.float32)
    for term in range(3):
        top = rest.astype(low).astype(jnp.float32)
        loss_terms = loss_terms + jnp.where(place == term * devices, top, 0.0)
        rest = rest - top

    def prepare(block):
        at = pl.ds(pl.multiple_of(block * members * share, LANES), members * share)
        left = normed[:, at]
        chunk = qkv_cols // 2
        for start in range(0, qkv_cols, chunk):
            store_terms(p, block, start, transposed(left, qkv_grad[:, start : start + chunk]))
        store_terms(p, block, qkv_cols, jnp.broadcast_to(loss_terms, (members * share, LANES)))

    stages, last = reduce_plan(lines, prepare, p, final, *reducing)

    def grad_rows(at):
        values = tokens[at, :].astype(jnp.float32)
        scale = rms_scale(values)
        unit = values * scale
        scaled = normed_grad[at, :] * gains[0:1, :]
        input_grad[at, :] = hidden_grad[at, :] + scale * (
            scaled - unit * jnp.mean(scaled * unit, -1, keepdims=True)
        )

    block = rows // lines
    for index, stage in enumerate(stages):
        if index == 2:
            for k in range(1, members):
                out(0, k).start()
            load.wait()
        if 2 <= index < lines:
            line_hop(index - 1)
        if index == 2 + lines:
            line_last(keep_up, share)
            for k in range(1, members):
                out(1, k).start()
        stage()
        if 2 <= index < 2 + lines:
            at = slice((index - 2) * block, (index - 1) * block)
            normed_grad[at, :] = against(qkv_grad[at, :], w[...])
        if index == 2 + lines:
            by_rows(rows, grad_rows)
    up_came[me] = up_sums[me]
    gate_own.wait()
    for kind in range(2):
        for k in range(1, members):
            out(kind, k).wait_recv()
    units = gate_came.shape[2] // lines
    for i in range(members):
        for zz in range(lines):
            to = slice((zz * members + i) * units, (zz * members + i + 1) * units)
            of = slice(zz * units, (zz + 1) * units)
            gate_final[:, to] = gate_came[i, :, of].astype(jnp.float32)
            up_final[:, to] = up_came[i, :, of].astype(jnp.float32)
    last()

    def tile(head, number):
        start = (head * HEAD_TILES + number) * LANES
        return final[:, start : start + LANES]

    def put(ref, group, heads):
        for number, value in enumerate(side_by_side(heads)):
            start = (group * HEAD_TILES + number) * LANES
            ref[:, start : start + LANES] = value

    for pair in range(KV // 2):
        put(query_final, pair, [tile(2 * pair + i, j) for i in range(2) for j in range(2)])
    for group in range(KV // 4):
        heads = [4 * group + i for i in range(4)]
        put(key_final, group, [tile(head, 2) for head in heads])
        parts = []
        for head in heads:
            thirds = [pltpu.roll(tile(head, number), 32 * (number + 1), 1) for number in range(HEAD_TILES)]
            in_tile = lanes_of(thirds[0])
            parts.append(jnp.where(in_tile < 32, thirds[0], jnp.where(in_tile < 64, thirds[1], thirds[2])))
        put(value_final, group, parts)

    load_own.wait()
    own_gains = own_rows[:, qkv_cols:].astype(jnp.float32)

    def product(grads, weights_of, width_of):
        sums = jnp.zeros((share, 1), jnp.float32)
        for start in range(0, width_of, 4 * LANES):
            at = slice(start, start + 4 * LANES)
            sums += jnp.sum(grads[:, at] * weights_of[:, at].astype(jnp.float32), -1, keepdims=True)
        return sums

    units_all = w_gate.shape[1]
    first_gain = product(final, own_rows, qkv_cols) / own_gains[:, 0:1]
    second_gain = product(gate_final, w_gate, units_all) + product(up_final, w_up, units_all)
    second_gain = second_gain / own_gains[:, 1:2]
    columns = lax.broadcasted_iota(jnp.int32, (share, LANES), 1)
    both_gains = jnp.where(columns == 0, first_gain, jnp.where(columns == 1, second_gain, 0.0))
    both_gains = jnp.concatenate([both_gains, jnp.zeros((LANES - share, LANES), jnp.float32)], 0)
    gain_final[...] = jnp.transpose(both_gains)[:8, :]
    tail = final[:, qkv_cols:]
    of_loss = lax.broadcasted_iota(jnp.int32, (1, LANES), 1) < 3 * devices
    loss[...] = jnp.sum(jnp.where(of_loss, tail[:1, :], 0.0), -1, keepdims=True) * (0.5 * norm[...])
    for kind in range(2):
        for k in range(1, members):
            out(kind, k).wait_send()


def finish(
    lines, weights, normed, qkv_grad, hidden_grad, tokens, gains, square, norm, w_gate, w_up, gate_sums, up_parts, identity
):
    rows, width = tokens.shape
    qkv_cols = qkv_grad.shape[1]
    share = weights.shape[0] // (lines * PLANE)
    columns = weights.shape[1]
    units_all = w_gate.shape[1]
    low = tokens.dtype
    vmem, anywhere = pl.BlockSpec(memory_space=pltpu.VMEM), pl.BlockSpec(memory_space=pl.ANY)
    dma = pltpu.SemaphoreType.DMA
    shapes = [
        (rows, width),
        (share, width),
        (share, KV * HD),
        (share, KV * HD),
        (share, units_all),
        (share, units_all),
        (8, LANES),
        (1, 1),
    ]
    return pl.pallas_call(
        finish_kernel,
        out_shape=[jax.ShapeDtypeStruct(shape, jnp.float32) for shape in shapes],
        in_specs=[anywhere] + [vmem] * 9 + [anywhere, vmem],
        out_specs=[vmem] * len(shapes),
        scratch_shapes=[
            pltpu.VMEM((width, qkv_cols), low),
            pltpu.VMEM((share, columns), low),
            pltpu.VMEM((rows, width), jnp.float32),
            pltpu.VMEM((share, columns), jnp.float32),
            pltpu.VMEM(gate_sums.shape, low),
            pltpu.VMEM(gate_sums.shape, low),
            pltpu.VMEM(gate_sums.shape, low),
            pltpu.VMEM(up_parts.shape, low),
            pltpu.VMEM(up_parts.shape, low),
            dma,
            dma,
            dma((PLANE,)),
            dma((PLANE,)),
            dma((PLANE,)),
            dma((PLANE,)),
            dma,
            dma((2, lines)),
            dma((2, lines)),
            *reduce_scratch(lines, share, columns, low),
        ],
        compiler_params=pltpu.CompilerParams(collective_id=identity, vmem_limit_bytes=VMEM_LIMIT),
        name="finish",
    )(weights, normed, qkv_grad, hidden_grad, tokens, gains, square, norm, w_gate, w_up, gate_sums, up_parts)


def emit_kernel(*refs):
    count = len(refs) // 2
    copies = [pltpu.make_async_copy(refs[i], refs[count + i], refs[-1].at[i]) for i in range(count)]
    for copy in copies:
        copy.start()
    for copy in copies:
        copy.wait()


def emit(arrays):
    anywhere = pl.BlockSpec(memory_space=pl.ANY)
    return pl.pallas_call(
        emit_kernel,
        out_shape=[jax.ShapeDtypeStruct(array.shape, array.dtype) for array in arrays],
        in_specs=[anywhere] * len(arrays),
        out_specs=[pl.BlockSpec(memory_space=pltpu.VMEM)] * len(arrays),
        scratch_shapes=[pltpu.SemaphoreType.DMA((len(arrays),))],
        compiler_params=pltpu.CompilerParams(vmem_limit_bytes=VMEM_LIMIT),
        name="emit",
    )(*arrays)


def plane_per_device(lines, *arrays):
    (
        tokens,
        lengths,
        deal,
        loss_mask,
        teacher,
        out_grad,
        attn_gain,
        w_query,
        w_key,
        w_value,
        w_out,
        ffn_gain,
        w_gate,
        w_up,
        w_down,
    ) = arrays
    devices = lines * PLANE
    width = tokens.shape[2]
    weight_rows = w_query.shape[0]
    scale = HD ** (-0.5)
    gain_rows = jnp.zeros((8, LANES), jnp.float32)
    gain_rows = gain_rows.at[0, :weight_rows].set(attn_gain.astype(jnp.float32))
    gain_rows = gain_rows.at[1, :weight_rows].set(ffn_gain.astype(jnp.float32))
    freq = rope_base ** (-(np.arange(HD // 2) * 2.0 / HD))
    freq = np.concatenate([freq, freq, np.zeros(LANES - HD)])[None].astype(np.float32)

    attended_low, normed_low, gains, cosine, sine, valid, attn_all, out_w, gate_up_w, qkv, probs = attend(
        scale,
        lines,
        w_query,
        w_key,
        w_value,
        w_gate,
        w_up,
        w_out,
        gain_rows,
        freq,
        loss_mask,
        deal,
        lengths,
        tokens[0],
        3,
    )
    attn_all = attn_all.reshape(devices * weight_rows, -1)
    gate_up_w = gate_up_w.reshape(devices * weight_rows, -1)

    result, square, norm, hidden_grad, branch_low, attended_grad, down_final, gate_grad, up_grad = feed_forward(
        lines,
        out_w.reshape(width, width),
        attended_low,
        tokens[0],
        teacher[0],
        out_grad[0],
        valid,
        gains,
        gate_up_w,
        w_down,
        5,
    )
    gate_grad, up_grad = [grad.reshape(lines, PLANE * weight_rows, -1) for grad in (gate_grad, up_grad)]
    qkv_grad, out_final, gate_sums = attend_back(
        scale, lines, attended_grad, qkv, probs, (cosine, sine), attended_low, branch_low, gate_grad, 9
    )

    input_grad, query_final, key_final, value_final, gate_final, up_final, gain_final, loss = finish(
        lines,
        attn_all,
        normed_low,
        qkv_grad,
        hidden_grad,
        tokens[0],
        gains,
        square,
        norm,
        w_gate,
        w_up,
        gate_sums,
        up_grad,
        11,
    )
    result, input_grad, query_final, key_final, value_final, out_final, gate_final, up_final, down_final = emit(
        (result, input_grad, query_final, key_final, value_final, out_final, gate_final, up_final, down_final)
    )
    return (
        result[None],
        loss.reshape(()),
        input_grad[None],
        gain_final[0, :weight_rows],
        query_final,
        key_final,
        value_final,
        out_final,
        gain_final[1, :weight_rows],
        gate_final,
        up_final,
        down_final,
    )


def suits_planes(mesh):
    sizes = dict(mesh.shape)
    return sizes["fsdp"] == 4 and sizes["ctx"] == KV


def solution(mesh):
    placed = (
        P("fsdp", "ctx", None),
        P("fsdp", None),
        P("fsdp", None),
        P("fsdp", "ctx"),
        P("fsdp", "ctx", None),
        P("fsdp", "ctx", None),
        P(("ctx", "fsdp")),
        P(("ctx", "fsdp"), None),
        P(("ctx", "fsdp"), None),
        P(("ctx", "fsdp"), None),
        P(("ctx", "fsdp"), None),
        P(("ctx", "fsdp")),
        P(("ctx", "fsdp"), None),
        P(("ctx", "fsdp"), None),
        P(("ctx", "fsdp"), None),
    )
    if suits_planes(mesh):
        per_device = functools.partial(plane_per_device, mesh.shape["ctx"] // ROWS_Y)
    else:
        per_device = ring_per_device
    return jax.shard_map(
        per_device,
        mesh=mesh,
        in_specs=placed,
        out_specs=(
            P("fsdp", "ctx", None),
            P(),
            P("fsdp", "ctx", None),
            P(("ctx", "fsdp")),
            P(("ctx", "fsdp"), None),
            P(("ctx", "fsdp"), None),
            P(("ctx", "fsdp"), None),
            P(("ctx", "fsdp"), None),
            P(("ctx", "fsdp")),
            P(("ctx", "fsdp"), None),
            P(("ctx", "fsdp"), None),
            P(("ctx", "fsdp"), None),
        ),
        check_vma=False,
    )
```

```python
import functools

import jax
import jax.numpy as jnp
import numpy as np
from jax import lax
from jax.experimental import pallas as pl
from jax.experimental.pallas import tpu as pltpu
from jax.sharding import PartitionSpec as P

HEADS = 16
KV = 8
HD = 96
NSEQ = 6


rope_base = 100000.0
epsilon = 1e-05
masked_score = -1e30


def shifted(value, axis, by):
    size = lax.axis_size(axis)
    return lax.ppermute(value, axis, [(i, (i + by) % size) for i in range(size)])


def rms_scale(values):
    return lax.rsqrt(jnp.mean(values * values, -1, keepdims=True) + epsilon)


def rotary_tables(inseq):
    freq = rope_base ** (-(jnp.arange(HD // 2, dtype=jnp.float32) * 2.0 / HD))
    angle = inseq.astype(jnp.float32)[:, None] * freq[None, :]
    return (jnp.cos(angle)[:, None, :], jnp.sin(angle)[:, None, :])


def rotary(values, cosine, sine):
    half = values.shape[-1] // 2
    first = values[..., :half]
    second = values[..., half:]
    return jnp.concatenate([first * cosine - second * sine, second * cosine + first * sine], -1)


def rotary_back(grads, cosine, sine):
    half = grads.shape[-1] // 2
    first = grads[..., :half]
    second = grads[..., half:]
    return jnp.concatenate([first * cosine + second * sine, second * cosine - first * sine], -1)


def transposed(left, right):
    return lax.dot_general(
        left, right, (((0,), (0,)), ((), ())), preferred_element_type=jnp.float32
    )


def against(left, right):
    return lax.dot_general(
        left, right, (((1,), (1,)), ((), ())), preferred_element_type=jnp.float32
    )


def permitted(query_place, query_seg, key_place, key_seg):
    same = (query_seg[:, None] == key_seg[None, :]) & (query_seg[:, None] < NSEQ)
    return same & (key_place[None, :] <= query_place[:, None]) | (
        key_place[None, :] == query_place[:, None]
    )


def ring_per_device(
    tokens,
    lengths,
    deal,
    loss_mask,
    teacher,
    out_grad,
    attn_gain,
    w_query,
    w_key,
    w_value,
    w_out,
    ffn_gain,
    w_gate,
    w_up,
    w_down,
):
    count_ctx = lax.axis_size("ctx")
    myself = lax.axis_index("ctx")
    tok_rows = tokens.shape[1]
    width = tokens.shape[2]
    half_block = tok_rows // 2
    groups = HEADS // KV
    scale = HD ** (-0.5)
    gain_one, query_w, key_w, value_w, out_w = (
        lax.all_gather(attn_gain, ("ctx", "fsdp"), axis=0, tiled=True),
        lax.all_gather(w_query, ("ctx", "fsdp"), axis=0, tiled=True),
        lax.all_gather(w_key, ("ctx", "fsdp"), axis=0, tiled=True),
        lax.all_gather(w_value, ("ctx", "fsdp"), axis=0, tiled=True),
        lax.all_gather(w_out, ("ctx", "fsdp"), axis=0, tiled=True),
    )
    gain_two, gate_w, up_w, down_w = (
        lax.all_gather(ffn_gain, ("ctx", "fsdp"), axis=0, tiled=True),
        lax.all_gather(w_gate, ("ctx", "fsdp"), axis=0, tiled=True),
        lax.all_gather(w_up, ("ctx", "fsdp"), axis=0, tiled=True),
        lax.all_gather(w_down, ("ctx", "fsdp"), axis=0, tiled=True),
    )
    dealt = jnp.arange(count_ctx * tok_rows, dtype=jnp.int32)
    local = dealt % tok_rows
    first = jnp.repeat(deal[0], tok_rows)
    block = jnp.where(local < half_block, first, 2 * count_ctx - 1 - first)
    places = block * half_block + local % half_block
    ends = jnp.cumsum(lengths[0])
    after = (places[:, None] >= ends[None, :]).astype(jnp.int32)
    seg_all = jnp.sum(after, 1)
    inseq_all = places - jnp.sum(after * lengths[0][None, :], 1)
    own_place = lax.dynamic_slice_in_dim(places, myself * tok_rows, tok_rows)
    own_seg = lax.dynamic_slice_in_dim(seg_all, myself * tok_rows, tok_rows)
    own_inseq = lax.dynamic_slice_in_dim(inseq_all, myself * tok_rows, tok_rows)
    cosine, sine = rotary_tables(own_inseq)
    inputs = tokens[0].astype(jnp.float32)
    scale_one = rms_scale(inputs)
    normed_one = inputs * scale_one
    gain_first = gain_one.astype(jnp.float32)
    normed_low = (normed_one * gain_first).astype(jnp.bfloat16)
    query_pre = jnp.dot(normed_low, query_w, preferred_element_type=jnp.float32).reshape(
        tok_rows, HEADS, HD
    )
    key_pre = jnp.dot(normed_low, key_w, preferred_element_type=jnp.float32).reshape(
        tok_rows, KV, HD
    )
    value_low = jnp.dot(normed_low, value_w, preferred_element_type=jnp.float32).astype(
        jnp.bfloat16
    )
    queries = rotary(query_pre, cosine, sine).astype(jnp.bfloat16).reshape(tok_rows, KV, groups, HD)
    keys = rotary(key_pre, cosine, sine).astype(jnp.bfloat16).reshape(tok_rows, KV * HD)

    def logits(key_block):
        return (
            jnp.einsum(
                "qcgd,kcd->cgqk",
                queries,
                key_block.reshape(-1, KV, HD),
                preferred_element_type=jnp.float32,
            )
            * scale
        )

    key_block = lax.all_gather(keys, "ctx", axis=0, tiled=True)
    value_block = lax.all_gather(value_low, "ctx", axis=0, tiled=True)
    allowed = permitted(own_place, own_seg, places, seg_all)
    top = jnp.full((KV, groups, tok_rows, 1), masked_score, jnp.float32)
    score = jnp.where(allowed, logits(key_block), masked_score)
    new_top = jnp.maximum(top, jnp.max(score, -1, keepdims=True))
    weight = jnp.where(allowed, jnp.exp(score - new_top), 0.0)
    summed = jnp.einsum(
        "cgqk,kcd->cgqd",
        weight.astype(jnp.bfloat16),
        value_block.reshape(-1, KV, HD),
        preferred_element_type=jnp.float32,
    )
    summed, top, total = (summed, new_top, jnp.sum(weight, -1, keepdims=True))
    attended = summed / total
    log_total = top + jnp.log(total)
    attended_low = (
        jnp.transpose(attended, (2, 0, 1, 3)).reshape(tok_rows, HEADS * HD).astype(jnp.bfloat16)
    )
    hidden = inputs + jnp.dot(attended_low, out_w, preferred_element_type=jnp.float32)
    scale_two = rms_scale(hidden)
    normed_two = hidden * scale_two
    gain_second = gain_two.astype(jnp.float32)
    ffn_low = (normed_two * gain_second).astype(jnp.bfloat16)
    gate = jnp.dot(ffn_low, gate_w, preferred_element_type=jnp.float32)
    up = jnp.dot(ffn_low, up_w, preferred_element_type=jnp.float32)
    sigmoid = jax.nn.sigmoid(gate)
    activated = gate * sigmoid
    mixed_low = (activated * up).astype(jnp.bfloat16)
    result = hidden + jnp.dot(mixed_low, down_w, preferred_element_type=jnp.float32)
    target = teacher[0].astype(jnp.float32)
    valid = (loss_mask[0] * (own_seg < NSEQ)).astype(jnp.float32)[:, None]
    differ = result - target
    square_sum, valid_count = lax.psum(
        (jnp.sum(valid * differ * differ), jnp.sum(valid)), ("ctx", "fsdp")
    )
    loss = square_sum / (valid_count * width)
    out_total = out_grad[0].astype(jnp.float32) + 2.0 * valid * differ / (valid_count * width)
    out_low = out_total.astype(jnp.bfloat16)
    down_grad = transposed(mixed_low, out_low)
    mixed_grad = against(out_low, down_w)
    silu_slope = sigmoid * (1.0 + gate * (1.0 - sigmoid))
    gate_low = (mixed_grad * up * silu_slope).astype(jnp.bfloat16)
    up_low = (mixed_grad * activated).astype(jnp.bfloat16)
    gate_grad = transposed(ffn_low, gate_low)
    up_grad = transposed(ffn_low, up_low)
    normed_grad = against(gate_low, gate_w) + against(up_low, up_w)
    gain_two_grad = jnp.sum(normed_grad * normed_two, 0)
    scaled_two = normed_grad * gain_second
    hidden_grad = out_total + scale_two * (
        scaled_two - normed_two * jnp.mean(scaled_two * normed_two, -1, keepdims=True)
    )
    ffn_final = (
        lax.psum_scatter(gain_two_grad, ("ctx", "fsdp"), scatter_dimension=0, tiled=True),
        lax.psum_scatter(gate_grad, ("ctx", "fsdp"), scatter_dimension=0, tiled=True),
        lax.psum_scatter(up_grad, ("ctx", "fsdp"), scatter_dimension=0, tiled=True),
        lax.psum_scatter(down_grad, ("ctx", "fsdp"), scatter_dimension=0, tiled=True),
    )
    branch_low = hidden_grad.astype(jnp.bfloat16)
    out_w_grad = transposed(attended_low, branch_low)
    attended_grad = against(branch_low, out_w).astype(jnp.bfloat16)
    grad_heads = jnp.transpose(attended_grad.reshape(tok_rows, KV, groups, HD), (1, 2, 0, 3))
    delta = jnp.sum(grad_heads.astype(jnp.float32) * attended, -1, keepdims=True)

    def cycle_step(step, state):
        key_block, value_block, key_acc, value_acc, query_acc = state
        source = (myself - step) % count_ctx
        allowed = permitted(
            own_place,
            own_seg,
            lax.dynamic_slice_in_dim(places, source * tok_rows, tok_rows),
            lax.dynamic_slice_in_dim(seg_all, source * tok_rows, tok_rows),
        )
        current_key = key_block
        current_value = value_block
        keys_three = current_key.reshape(tok_rows, KV, HD)
        values_three = current_value.reshape(tok_rows, KV, HD)
        prob = jnp.where(allowed, jnp.exp(logits(current_key) - log_total), 0.0)
        prob_grad = jnp.einsum(
            "cgqd,kcd->cgqk", grad_heads, values_three, preferred_element_type=jnp.float32
        )
        score_low = (prob * (prob_grad - delta)).astype(jnp.bfloat16)
        query_add = (
            jnp.einsum("cgqk,kcd->cgqd", score_low, keys_three, preferred_element_type=jnp.float32)
            * scale
        )
        key_add = (
            jnp.einsum(
                "cgqk,qcgd->kcd", score_low, queries, preferred_element_type=jnp.float32
            ).reshape(tok_rows, KV * HD)
            * scale
        )
        value_add = jnp.einsum(
            "cgqk,cgqd->kcd",
            prob.astype(jnp.bfloat16),
            grad_heads,
            preferred_element_type=jnp.float32,
        ).reshape(tok_rows, KV * HD)
        key_block, value_block = shifted((key_block, value_block), "ctx", 1)
        key_acc, value_acc = (
            shifted((key_acc + key_add).astype(jnp.bfloat16), "ctx", 1).astype(jnp.float32),
            shifted((value_acc + value_add).astype(jnp.bfloat16), "ctx", 1).astype(jnp.float32),
        )
        return (key_block, value_block, key_acc, value_acc, query_acc + query_add)

    cycle_start = (
        keys,
        value_low,
        jnp.zeros((tok_rows, KV * HD), jnp.float32),
        jnp.zeros((tok_rows, KV * HD), jnp.float32),
        jnp.zeros((KV, groups, tok_rows, HD), jnp.float32),
    )
    cycle_end = lax.fori_loop(0, count_ctx, cycle_step, cycle_start)
    key_acc = cycle_end[2]
    value_acc = cycle_end[3]
    query_acc = cycle_end[4]
    query_grad = jnp.transpose(query_acc, (2, 0, 1, 3)).reshape(tok_rows, HEADS, HD)
    query_low = (
        rotary_back(query_grad, cosine, sine).reshape(tok_rows, HEADS * HD).astype(jnp.bfloat16)
    )
    key_low = (
        rotary_back(key_acc.reshape(tok_rows, KV, HD), cosine, sine)
        .reshape(tok_rows, KV * HD)
        .astype(jnp.bfloat16)
    )
    value_grad_low = value_acc.astype(jnp.bfloat16)
    query_w_grad = transposed(normed_low, query_low)
    key_w_grad = transposed(normed_low, key_low)
    value_w_grad = transposed(normed_low, value_grad_low)
    normed_one_grad = (
        against(query_low, query_w) + against(key_low, key_w) + against(value_grad_low, value_w)
    )
    gain_one_grad = jnp.sum(normed_one_grad * normed_one, 0)
    scaled_one = normed_one_grad * gain_first
    input_grad = hidden_grad + scale_one * (
        scaled_one - normed_one * jnp.mean(scaled_one * normed_one, -1, keepdims=True)
    )
    attn_final = (
        lax.psum_scatter(gain_one_grad, ("ctx", "fsdp"), scatter_dimension=0, tiled=True),
        lax.psum_scatter(query_w_grad, ("ctx", "fsdp"), scatter_dimension=0, tiled=True),
        lax.psum_scatter(key_w_grad, ("ctx", "fsdp"), scatter_dimension=0, tiled=True),
        lax.psum_scatter(value_w_grad, ("ctx", "fsdp"), scatter_dimension=0, tiled=True),
        lax.psum_scatter(out_w_grad, ("ctx", "fsdp"), scatter_dimension=0, tiled=True),
    )
    return (
        result.astype(jnp.bfloat16)[None],
        loss,
        input_grad[None],
        attn_final[0],
        attn_final[1],
        attn_final[2],
        attn_final[3],
        attn_final[4],
        ffn_final[0],
        ffn_final[1],
        ffn_final[2],
        ffn_final[3],
    )


MESH = pl.DeviceIdType.MESH
ROWS_Y = 2
PLANE = 8
LANES = 128
VMEM_LIMIT = 60 * 2**20


def coordinates():
    ctx = lax.axis_index("ctx")
    fsdp = lax.axis_index("fsdp")
    return ctx // 2, ctx % 2, fsdp // 2, fsdp % 2


def device(z, y, x, c):
    return (z * 2 + y, x * 2 + c)


def greet(devices):
    barrier = pltpu.get_barrier_semaphore()
    for other in devices:
        pl.semaphore_signal(barrier, inc=1, device_id=other, device_id_type=MESH)
    pl.semaphore_wait(barrier, len(devices))


def remote(src, dst, send, recv, target):
    return pltpu.make_async_remote_copy(
        src_ref=src,
        dst_ref=dst,
        send_sem=send,
        recv_sem=recv,
        device_id=target,
        device_id_type=MESH,
    )


def line_gather(place, lines, x_ref, slot, send, recv, here=None):
    z, y, x, c = place
    mine = None if here is None else pltpu.make_async_copy(x_ref, slot(z), here)
    ways = ((0, -1, device(z + 1, y, x, c)), (1, 1, device(z - 1, y, x, c)))

    def along(way, sign, to, s):
        zz = z + sign * (s - 1)
        return remote(x_ref if s == 1 else slot(zz), slot(zz), send.at[way, s], recv.at[way, s], to)

    def sends(sign, s):
        if sign < 0:
            return (z - (s - 1) >= 0) & (z + 1 < lines)
        return (z + (s - 1) < lines) & (z - 1 >= 0)

    def present(sign, s):
        return z - s >= 0 if sign < 0 else z + s < lines

    def start(s):
        for way, sign, to in ways:
            pl.when(sends(sign, s))(lambda way=way, sign=sign, to=to: along(way, sign, to, s).start())

    def begin():
        if mine is not None:
            mine.start()
        start(1)

    def pass_on(s):
        for way, sign, to in ways:
            pl.when(present(sign, s))(lambda way=way, sign=sign, to=to: along(way, sign, to, s).wait_recv())
        if s + 1 < lines:
            start(s + 1)

    def last():
        for s in range(1, lines):
            for way, sign, to in ways:
                pl.when(sends(sign, s))(lambda way=way, sign=sign, to=to, s=s: along(way, sign, to, s).wait_send())
        if mine is not None:
            mine.wait()

    return begin, pass_on, last


def line_reduce(place, lines, parts, up, down, send, recv):
    z, y, x, c = place
    ways = ((0, up, device(z + 1, y, x, c)), (1, down, device(z - 1, y, x, c)))

    def copy(way, t, own):
        _, sums, to = ways[way]
        src = parts.at[t] if own else sums.at[t]
        return remote(src, sums.at[t], send.at[way, t], recv.at[way, t], to)

    def begin():
        @pl.when(z == 0)
        def _():
            for t in range(lines - 1, 0, -1):
                copy(0, t, True).start()

        @pl.when(z == lines - 1)
        def _():
            for t in range(lines - 1):
                copy(1, t, True).start()

    def add_on(way, t):
        copy(way, t, False).wait_recv()
        add_rows(ways[way][1].at[t], parts.at[t])
        copy(way, t, False).start()

    def hop(moment):
        for t in range(lines):
            for zz in range(1, lines - 1):
                if zz < t and zz + (lines - 1 - t) == moment:
                    pl.when(z == zz)(functools.partial(add_on, 0, t))
                if zz > t and (lines - 1 - zz) + t == moment:
                    pl.when(z == zz)(functools.partial(add_on, 1, t))

    def last(write, step=32):
        for way, first in ((0, 0), (1, lines - 1)):

            @pl.when(z != first)
            def _():
                copy(way, z, False).wait_recv()

        def body(i, carry):
            at = pl.ds(pl.multiple_of(i * step, step), step)
            from_below = jnp.where(z > 0, up[z, at, :].astype(jnp.float32), 0.0)
            from_above = jnp.where(z < lines - 1, down[z, at, :].astype(jnp.float32), 0.0)
            write(i, parts[z, at, :].astype(jnp.float32) + from_below + from_above)
            return carry

        lax.fori_loop(0, parts.shape[1] // step, body, 0)
        for zz in range(lines):

            @pl.when(z == zz)
            def _():
                for t in range(lines):
                    if t > zz:
                        copy(0, t, zz == 0).wait_send()
                    if t < zz:
                        copy(1, t, zz == lines - 1).wait_send()

    return begin, hop, last


def column_cut(width):
    tiles = width // LANES
    return (tiles + 1) // 2 * LANES


def line_of(z, y, x, c, lines):
    return [device(lax.rem(z + k, lines), y, x, c) for k in range(1, lines)]


def reduce_plan(lines, prepare, p_ref, o_ref, held, corner_a, corner_b, from_side, from_over, along, send, recv):
    z, y, x, c = coordinates()
    parts = lines
    rows, width = held.shape[2], held.shape[3]
    cut = column_cut(width)
    first, second = pl.ds(0, cut), pl.ds(cut, width - cut)
    side, over, sibling = device(z, y, 1 - x, c), device(z, 1 - y, x, c), device(z, y, x, 1 - c)
    def given(part, yy, xx, cc):
        member = yy * 4 + xx * 2 + cc
        return p_ref.at[lax.rem(z + part + 1, lines), member]

    def make(part, kind, src, dst, to):
        return remote(src, dst, send.at[part, kind], recv.at[part, kind], to)

    lane = lambda part, yy, xx: held.at[part, yy * 2 + xx]

    def over_core(part):
        return [
            make(part, yy * 2 + xx, given(part, yy, xx, 1 - c), lane(part, yy, xx), sibling)
            for yy in range(2)
            for xx in range(2)
        ]

    def to_corner(part):
        return (
            make(part, 4, lane(part, 1 - y, 1 - x).at[:, first], corner_a.at[part], over),
            make(part, 5, lane(part, 1 - y, 1 - x).at[:, second], corner_b.at[part], side),
        )

    def to_neighbour(part, way):
        columns = (first, second)[way % 2]
        if way < 2:
            return make(part, 6 + way, lane(part, y, 1 - x).at[:, columns], from_side.at[part, :, columns], side)
        return make(part, 6 + way, lane(part, 1 - y, x).at[:, columns], from_over.at[part, :, columns], over)

    def along_z(part):
        to = lax.rem(z + part + 1, lines)
        return make(part, 10, lane(part, y, x), along.at[part], device(to, y, x, c))

    step = 16

    def add_core(part):
        for copy in over_core(part):
            copy.wait_recv()
        for yy, xx in ((1 - y, 1 - x), (y, 1 - x), (1 - y, x), (y, x)):
            mine, other = given(part, yy, xx, c), lane(part, yy, xx)

            def body(i, carry):
                at = pl.ds(pl.multiple_of(i * step, step), step)
                total = mine[at, :].astype(jnp.float32) + other[at, :].astype(jnp.float32)
                other[at, :] = total.astype(other.dtype)
                return carry

            lax.fori_loop(0, rows // step, body, 0)
        for copy in to_corner(part):
            copy.start()
        to_neighbour(part, 1).start()
        to_neighbour(part, 2).start()

    def add_corner(part):
        copies = to_corner(part)
        pairs = (
            (copies[0], lane(part, y, 1 - x), corner_a.at[part], first),
            (copies[1], lane(part, 1 - y, x), corner_b.at[part], second),
        )
        for copy, mine, other, columns in pairs:
            copy.wait_recv()

            def body(i, carry):
                at = pl.ds(pl.multiple_of(i * step, step), step)
                total = mine[at, columns].astype(jnp.float32) + other[at, :].astype(jnp.float32)
                mine[at, columns] = total.astype(mine.dtype)
                return carry

            lax.fori_loop(0, rows // step, body, 0)
        to_neighbour(part, 0).start()
        to_neighbour(part, 3).start()

    def add_neighbours(part):
        for way in range(4):
            to_neighbour(part, way).wait_recv()
        last = part == parts - 1
        mine = lane(part, y, x)

        def body(i, carry):
            at = pl.ds(pl.multiple_of(i * step, step), step)
            total = mine[at, :].astype(jnp.float32) + from_side[part, at, :].astype(jnp.float32)
            total += from_over[part, at, :].astype(jnp.float32)
            if last:
                o_ref[at, :] = total
            else:
                mine[at, :] = total.astype(mine.dtype)
            return carry

        lax.fori_loop(0, rows // step, body, 0)
        if not last:
            along_z(part).start()

    def ready(part):
        prepare(lax.rem(z + part + 1, lines))
        for copy in over_core(part):
            copy.start()

    kinds = (ready, add_core, add_corner, add_neighbours)

    def run(number):
        for lag, kind in enumerate(kinds):
            if 0 <= number - lag < parts:
                kind(number - lag)

    def last():
        for part in range(parts - 1):
            along_z(part).wait_recv()

        def body(i, carry):
            at = pl.ds(pl.multiple_of(i * step, step), step)
            total = o_ref[at, :]
            for part in range(parts - 1):
                total += along[part, at, :].astype(jnp.float32)
            o_ref[at, :] = total
            return carry

        lax.fori_loop(0, rows // step, body, 0)
        for part in range(parts - 1):
            along_z(part).wait_send()
        for part in range(parts):
            for copy in (*over_core(part), *to_corner(part), *(to_neighbour(part, way) for way in range(4))):
                copy.wait_send()

    return [functools.partial(run, number) for number in range(parts + len(kinds) - 1)], last


def reduce_scratch(lines, share, columns, low):
    cut = column_cut(columns)
    return [
        pltpu.VMEM((lines, PLANE, share, columns), low),
        pltpu.VMEM((lines, 4, share, columns), low),
        pltpu.VMEM((lines, share, cut), low),
        pltpu.VMEM((lines, share, columns - cut), low),
        pltpu.VMEM((lines, share, columns), low),
        pltpu.VMEM((lines, share, columns), low),
        pltpu.VMEM((lines - 1, share, columns), low),
        pltpu.SemaphoreType.DMA((lines, 11)),
        pltpu.SemaphoreType.DMA((lines, 11)),
    ]


def store_terms(p, block, start, value):
    members, share = p.shape[1:3]
    width = value.shape[1]
    p[block, :, :, start : start + width] = value.astype(p.dtype).reshape(members, share, width)


def halves(width):
    cut = column_cut(width)
    return pl.ds(0, cut), pl.ds(cut, width - cut)


class PlaneGather:
    def __init__(self, place, at, width, send, recv):
        z, y, x, c = place
        side, over, sibling = device(z, y, 1 - x, c), device(z, 1 - y, x, c), device(z, y, x, 1 - c)
        self.send, self.recv = send, recv
        own, next_x, next_y, corner = at(y, x), at(y, 1 - x), at(1 - y, x), at(1 - y, 1 - x)
        first, second = [lambda ref, of=of: ref.at[..., of] for of in halves(width)]
        self.table = (
            (first(own), side),
            (second(own), side),
            (first(own), over),
            (second(own), over),
            (own, sibling),
            (first(next_x), over),
            (second(next_y), side),
            (first(next_x), sibling),
            (second(next_x), sibling),
            (first(next_y), sibling),
            (second(next_y), sibling),
            (first(corner), sibling),
            (second(corner), sibling),
        )

    def copy(self, kind):
        ref, to = self.table[kind]
        return remote(ref, ref, self.send.at[kind], self.recv.at[kind], to)

    def begin(self):
        for kind in (0, 3, 4, 1, 2):
            self.copy(kind).start()

    def came(self, *kinds):
        for kind in kinds:
            self.copy(kind).wait_recv()

    def forward_on(self):
        for kind, onward in ((0, (5, 7)), (3, (6, 10)), (1, (8,)), (2, (9,))):
            self.came(kind)
            for other in onward:
                self.copy(other).start()

    def corner_on(self):
        for kind, onward in ((5, 11), (6, 12)):
            self.came(kind)
            self.copy(onward).start()

    def rest(self):
        self.came(4, *range(7, GATHER_KINDS))

    def drain(self):
        for kind in range(GATHER_KINDS):
            self.copy(kind).wait_send()


GATHER_KINDS = 13
REDUCE_KINDS = 10


def reduce_steps(place, at_rows, partial, held, corner_a, corner_b, from_side, from_over, send, recv):
    z, y, x, c = place
    side, over, sibling = device(z, y, 1 - x, c), device(z, 1 - y, x, c), device(z, y, x, 1 - c)
    first, second = halves(held.shape[-1])
    lane = lambda yy, xx: held.at[yy * 2 + xx, at_rows]
    next_x, next_y, corner = lane(y, 1 - x), lane(1 - y, x), lane(1 - y, 1 - x)

    def to_core(yy, xx):
        kind = yy * 2 + xx
        src = partial.at[yy * 4 + xx * 2 + 1 - c, at_rows]
        return remote(src, lane(yy, xx), send.at[kind], recv.at[kind], sibling)

    table = (
        (corner.at[:, first], corner_a.at[at_rows], over),
        (corner.at[:, second], corner_b.at[at_rows], side),
        (next_x.at[:, first], from_side.at[at_rows, first], side),
        (next_x.at[:, second], from_side.at[at_rows, second], side),
        (next_y.at[:, first], from_over.at[at_rows, first], over),
        (next_y.at[:, second], from_over.at[at_rows, second], over),
    )

    def copy(kind):
        src, dst, to = table[kind]
        return remote(src, dst, send.at[4 + kind], recv.at[4 + kind], to)

    return to_core, copy


def add_rows(target, other, columns=None, step=32):
    def body(i, carry):
        at = pl.ds(pl.multiple_of(i * step, step), step)
        mine = target[at, :] if columns is None else target[at, columns]
        total = (mine.astype(jnp.float32) + other[at, :].astype(jnp.float32)).astype(target.dtype)
        if columns is None:
            target[at, :] = total
        else:
            target[at, columns] = total
        return carry

    lax.fori_loop(0, other.shape[0] // step, body, 0)


def feed_forward_kernel(
    out_rows, attended, tokens, teacher_rows, out_grad_rows, valid, gains, gate_up_rows, down_rows,
    result, square, norm, hidden_grad, branch, attended_grad, down_final, gate_grad, up_grad,
    out_w, gate_up_w, teacher, out_grad, down_w, down_up, down_down, normed_all, kept, mixed, grads_all, partial, held, corner_a, corner_b, from_side, from_over, hidden, total_grad, scales, squares,
    load_sem, here, line_send, line_recv, down_send, down_recv, gather_send, gather_recv, reduce_send, reduce_recv,
):
    place = coordinates()
    z, y, x, c = place
    width = tokens.shape[1]
    pairs = ((out_rows, out_w), (gate_up_rows, gate_up_w), (teacher_rows, teacher), (out_grad_rows, out_grad))
    loads = [pltpu.make_async_copy(src, dst, load_sem.at[i]) for i, (src, dst) in enumerate(pairs)]
    for load in loads:
        load.start()
    lines, units = down_w.shape[:2]
    greet([device(z, y, 1 - x, c), device(z, 1 - y, x, c), device(z, y, x, 1 - c)] + line_of(z, y, x, c, lines))
    rows = tokens.shape[0]
    share = lines * units
    line_begin, line_pass, line_last = line_gather(
        place, lines, down_rows, lambda zz: down_w.at[zz], line_send, line_recv, here
    )
    line_begin()
    first, second = halves(width)
    mine = y * 4 + x * 2 + c
    chips = ((y, x), (y, 1 - x), (1 - y, x), (1 - y, 1 - x))

    gain = gains[1:2, :]
    count = jnp.sum(gains[2:3, :], -1, keepdims=True) / (width // (lines * PLANE))
    norm[...] = 2.0 / (count * width)
    loads[0].wait()
    hidden[...] = tokens[...].astype(jnp.float32) + jnp.dot(
        attended[...], out_w[...], preferred_element_type=jnp.float32
    )

    def norm_rows(at):
        values = hidden[at, :]
        scale = rms_scale(values)
        scales[at, :] = scale
        normed_all[mine, at, :] = (values * scale * gain[...]).astype(normed_all.dtype)

    parts = 2
    part_rows = rows // parts
    at_part = [pl.ds(part * part_rows, part_rows) for part in range(parts)]

    def of_part(part, body):
        by_rows(part_rows, lambda at: body(pl.ds(pl.multiple_of(part * part_rows + at.start, ROW_STEP), ROW_STEP)))

    class Phase(PlaneGather):
        def __init__(self, phase, part, whole):
            at_rows = at_part[part]
            self.part, self.at_rows = part, at_rows
            at = lambda yy, xx: whole.at[yy * 4 + xx * 2 + c, at_rows]
            super().__init__(place, at, width, gather_send.at[phase, part], gather_recv.at[phase, part])
            self.to_core, self.pass_on = reduce_steps(
                place, at_rows, partial, held, corner_a, corner_b, from_side, from_over,
                reduce_send.at[phase, part], reduce_recv.at[phase, part],
            )

        def join(self, yy, xx):
            self.to_core(yy, xx).wait_recv()
            add_rows(held.at[yy * 2 + xx, self.at_rows], partial.at[yy * 4 + xx * 2 + c, self.at_rows])

        def join_next(self, number):
            self.join(*chips[number])
            self.pass_on(2 + number).start()

        def join_corner(self):
            self.join(*chips[3])
            self.pass_on(0).start()
            self.pass_on(1).start()

        def add_corner(self):
            self.pass_on(0).wait_recv()
            add_rows(held.at[y * 2 + 1 - x, self.at_rows], corner_a.at[self.at_rows], first)
            self.pass_on(2).start()
            self.pass_on(1).wait_recv()
            add_rows(held.at[(1 - y) * 2 + x, self.at_rows], corner_b.at[self.at_rows], second)
            self.pass_on(5).start()

        def complete(self):
            for kind in (2, 3, 4, 5):
                self.pass_on(kind).wait_recv()
            for kind in range(6):
                self.pass_on(kind).wait_send()
            for yy, xx in chips:
                self.to_core(yy, xx).wait_send()

    def pair_of(number):
        yy, xx = chips[number]
        return pl.ds(yy * 4 + xx * 2, 2)

    one, two = [Phase(0, part, normed_all) for part in range(parts)]
    of_part(0, norm_rows)
    one.begin()
    of_part(1, norm_rows)

    def summed(at):
        total = held[y * 2 + x, at, :].astype(jnp.float32) + from_side[at, :].astype(jnp.float32)
        return total + from_over[at, :].astype(jnp.float32)

    def units_of(phase, number):
        where = (pair_of(number), phase.at_rows)
        both = jnp.dot(
            normed_all[where].reshape(rows, width), gate_up_w[...], preferred_element_type=jnp.float32
        )
        gate, up = both[:, :share], both[:, share:]
        sigmoid = 1.0 / (1.0 + jnp.exp(-gate))
        activated = gate * sigmoid
        slope = up * (sigmoid + activated * (1.0 - sigmoid))
        kept[(*where, slice(0, share))] = slope.astype(kept.dtype).reshape(2, part_rows, share)
        kept[(*where, slice(share, 2 * share))] = activated.astype(kept.dtype).reshape(2, part_rows, share)
        mixed[where] = (activated * up).astype(mixed.dtype).reshape(2, part_rows, share)

    def down_of(phase, number):
        where = (pair_of(number), phase.at_rows)
        out = jnp.dot(
            mixed[where].reshape(rows, share),
            down_w[...].reshape(share, width),
            preferred_element_type=jnp.float32,
        )
        partial[where] = out.astype(partial.dtype).reshape(2, part_rows, width)
        phase.to_core(*chips[number]).start()

    one.came(4)
    loads[1].wait()
    units_of(one, 0)
    line_pass(1)
    one.forward_on()
    two.begin()
    one.came(7, 8)
    units_of(one, 1)
    one.came(9, 10)
    units_of(one, 2)
    one.corner_on()
    for moment in range(2, lines - 1):
        line_pass(moment)
    two.came(4)
    units_of(two, 0)
    two.forward_on()
    one.came(11, 12)
    units_of(one, 3)
    two.came(7, 8)
    units_of(two, 1)
    two.came(9, 10)
    units_of(two, 2)
    two.corner_on()
    line_pass(lines - 1)
    line_last()
    down_of(one, 1)
    down_of(one, 2)
    one.join_next(1)
    down_of(one, 3)
    one.join_next(2)
    two.came(11, 12)
    units_of(two, 3)
    one.join_corner()
    down_of(two, 1)
    down_of(two, 2)
    two.join_next(1)
    down_of(one, 0)
    down_of(two, 3)
    two.join_next(2)
    one.join(*chips[0])
    one.add_corner()
    two.join_corner()
    down_of(two, 0)
    two.join(*chips[0])
    one.complete()
    loads[2].wait()
    loads[3].wait()

    def result_rows(at):
        values = hidden[at, :] + summed(at)
        result[at, :] = values.astype(result.dtype)
        differ = values - teacher[at, :].astype(jnp.float32)
        weighed = valid[at, :] * differ
        squares[at, :] = jnp.sum(weighed * differ, -1, keepdims=True)
        total = out_grad[at, :].astype(jnp.float32) + weighed * norm[...]
        total_grad[at, :] = total
        grads_all[mine, at, :] = total.astype(grads_all.dtype)

    def back_of(phase, number):
        where = (pair_of(number), phase.at_rows)
        mixed_grad = against(grads_all[where].reshape(rows, width), down_w[...].reshape(share, width))
        slope = kept[(*where, slice(0, share))].reshape(rows, share).astype(jnp.float32)
        activated = kept[(*where, slice(share, 2 * share))].reshape(rows, share).astype(jnp.float32)
        low_gate = (mixed_grad * slope).astype(kept.dtype)
        low_up = (mixed_grad * activated).astype(kept.dtype)
        kept[(*where, slice(0, share))] = low_gate.reshape(2, part_rows, share)
        kept[(*where, slice(share, 2 * share))] = low_up.reshape(2, part_rows, share)
        out = against(low_gate, gate_up_w[:, :share]) + against(low_up, gate_up_w[:, share:])
        partial[where] = out.astype(partial.dtype).reshape(2, part_rows, width)
        phase.to_core(*chips[number]).start()

    three, four = [Phase(1, part, grads_all) for part in range(parts)]
    of_part(0, result_rows)
    three.begin()
    two.add_corner()
    three.came(4)
    back_of(three, 0)
    two.complete()
    of_part(1, result_rows)
    square[...] = jnp.sum(squares[...], 0, keepdims=True)
    three.forward_on()
    four.begin()
    three.came(7, 8)
    back_of(three, 1)
    three.came(9, 10)
    back_of(three, 2)
    three.join_next(1)
    four.came(4)
    back_of(four, 0)
    three.corner_on()
    three.join_next(2)
    three.came(11, 12)
    back_of(three, 3)
    four.forward_on()
    three.join_corner()
    four.came(7, 8)
    back_of(four, 1)
    three.join(*chips[0])
    four.came(9, 10)
    back_of(four, 2)
    four.join_next(1)
    four.corner_on()
    four.join_next(2)
    three.add_corner()
    four.came(11, 12)
    back_of(four, 3)
    four.join(*chips[0])
    four.join_corner()
    tokens_all = normed_all.shape[0] * rows
    block = 256

    def down_block(i, carry):
        at = pl.ds(pl.multiple_of(i * block, block), block)
        left = mixed[:, :, at].reshape(tokens_all, block)
        grads = transposed(left, grads_all[...].reshape(tokens_all, width)).astype(down_w.dtype)
        per = block // units
        down_w[pl.ds(i * per, per)] = grads.reshape(per, units, width)
        return carry

    def both_block(i, carry):
        at = pl.ds(pl.multiple_of(i * block, block), block)
        left = normed_all[:, :, at].reshape(tokens_all, block)
        both = transposed(left, kept[...].reshape(tokens_all, 2 * share)).astype(gate_grad.dtype)
        gate_grad[at, :] = both[:, :share]
        up_grad[at, :] = both[:, share:]
        return carry

    lax.fori_loop(0, share // block, down_block, 0)
    down_begin, down_hop, down_last = line_reduce(place, lines, down_w, down_up, down_down, down_send, down_recv)
    down_begin()
    blocks = width // block
    lax.fori_loop(0, blocks // 3, both_block, 0)
    three.complete()
    four.add_corner()
    down_hop(1)
    lax.fori_loop(blocks // 3, blocks, both_block, 0)
    def grad_rows(at):
        grads = summed(at)
        normed = hidden[at, :] * scales[at, :]
        scaled = grads * gain[...]
        values = total_grad[at, :] + scales[at, :] * (scaled - normed * jnp.mean(scaled * normed, -1, keepdims=True))
        hidden_grad[at, :] = values
        branch[at, :] = values.astype(branch.dtype)

    of_part(0, grad_rows)
    four.complete()
    of_part(1, grad_rows)
    for moment in range(2, lines - 1):
        down_hop(moment)
    attended_grad[...] = against(branch[...], out_w[...]).astype(attended_grad.dtype)

    def keep_down(i, sums):
        down_final[pl.ds(pl.multiple_of(i * 32, 32), 32), :] = sums

    down_last(keep_down)
    for phase in (one, two, three, four):
        phase.drain()


def feed_forward(lines, out_rows, attended, tokens, teacher, out_grad, valid, gains, gate_up_w, down_rows, identity):
    rows, width = tokens.shape
    units = down_rows.shape[0]
    share = lines * units
    low = tokens.dtype
    shape = jax.ShapeDtypeStruct
    vmem, anywhere = pl.BlockSpec(memory_space=pltpu.VMEM), pl.BlockSpec(memory_space=pl.ANY)
    cut = column_cut(width)
    return pl.pallas_call(
        feed_forward_kernel,
        out_shape=[
            shape((rows, width), low),
            shape((1, 1), jnp.float32),
            shape((1, 1), jnp.float32),
            shape((rows, width), jnp.float32),
            shape((rows, width), low),
            shape((rows, width), low),
            shape((units, width), jnp.float32),
            shape((width, share), low),
            shape((width, share), low),
        ],
        in_specs=[anywhere, vmem, vmem, anywhere, anywhere, vmem, vmem, anywhere, anywhere],
        out_specs=[vmem] * 9,
        scratch_shapes=[
            pltpu.VMEM((width, width), low),
            pltpu.VMEM((width, 2 * share), low),
            pltpu.VMEM((rows, width), low),
            pltpu.VMEM((rows, width), low),
            pltpu.VMEM((lines, units, width), low),
            pltpu.VMEM((lines, units, width), low),
            pltpu.VMEM((lines, units, width), low),
            pltpu.VMEM((PLANE, rows, width), low),
            pltpu.VMEM((PLANE, rows, 2 * share), low),
            pltpu.VMEM((PLANE, rows, share), low),
            pltpu.VMEM((PLANE, rows, width), low),
            pltpu.VMEM((PLANE, rows, width), low),
            pltpu.VMEM((4, rows, width), low),
            pltpu.VMEM((rows, cut), low),
            pltpu.VMEM((rows, width - cut), low),
            pltpu.VMEM((rows, width), low),
            pltpu.VMEM((rows, width), low),
            pltpu.VMEM((rows, width), jnp.float32),
            pltpu.VMEM((rows, width), jnp.float32),
            pltpu.VMEM((rows, 1), jnp.float32),
            pltpu.VMEM((rows, 1), jnp.float32),
            pltpu.SemaphoreType.DMA((4,)),
            pltpu.SemaphoreType.DMA,
            pltpu.SemaphoreType.DMA((2, lines)),
            pltpu.SemaphoreType.DMA((2, lines)),
            pltpu.SemaphoreType.DMA((2, lines)),
            pltpu.SemaphoreType.DMA((2, lines)),
            pltpu.SemaphoreType.DMA((2, 2, GATHER_KINDS)),
            pltpu.SemaphoreType.DMA((2, 2, GATHER_KINDS)),
            pltpu.SemaphoreType.DMA((2, 2, REDUCE_KINDS)),
            pltpu.SemaphoreType.DMA((2, 2, REDUCE_KINDS)),
        ],
        compiler_params=pltpu.CompilerParams(collective_id=identity, vmem_limit_bytes=VMEM_LIMIT),
        cost_estimate=pl.CostEstimate(flops=40 * PLANE * rows * width * share // 2, bytes_accessed=30 * 2**20, transcendentals=0),
        name="feed_forward",
    )(out_rows, attended, tokens, teacher, out_grad, valid, gains, gate_up_w, down_rows)


HEAD_TILES = 3
ROW_STEP = 64


def by_rows(rows, body, step=ROW_STEP):
    def run(i, carry):
        body(pl.ds(pl.multiple_of(i * step, step), step))
        return carry

    lax.fori_loop(0, rows // step, run, 0)


def lanes_of(values):
    return lax.broadcasted_iota(jnp.int32, values.shape, len(values.shape) - 1)


def turned(tile, cosine, sine):
    half = HD // 2
    partner = jnp.where(lanes_of(tile) < half, -pltpu.roll(tile, LANES - half, 1), pltpu.roll(tile, half, 1))
    return tile * cosine + partner * sine


def packed_pair(first, second, even):
    lane = lanes_of(first)
    moved = pltpu.roll(second, HD, 1)
    full_even = jnp.where(lane < HD, first, moved)
    full_odd = jnp.where(lane < 32, pltpu.roll(first, 64, 1), pltpu.roll(second, 32, 1))
    return jnp.where(even, full_even, full_odd), jnp.where(even, moved, first)


def unpacked_pair(full, part, even):
    lane = lanes_of(full)
    zero = jnp.zeros_like(full)
    first_even = jnp.where(lane < HD, full, zero)
    second_even = jnp.where(lane < 32, pltpu.roll(full, 32, 1), jnp.where(lane < HD, pltpu.roll(part, 32, 1), zero))
    first_odd = jnp.where(lane < 64, part, jnp.where(lane < HD, pltpu.roll(full, 64, 1), zero))
    second_odd = jnp.where(lane < HD, pltpu.roll(full, HD, 1), zero)
    return jnp.where(even, first_even, first_odd), jnp.where(even, second_even, second_odd)


def keys_and_values(qkv, keys, values, count, rows):
    def body(src, carry):
        block = qkv[src].astype(jnp.float32)
        tiles = [block[:, i * LANES : (i + 1) * LANES] for i in range(HEAD_TILES)]
        lane = lanes_of(tiles[0])
        key = jnp.where(lane < HD, tiles[2], 0.0)
        value = jnp.where(lane < 64, pltpu.roll(tiles[1], 64, 1), pltpu.roll(tiles[2], HD, 1))
        value = jnp.where(lane < 32, pltpu.roll(tiles[0], 32, 1), value)
        value = jnp.where(lane < HD, value, 0.0)
        at = pl.ds(pl.multiple_of(src * rows, rows), rows)
        for half in range(2):
            keys[half, at, :] = key[half * rows : (half + 1) * rows].astype(keys.dtype)
            values[half, at, :] = value[half * rows : (half + 1) * rows].astype(values.dtype)
        return carry

    lax.fori_loop(0, count, body, 0)


def segment_of(lengths, place):
    start, end = jnp.zeros_like(place), 0
    for length in [lengths[0, j] for j in range(NSEQ)]:
        end = end + length
        start = start + jnp.where(place >= end, length, 0)
    return start, end


def side_by_side(heads):
    full, part = packed_pair(heads[0], heads[1], True)
    full_odd, part_odd = packed_pair(heads[2], heads[3], False)
    middle = jnp.where(lanes_of(part) < 64, part, pltpu.roll(part_odd, 64, 1))
    return full, middle, full_odd


def apart(ref, group):
    start = group * HEAD_TILES * LANES
    tiles = [ref[:, start + i * LANES : start + (i + 1) * LANES].astype(jnp.float32) for i in range(HEAD_TILES)]
    return unpacked_pair(tiles[0], tiles[1], True) + unpacked_pair(tiles[2], pltpu.roll(tiles[1], 64, 1), False)


def arrange_rows(rows_in, w_query, w_key, w_value, gain_rows, count):
    share = rows_in.shape[0]
    groups = HEADS // KV
    queries = [head for group in range(HEADS // 4) for head in apart(w_query, group)]
    keys = [head for group in range(KV // 4) for head in apart(w_key, group)]
    values = [head for group in range(KV // 4) for head in apart(w_value, group)]
    lane = lanes_of(keys[0])
    for head in range(KV):
        for number, tile in enumerate(queries[head * groups : (head + 1) * groups] + [keys[head]]):
            third = pltpu.roll(values[head], HD - 32 * number, 1)
            start = (head * HEAD_TILES + number) * LANES
            rows_in[:, start : start + LANES] = jnp.where(lane < HD, tile, third).astype(rows_in.dtype)
    row = lax.broadcasted_iota(jnp.int32, (LANES, LANES), 0)
    columns = jnp.where(row == 0, gain_rows[0:1, :], jnp.where(row == 1, gain_rows[1:2, :], 0.0))
    columns = jnp.where(row == 2, count, columns)
    rows_in[:, KV * HEAD_TILES * LANES :] = jnp.transpose(columns)[:share, :].astype(rows_in.dtype)


def attend_kernel(
    scale, lines, w_query, w_key, w_value, w_gate, w_up, out_rows, gain_rows, freq, mask, deal, lengths, tokens,
    attended, normed, gains, cosine, sine, valid, weights, out_w, unit_w, qkv_out, probs,
    rows_in, unit_rows, w, place_row, sent, qkv, keys, values, prob_blocks, o_sent, o_came,
    send, recv, o_send, o_recv, p_sem, q_sem, w_sem, w_line_send, w_line_recv, w_send, w_recv, w_here, g_send, g_recv, g_here,
    o_line_send, o_line_recv,
    u_send, u_recv, u_here, l_send, l_recv,
):
    z, y, x, c = coordinates()
    count = sent.shape[0]
    me = z * 2 + y
    even = y == 0
    rows, width = tokens.shape
    half_rows = rows // 2
    head_cols = HEAD_TILES * LANES
    to_device = lambda i: (i, x * 2 + c)
    peer = lambda k: lax.rem(me + k, count)

    member = y * 4 + x * 2 + c
    in_plane = lambda i: (z * 2 + i // 4, i % 4)
    unit_peer = lambda k: lax.rem(member + k, PLANE)
    others = [device(z, yy, xx, cc) for yy, xx, cc in ((y, 1 - x, c), (y, x, 1 - c), (y, 1 - x, 1 - c))]
    others += [device(z, 1 - y, xx, cc) for xx, cc in ((1 - x, c), (x, 1 - c), (1 - x, 1 - c))]
    units = w_gate.shape[1] // (lines * PLANE)
    for i in range(PLANE):
        for zz in range(lines):
            start = (zz * PLANE + i) * units
            unit_rows[i, :, zz * units : (zz + 1) * units] = w_gate[:, start : start + units]
            unit_rows[i, :, (lines + zz) * units : (lines + zz + 1) * units] = w_up[:, start : start + units]
    greet([to_device(peer(k)) for k in range(1, count)] + others)

    def unit_out(k):
        i = unit_peer(k)
        return remote(unit_rows.at[i], unit_w.at[z, member], u_send.at[k], u_recv.at[k], in_plane(i))

    unit_own = pltpu.make_async_copy(unit_rows.at[member], unit_w.at[z, member], u_here)
    unit_own.start()
    columns = rows_in.shape[1]
    line_gathers, plane_gathers = [], []
    for part, of in enumerate(halves(columns)):
        line_gathers.append(
            line_gather(
                (z, y, x, c), lines, rows_in.at[:, of], lambda zz, of=of: w.at[zz, member, :, of],
                w_line_send.at[part], w_line_recv.at[part], w_here.at[part],
            )
        )
        plane_gathers.append(
            PlaneGather(
                (z, y, x, c), lambda yy, xx, of=of: w.at[:, yy * 4 + xx * 2 + c, :, of], of.size,
                w_send.at[part], w_recv.at[part],
            )
        )
    (one_begin, one_pass, one_last), (two_begin, two_pass, two_last) = line_gathers
    one, two = plane_gathers
    out_begin, out_pass, out_last = line_gather(
        (z, y, x, c), lines, out_rows, lambda zz: out_w.at[zz, member], o_line_send, o_line_recv, g_here
    )
    out_gather = PlaneGather(
        (z, y, x, c), lambda yy, xx: out_w.at[:, yy * 4 + xx * 2 + c], out_rows.shape[1], g_send, g_recv
    )
    line_begin, line_pass, line_last = line_gather(
        (z, y, x, c), lines, unit_w.at[z], lambda zz: unit_w.at[zz], l_send, l_recv
    )
    for k in range(1, PLANE):
        unit_out(k).start()
    first_block = deal[0, me]
    total = functools.reduce(lambda a, b: a + b, [lengths[0, j] for j in range(NSEQ)])
    token = lax.broadcasted_iota(jnp.int32, (1, rows), 1)
    in_pack = jnp.where(token < half_rows, first_block * half_rows, (2 * count - 2 - first_block) * half_rows) + token
    counted = jnp.where(in_pack < total, mask[...].astype(jnp.float32), 0.0)
    arrange_rows(rows_in, w_query, w_key, w_value, gain_rows, jnp.sum(counted, -1, keepdims=True))
    one_begin()
    valid[...] = jnp.transpose(jnp.broadcast_to(counted, (LANES, rows)))[:, :1]
    token = lax.broadcasted_iota(jnp.int32, (rows, 1), 0)
    in_pack = jnp.where(token < half_rows, first_block * half_rows, (2 * count - 2 - first_block) * half_rows) + token
    angle = (in_pack - segment_of(lengths, in_pack)[0]).astype(jnp.float32) * freq[...]
    cosine[...] = jnp.cos(angle)
    sine[...] = jnp.sin(angle)
    one_pass(1)
    two_begin()
    for moment in range(2, lines):
        one_pass(moment)
        two_pass(moment - 1)
    one_last()
    one.begin()
    two_pass(lines - 1)
    two_last()
    unit_own.wait()
    for k in range(1, PLANE):
        unit_out(k).wait_recv()
    line_begin()
    out_begin()
    one.forward_on()
    two.begin()
    for moment in range(1, lines - 1):
        out_pass(moment)
    one.corner_on()
    out_pass(lines - 1)
    out_last()
    two.forward_on()
    line_pass(1)
    one.rest()
    two.corner_on()
    two.rest()
    keep_weights = pltpu.make_async_copy(w, weights, w_sem)
    keep_weights.start()

    def columns_of(start, size):
        return w[:, :, :, pl.ds(start, size)].reshape(width, size)

    extras = columns_of(count * head_cols, LANES)
    gains[...] = jnp.transpose(extras.astype(jnp.float32))[: gains.shape[0], :]
    gain = gains[0:1, :]

    def norm_rows(at):
        values_at = tokens[at, :].astype(jnp.float32)
        normed[at, :] = (values_at * rms_scale(values_at) * gain).astype(normed.dtype)

    by_rows(rows, norm_rows)

    def out(k):
        return remote(sent.at[peer(k)], qkv.at[me], send.at[k], recv.at[k], to_device(peer(k)))

    def project(k, carry):
        i = peer(k)
        columns = columns_of(pl.multiple_of(i * head_cols, LANES), head_cols)
        both = jnp.dot(normed[...], columns, preferred_element_type=jnp.float32)
        for tile in range(HEAD_TILES):
            at = slice(tile * LANES, (tile + 1) * LANES)
            sent[i, :, at] = turned(both[:, at], cosine[...], sine[...]).astype(sent.dtype)

        @pl.when(k < count)
        def _():
            out(k).start()

        return carry

    lax.fori_loop(1, count + 1, project, 0)
    out_gather.begin()
    line_pass(2)
    qkv[me] = sent[me]
    for src in range(count):
        columns = slice(src * half_rows, (src + 1) * half_rows)
        steps = lax.broadcasted_iota(jnp.int32, (1, half_rows), 1)
        place_row[0, :, columns] = deal[0, src] * half_rows + steps
        place_row[1, :, columns] = (2 * count - 1 - deal[0, src]) * half_rows + steps

    def arrive(k, carry):
        out(k).wait_recv()
        return carry

    out_gather.forward_on()
    out_gather.corner_on()
    lax.fori_loop(1, count, arrive, 0)
    keep_qkv = pltpu.make_async_copy(qkv, qkv_out, q_sem)
    keep_qkv.start()
    keys_and_values(qkv, keys, values, count, half_rows)

    def back(k):
        return remote(o_sent.at[peer(k)], o_came.at[me], o_send.at[k], o_recv.at[k], to_device(peer(k)))

    def keep(src, half):
        return pltpu.make_async_copy(prob_blocks.at[src, half], probs.at[src, half], p_sem.at[src, half])

    def attend(k, carry):
        src = peer(k)
        halves_out = []
        for half in range(2):
            at = pl.ds(half * half_rows, half_rows)
            queries = jnp.concatenate([qkv[src, at, :LANES], qkv[src, at, LANES : 2 * LANES]], 0)
            score = against(queries, keys[half]) * scale
            first = deal[0, src]
            block = first if half == 0 else 2 * count - 1 - first
            own = block * half_rows + lax.broadcasted_iota(jnp.int32, (half_rows, 1), 0)
            start, end = segment_of(lengths, own)
            lowest = jnp.where(own < end, start, own)
            place = place_row[half]
            allowed = (place >= lowest) & (place <= own)
            bias = jnp.where(allowed, 0.0, masked_score)
            score = score + jnp.concatenate([bias, bias], 0)
            top = jnp.max(score, -1, keepdims=True)
            weight = jnp.exp(score - top)
            total = jnp.sum(weight, -1, keepdims=True)
            low = (weight * (1.0 / total)).astype(prob_blocks.dtype)
            prob_blocks[src, half] = low
            keep(src, half).start()
            summed = jnp.dot(low, values[half], preferred_element_type=jnp.float32)
            full, part = packed_pair(summed[:half_rows], summed[half_rows:], even)
            o_sent[src, at, :] = full.astype(o_sent.dtype)
            halves_out.append(part)
        lane = lanes_of(halves_out[0])
        part = jnp.where(lane < 64, halves_out[0], pltpu.roll(halves_out[1], 64, 1))
        o_sent[src, pl.ds(rows, half_rows), :] = part.astype(o_sent.dtype)

        @pl.when(k < count)
        def _():
            back(k).start()

        return carry

    lax.fori_loop(1, count + 1, attend, 0)
    o_came[me] = o_sent[me]

    def return_arrive(k, carry):
        back(k).wait_recv()
        return carry

    lax.fori_loop(1, count, return_arrive, 0)
    for pair in range(count // 2):
        at = pair * head_cols
        attended[:, at : at + LANES] = o_came[2 * pair, :rows, :]
        attended[:, at + 2 * LANES : at + 3 * LANES] = o_came[2 * pair + 1, :rows, :]
        one = o_came[2 * pair, rows:, :].astype(jnp.float32)
        two = o_came[2 * pair + 1, rows:, :].astype(jnp.float32)
        lane = lanes_of(one)
        middle = slice(at + LANES, at + 2 * LANES)
        attended[:half_rows, middle] = jnp.where(lane < 64, one, pltpu.roll(two, 64, 1)).astype(attended.dtype)
        attended[half_rows:, middle] = jnp.where(lane < 64, pltpu.roll(one, 64, 1), two).astype(attended.dtype)

    def drain(k, carry):
        out(k).wait_send()
        back(k).wait_send()
        return carry

    lax.fori_loop(1, count, drain, 0)

    def drain_probs(src, carry):
        keep(src, 0).wait()
        keep(src, 1).wait()
        return carry

    lax.fori_loop(0, count, drain_probs, 0)
    keep_qkv.wait()
    out_gather.rest()
    for gather in (out_gather, *plane_gathers):
        gather.drain()
    for moment in range(3, lines):
        line_pass(moment)
    line_last()
    for k in range(1, PLANE):
        unit_out(k).wait_send()
    keep_weights.wait()


def attend(scale, lines, w_query, w_key, w_value, w_gate, w_up, out_rows, gain_rows, freq, mask, deal, lengths, tokens, identity):
    rows, width = tokens.shape
    share, units = out_rows.shape[0], w_gate.shape[1] // PLANE
    count = KV
    columns = count * HEAD_TILES * LANES + LANES
    half_rows = rows // 2
    half = count * half_rows
    head_cols = HEAD_TILES * LANES
    low = tokens.dtype
    shape = jax.ShapeDtypeStruct
    vmem, anywhere = pl.BlockSpec(memory_space=pltpu.VMEM), pl.BlockSpec(memory_space=pl.ANY)
    smem = pl.BlockSpec(memory_space=pltpu.SMEM)
    dma = pltpu.SemaphoreType.DMA
    return pl.pallas_call(
        functools.partial(attend_kernel, scale, lines),
        out_shape=[
            shape((rows, width), low),
            shape((rows, width), low),
            shape((8, width), jnp.float32),
            shape((rows, LANES), jnp.float32),
            shape((rows, LANES), jnp.float32),
            shape((rows, 1), jnp.float32),
            shape((lines, PLANE, share, columns), low),
            shape((lines, PLANE) + out_rows.shape, low),
            shape((lines, PLANE, share, 2 * units), low),
            shape((count, rows, head_cols), low),
            shape((count, 2, rows, half), low),
        ],
        in_specs=[vmem] * 5 + [anywhere] + [vmem] * 3 + [smem, smem, vmem],
        out_specs=[vmem] * 6 + [anywhere] * 5,
        scratch_shapes=[
            pltpu.VMEM((share, columns), low),
            pltpu.VMEM((PLANE, share, 2 * units), low),
            pltpu.VMEM((lines, PLANE, share, columns), low),
            pltpu.VMEM((2, 1, half), jnp.int32),
            pltpu.VMEM((count, rows, head_cols), low),
            pltpu.VMEM((count, rows, head_cols), low),
            pltpu.VMEM((2, half, LANES), low),
            pltpu.VMEM((2, half, LANES), low),
            pltpu.VMEM((count, 2, rows, half), low),
            pltpu.VMEM((count, rows + half_rows, LANES), low),
            pltpu.VMEM((count, rows + half_rows, LANES), low),
            dma((count,)),
            dma((count,)),
            dma((count,)),
            dma((count,)),
            dma((count, 2)),
            dma,
            dma,
            dma((2, 2, lines)),
            dma((2, 2, lines)),
            dma((2, GATHER_KINDS)),
            dma((2, GATHER_KINDS)),
            dma((2,)),
            dma((GATHER_KINDS,)),
            dma((GATHER_KINDS,)),
            dma,
            dma((2, lines)),
            dma((2, lines)),
            dma((PLANE,)),
            dma((PLANE,)),
            dma,
            dma((2, lines)),
            dma((2, lines)),
        ],
        compiler_params=pltpu.CompilerParams(collective_id=identity, vmem_limit_bytes=VMEM_LIMIT),
        name="attend",
    )(w_query, w_key, w_value, w_gate, w_up, out_rows, gain_rows, freq, mask, deal, lengths, tokens)


def attend_back_kernel(
    scale, lines, attended_grad, qkv, probs, cosine, sine, attended, branch, gate_parts, qkv_grad, out_final, gate_sums,
    sent, came, keys, values, prob_blocks, dk_sum, dv_sum, back_sent, back_came,
    send, recv, back_send, back_recv, p_sem, up, down, l_send, l_recv, p, *reducing,
):
    z, y, x, c = coordinates()
    count = sent.shape[0]
    me = z * 2 + y
    even = y == 0
    rows, width = attended_grad.shape
    half_rows = rows // 2
    head_cols = HEAD_TILES * LANES
    to_device = lambda i: (i, x * 2 + c)
    peer = lambda k: lax.rem(me + k, count)
    source = lambda k: lax.rem(me + count - k, count)

    def load(src, half):
        return pltpu.make_async_copy(probs.at[src, half], prob_blocks.at[src, half], p_sem.at[src, half])

    def load_start(k, carry):
        load(source(k), 0).start()
        load(source(k), 1).start()
        return carry

    lax.fori_loop(0, count, load_start, 0)
    greet([to_device(peer(k)) for k in range(1, count)] + [device(z, y, 1 - x, c), device(z, y, x, 1 - c)])
    members, share = p.shape[1:3]

    def prepare(block):
        at = pl.ds(pl.multiple_of(block * members * share, LANES), members * share)
        store_terms(p, block, 0, transposed(attended[:, at], branch[...]))

    reduce_stages, reduce_last = reduce_plan(lines, prepare, p, out_final, *reducing)
    line_begin, line_hop, line_last = line_reduce((z, y, x, c), lines, gate_parts, up, down, l_send, l_recv)
    for pair in range(count // 2):
        at = pair * head_cols
        sent[2 * pair, :rows, :] = attended_grad[:, at : at + LANES]
        sent[2 * pair + 1, :rows, :] = attended_grad[:, at + 2 * LANES : at + 3 * LANES]
        middle = attended_grad[:, at + LANES : at + 2 * LANES].astype(jnp.float32)
        one, two = middle[:half_rows], middle[half_rows:]
        lane = lanes_of(one)
        sent[2 * pair, rows:, :] = jnp.where(lane < 64, one, pltpu.roll(two, 64, 1)).astype(sent.dtype)
        sent[2 * pair + 1, rows:, :] = jnp.where(lane < 64, pltpu.roll(one, 64, 1), two).astype(sent.dtype)

    def out(k):
        return remote(sent.at[peer(k)], came.at[me], send.at[k], recv.at[k], to_device(peer(k)))

    def begin(k, carry):
        out(k).start()
        return carry

    lax.fori_loop(1, count, begin, 0)
    reduce_stages[0]()
    came[me] = sent[me]
    keys_and_values(qkv, keys, values, count, half_rows)
    dk_sum[...] = jnp.zeros_like(dk_sum)
    dv_sum[...] = jnp.zeros_like(dv_sum)

    def grads(k, carry):
        src = source(k)

        @pl.when(k > 0)
        def _():
            out(k).wait_recv()

        for half in range(2):
            at = pl.ds(half * half_rows, half_rows)
            full = came[src, at, :].astype(jnp.float32)
            part = came[src, pl.ds(rows, half_rows), :].astype(jnp.float32)
            if half:
                part = pltpu.roll(part, 64, 1)
            pair = jnp.concatenate(unpacked_pair(full, part, even), 0).astype(came.dtype)
            queries = jnp.concatenate([qkv[src, at, :LANES], qkv[src, at, LANES : 2 * LANES]], 0)
            load(src, half).wait()
            low = prob_blocks[src, half]
            prob = low.astype(jnp.float32)
            prob_grad = against(pair, values[half])
            delta = jnp.sum(prob * prob_grad, -1, keepdims=True)
            score_low = (prob * (prob_grad - delta)).astype(low.dtype)
            dq = jnp.dot(score_low, keys[half], preferred_element_type=jnp.float32) * scale
            back_sent[src, at, :LANES] = dq[:half_rows].astype(back_sent.dtype)
            back_sent[src, at, LANES : 2 * LANES] = dq[half_rows:].astype(back_sent.dtype)
            dk_sum[half] += transposed(score_low, queries)
            dv_sum[half] += transposed(low, pair)
        pl.when(k == 2)(line_begin)
        for number in range(1, len(reduce_stages)):
            pl.when(k == number)(reduce_stages[number])
        return carry

    lax.fori_loop(0, count, grads, 0)

    def back(k):
        return remote(back_sent.at[peer(k)], back_came.at[me], back_send.at[k], back_recv.at[k], to_device(peer(k)))

    def finish(k, carry):
        src = peer(k)
        in_half = pl.ds(pl.multiple_of(src * half_rows, half_rows), half_rows)
        for half in range(2):
            at = pl.ds(half * half_rows, half_rows)
            dk = dk_sum[half, in_half, :] * scale
            dv = dv_sum[half, in_half, :]
            lane = lanes_of(dk)
            for tile in range(HEAD_TILES):
                columns = slice(tile * LANES, (tile + 1) * LANES)
                head = dk if tile == 2 else back_sent[src, at, columns].astype(jnp.float32)
                third = pltpu.roll(dv, HD - 32 * tile, 1)
                back_sent[src, at, columns] = jnp.where(lane < HD, head, third).astype(back_sent.dtype)

        @pl.when(k < count)
        def _():
            back(k).start()

        return carry

    lax.fori_loop(1, count + 1, finish, 0)
    for moment in range(1, lines - 1):
        line_hop(moment)
    reduce_last()
    back_came[me] = back_sent[me]

    def turn_back(k, carry):
        src = source(k)

        @pl.when(k > 0)
        def _():
            back(k).wait_recv()

        for tile in range(HEAD_TILES):
            columns = slice(tile * LANES, (tile + 1) * LANES)
            values_at = back_came[src, :, columns].astype(jnp.float32)
            turned_at = turned(values_at, cosine[...], -sine[...])
            at = pl.ds(pl.multiple_of(src * head_cols + tile * LANES, LANES), LANES)
            qkv_grad[:, at] = turned_at.astype(qkv_grad.dtype)
        return carry

    lax.fori_loop(0, count, turn_back, 0)

    def keep_sums(i, sums):
        gate_sums[i] = sums.astype(gate_sums.dtype)

    line_last(keep_sums, gate_sums.shape[1])

    def drain(k, carry):
        out(k).wait_send()
        back(k).wait_send()
        return carry

    lax.fori_loop(1, count, drain, 0)


def attend_back(scale, lines, attended_grad, qkv, probs, tables, attended, branch, gate_parts, identity):
    rows, width = attended_grad.shape
    count, _, head_cols = qkv.shape
    half = probs.shape[-1]
    half_rows = rows // 2
    share = width // (lines * PLANE)
    low = attended_grad.dtype
    vmem, anywhere = pl.BlockSpec(memory_space=pltpu.VMEM), pl.BlockSpec(memory_space=pl.ANY)
    dma = pltpu.SemaphoreType.DMA
    return pl.pallas_call(
        functools.partial(attend_back_kernel, scale, lines),
        out_shape=[
            jax.ShapeDtypeStruct((rows, count * head_cols), low),
            jax.ShapeDtypeStruct((share, width), jnp.float32),
            jax.ShapeDtypeStruct((PLANE, share, gate_parts.shape[2]), low),
        ],
        in_specs=[vmem, vmem, anywhere] + [vmem] * 5,
        out_specs=[vmem, vmem, vmem],
        scratch_shapes=[
            pltpu.VMEM((count, rows + half_rows, LANES), low),
            pltpu.VMEM((count, rows + half_rows, LANES), low),
            pltpu.VMEM((2, half, LANES), low),
            pltpu.VMEM((2, half, LANES), low),
            pltpu.VMEM((count, 2, rows, half), low),
            pltpu.VMEM((2, half, LANES), jnp.float32),
            pltpu.VMEM((2, half, LANES), jnp.float32),
            pltpu.VMEM((count, rows, head_cols), low),
            pltpu.VMEM((count, rows, head_cols), low),
            dma((count,)),
            dma((count,)),
            dma((count,)),
            dma((count,)),
            dma((count, 2)),
            pltpu.VMEM(gate_parts.shape, low),
            pltpu.VMEM(gate_parts.shape, low),
            dma((2, lines)),
            dma((2, lines)),
            *reduce_scratch(lines, share, width, low),
        ],
        compiler_params=pltpu.CompilerParams(collective_id=identity, vmem_limit_bytes=VMEM_LIMIT),
        name="attend_back",
    )(attended_grad, qkv, probs, *tables, attended, branch, gate_parts)


def finish_kernel(
    weights, normed, qkv_grad, hidden_grad, tokens, gains, square, norm, w_gate, w_up, gate_sums, up_parts,
    input_grad, query_final, key_final, value_final, gate_final, up_final, gain_final, loss,
    w, own_rows, normed_grad, final, up_sums, gate_came, up_came, line_up, line_down,
    w_sem, own_sem, gate_send, gate_recv, up_send, up_recv, here, l_send, l_recv, p, *reducing,
):
    z, y, x, c = coordinates()
    lines, members, share = p.shape[:3]
    rows, width = tokens.shape
    qkv_cols = qkv_grad.shape[1]
    low = normed.dtype
    load = pltpu.make_async_copy(weights.at[:, pl.ds(0, qkv_cols)], w, w_sem)
    load.start()
    number = (z * 2 + y) * 4 + x * 2 + c
    own_at = pl.ds(pl.multiple_of(number * share, 16), share)
    load_own = pltpu.make_async_copy(weights.at[own_at, :], own_rows, own_sem)
    load_own.start()
    me = y * 4 + x * 2 + c
    peer = lambda k: lax.rem(me + k, members)
    member = lambda i: (z * 2 + i // 4, i % 4)
    greet([member(peer(k)) for k in range(1, members)] + line_of(z, y, x, c, lines))

    def out(kind, k):
        src, came, send, recv = (
            (gate_sums, gate_came, gate_send, gate_recv),
            (up_sums, up_came, up_send, up_recv),
        )[kind]
        return remote(src.at[peer(k)], came.at[me], send.at[k], recv.at[k], member(peer(k)))

    gate_own = pltpu.make_async_copy(gate_sums.at[me], gate_came.at[me], here)
    gate_own.start()
    line_begin, line_hop, line_last = line_reduce((z, y, x, c), lines, up_parts, line_up, line_down, l_send, l_recv)
    line_begin()

    def keep_up(i, sums):
        up_sums[i] = sums.astype(up_sums.dtype)

    devices = lines * PLANE
    place = lax.broadcasted_iota(jnp.int32, (1, LANES), 1) - number
    rest = square[...]
    loss_terms = jnp.zeros((1, LANES), jnp.float32)
    for term in range(3):
        top = rest.astype(low).astype(jnp.float32)
        loss_terms = loss_terms + jnp.where(place == term * devices, top, 0.0)
        rest = rest - top

    def prepare(block):
        at = pl.ds(pl.multiple_of(block * members * share, LANES), members * share)
        left = normed[:, at]
        chunk = qkv_cols // 2
        for start in range(0, qkv_cols, chunk):
            store_terms(p, block, start, transposed(left, qkv_grad[:, start : start + chunk]))
        store_terms(p, block, qkv_cols, jnp.broadcast_to(loss_terms, (members * share, LANES)))

    stages, last = reduce_plan(lines, prepare, p, final, *reducing)

    def grad_rows(at):
        values = tokens[at, :].astype(jnp.float32)
        scale = rms_scale(values)
        unit = values * scale
        scaled = normed_grad[at, :] * gains[0:1, :]
        input_grad[at, :] = hidden_grad[at, :] + scale * (
            scaled - unit * jnp.mean(scaled * unit, -1, keepdims=True)
        )

    block = rows // lines
    for index, stage in enumerate(stages):
        if index == 2:
            for k in range(1, members):
                out(0, k).start()
            load.wait()
        if 2 <= index < lines:
            line_hop(index - 1)
        if index == 2 + lines:
            line_last(keep_up, share)
            for k in range(1, members):
                out(1, k).start()
        stage()
        if 2 <= index < 2 + lines:
            at = slice((index - 2) * block, (index - 1) * block)
            normed_grad[at, :] = against(qkv_grad[at, :], w[...])
        if index == 2 + lines:
            by_rows(rows, grad_rows)
    up_came[me] = up_sums[me]
    gate_own.wait()
    for kind in range(2):
        for k in range(1, members):
            out(kind, k).wait_recv()
    units = gate_came.shape[2] // lines
    for i in range(members):
        for zz in range(lines):
            to = slice((zz * members + i) * units, (zz * members + i + 1) * units)
            of = slice(zz * units, (zz + 1) * units)
            gate_final[:, to] = gate_came[i, :, of].astype(jnp.float32)
            up_final[:, to] = up_came[i, :, of].astype(jnp.float32)
    last()

    def tile(head, number):
        start = (head * HEAD_TILES + number) * LANES
        return final[:, start : start + LANES]

    def put(ref, group, heads):
        for number, value in enumerate(side_by_side(heads)):
            start = (group * HEAD_TILES + number) * LANES
            ref[:, start : start + LANES] = value

    for pair in range(KV // 2):
        put(query_final, pair, [tile(2 * pair + i, j) for i in range(2) for j in range(2)])
    for group in range(KV // 4):
        heads = [4 * group + i for i in range(4)]
        put(key_final, group, [tile(head, 2) for head in heads])
        parts = []
        for head in heads:
            thirds = [pltpu.roll(tile(head, number), 32 * (number + 1), 1) for number in range(HEAD_TILES)]
            in_tile = lanes_of(thirds[0])
            parts.append(jnp.where(in_tile < 32, thirds[0], jnp.where(in_tile < 64, thirds[1], thirds[2])))
        put(value_final, group, parts)

    load_own.wait()
    own_gains = own_rows[:, qkv_cols:].astype(jnp.float32)

    def product(grads, weights_of, width_of):
        sums = jnp.zeros((share, 1), jnp.float32)
        for start in range(0, width_of, 4 * LANES):
            at = slice(start, start + 4 * LANES)
            sums += jnp.sum(grads[:, at] * weights_of[:, at].astype(jnp.float32), -1, keepdims=True)
        return sums

    units_all = w_gate.shape[1]
    first_gain = product(final, own_rows, qkv_cols) / own_gains[:, 0:1]
    second_gain = product(gate_final, w_gate, units_all) + product(up_final, w_up, units_all)
    second_gain = second_gain / own_gains[:, 1:2]
    columns = lax.broadcasted_iota(jnp.int32, (share, LANES), 1)
    both_gains = jnp.where(columns == 0, first_gain, jnp.where(columns == 1, second_gain, 0.0))
    both_gains = jnp.concatenate([both_gains, jnp.zeros((LANES - share, LANES), jnp.float32)], 0)
    gain_final[...] = jnp.transpose(both_gains)[:8, :]
    tail = final[:, qkv_cols:]
    of_loss = lax.broadcasted_iota(jnp.int32, (1, LANES), 1) < 3 * devices
    loss[...] = jnp.sum(jnp.where(of_loss, tail[:1, :], 0.0), -1, keepdims=True) * (0.5 * norm[...])
    for kind in range(2):
        for k in range(1, members):
            out(kind, k).wait_send()


def finish(
    lines, weights, normed, qkv_grad, hidden_grad, tokens, gains, square, norm, w_gate, w_up, gate_sums, up_parts, identity
):
    rows, width = tokens.shape
    qkv_cols = qkv_grad.shape[1]
    share = weights.shape[0] // (lines * PLANE)
    columns = weights.shape[1]
    units_all = w_gate.shape[1]
    low = tokens.dtype
    vmem, anywhere = pl.BlockSpec(memory_space=pltpu.VMEM), pl.BlockSpec(memory_space=pl.ANY)
    dma = pltpu.SemaphoreType.DMA
    shapes = [
        (rows, width),
        (share, width),
        (share, KV * HD),
        (share, KV * HD),
        (share, units_all),
        (share, units_all),
        (8, LANES),
        (1, 1),
    ]
    return pl.pallas_call(
        finish_kernel,
        out_shape=[jax.ShapeDtypeStruct(shape, jnp.float32) for shape in shapes],
        in_specs=[anywhere] + [vmem] * 9 + [anywhere, vmem],
        out_specs=[vmem] * len(shapes),
        scratch_shapes=[
            pltpu.VMEM((width, qkv_cols), low),
            pltpu.VMEM((share, columns), low),
            pltpu.VMEM((rows, width), jnp.float32),
            pltpu.VMEM((share, columns), jnp.float32),
            pltpu.VMEM(gate_sums.shape, low),
            pltpu.VMEM(gate_sums.shape, low),
            pltpu.VMEM(gate_sums.shape, low),
            pltpu.VMEM(up_parts.shape, low),
            pltpu.VMEM(up_parts.shape, low),
            dma,
            dma,
            dma((PLANE,)),
            dma((PLANE,)),
            dma((PLANE,)),
            dma((PLANE,)),
            dma,
            dma((2, lines)),
            dma((2, lines)),
            *reduce_scratch(lines, share, columns, low),
        ],
        compiler_params=pltpu.CompilerParams(collective_id=identity, vmem_limit_bytes=VMEM_LIMIT),
        name="finish",
    )(weights, normed, qkv_grad, hidden_grad, tokens, gains, square, norm, w_gate, w_up, gate_sums, up_parts)


def emit_kernel(*refs):
    count = len(refs) // 2
    copies = [pltpu.make_async_copy(refs[i], refs[count + i], refs[-1].at[i]) for i in range(count)]
    for copy in copies:
        copy.start()
    for copy in copies:
        copy.wait()


def emit(arrays):
    anywhere = pl.BlockSpec(memory_space=pl.ANY)
    return pl.pallas_call(
        emit_kernel,
        out_shape=[jax.ShapeDtypeStruct(array.shape, array.dtype) for array in arrays],
        in_specs=[anywhere] * len(arrays),
        out_specs=[pl.BlockSpec(memory_space=pltpu.VMEM)] * len(arrays),
        scratch_shapes=[pltpu.SemaphoreType.DMA((len(arrays),))],
        compiler_params=pltpu.CompilerParams(vmem_limit_bytes=VMEM_LIMIT),
        name="emit",
    )(*arrays)


def plane_per_device(lines, *arrays):
    (
        tokens,
        lengths,
        deal,
        loss_mask,
        teacher,
        out_grad,
        attn_gain,
        w_query,
        w_key,
        w_value,
        w_out,
        ffn_gain,
        w_gate,
        w_up,
        w_down,
    ) = arrays
    devices = lines * PLANE
    width = tokens.shape[2]
    weight_rows = w_query.shape[0]
    scale = HD ** (-0.5)
    gain_rows = jnp.zeros((8, LANES), jnp.float32)
    gain_rows = gain_rows.at[0, :weight_rows].set(attn_gain.astype(jnp.float32))
    gain_rows = gain_rows.at[1, :weight_rows].set(ffn_gain.astype(jnp.float32))
    freq = rope_base ** (-(np.arange(HD // 2) * 2.0 / HD))
    freq = np.concatenate([freq, freq, np.zeros(LANES - HD)])[None].astype(np.float32)

    attended_low, normed_low, gains, cosine, sine, valid, attn_all, out_w, gate_up_w, qkv, probs = attend(
        scale,
        lines,
        w_query,
        w_key,
        w_value,
        w_gate,
        w_up,
        w_out,
        gain_rows,
        freq,
        loss_mask,
        deal,
        lengths,
        tokens[0],
        3,
    )
    attn_all = attn_all.reshape(devices * weight_rows, -1)
    gate_up_w = gate_up_w.reshape(devices * weight_rows, -1)

    result, square, norm, hidden_grad, branch_low, attended_grad, down_final, gate_grad, up_grad = feed_forward(
        lines,
        out_w.reshape(width, width),
        attended_low,
        tokens[0],
        teacher[0],
        out_grad[0],
        valid,
        gains,
        gate_up_w,
        w_down,
        5,
    )
    gate_grad, up_grad = [grad.reshape(lines, PLANE * weight_rows, -1) for grad in (gate_grad, up_grad)]
    qkv_grad, out_final, gate_sums = attend_back(
        scale, lines, attended_grad, qkv, probs, (cosine, sine), attended_low, branch_low, gate_grad, 9
    )

    input_grad, query_final, key_final, value_final, gate_final, up_final, gain_final, loss = finish(
        lines,
        attn_all,
        normed_low,
        qkv_grad,
        hidden_grad,
        tokens[0],
        gains,
        square,
        norm,
        w_gate,
        w_up,
        gate_sums,
        up_grad,
        11,
    )
    result, input_grad, query_final, key_final, value_final, out_final, gate_final, up_final, down_final = emit(
        (result, input_grad, query_final, key_final, value_final, out_final, gate_final, up_final, down_final)
    )
    return (
        result[None],
        loss.reshape(()),
        input_grad[None],
        gain_final[0, :weight_rows],
        query_final,
        key_final,
        value_final,
        out_final,
        gain_final[1, :weight_rows],
        gate_final,
        up_final,
        down_final,
    )


def suits_planes(mesh):
    sizes = dict(mesh.shape)
    return sizes["fsdp"] == 4 and sizes["ctx"] == KV


def solution(mesh):
    placed = (
        P("fsdp", "ctx", None),
        P("fsdp", None),
        P("fsdp", None),
        P("fsdp", "ctx"),
        P("fsdp", "ctx", None),
        P("fsdp", "ctx", None),
        P(("ctx", "fsdp")),
        P(("ctx", "fsdp"), None),
        P(("ctx", "fsdp"), None),
        P(("ctx", "fsdp"), None),
        P(("ctx", "fsdp"), None),
        P(("ctx", "fsdp")),
        P(("ctx", "fsdp"), None),
        P(("ctx", "fsdp"), None),
        P(("ctx", "fsdp"), None),
    )
    if suits_planes(mesh):
        per_device = functools.partial(plane_per_device, mesh.shape["ctx"] // ROWS_Y)
    else:
        per_device = ring_per_device
    return jax.shard_map(
        per_device,
        mesh=mesh,
        in_specs=placed,
        out_specs=(
            P("fsdp", "ctx", None),
            P(),
            P("fsdp", "ctx", None),
            P(("ctx", "fsdp")),
            P(("ctx", "fsdp"), None),
            P(("ctx", "fsdp"), None),
            P(("ctx", "fsdp"), None),
            P(("ctx", "fsdp"), None),
            P(("ctx", "fsdp")),
            P(("ctx", "fsdp"), None),
            P(("ctx", "fsdp"), None),
            P(("ctx", "fsdp"), None),
        ),
        check_vma=False,
    )
```

```python
import functools

import jax
import jax.numpy as jnp
import numpy as np
from jax import lax
from jax.experimental import pallas as pl
from jax.experimental.pallas import tpu as pltpu
from jax.sharding import PartitionSpec as P

HEADS = 16
KV = 8
HD = 96
NSEQ = 6


rope_base = 100000.0
epsilon = 1e-05
masked_score = -1e30


def shifted(value, axis, by):
    size = lax.axis_size(axis)
    return lax.ppermute(value, axis, [(i, (i + by) % size) for i in range(size)])


def rms_scale(values):
    return lax.rsqrt(jnp.mean(values * values, -1, keepdims=True) + epsilon)


def rotary_tables(inseq):
    freq = rope_base ** (-(jnp.arange(HD // 2, dtype=jnp.float32) * 2.0 / HD))
    angle = inseq.astype(jnp.float32)[:, None] * freq[None, :]
    return (jnp.cos(angle)[:, None, :], jnp.sin(angle)[:, None, :])


def rotary(values, cosine, sine):
    half = values.shape[-1] // 2
    first = values[..., :half]
    second = values[..., half:]
    return jnp.concatenate([first * cosine - second * sine, second * cosine + first * sine], -1)


def rotary_back(grads, cosine, sine):
    half = grads.shape[-1] // 2
    first = grads[..., :half]
    second = grads[..., half:]
    return jnp.concatenate([first * cosine + second * sine, second * cosine - first * sine], -1)


def transposed(left, right):
    return lax.dot_general(
        left, right, (((0,), (0,)), ((), ())), preferred_element_type=jnp.float32
    )


def against(left, right):
    return lax.dot_general(
        left, right, (((1,), (1,)), ((), ())), preferred_element_type=jnp.float32
    )


def permitted(query_place, query_seg, key_place, key_seg):
    same = (query_seg[:, None] == key_seg[None, :]) & (query_seg[:, None] < NSEQ)
    return same & (key_place[None, :] <= query_place[:, None]) | (
        key_place[None, :] == query_place[:, None]
    )


def ring_per_device(
    tokens,
    lengths,
    deal,
    loss_mask,
    teacher,
    out_grad,
    attn_gain,
    w_query,
    w_key,
    w_value,
    w_out,
    ffn_gain,
    w_gate,
    w_up,
    w_down,
):
    count_ctx = lax.axis_size("ctx")
    myself = lax.axis_index("ctx")
    tok_rows = tokens.shape[1]
    width = tokens.shape[2]
    half_block = tok_rows // 2
    groups = HEADS // KV
    scale = HD ** (-0.5)
    gain_one, query_w, key_w, value_w, out_w = (
        lax.all_gather(attn_gain, ("ctx", "fsdp"), axis=0, tiled=True),
        lax.all_gather(w_query, ("ctx", "fsdp"), axis=0, tiled=True),
        lax.all_gather(w_key, ("ctx", "fsdp"), axis=0, tiled=True),
        lax.all_gather(w_value, ("ctx", "fsdp"), axis=0, tiled=True),
        lax.all_gather(w_out, ("ctx", "fsdp"), axis=0, tiled=True),
    )
    gain_two, gate_w, up_w, down_w = (
        lax.all_gather(ffn_gain, ("ctx", "fsdp"), axis=0, tiled=True),
        lax.all_gather(w_gate, ("ctx", "fsdp"), axis=0, tiled=True),
        lax.all_gather(w_up, ("ctx", "fsdp"), axis=0, tiled=True),
        lax.all_gather(w_down, ("ctx", "fsdp"), axis=0, tiled=True),
    )
    dealt = jnp.arange(count_ctx * tok_rows, dtype=jnp.int32)
    local = dealt % tok_rows
    first = jnp.repeat(deal[0], tok_rows)
    block = jnp.where(local < half_block, first, 2 * count_ctx - 1 - first)
    places = block * half_block + local % half_block
    ends = jnp.cumsum(lengths[0])
    after = (places[:, None] >= ends[None, :]).astype(jnp.int32)
    seg_all = jnp.sum(after, 1)
    inseq_all = places - jnp.sum(after * lengths[0][None, :], 1)
    own_place = lax.dynamic_slice_in_dim(places, myself * tok_rows, tok_rows)
    own_seg = lax.dynamic_slice_in_dim(seg_all, myself * tok_rows, tok_rows)
    own_inseq = lax.dynamic_slice_in_dim(inseq_all, myself * tok_rows, tok_rows)
    cosine, sine = rotary_tables(own_inseq)
    inputs = tokens[0].astype(jnp.float32)
    scale_one = rms_scale(inputs)
    normed_one = inputs * scale_one
    gain_first = gain_one.astype(jnp.float32)
    normed_low = (normed_one * gain_first).astype(jnp.bfloat16)
    query_pre = jnp.dot(normed_low, query_w, preferred_element_type=jnp.float32).reshape(
        tok_rows, HEADS, HD
    )
    key_pre = jnp.dot(normed_low, key_w, preferred_element_type=jnp.float32).reshape(
        tok_rows, KV, HD
    )
    value_low = jnp.dot(normed_low, value_w, preferred_element_type=jnp.float32).astype(
        jnp.bfloat16
    )
    queries = rotary(query_pre, cosine, sine).astype(jnp.bfloat16).reshape(tok_rows, KV, groups, HD)
    keys = rotary(key_pre, cosine, sine).astype(jnp.bfloat16).reshape(tok_rows, KV * HD)

    def logits(key_block):
        return (
            jnp.einsum(
                "qcgd,kcd->cgqk",
                queries,
                key_block.reshape(-1, KV, HD),
                preferred_element_type=jnp.float32,
            )
            * scale
        )

    key_block = lax.all_gather(keys, "ctx", axis=0, tiled=True)
    value_block = lax.all_gather(value_low, "ctx", axis=0, tiled=True)
    allowed = permitted(own_place, own_seg, places, seg_all)
    top = jnp.full((KV, groups, tok_rows, 1), masked_score, jnp.float32)
    score = jnp.where(allowed, logits(key_block), masked_score)
    new_top = jnp.maximum(top, jnp.max(score, -1, keepdims=True))
    weight = jnp.where(allowed, jnp.exp(score - new_top), 0.0)
    summed = jnp.einsum(
        "cgqk,kcd->cgqd",
        weight.astype(jnp.bfloat16),
        value_block.reshape(-1, KV, HD),
        preferred_element_type=jnp.float32,
    )
    summed, top, total = (summed, new_top, jnp.sum(weight, -1, keepdims=True))
    attended = summed / total
    log_total = top + jnp.log(total)
    attended_low = (
        jnp.transpose(attended, (2, 0, 1, 3)).reshape(tok_rows, HEADS * HD).astype(jnp.bfloat16)
    )
    hidden = inputs + jnp.dot(attended_low, out_w, preferred_element_type=jnp.float32)
    scale_two = rms_scale(hidden)
    normed_two = hidden * scale_two
    gain_second = gain_two.astype(jnp.float32)
    ffn_low = (normed_two * gain_second).astype(jnp.bfloat16)
    gate = jnp.dot(ffn_low, gate_w, preferred_element_type=jnp.float32)
    up = jnp.dot(ffn_low, up_w, preferred_element_type=jnp.float32)
    sigmoid = jax.nn.sigmoid(gate)
    activated = gate * sigmoid
    mixed_low = (activated * up).astype(jnp.bfloat16)
    result = hidden + jnp.dot(mixed_low, down_w, preferred_element_type=jnp.float32)
    target = teacher[0].astype(jnp.float32)
    valid = (loss_mask[0] * (own_seg < NSEQ)).astype(jnp.float32)[:, None]
    differ = result - target
    square_sum, valid_count = lax.psum(
        (jnp.sum(valid * differ * differ), jnp.sum(valid)), ("ctx", "fsdp")
    )
    loss = square_sum / (valid_count * width)
    out_total = out_grad[0].astype(jnp.float32) + 2.0 * valid * differ / (valid_count * width)
    out_low = out_total.astype(jnp.bfloat16)
    down_grad = transposed(mixed_low, out_low)
    mixed_grad = against(out_low, down_w)
    silu_slope = sigmoid * (1.0 + gate * (1.0 - sigmoid))
    gate_low = (mixed_grad * up * silu_slope).astype(jnp.bfloat16)
    up_low = (mixed_grad * activated).astype(jnp.bfloat16)
    gate_grad = transposed(ffn_low, gate_low)
    up_grad = transposed(ffn_low, up_low)
    normed_grad = against(gate_low, gate_w) + against(up_low, up_w)
    gain_two_grad = jnp.sum(normed_grad * normed_two, 0)
    scaled_two = normed_grad * gain_second
    hidden_grad = out_total + scale_two * (
        scaled_two - normed_two * jnp.mean(scaled_two * normed_two, -1, keepdims=True)
    )
    ffn_final = (
        lax.psum_scatter(gain_two_grad, ("ctx", "fsdp"), scatter_dimension=0, tiled=True),
        lax.psum_scatter(gate_grad, ("ctx", "fsdp"), scatter_dimension=0, tiled=True),
        lax.psum_scatter(up_grad, ("ctx", "fsdp"), scatter_dimension=0, tiled=True),
        lax.psum_scatter(down_grad, ("ctx", "fsdp"), scatter_dimension=0, tiled=True),
    )
    branch_low = hidden_grad.astype(jnp.bfloat16)
    out_w_grad = transposed(attended_low, branch_low)
    attended_grad = against(branch_low, out_w).astype(jnp.bfloat16)
    grad_heads = jnp.transpose(attended_grad.reshape(tok_rows, KV, groups, HD), (1, 2, 0, 3))
    delta = jnp.sum(grad_heads.astype(jnp.float32) * attended, -1, keepdims=True)

    def cycle_step(step, state):
        key_block, value_block, key_acc, value_acc, query_acc = state
        source = (myself - step) % count_ctx
        allowed = permitted(
            own_place,
            own_seg,
            lax.dynamic_slice_in_dim(places, source * tok_rows, tok_rows),
            lax.dynamic_slice_in_dim(seg_all, source * tok_rows, tok_rows),
        )
        current_key = key_block
        current_value = value_block
        keys_three = current_key.reshape(tok_rows, KV, HD)
        values_three = current_value.reshape(tok_rows, KV, HD)
        prob = jnp.where(allowed, jnp.exp(logits(current_key) - log_total), 0.0)
        prob_grad = jnp.einsum(
            "cgqd,kcd->cgqk", grad_heads, values_three, preferred_element_type=jnp.float32
        )
        score_low = (prob * (prob_grad - delta)).astype(jnp.bfloat16)
        query_add = (
            jnp.einsum("cgqk,kcd->cgqd", score_low, keys_three, preferred_element_type=jnp.float32)
            * scale
        )
        key_add = (
            jnp.einsum(
                "cgqk,qcgd->kcd", score_low, queries, preferred_element_type=jnp.float32
            ).reshape(tok_rows, KV * HD)
            * scale
        )
        value_add = jnp.einsum(
            "cgqk,cgqd->kcd",
            prob.astype(jnp.bfloat16),
            grad_heads,
            preferred_element_type=jnp.float32,
        ).reshape(tok_rows, KV * HD)
        key_block, value_block = shifted((key_block, value_block), "ctx", 1)
        key_acc, value_acc = (
            shifted((key_acc + key_add).astype(jnp.bfloat16), "ctx", 1).astype(jnp.float32),
            shifted((value_acc + value_add).astype(jnp.bfloat16), "ctx", 1).astype(jnp.float32),
        )
        return (key_block, value_block, key_acc, value_acc, query_acc + query_add)

    cycle_start = (
        keys,
        value_low,
        jnp.zeros((tok_rows, KV * HD), jnp.float32),
        jnp.zeros((tok_rows, KV * HD), jnp.float32),
        jnp.zeros((KV, groups, tok_rows, HD), jnp.float32),
    )
    cycle_end = lax.fori_loop(0, count_ctx, cycle_step, cycle_start)
    key_acc = cycle_end[2]
    value_acc = cycle_end[3]
    query_acc = cycle_end[4]
    query_grad = jnp.transpose(query_acc, (2, 0, 1, 3)).reshape(tok_rows, HEADS, HD)
    query_low = (
        rotary_back(query_grad, cosine, sine).reshape(tok_rows, HEADS * HD).astype(jnp.bfloat16)
    )
    key_low = (
        rotary_back(key_acc.reshape(tok_rows, KV, HD), cosine, sine)
        .reshape(tok_rows, KV * HD)
        .astype(jnp.bfloat16)
    )
    value_grad_low = value_acc.astype(jnp.bfloat16)
    query_w_grad = transposed(normed_low, query_low)
    key_w_grad = transposed(normed_low, key_low)
    value_w_grad = transposed(normed_low, value_grad_low)
    normed_one_grad = (
        against(query_low, query_w) + against(key_low, key_w) + against(value_grad_low, value_w)
    )
    gain_one_grad = jnp.sum(normed_one_grad * normed_one, 0)
    scaled_one = normed_one_grad * gain_first
    input_grad = hidden_grad + scale_one * (
        scaled_one - normed_one * jnp.mean(scaled_one * normed_one, -1, keepdims=True)
    )
    attn_final = (
        lax.psum_scatter(gain_one_grad, ("ctx", "fsdp"), scatter_dimension=0, tiled=True),
        lax.psum_scatter(query_w_grad, ("ctx", "fsdp"), scatter_dimension=0, tiled=True),
        lax.psum_scatter(key_w_grad, ("ctx", "fsdp"), scatter_dimension=0, tiled=True),
        lax.psum_scatter(value_w_grad, ("ctx", "fsdp"), scatter_dimension=0, tiled=True),
        lax.psum_scatter(out_w_grad, ("ctx", "fsdp"), scatter_dimension=0, tiled=True),
    )
    return (
        result.astype(jnp.bfloat16)[None],
        loss,
        input_grad[None],
        attn_final[0],
        attn_final[1],
        attn_final[2],
        attn_final[3],
        attn_final[4],
        ffn_final[0],
        ffn_final[1],
        ffn_final[2],
        ffn_final[3],
    )


MESH = pl.DeviceIdType.MESH
ROWS_Y = 2
PLANE = 8
LANES = 128
VMEM_LIMIT = 60 * 2**20


def coordinates():
    ctx = lax.axis_index("ctx")
    fsdp = lax.axis_index("fsdp")
    return ctx // 2, ctx % 2, fsdp // 2, fsdp % 2


def device(z, y, x, c):
    return (z * 2 + y, x * 2 + c)


def greet(devices):
    barrier = pltpu.get_barrier_semaphore()
    for other in devices:
        pl.semaphore_signal(barrier, inc=1, device_id=other, device_id_type=MESH)
    pl.semaphore_wait(barrier, len(devices))


def remote(src, dst, send, recv, target):
    return pltpu.make_async_remote_copy(
        src_ref=src,
        dst_ref=dst,
        send_sem=send,
        recv_sem=recv,
        device_id=target,
        device_id_type=MESH,
    )


def transfers(sources, targets, sem):
    return [pltpu.make_async_copy(src, dst, sem.at[i]) for i, (src, dst) in enumerate(zip(sources, targets))]


def line_gather(place, lines, x_ref, slot, send, recv, here=None):
    z, y, x, c = place
    mine = None if here is None else pltpu.make_async_copy(x_ref, slot(z), here)
    ways = ((0, -1, device(z + 1, y, x, c)), (1, 1, device(z - 1, y, x, c)))

    def along(way, sign, to, s):
        zz = z + sign * (s - 1)
        return remote(x_ref if s == 1 else slot(zz), slot(zz), send.at[way, s], recv.at[way, s], to)

    def sends(sign, s):
        if sign < 0:
            return (z - (s - 1) >= 0) & (z + 1 < lines)
        return (z + (s - 1) < lines) & (z - 1 >= 0)

    def present(sign, s):
        return z - s >= 0 if sign < 0 else z + s < lines

    def start(s):
        for way, sign, to in ways:
            pl.when(sends(sign, s))(lambda way=way, sign=sign, to=to: along(way, sign, to, s).start())

    def begin():
        if mine is not None:
            mine.start()
        start(1)

    def pass_on(s):
        for way, sign, to in ways:
            pl.when(present(sign, s))(lambda way=way, sign=sign, to=to: along(way, sign, to, s).wait_recv())
        if s + 1 < lines:
            start(s + 1)

    def last():
        for s in range(1, lines):
            for way, sign, to in ways:
                pl.when(sends(sign, s))(lambda way=way, sign=sign, to=to, s=s: along(way, sign, to, s).wait_send())
        if mine is not None:
            mine.wait()

    return begin, pass_on, last


def line_reduce(place, lines, parts, up, down, send, recv):
    z, y, x, c = place
    ways = ((0, up, device(z + 1, y, x, c)), (1, down, device(z - 1, y, x, c)))

    def copy(way, t, own):
        _, sums, to = ways[way]
        src = parts.at[t] if own else sums.at[t]
        return remote(src, sums.at[t], send.at[way, t], recv.at[way, t], to)

    def begin():
        @pl.when(z == 0)
        def _():
            for t in range(lines - 1, 0, -1):
                copy(0, t, True).start()

        @pl.when(z == lines - 1)
        def _():
            for t in range(lines - 1):
                copy(1, t, True).start()

    def add_on(way, t):
        copy(way, t, False).wait_recv()
        add_rows(ways[way][1].at[t], parts.at[t])
        copy(way, t, False).start()

    def hop(moment):
        for t in range(lines):
            for zz in range(1, lines - 1):
                if zz < t and zz + (lines - 1 - t) == moment:
                    pl.when(z == zz)(functools.partial(add_on, 0, t))
                if zz > t and (lines - 1 - zz) + t == moment:
                    pl.when(z == zz)(functools.partial(add_on, 1, t))

    def last(write, step=32):
        for way, first in ((0, 0), (1, lines - 1)):

            @pl.when(z != first)
            def _():
                copy(way, z, False).wait_recv()

        def body(i, carry):
            at = pl.ds(pl.multiple_of(i * step, step), step)
            from_below = jnp.where(z > 0, up[z, at, :].astype(jnp.float32), 0.0)
            from_above = jnp.where(z < lines - 1, down[z, at, :].astype(jnp.float32), 0.0)
            write(i, parts[z, at, :].astype(jnp.float32) + from_below + from_above)
            return carry

        lax.fori_loop(0, parts.shape[1] // step, body, 0)
        for zz in range(lines):

            @pl.when(z == zz)
            def _():
                for t in range(lines):
                    if t > zz:
                        copy(0, t, zz == 0).wait_send()
                    if t < zz:
                        copy(1, t, zz == lines - 1).wait_send()

    return begin, hop, last


def column_cut(width):
    tiles = width // LANES
    return (tiles + 1) // 2 * LANES


def line_of(z, y, x, c, lines):
    return [device(lax.rem(z + k, lines), y, x, c) for k in range(1, lines)]


def reduce_plan(lines, prepare, p_ref, o_ref, held, corner_a, corner_b, from_side, from_over, along, send, recv):
    z, y, x, c = coordinates()
    parts = lines
    rows, width = held.shape[2], held.shape[3]
    cut = column_cut(width)
    first, second = pl.ds(0, cut), pl.ds(cut, width - cut)
    side, over, sibling = device(z, y, 1 - x, c), device(z, 1 - y, x, c), device(z, y, x, 1 - c)
    def given(part, yy, xx, cc):
        member = yy * 4 + xx * 2 + cc
        return p_ref.at[lax.rem(z + part + 1, lines), member]

    def make(part, kind, src, dst, to):
        return remote(src, dst, send.at[part, kind], recv.at[part, kind], to)

    lane = lambda part, yy, xx: held.at[part, yy * 2 + xx]

    def over_core(part):
        return [
            make(part, yy * 2 + xx, given(part, yy, xx, 1 - c), lane(part, yy, xx), sibling)
            for yy in range(2)
            for xx in range(2)
        ]

    def to_corner(part):
        return (
            make(part, 4, lane(part, 1 - y, 1 - x).at[:, first], corner_a.at[part], over),
            make(part, 5, lane(part, 1 - y, 1 - x).at[:, second], corner_b.at[part], side),
        )

    def to_neighbour(part, way):
        columns = (first, second)[way % 2]
        if way < 2:
            return make(part, 6 + way, lane(part, y, 1 - x).at[:, columns], from_side.at[part, :, columns], side)
        return make(part, 6 + way, lane(part, 1 - y, x).at[:, columns], from_over.at[part, :, columns], over)

    def along_z(part):
        to = lax.rem(z + part + 1, lines)
        return make(part, 10, lane(part, y, x), along.at[part], device(to, y, x, c))

    step = 16

    def add_core(part):
        for copy in over_core(part):
            copy.wait_recv()
        for yy, xx in ((1 - y, 1 - x), (y, 1 - x), (1 - y, x), (y, x)):
            mine, other = given(part, yy, xx, c), lane(part, yy, xx)

            def body(i, carry):
                at = pl.ds(pl.multiple_of(i * step, step), step)
                total = mine[at, :].astype(jnp.float32) + other[at, :].astype(jnp.float32)
                other[at, :] = total.astype(other.dtype)
                return carry

            lax.fori_loop(0, rows // step, body, 0)
        for copy in to_corner(part):
            copy.start()
        to_neighbour(part, 1).start()
        to_neighbour(part, 2).start()

    def add_corner(part):
        copies = to_corner(part)
        pairs = (
            (copies[0], lane(part, y, 1 - x), corner_a.at[part], first),
            (copies[1], lane(part, 1 - y, x), corner_b.at[part], second),
        )
        for copy, mine, other, columns in pairs:
            copy.wait_recv()

            def body(i, carry):
                at = pl.ds(pl.multiple_of(i * step, step), step)
                total = mine[at, columns].astype(jnp.float32) + other[at, :].astype(jnp.float32)
                mine[at, columns] = total.astype(mine.dtype)
                return carry

            lax.fori_loop(0, rows // step, body, 0)
        to_neighbour(part, 0).start()
        to_neighbour(part, 3).start()

    def add_neighbours(part):
        for way in range(4):
            to_neighbour(part, way).wait_recv()
        last = part == parts - 1
        mine = lane(part, y, x)

        def body(i, carry):
            at = pl.ds(pl.multiple_of(i * step, step), step)
            total = mine[at, :].astype(jnp.float32) + from_side[part, at, :].astype(jnp.float32)
            total += from_over[part, at, :].astype(jnp.float32)
            if last:
                o_ref[at, :] = total
            else:
                mine[at, :] = total.astype(mine.dtype)
            return carry

        lax.fori_loop(0, rows // step, body, 0)
        if not last:
            along_z(part).start()

    def ready(part):
        prepare(lax.rem(z + part + 1, lines))
        for copy in over_core(part):
            copy.start()

    kinds = (ready, add_core, add_corner, add_neighbours)

    def run(number):
        for lag, kind in enumerate(kinds):
            if 0 <= number - lag < parts:
                kind(number - lag)

    def last():
        for part in range(parts - 1):
            along_z(part).wait_recv()

        def body(i, carry):
            at = pl.ds(pl.multiple_of(i * step, step), step)
            total = o_ref[at, :]
            for part in range(parts - 1):
                total += along[part, at, :].astype(jnp.float32)
            o_ref[at, :] = total
            return carry

        lax.fori_loop(0, rows // step, body, 0)
        for part in range(parts - 1):
            along_z(part).wait_send()
        for part in range(parts):
            for copy in (*over_core(part), *to_corner(part), *(to_neighbour(part, way) for way in range(4))):
                copy.wait_send()

    return [functools.partial(run, number) for number in range(parts + len(kinds) - 1)], last


def reduce_scratch(lines, share, columns, low):
    cut = column_cut(columns)
    return [
        pltpu.VMEM((lines, PLANE, share, columns), low),
        pltpu.VMEM((lines, 4, share, columns), low),
        pltpu.VMEM((lines, share, cut), low),
        pltpu.VMEM((lines, share, columns - cut), low),
        pltpu.VMEM((lines, share, columns), low),
        pltpu.VMEM((lines, share, columns), low),
        pltpu.VMEM((lines - 1, share, columns), low),
        pltpu.SemaphoreType.DMA((lines, 11)),
        pltpu.SemaphoreType.DMA((lines, 11)),
    ]


def store_terms(p, block, start, value):
    members, share = p.shape[1:3]
    width = value.shape[1]
    p[block, :, :, start : start + width] = value.astype(p.dtype).reshape(members, share, width)


def halves(width):
    cut = column_cut(width)
    return pl.ds(0, cut), pl.ds(cut, width - cut)


class PlaneGather:
    def __init__(self, place, at, width, send, recv):
        z, y, x, c = place
        side, over, sibling = device(z, y, 1 - x, c), device(z, 1 - y, x, c), device(z, y, x, 1 - c)
        self.send, self.recv = send, recv
        own, next_x, next_y, corner = at(y, x), at(y, 1 - x), at(1 - y, x), at(1 - y, 1 - x)
        first, second = [lambda ref, of=of: ref.at[..., of] for of in halves(width)]
        self.table = (
            (first(own), side),
            (second(own), side),
            (first(own), over),
            (second(own), over),
            (own, sibling),
            (first(next_x), over),
            (second(next_y), side),
            (first(next_x), sibling),
            (second(next_x), sibling),
            (first(next_y), sibling),
            (second(next_y), sibling),
            (first(corner), sibling),
            (second(corner), sibling),
        )

    def copy(self, kind):
        ref, to = self.table[kind]
        return remote(ref, ref, self.send.at[kind], self.recv.at[kind], to)

    def begin(self):
        for kind in (0, 3, 4, 1, 2):
            self.copy(kind).start()

    def came(self, *kinds):
        for kind in kinds:
            self.copy(kind).wait_recv()

    def forward_on(self):
        for kind, onward in ((0, (5, 7)), (3, (6, 10)), (1, (8,)), (2, (9,))):
            self.came(kind)
            for other in onward:
                self.copy(other).start()

    def corner_on(self):
        for kind, onward in ((5, 11), (6, 12)):
            self.came(kind)
            self.copy(onward).start()

    def rest(self):
        self.came(4, *range(7, GATHER_KINDS))

    def drain(self):
        for kind in range(GATHER_KINDS):
            self.copy(kind).wait_send()


GATHER_KINDS = 13
REDUCE_KINDS = 10


def reduce_steps(place, at_rows, partial, held, corner_a, corner_b, from_side, from_over, send, recv):
    z, y, x, c = place
    side, over, sibling = device(z, y, 1 - x, c), device(z, 1 - y, x, c), device(z, y, x, 1 - c)
    first, second = halves(held.shape[-1])
    lane = lambda yy, xx: held.at[yy * 2 + xx, at_rows]
    next_x, next_y, corner = lane(y, 1 - x), lane(1 - y, x), lane(1 - y, 1 - x)

    def to_core(yy, xx):
        kind = yy * 2 + xx
        src = partial.at[yy * 4 + xx * 2 + 1 - c, at_rows]
        return remote(src, lane(yy, xx), send.at[kind], recv.at[kind], sibling)

    table = (
        (corner.at[:, first], corner_a.at[at_rows], over),
        (corner.at[:, second], corner_b.at[at_rows], side),
        (next_x.at[:, first], from_side.at[at_rows, first], side),
        (next_x.at[:, second], from_side.at[at_rows, second], side),
        (next_y.at[:, first], from_over.at[at_rows, first], over),
        (next_y.at[:, second], from_over.at[at_rows, second], over),
    )

    def copy(kind):
        src, dst, to = table[kind]
        return remote(src, dst, send.at[4 + kind], recv.at[4 + kind], to)

    return to_core, copy


def add_rows(target, other, columns=None, step=32):
    def body(i, carry):
        at = pl.ds(pl.multiple_of(i * step, step), step)
        mine = target[at, :] if columns is None else target[at, columns]
        total = (mine.astype(jnp.float32) + other[at, :].astype(jnp.float32)).astype(target.dtype)
        if columns is None:
            target[at, :] = total
        else:
            target[at, columns] = total
        return carry

    lax.fori_loop(0, other.shape[0] // step, body, 0)


def feed_forward_kernel(
    out_rows, attended, tokens, teacher_rows, out_grad_rows, valid, gains, gate_up_rows, down_rows,
    result_out, square, norm, hidden_grad, branch, attended_grad, down_final, down_out, gate_out, up_out,
    result, down_rest, gate_grad, up_grad, store_sem, out_w, gate_up_w, teacher, out_grad, down_w, down_up, down_down, normed_all, kept, mixed, grads_all, partial, held, corner_a, corner_b, from_side, from_over, hidden, total_grad, scales, squares,
    load_sem, here, line_send, line_recv, down_send, down_recv, gather_send, gather_recv, reduce_send, reduce_recv,
):
    place = coordinates()
    z, y, x, c = place
    width = tokens.shape[1]
    pairs = ((out_rows, out_w), (gate_up_rows, gate_up_w), (teacher_rows, teacher), (out_grad_rows, out_grad))
    loads = [pltpu.make_async_copy(src, dst, load_sem.at[i]) for i, (src, dst) in enumerate(pairs)]
    for load in loads:
        load.start()
    lines, units = down_w.shape[:2]
    greet([device(z, y, 1 - x, c), device(z, 1 - y, x, c), device(z, y, x, 1 - c)] + line_of(z, y, x, c, lines))
    rows = tokens.shape[0]
    share = lines * units
    first, second = halves(width)
    down_lines = [
        line_gather(
            place, lines, down_rows.at[:, of], lambda zz, of=of: down_w.at[zz, :, of],
            line_send.at[i], line_recv.at[i], here.at[i],
        )
        for i, of in enumerate((first, second))
    ]
    (begin_one, pass_one, last_one), (begin_two, pass_two, last_two) = down_lines
    begin_one()
    begin_two()
    mine = y * 4 + x * 2 + c
    chips = ((y, x), (y, 1 - x), (1 - y, x), (1 - y, 1 - x))

    gain = gains[1:2, :]
    count = jnp.sum(gains[2:3, :], -1, keepdims=True) / (width // (lines * PLANE))
    norm[...] = 2.0 / (count * width)
    loads[0].wait()
    hidden[...] = tokens[...].astype(jnp.float32) + jnp.dot(
        attended[...], out_w[...], preferred_element_type=jnp.float32
    )

    def norm_rows(at):
        values = hidden[at, :]
        scale = rms_scale(values)
        scales[at, :] = scale
        normed_all[mine, at, :] = (values * scale * gain[...]).astype(normed_all.dtype)

    parts = 2
    part_rows = rows // parts
    at_part = [pl.ds(part * part_rows, part_rows) for part in range(parts)]

    def of_part(part, body):
        by_rows(part_rows, lambda at: body(pl.ds(pl.multiple_of(part * part_rows + at.start, ROW_STEP), ROW_STEP)))

    class Phase(PlaneGather):
        def __init__(self, phase, part, whole):
            at_rows = at_part[part]
            self.part, self.at_rows = part, at_rows
            at = lambda yy, xx: whole.at[yy * 4 + xx * 2 + c, at_rows]
            super().__init__(place, at, width, gather_send.at[phase, part], gather_recv.at[phase, part])
            self.to_core, self.pass_on = reduce_steps(
                place, at_rows, partial, held, corner_a, corner_b, from_side, from_over,
                reduce_send.at[phase, part], reduce_recv.at[phase, part],
            )

        def join(self, yy, xx):
            self.to_core(yy, xx).wait_recv()
            add_rows(held.at[yy * 2 + xx, self.at_rows], partial.at[yy * 4 + xx * 2 + c, self.at_rows])

        def join_next(self, number):
            self.join(*chips[number])
            self.pass_on(2 + number).start()

        def join_corner(self):
            self.join(*chips[3])
            self.pass_on(0).start()
            self.pass_on(1).start()

        def add_corner(self):
            self.pass_on(0).wait_recv()
            add_rows(held.at[y * 2 + 1 - x, self.at_rows], corner_a.at[self.at_rows], first)
            self.pass_on(2).start()
            self.pass_on(1).wait_recv()
            add_rows(held.at[(1 - y) * 2 + x, self.at_rows], corner_b.at[self.at_rows], second)
            self.pass_on(5).start()

        def complete(self):
            for kind in (2, 3, 4, 5):
                self.pass_on(kind).wait_recv()
            for kind in range(6):
                self.pass_on(kind).wait_send()
            for yy, xx in chips:
                self.to_core(yy, xx).wait_send()

    def pair_of(number):
        yy, xx = chips[number]
        return pl.ds(yy * 4 + xx * 2, 2)

    one, two = [Phase(0, part, normed_all) for part in range(parts)]
    of_part(0, norm_rows)
    one.begin()
    of_part(1, norm_rows)

    def summed(at):
        total = held[y * 2 + x, at, :].astype(jnp.float32) + from_side[at, :].astype(jnp.float32)
        return total + from_over[at, :].astype(jnp.float32)

    def units_of(phase, number):
        where = (pair_of(number), phase.at_rows)
        both = jnp.dot(
            normed_all[where].reshape(rows, width), gate_up_w[...], preferred_element_type=jnp.float32
        )
        gate, up = both[:, :share], both[:, share:]
        sigmoid = 1.0 / (1.0 + jnp.exp(-gate))
        activated = gate * sigmoid
        slope = up * (sigmoid + activated * (1.0 - sigmoid))
        kept[(*where, slice(0, share))] = slope.astype(kept.dtype).reshape(2, part_rows, share)
        kept[(*where, slice(share, 2 * share))] = activated.astype(kept.dtype).reshape(2, part_rows, share)
        mixed[where] = (activated * up).astype(mixed.dtype).reshape(2, part_rows, share)

    def down_of(phase, number):
        where = (pair_of(number), phase.at_rows)
        out = jnp.dot(
            mixed[where].reshape(rows, share),
            down_w[...].reshape(share, width),
            preferred_element_type=jnp.float32,
        )
        partial[where] = out.astype(partial.dtype).reshape(2, part_rows, width)
        phase.to_core(*chips[number]).start()

    one.came(4)
    loads[1].wait()
    units_of(one, 0)
    pass_one(1)
    pass_two(1)
    one.forward_on()
    two.begin()
    for moment in range(2, lines - 1):
        pass_one(moment)
    one.came(7, 8)
    units_of(one, 1)
    for moment in range(2, lines - 1):
        pass_two(moment)
    one.came(9, 10)
    units_of(one, 2)
    pass_one(lines - 1)
    one.corner_on()
    two.came(4)
    units_of(two, 0)
    pass_two(lines - 1)
    last_one()
    last_two()
    two.forward_on()
    one.came(11, 12)
    units_of(one, 3)
    down_of(one, 1)
    two.came(7, 8)
    units_of(two, 1)
    down_of(one, 2)
    one.join_next(1)
    two.came(9, 10)
    units_of(two, 2)
    two.corner_on()
    down_of(one, 3)
    one.join_next(2)
    two.came(11, 12)
    units_of(two, 3)
    one.join_corner()
    down_of(two, 1)
    down_of(two, 2)
    two.join_next(1)
    down_of(one, 0)
    down_of(two, 3)
    two.join_next(2)
    one.join(*chips[0])
    one.add_corner()
    two.join_corner()
    down_of(two, 0)
    two.join(*chips[0])
    one.complete()
    loads[2].wait()
    loads[3].wait()

    def result_rows(at):
        values = hidden[at, :] + summed(at)
        result[at, :] = values.astype(result.dtype)
        differ = values - teacher[at, :].astype(jnp.float32)
        weighed = valid[at, :] * differ
        squares[at, :] = jnp.sum(weighed * differ, -1, keepdims=True)
        total = out_grad[at, :].astype(jnp.float32) + weighed * norm[...]
        total_grad[at, :] = total
        grads_all[mine, at, :] = total.astype(grads_all.dtype)

    def back_of(phase, number):
        where = (pair_of(number), phase.at_rows)
        mixed_grad = against(grads_all[where].reshape(rows, width), down_w[...].reshape(share, width))
        slope = kept[(*where, slice(0, share))].reshape(rows, share).astype(jnp.float32)
        activated = kept[(*where, slice(share, 2 * share))].reshape(rows, share).astype(jnp.float32)
        low_gate = (mixed_grad * slope).astype(kept.dtype)
        low_up = (mixed_grad * activated).astype(kept.dtype)
        kept[(*where, slice(0, share))] = low_gate.reshape(2, part_rows, share)
        kept[(*where, slice(share, 2 * share))] = low_up.reshape(2, part_rows, share)
        out = against(low_gate, gate_up_w[:, :share]) + against(low_up, gate_up_w[:, share:])
        partial[where] = out.astype(partial.dtype).reshape(2, part_rows, width)
        phase.to_core(*chips[number]).start()

    three, four = [Phase(1, part, grads_all) for part in range(parts)]
    of_part(0, result_rows)
    three.begin()
    two.add_corner()
    three.came(4)
    back_of(three, 0)
    two.complete()
    of_part(1, result_rows)
    square[...] = jnp.sum(squares[...], 0, keepdims=True)
    stores = transfers((result, down_rest, gate_grad, up_grad), (result_out, down_out, gate_out, up_out), store_sem)
    stores[0].start()
    three.forward_on()
    four.begin()
    three.came(7, 8)
    back_of(three, 1)
    three.came(9, 10)
    back_of(three, 2)
    three.join_next(1)
    four.came(4)
    back_of(four, 0)
    three.corner_on()
    three.join_next(2)
    three.came(11, 12)
    back_of(three, 3)
    four.forward_on()
    three.join_corner()
    four.came(7, 8)
    back_of(four, 1)
    three.join(*chips[0])
    four.came(9, 10)
    back_of(four, 2)
    four.join_next(1)
    four.corner_on()
    four.join_next(2)
    three.add_corner()
    four.came(11, 12)
    back_of(four, 3)
    four.join(*chips[0])
    four.join_corner()
    tokens_all = normed_all.shape[0] * rows
    block = 256

    def down_block(of, to):
        def run(i, carry):
            at = pl.ds(pl.multiple_of(i * block, block), block)
            left = mixed[:, :, at].reshape(tokens_all, block)
            grads = transposed(left, grads_all[:, :, of].reshape(tokens_all, of.size)).astype(to.dtype)
            per = block // units
            to[pl.ds(i * per, per)] = grads.reshape(per, units, of.size)
            return carry

        lax.fori_loop(0, share // block, run, 0)

    def both_block(i, carry):
        at = pl.ds(pl.multiple_of(i * block, block), block)
        left = normed_all[:, :, at].reshape(tokens_all, block)
        both = transposed(left, kept[...].reshape(tokens_all, 2 * share)).astype(gate_grad.dtype)
        gate_grad[at, :] = both[:, :share]
        up_grad[at, :] = both[:, share:]
        return carry

    down_parts = down_w.at[:, :, first]
    down_begin, down_hop, down_last = line_reduce(
        place, lines, down_parts, down_up, down_down, down_send, down_recv
    )
    down_block(first, down_parts)
    down_begin()
    down_block(second, down_rest)
    blocks = width // block
    third = blocks // 3
    lax.fori_loop(0, third, both_block, 0)
    three.complete()
    four.add_corner()
    down_hop(1)
    lax.fori_loop(third, 2 * third, both_block, 0)
    for moment in range(2, lines - 1):
        down_hop(moment)
    lax.fori_loop(2 * third, blocks, both_block, 0)
    for store in stores[1:]:
        store.start()

    def grad_rows(at):
        grads = summed(at)
        normed = hidden[at, :] * scales[at, :]
        scaled = grads * gain[...]
        values = total_grad[at, :] + scales[at, :] * (scaled - normed * jnp.mean(scaled * normed, -1, keepdims=True))
        hidden_grad[at, :] = values
        branch[at, :] = values.astype(branch.dtype)

    of_part(0, grad_rows)
    four.complete()
    of_part(1, grad_rows)
    attended_grad[...] = against(branch[...], out_w[...]).astype(attended_grad.dtype)


    def keep_down(i, sums):
        down_final[pl.ds(pl.multiple_of(i * 32, 32), 32), :] = sums

    down_last(keep_down)
    for phase in (one, two, three, four):
        phase.drain()
    for store in stores:
        store.wait()


def feed_forward(lines, out_rows, attended, tokens, teacher, out_grad, valid, gains, gate_up_w, down_rows, identity):
    rows, width = tokens.shape
    units = down_rows.shape[0]
    share = lines * units
    low = tokens.dtype
    shape = jax.ShapeDtypeStruct
    vmem, anywhere = pl.BlockSpec(memory_space=pltpu.VMEM), pl.BlockSpec(memory_space=pl.ANY)
    cut = column_cut(width)
    return pl.pallas_call(
        feed_forward_kernel,
        out_shape=[
            shape((rows, width), low),
            shape((1, 1), jnp.float32),
            shape((1, 1), jnp.float32),
            shape((rows, width), jnp.float32),
            shape((rows, width), low),
            shape((rows, width), low),
            shape((units, cut), jnp.float32),
            shape((lines, units, width - cut), low),
            shape((width, share), low),
            shape((width, share), low),
        ],
        in_specs=[anywhere, vmem, vmem, anywhere, anywhere, vmem, vmem, anywhere, anywhere],
        out_specs=[anywhere] + [vmem] * 6 + [anywhere] * 3,
        scratch_shapes=[
            pltpu.VMEM((rows, width), low),
            pltpu.VMEM((lines, units, width - cut), low),
            pltpu.VMEM((width, share), low),
            pltpu.VMEM((width, share), low),
            pltpu.SemaphoreType.DMA((4,)),
            pltpu.VMEM((width, width), low),
            pltpu.VMEM((width, 2 * share), low),
            pltpu.VMEM((rows, width), low),
            pltpu.VMEM((rows, width), low),
            pltpu.VMEM((lines, units, width), low),
            pltpu.VMEM((lines, units, cut), low),
            pltpu.VMEM((lines, units, cut), low),
            pltpu.VMEM((PLANE, rows, width), low),
            pltpu.VMEM((PLANE, rows, 2 * share), low),
            pltpu.VMEM((PLANE, rows, share), low),
            pltpu.VMEM((PLANE, rows, width), low),
            pltpu.VMEM((PLANE, rows, width), low),
            pltpu.VMEM((4, rows, width), low),
            pltpu.VMEM((rows, cut), low),
            pltpu.VMEM((rows, width - cut), low),
            pltpu.VMEM((rows, width), low),
            pltpu.VMEM((rows, width), low),
            pltpu.VMEM((rows, width), jnp.float32),
            pltpu.VMEM((rows, width), jnp.float32),
            pltpu.VMEM((rows, 1), jnp.float32),
            pltpu.VMEM((rows, 1), jnp.float32),
            pltpu.SemaphoreType.DMA((4,)),
            pltpu.SemaphoreType.DMA((2,)),
            pltpu.SemaphoreType.DMA((2, 2, lines)),
            pltpu.SemaphoreType.DMA((2, 2, lines)),
            pltpu.SemaphoreType.DMA((2, lines)),
            pltpu.SemaphoreType.DMA((2, lines)),
            pltpu.SemaphoreType.DMA((2, 2, GATHER_KINDS)),
            pltpu.SemaphoreType.DMA((2, 2, GATHER_KINDS)),
            pltpu.SemaphoreType.DMA((2, 2, REDUCE_KINDS)),
            pltpu.SemaphoreType.DMA((2, 2, REDUCE_KINDS)),
        ],
        compiler_params=pltpu.CompilerParams(collective_id=identity, vmem_limit_bytes=VMEM_LIMIT),
        cost_estimate=pl.CostEstimate(flops=40 * PLANE * rows * width * share // 2, bytes_accessed=30 * 2**20, transcendentals=0),
        name="feed_forward",
    )(out_rows, attended, tokens, teacher, out_grad, valid, gains, gate_up_w, down_rows)


HEAD_TILES = 3
ROW_STEP = 64


def by_rows(rows, body, step=ROW_STEP):
    def run(i, carry):
        body(pl.ds(pl.multiple_of(i * step, step), step))
        return carry

    lax.fori_loop(0, rows // step, run, 0)


def lanes_of(values):
    return lax.broadcasted_iota(jnp.int32, values.shape, len(values.shape) - 1)


def turned(tile, cosine, sine):
    half = HD // 2
    partner = jnp.where(lanes_of(tile) < half, -pltpu.roll(tile, LANES - half, 1), pltpu.roll(tile, half, 1))
    return tile * cosine + partner * sine


def packed_pair(first, second, even):
    lane = lanes_of(first)
    moved = pltpu.roll(second, HD, 1)
    full_even = jnp.where(lane < HD, first, moved)
    full_odd = jnp.where(lane < 32, pltpu.roll(first, 64, 1), pltpu.roll(second, 32, 1))
    return jnp.where(even, full_even, full_odd), jnp.where(even, moved, first)


def unpacked_pair(full, part, even):
    lane = lanes_of(full)
    zero = jnp.zeros_like(full)
    first_even = jnp.where(lane < HD, full, zero)
    second_even = jnp.where(lane < 32, pltpu.roll(full, 32, 1), jnp.where(lane < HD, pltpu.roll(part, 32, 1), zero))
    first_odd = jnp.where(lane < 64, part, jnp.where(lane < HD, pltpu.roll(full, 64, 1), zero))
    second_odd = jnp.where(lane < HD, pltpu.roll(full, HD, 1), zero)
    return jnp.where(even, first_even, first_odd), jnp.where(even, second_even, second_odd)


def keys_and_values(qkv, keys, values, count, rows):
    def body(src, carry):
        block = qkv[src].astype(jnp.float32)
        tiles = [block[:, i * LANES : (i + 1) * LANES] for i in range(HEAD_TILES)]
        lane = lanes_of(tiles[0])
        key = jnp.where(lane < HD, tiles[2], 0.0)
        value = jnp.where(lane < 64, pltpu.roll(tiles[1], 64, 1), pltpu.roll(tiles[2], HD, 1))
        value = jnp.where(lane < 32, pltpu.roll(tiles[0], 32, 1), value)
        value = jnp.where(lane < HD, value, 0.0)
        at = pl.ds(pl.multiple_of(src * rows, rows), rows)
        for half in range(2):
            keys[half, at, :] = key[half * rows : (half + 1) * rows].astype(keys.dtype)
            values[half, at, :] = value[half * rows : (half + 1) * rows].astype(values.dtype)
        return carry

    lax.fori_loop(0, count, body, 0)


def segment_of(lengths, place):
    start, end = jnp.zeros_like(place), 0
    for length in [lengths[0, j] for j in range(NSEQ)]:
        end = end + length
        start = start + jnp.where(place >= end, length, 0)
    return start, end


def side_by_side(heads):
    full, part = packed_pair(heads[0], heads[1], True)
    full_odd, part_odd = packed_pair(heads[2], heads[3], False)
    middle = jnp.where(lanes_of(part) < 64, part, pltpu.roll(part_odd, 64, 1))
    return full, middle, full_odd


def apart(ref, group):
    start = group * HEAD_TILES * LANES
    tiles = [ref[:, start + i * LANES : start + (i + 1) * LANES].astype(jnp.float32) for i in range(HEAD_TILES)]
    return unpacked_pair(tiles[0], tiles[1], True) + unpacked_pair(tiles[2], pltpu.roll(tiles[1], 64, 1), False)


def arrange_rows(rows_in, w_query, w_key, w_value, gain_rows, count):
    share = rows_in.shape[0]
    groups = HEADS // KV
    queries = [head for group in range(HEADS // 4) for head in apart(w_query, group)]
    keys = [head for group in range(KV // 4) for head in apart(w_key, group)]
    values = [head for group in range(KV // 4) for head in apart(w_value, group)]
    lane = lanes_of(keys[0])
    for head in range(KV):
        for number, tile in enumerate(queries[head * groups : (head + 1) * groups] + [keys[head]]):
            third = pltpu.roll(values[head], HD - 32 * number, 1)
            start = (head * HEAD_TILES + number) * LANES
            rows_in[:, start : start + LANES] = jnp.where(lane < HD, tile, third).astype(rows_in.dtype)
    row = lax.broadcasted_iota(jnp.int32, (LANES, LANES), 0)
    columns = jnp.where(row == 0, gain_rows[0:1, :], jnp.where(row == 1, gain_rows[1:2, :], 0.0))
    columns = jnp.where(row == 2, count, columns)
    rows_in[:, KV * HEAD_TILES * LANES :] = jnp.transpose(columns)[:share, :].astype(rows_in.dtype)


def attend_kernel(
    scale, lines, w_query, w_key, w_value, w_gate, w_up, out_rows, gain_rows, freq, mask, deal, lengths, tokens,
    attended, normed, gains, cosine, sine, valid, weights, out_w, unit_w, qkv_out, probs,
    rows_in, unit_rows, w, place_row, sent, qkv, keys, values, prob_blocks, o_sent, o_came,
    send, recv, o_send, o_recv, p_sem, q_sem, w_sem, w_line_send, w_line_recv, w_send, w_recv, w_here, g_send, g_recv, g_here,
    o_line_send, o_line_recv,
    u_send, u_recv, u_here, l_send, l_recv,
):
    z, y, x, c = coordinates()
    count = sent.shape[0]
    me = z * 2 + y
    even = y == 0
    rows, width = tokens.shape
    half_rows = rows // 2
    head_cols = HEAD_TILES * LANES
    to_device = lambda i: (i, x * 2 + c)
    peer = lambda k: lax.rem(me + k, count)

    member = y * 4 + x * 2 + c
    in_plane = lambda i: (z * 2 + i // 4, i % 4)
    unit_peer = lambda k: lax.rem(member + k, PLANE)
    others = [device(z, yy, xx, cc) for yy, xx, cc in ((y, 1 - x, c), (y, x, 1 - c), (y, 1 - x, 1 - c))]
    others += [device(z, 1 - y, xx, cc) for xx, cc in ((1 - x, c), (x, 1 - c), (1 - x, 1 - c))]
    units = w_gate.shape[1] // (lines * PLANE)
    for i in range(PLANE):
        for zz in range(lines):
            start = (zz * PLANE + i) * units
            unit_rows[i, :, zz * units : (zz + 1) * units] = w_gate[:, start : start + units]
            unit_rows[i, :, (lines + zz) * units : (lines + zz + 1) * units] = w_up[:, start : start + units]
    greet([to_device(peer(k)) for k in range(1, count)] + others)

    def unit_out(k):
        i = unit_peer(k)
        return remote(unit_rows.at[i], unit_w.at[z, member], u_send.at[k], u_recv.at[k], in_plane(i))

    unit_own = pltpu.make_async_copy(unit_rows.at[member], unit_w.at[z, member], u_here)
    unit_own.start()
    columns = rows_in.shape[1]
    line_gathers, plane_gathers = [], []
    for part, of in enumerate(halves(columns)):
        line_gathers.append(
            line_gather(
                (z, y, x, c), lines, rows_in.at[:, of], lambda zz, of=of: w.at[zz, member, :, of],
                w_line_send.at[part], w_line_recv.at[part], w_here.at[part],
            )
        )
        plane_gathers.append(
            PlaneGather(
                (z, y, x, c), lambda yy, xx, of=of: w.at[:, yy * 4 + xx * 2 + c, :, of], of.size,
                w_send.at[part], w_recv.at[part],
            )
        )
    (one_begin, one_pass, one_last), (two_begin, two_pass, two_last) = line_gathers
    one, two = plane_gathers
    out_begin, out_pass, out_last = line_gather(
        (z, y, x, c), lines, out_rows, lambda zz: out_w.at[zz, member], o_line_send, o_line_recv, g_here
    )
    out_gather = PlaneGather(
        (z, y, x, c), lambda yy, xx: out_w.at[:, yy * 4 + xx * 2 + c], out_rows.shape[1], g_send, g_recv
    )
    line_begin, line_pass, line_last = line_gather(
        (z, y, x, c), lines, unit_w.at[z], lambda zz: unit_w.at[zz], l_send, l_recv
    )
    for k in range(1, PLANE):
        unit_out(k).start()
    first_block = deal[0, me]
    total = functools.reduce(lambda a, b: a + b, [lengths[0, j] for j in range(NSEQ)])
    token = lax.broadcasted_iota(jnp.int32, (1, rows), 1)
    in_pack = jnp.where(token < half_rows, first_block * half_rows, (2 * count - 2 - first_block) * half_rows) + token
    counted = jnp.where(in_pack < total, mask[...].astype(jnp.float32), 0.0)
    arrange_rows(rows_in, w_query, w_key, w_value, gain_rows, jnp.sum(counted, -1, keepdims=True))
    one_begin()
    valid[...] = jnp.transpose(jnp.broadcast_to(counted, (LANES, rows)))[:, :1]
    token = lax.broadcasted_iota(jnp.int32, (rows, 1), 0)
    in_pack = jnp.where(token < half_rows, first_block * half_rows, (2 * count - 2 - first_block) * half_rows) + token
    angle = (in_pack - segment_of(lengths, in_pack)[0]).astype(jnp.float32) * freq[...]
    cosine[...] = jnp.cos(angle)
    sine[...] = jnp.sin(angle)
    one_pass(1)
    two_begin()
    for moment in range(2, lines):
        one_pass(moment)
        two_pass(moment - 1)
    one_last()
    one.begin()
    two_pass(lines - 1)
    two_last()
    unit_own.wait()
    for k in range(1, PLANE):
        unit_out(k).wait_recv()
    line_begin()
    out_begin()
    one.forward_on()
    two.begin()
    for moment in range(1, lines - 1):
        out_pass(moment)
    one.corner_on()
    out_pass(lines - 1)
    out_last()
    two.forward_on()
    line_pass(1)
    one.rest()
    two.corner_on()
    two.rest()
    keep_weights = pltpu.make_async_copy(w, weights, w_sem)
    keep_weights.start()

    def columns_of(start, size):
        return w[:, :, :, pl.ds(start, size)].reshape(width, size)

    extras = columns_of(count * head_cols, LANES)
    gains[...] = jnp.transpose(extras.astype(jnp.float32))[: gains.shape[0], :]
    gain = gains[0:1, :]

    def norm_rows(at):
        values_at = tokens[at, :].astype(jnp.float32)
        normed[at, :] = (values_at * rms_scale(values_at) * gain).astype(normed.dtype)

    by_rows(rows, norm_rows)

    def out(k):
        return remote(sent.at[peer(k)], qkv.at[me], send.at[k], recv.at[k], to_device(peer(k)))

    def project(k, carry):
        i = peer(k)
        columns = columns_of(pl.multiple_of(i * head_cols, LANES), head_cols)
        both = jnp.dot(normed[...], columns, preferred_element_type=jnp.float32)
        for tile in range(HEAD_TILES):
            at = slice(tile * LANES, (tile + 1) * LANES)
            sent[i, :, at] = turned(both[:, at], cosine[...], sine[...]).astype(sent.dtype)

        @pl.when(k < count)
        def _():
            out(k).start()

        return carry

    lax.fori_loop(1, count + 1, project, 0)
    out_gather.begin()
    line_pass(2)
    qkv[me] = sent[me]
    for src in range(count):
        columns = slice(src * half_rows, (src + 1) * half_rows)
        steps = lax.broadcasted_iota(jnp.int32, (1, half_rows), 1)
        place_row[0, :, columns] = deal[0, src] * half_rows + steps
        place_row[1, :, columns] = (2 * count - 1 - deal[0, src]) * half_rows + steps

    def arrive(k, carry):
        out(k).wait_recv()
        return carry

    out_gather.forward_on()
    out_gather.corner_on()
    lax.fori_loop(1, count, arrive, 0)
    keep_qkv = pltpu.make_async_copy(qkv, qkv_out, q_sem)
    keep_qkv.start()
    keys_and_values(qkv, keys, values, count, half_rows)

    def back(k):
        return remote(o_sent.at[peer(k)], o_came.at[me], o_send.at[k], o_recv.at[k], to_device(peer(k)))

    def keep(src, half):
        return pltpu.make_async_copy(prob_blocks.at[src, half], probs.at[src, half], p_sem.at[src, half])

    def attend(k, carry):
        src = peer(k)
        halves_out = []
        for half in range(2):
            at = pl.ds(half * half_rows, half_rows)
            queries = jnp.concatenate([qkv[src, at, :LANES], qkv[src, at, LANES : 2 * LANES]], 0)
            score = against(queries, keys[half]) * scale
            first = deal[0, src]
            block = first if half == 0 else 2 * count - 1 - first
            own = block * half_rows + lax.broadcasted_iota(jnp.int32, (half_rows, 1), 0)
            start, end = segment_of(lengths, own)
            lowest = jnp.where(own < end, start, own)
            place = place_row[half]
            allowed = (place >= lowest) & (place <= own)
            bias = jnp.where(allowed, 0.0, masked_score)
            score = score + jnp.concatenate([bias, bias], 0)
            top = jnp.max(score, -1, keepdims=True)
            weight = jnp.exp(score - top)
            total = jnp.sum(weight, -1, keepdims=True)
            low = (weight * (1.0 / total)).astype(prob_blocks.dtype)
            prob_blocks[src, half] = low
            keep(src, half).start()
            summed = jnp.dot(low, values[half], preferred_element_type=jnp.float32)
            full, part = packed_pair(summed[:half_rows], summed[half_rows:], even)
            o_sent[src, at, :] = full.astype(o_sent.dtype)
            halves_out.append(part)
        lane = lanes_of(halves_out[0])
        part = jnp.where(lane < 64, halves_out[0], pltpu.roll(halves_out[1], 64, 1))
        o_sent[src, pl.ds(rows, half_rows), :] = part.astype(o_sent.dtype)

        @pl.when(k < count)
        def _():
            back(k).start()

        return carry

    lax.fori_loop(1, count + 1, attend, 0)
    o_came[me] = o_sent[me]

    def return_arrive(k, carry):
        back(k).wait_recv()
        return carry

    lax.fori_loop(1, count, return_arrive, 0)
    for pair in range(count // 2):
        at = pair * head_cols
        attended[:, at : at + LANES] = o_came[2 * pair, :rows, :]
        attended[:, at + 2 * LANES : at + 3 * LANES] = o_came[2 * pair + 1, :rows, :]
        one = o_came[2 * pair, rows:, :].astype(jnp.float32)
        two = o_came[2 * pair + 1, rows:, :].astype(jnp.float32)
        lane = lanes_of(one)
        middle = slice(at + LANES, at + 2 * LANES)
        attended[:half_rows, middle] = jnp.where(lane < 64, one, pltpu.roll(two, 64, 1)).astype(attended.dtype)
        attended[half_rows:, middle] = jnp.where(lane < 64, pltpu.roll(one, 64, 1), two).astype(attended.dtype)

    def drain(k, carry):
        out(k).wait_send()
        back(k).wait_send()
        return carry

    lax.fori_loop(1, count, drain, 0)

    def drain_probs(src, carry):
        keep(src, 0).wait()
        keep(src, 1).wait()
        return carry

    lax.fori_loop(0, count, drain_probs, 0)
    keep_qkv.wait()
    out_gather.rest()
    for gather in (out_gather, *plane_gathers):
        gather.drain()
    for moment in range(3, lines):
        line_pass(moment)
    line_last()
    for k in range(1, PLANE):
        unit_out(k).wait_send()
    keep_weights.wait()


def attend(scale, lines, w_query, w_key, w_value, w_gate, w_up, out_rows, gain_rows, freq, mask, deal, lengths, tokens, identity):
    rows, width = tokens.shape
    share, units = out_rows.shape[0], w_gate.shape[1] // PLANE
    count = KV
    columns = count * HEAD_TILES * LANES + LANES
    half_rows = rows // 2
    half = count * half_rows
    head_cols = HEAD_TILES * LANES
    low = tokens.dtype
    shape = jax.ShapeDtypeStruct
    vmem, anywhere = pl.BlockSpec(memory_space=pltpu.VMEM), pl.BlockSpec(memory_space=pl.ANY)
    smem = pl.BlockSpec(memory_space=pltpu.SMEM)
    dma = pltpu.SemaphoreType.DMA
    return pl.pallas_call(
        functools.partial(attend_kernel, scale, lines),
        out_shape=[
            shape((rows, width), low),
            shape((rows, width), low),
            shape((8, width), jnp.float32),
            shape((rows, LANES), jnp.float32),
            shape((rows, LANES), jnp.float32),
            shape((rows, 1), jnp.float32),
            shape((lines, PLANE, share, columns), low),
            shape((lines, PLANE) + out_rows.shape, low),
            shape((lines, PLANE, share, 2 * units), low),
            shape((count, rows, head_cols), low),
            shape((count, 2, rows, half), low),
        ],
        in_specs=[vmem] * 5 + [anywhere] + [vmem] * 3 + [smem, smem, vmem],
        out_specs=[vmem] * 6 + [anywhere] * 5,
        scratch_shapes=[
            pltpu.VMEM((share, columns), low),
            pltpu.VMEM((PLANE, share, 2 * units), low),
            pltpu.VMEM((lines, PLANE, share, columns), low),
            pltpu.VMEM((2, 1, half), jnp.int32),
            pltpu.VMEM((count, rows, head_cols), low),
            pltpu.VMEM((count, rows, head_cols), low),
            pltpu.VMEM((2, half, LANES), low),
            pltpu.VMEM((2, half, LANES), low),
            pltpu.VMEM((count, 2, rows, half), low),
            pltpu.VMEM((count, rows + half_rows, LANES), low),
            pltpu.VMEM((count, rows + half_rows, LANES), low),
            dma((count,)),
            dma((count,)),
            dma((count,)),
            dma((count,)),
            dma((count, 2)),
            dma,
            dma,
            dma((2, 2, lines)),
            dma((2, 2, lines)),
            dma((2, GATHER_KINDS)),
            dma((2, GATHER_KINDS)),
            dma((2,)),
            dma((GATHER_KINDS,)),
            dma((GATHER_KINDS,)),
            dma,
            dma((2, lines)),
            dma((2, lines)),
            dma((PLANE,)),
            dma((PLANE,)),
            dma,
            dma((2, lines)),
            dma((2, lines)),
        ],
        compiler_params=pltpu.CompilerParams(collective_id=identity, vmem_limit_bytes=VMEM_LIMIT),
        name="attend",
    )(w_query, w_key, w_value, w_gate, w_up, out_rows, gain_rows, freq, mask, deal, lengths, tokens)


def attend_back_kernel(
    scale, lines, attended_grad, probs, cosine, sine, qkv_in, attended_in, branch_in, gate_in, down_in,
    qkv_grad, out_final, gate_sums, down_final,
    qkv, attended, branch, gate_parts, down_parts, in_sem,
    sent, came, keys, values, prob_blocks, dk_sum, dv_sum, back_sent, back_came,
    send, recv, back_send, back_recv, p_sem, up, down, l_send, l_recv, down_up, down_down, d_send, d_recv, p, *reducing,
):
    z, y, x, c = coordinates()
    count = sent.shape[0]
    me = z * 2 + y
    even = y == 0
    rows, width = attended_grad.shape
    half_rows = rows // 2
    head_cols = HEAD_TILES * LANES
    to_device = lambda i: (i, x * 2 + c)
    peer = lambda k: lax.rem(me + k, count)
    source = lambda k: lax.rem(me + count - k, count)

    loads = transfers(
        (attended_in, branch_in, qkv_in, gate_in, down_in), (attended, branch, qkv, gate_parts, down_parts), in_sem
    )
    for load_in in loads:
        load_in.start()

    def load(src, half):
        return pltpu.make_async_copy(probs.at[src, half], prob_blocks.at[src, half], p_sem.at[src, half])

    def load_start(k, carry):
        load(source(k), 0).start()
        load(source(k), 1).start()
        return carry

    lax.fori_loop(0, count, load_start, 0)
    greet([to_device(peer(k)) for k in range(1, count)] + [device(z, y, 1 - x, c), device(z, y, x, 1 - c)])
    members, share = p.shape[1:3]

    def prepare(block):
        at = pl.ds(pl.multiple_of(block * members * share, LANES), members * share)
        store_terms(p, block, 0, transposed(attended[:, at], branch[...]))

    reduce_stages, reduce_last = reduce_plan(lines, prepare, p, out_final, *reducing)
    line_begin, line_hop, line_last = line_reduce((z, y, x, c), lines, gate_parts, up, down, l_send, l_recv)
    down_begin, down_hop, down_last = line_reduce((z, y, x, c), lines, down_parts, down_up, down_down, d_send, d_recv)
    for pair in range(count // 2):
        at = pair * head_cols
        sent[2 * pair, :rows, :] = attended_grad[:, at : at + LANES]
        sent[2 * pair + 1, :rows, :] = attended_grad[:, at + 2 * LANES : at + 3 * LANES]
        middle = attended_grad[:, at + LANES : at + 2 * LANES].astype(jnp.float32)
        one, two = middle[:half_rows], middle[half_rows:]
        lane = lanes_of(one)
        sent[2 * pair, rows:, :] = jnp.where(lane < 64, one, pltpu.roll(two, 64, 1)).astype(sent.dtype)
        sent[2 * pair + 1, rows:, :] = jnp.where(lane < 64, pltpu.roll(one, 64, 1), two).astype(sent.dtype)

    def out(k):
        return remote(sent.at[peer(k)], came.at[me], send.at[k], recv.at[k], to_device(peer(k)))

    def begin(k, carry):
        out(k).start()
        return carry

    lax.fori_loop(1, count, begin, 0)
    for load_in in loads[:2]:
        load_in.wait()
    reduce_stages[0]()
    came[me] = sent[me]
    for load_in in loads[2:]:
        load_in.wait()
    keys_and_values(qkv, keys, values, count, half_rows)
    dk_sum[...] = jnp.zeros_like(dk_sum)
    dv_sum[...] = jnp.zeros_like(dv_sum)

    def grads(k, carry):
        src = source(k)

        @pl.when(k > 0)
        def _():
            out(k).wait_recv()

        for half in range(2):
            at = pl.ds(half * half_rows, half_rows)
            full = came[src, at, :].astype(jnp.float32)
            part = came[src, pl.ds(rows, half_rows), :].astype(jnp.float32)
            if half:
                part = pltpu.roll(part, 64, 1)
            pair = jnp.concatenate(unpacked_pair(full, part, even), 0).astype(came.dtype)
            queries = jnp.concatenate([qkv[src, at, :LANES], qkv[src, at, LANES : 2 * LANES]], 0)
            load(src, half).wait()
            low = prob_blocks[src, half]
            prob = low.astype(jnp.float32)
            prob_grad = against(pair, values[half])
            delta = jnp.sum(prob * prob_grad, -1, keepdims=True)
            score_low = (prob * (prob_grad - delta)).astype(low.dtype)
            dq = jnp.dot(score_low, keys[half], preferred_element_type=jnp.float32) * scale
            back_sent[src, at, :LANES] = dq[:half_rows].astype(back_sent.dtype)
            back_sent[src, at, LANES : 2 * LANES] = dq[half_rows:].astype(back_sent.dtype)
            dk_sum[half] += transposed(score_low, queries)
            dv_sum[half] += transposed(low, pair)
        pl.when(k == 2)(line_begin)
        pl.when(k == 5)(down_begin)
        for number in range(1, len(reduce_stages)):
            pl.when(k == number)(reduce_stages[number])
        return carry

    lax.fori_loop(0, count, grads, 0)

    def back(k):
        return remote(back_sent.at[peer(k)], back_came.at[me], back_send.at[k], back_recv.at[k], to_device(peer(k)))

    def finish(k, carry):
        src = peer(k)
        in_half = pl.ds(pl.multiple_of(src * half_rows, half_rows), half_rows)
        for half in range(2):
            at = pl.ds(half * half_rows, half_rows)
            dk = dk_sum[half, in_half, :] * scale
            dv = dv_sum[half, in_half, :]
            lane = lanes_of(dk)
            for tile in range(HEAD_TILES):
                columns = slice(tile * LANES, (tile + 1) * LANES)
                head = dk if tile == 2 else back_sent[src, at, columns].astype(jnp.float32)
                third = pltpu.roll(dv, HD - 32 * tile, 1)
                back_sent[src, at, columns] = jnp.where(lane < HD, head, third).astype(back_sent.dtype)

        @pl.when(k < count)
        def _():
            back(k).start()

        return carry

    lax.fori_loop(1, count + 1, finish, 0)
    for moment in range(1, lines - 1):
        line_hop(moment)
        down_hop(moment)
    reduce_last()
    back_came[me] = back_sent[me]

    def turn_back(k, carry):
        src = source(k)

        @pl.when(k > 0)
        def _():
            back(k).wait_recv()

        for tile in range(HEAD_TILES):
            columns = slice(tile * LANES, (tile + 1) * LANES)
            values_at = back_came[src, :, columns].astype(jnp.float32)
            turned_at = turned(values_at, cosine[...], -sine[...])
            at = pl.ds(pl.multiple_of(src * head_cols + tile * LANES, LANES), LANES)
            qkv_grad[:, at] = turned_at.astype(qkv_grad.dtype)
        return carry

    lax.fori_loop(0, count, turn_back, 0)

    def keep_sums(i, sums):
        gate_sums[i] = sums.astype(gate_sums.dtype)

    line_last(keep_sums, gate_sums.shape[1])

    def keep_down(i, sums):
        down_final[pl.ds(pl.multiple_of(i * 32, 32), 32), :] = sums

    down_last(keep_down)

    def drain(k, carry):
        out(k).wait_send()
        back(k).wait_send()
        return carry

    lax.fori_loop(1, count, drain, 0)


def attend_back(scale, lines, attended_grad, qkv, probs, tables, attended, branch, gate_parts, down_parts, identity):
    rows, width = attended_grad.shape
    count, _, head_cols = qkv.shape
    half = probs.shape[-1]
    half_rows = rows // 2
    share = width // (lines * PLANE)
    low = attended_grad.dtype
    vmem, anywhere = pl.BlockSpec(memory_space=pltpu.VMEM), pl.BlockSpec(memory_space=pl.ANY)
    dma = pltpu.SemaphoreType.DMA
    return pl.pallas_call(
        functools.partial(attend_back_kernel, scale, lines),
        out_shape=[
            jax.ShapeDtypeStruct((rows, count * head_cols), low),
            jax.ShapeDtypeStruct((share, width), jnp.float32),
            jax.ShapeDtypeStruct((PLANE, share, gate_parts.shape[2]), low),
            jax.ShapeDtypeStruct(down_parts.shape[1:], jnp.float32),
        ],
        in_specs=[vmem, anywhere, vmem, vmem] + [anywhere] * 5,
        out_specs=[vmem] * 4,
        scratch_shapes=[
            pltpu.VMEM(qkv.shape, low),
            pltpu.VMEM(attended.shape, low),
            pltpu.VMEM(branch.shape, low),
            pltpu.VMEM(gate_parts.shape, low),
            pltpu.VMEM(down_parts.shape, low),
            dma((5,)),
            pltpu.VMEM((count, rows + half_rows, LANES), low),
            pltpu.VMEM((count, rows + half_rows, LANES), low),
            pltpu.VMEM((2, half, LANES), low),
            pltpu.VMEM((2, half, LANES), low),
            pltpu.VMEM((count, 2, rows, half), low),
            pltpu.VMEM((2, half, LANES), jnp.float32),
            pltpu.VMEM((2, half, LANES), jnp.float32),
            pltpu.VMEM((count, rows, head_cols), low),
            pltpu.VMEM((count, rows, head_cols), low),
            dma((count,)),
            dma((count,)),
            dma((count,)),
            dma((count,)),
            dma((count, 2)),
            pltpu.VMEM(gate_parts.shape, low),
            pltpu.VMEM(gate_parts.shape, low),
            dma((2, lines)),
            dma((2, lines)),
            pltpu.VMEM(down_parts.shape, low),
            pltpu.VMEM(down_parts.shape, low),
            dma((2, lines)),
            dma((2, lines)),
            *reduce_scratch(lines, share, width, low),
        ],
        compiler_params=pltpu.CompilerParams(collective_id=identity, vmem_limit_bytes=VMEM_LIMIT),
        name="attend_back",
    )(attended_grad, probs, *tables, qkv, attended, branch, gate_parts, down_parts)


def finish_kernel(
    weights, normed, qkv_grad, gains, square, norm, up_parts, gate_sums, hidden_in, tokens_in, gate_in, up_in,
    input_grad, query_final, key_final, value_final, gate_final, up_final, gain_final, loss,
    hidden_grad, tokens, w_gate, w_up, in_sem, w, own_rows, normed_grad, final, up_sums, gate_came, up_came, line_up, line_down,
    w_sem, own_sem, gate_send, gate_recv, up_send, up_recv, here, l_send, l_recv, p, *reducing,
):
    z, y, x, c = coordinates()
    lines, members, share = p.shape[:3]
    rows, width = tokens.shape
    qkv_cols = qkv_grad.shape[1]
    low = normed.dtype
    load = pltpu.make_async_copy(weights.at[:, pl.ds(0, qkv_cols)], w, w_sem)
    load.start()
    loads = transfers((hidden_in, tokens_in, gate_in, up_in), (hidden_grad, tokens, w_gate, w_up), in_sem)
    for load_in in loads:
        load_in.start()
    number = (z * 2 + y) * 4 + x * 2 + c
    own_at = pl.ds(pl.multiple_of(number * share, 16), share)
    load_own = pltpu.make_async_copy(weights.at[own_at, :], own_rows, own_sem)
    load_own.start()
    me = y * 4 + x * 2 + c
    peer = lambda k: lax.rem(me + k, members)
    member = lambda i: (z * 2 + i // 4, i % 4)
    greet([member(peer(k)) for k in range(1, members)] + line_of(z, y, x, c, lines))

    def out(kind, k):
        src, came, send, recv = (
            (gate_sums, gate_came, gate_send, gate_recv),
            (up_sums, up_came, up_send, up_recv),
        )[kind]
        return remote(src.at[peer(k)], came.at[me], send.at[k], recv.at[k], member(peer(k)))

    gate_own = pltpu.make_async_copy(gate_sums.at[me], gate_came.at[me], here)
    gate_own.start()
    for k in range(1, members):
        out(0, k).start()
    line_begin, line_hop, line_last = line_reduce((z, y, x, c), lines, up_parts, line_up, line_down, l_send, l_recv)
    line_begin()

    def keep_up(i, sums):
        up_sums[i] = sums.astype(up_sums.dtype)

    devices = lines * PLANE
    place = lax.broadcasted_iota(jnp.int32, (1, LANES), 1) - number
    rest = square[...]
    loss_terms = jnp.zeros((1, LANES), jnp.float32)
    for term in range(3):
        top = rest.astype(low).astype(jnp.float32)
        loss_terms = loss_terms + jnp.where(place == term * devices, top, 0.0)
        rest = rest - top

    def prepare(block):
        at = pl.ds(pl.multiple_of(block * members * share, LANES), members * share)
        left = normed[:, at]
        chunk = qkv_cols // 2
        for start in range(0, qkv_cols, chunk):
            store_terms(p, block, start, transposed(left, qkv_grad[:, start : start + chunk]))
        store_terms(p, block, qkv_cols, jnp.broadcast_to(loss_terms, (members * share, LANES)))

    stages, last = reduce_plan(lines, prepare, p, final, *reducing)

    def grad_rows(at):
        values = tokens[at, :].astype(jnp.float32)
        scale = rms_scale(values)
        unit = values * scale
        scaled = normed_grad[at, :] * gains[0:1, :]
        input_grad[at, :] = hidden_grad[at, :] + scale * (
            scaled - unit * jnp.mean(scaled * unit, -1, keepdims=True)
        )

    block = rows // lines
    for index, stage in enumerate(stages):
        if index == 2:
            load.wait()
            for load_in in loads:
                load_in.wait()
        if 2 <= index < lines:
            line_hop(index - 1)
        if index == 1 + lines:
            line_last(keep_up, share)
            for k in range(1, members):
                out(1, k).start()
        stage()
        if 2 <= index < 2 + lines:
            at = slice((index - 2) * block, (index - 1) * block)
            normed_grad[at, :] = against(qkv_grad[at, :], w[...])
        if index == 2 + lines:
            by_rows(rows, grad_rows)
    up_came[me] = up_sums[me]
    gate_own.wait()
    for kind in range(2):
        for k in range(1, members):
            out(kind, k).wait_recv()
    units = gate_came.shape[2] // lines
    for i in range(members):
        for zz in range(lines):
            to = slice((zz * members + i) * units, (zz * members + i + 1) * units)
            of = slice(zz * units, (zz + 1) * units)
            gate_final[:, to] = gate_came[i, :, of].astype(jnp.float32)
            up_final[:, to] = up_came[i, :, of].astype(jnp.float32)
    last()

    def tile(head, number):
        start = (head * HEAD_TILES + number) * LANES
        return final[:, start : start + LANES]

    def put(ref, group, heads):
        for number, value in enumerate(side_by_side(heads)):
            start = (group * HEAD_TILES + number) * LANES
            ref[:, start : start + LANES] = value

    for pair in range(KV // 2):
        put(query_final, pair, [tile(2 * pair + i, j) for i in range(2) for j in range(2)])
    for group in range(KV // 4):
        heads = [4 * group + i for i in range(4)]
        put(key_final, group, [tile(head, 2) for head in heads])
        parts = []
        for head in heads:
            thirds = [pltpu.roll(tile(head, number), 32 * (number + 1), 1) for number in range(HEAD_TILES)]
            in_tile = lanes_of(thirds[0])
            parts.append(jnp.where(in_tile < 32, thirds[0], jnp.where(in_tile < 64, thirds[1], thirds[2])))
        put(value_final, group, parts)

    load_own.wait()
    own_gains = own_rows[:, qkv_cols:].astype(jnp.float32)

    def product(grads, weights_of, width_of):
        sums = jnp.zeros((share, 1), jnp.float32)
        for start in range(0, width_of, 4 * LANES):
            at = slice(start, start + 4 * LANES)
            sums += jnp.sum(grads[:, at] * weights_of[:, at].astype(jnp.float32), -1, keepdims=True)
        return sums

    units_all = w_gate.shape[1]
    first_gain = product(final, own_rows, qkv_cols) / own_gains[:, 0:1]
    second_gain = product(gate_final, w_gate, units_all) + product(up_final, w_up, units_all)
    second_gain = second_gain / own_gains[:, 1:2]
    columns = lax.broadcasted_iota(jnp.int32, (share, LANES), 1)
    both_gains = jnp.where(columns == 0, first_gain, jnp.where(columns == 1, second_gain, 0.0))
    both_gains = jnp.concatenate([both_gains, jnp.zeros((LANES - share, LANES), jnp.float32)], 0)
    gain_final[...] = jnp.transpose(both_gains)[:8, :]
    tail = final[:, qkv_cols:]
    of_loss = lax.broadcasted_iota(jnp.int32, (1, LANES), 1) < 3 * devices
    loss[...] = jnp.sum(jnp.where(of_loss, tail[:1, :], 0.0), -1, keepdims=True) * (0.5 * norm[...])
    for kind in range(2):
        for k in range(1, members):
            out(kind, k).wait_send()


def finish(
    lines, weights, normed, qkv_grad, hidden_grad, tokens, gains, square, norm, w_gate, w_up, gate_sums, up_parts, identity
):
    rows, width = tokens.shape
    qkv_cols = qkv_grad.shape[1]
    share = weights.shape[0] // (lines * PLANE)
    columns = weights.shape[1]
    units_all = w_gate.shape[1]
    low = tokens.dtype
    vmem, anywhere = pl.BlockSpec(memory_space=pltpu.VMEM), pl.BlockSpec(memory_space=pl.ANY)
    dma = pltpu.SemaphoreType.DMA
    shapes = [
        (rows, width),
        (share, width),
        (share, KV * HD),
        (share, KV * HD),
        (share, units_all),
        (share, units_all),
        (8, LANES),
        (1, 1),
    ]
    return pl.pallas_call(
        finish_kernel,
        out_shape=[jax.ShapeDtypeStruct(shape, jnp.float32) for shape in shapes],
        in_specs=[anywhere] + [vmem] * 6 + [anywhere] * 5,
        out_specs=[vmem] * len(shapes),
        scratch_shapes=[
            pltpu.VMEM(hidden_grad.shape, jnp.float32),
            pltpu.VMEM(tokens.shape, low),
            pltpu.VMEM(w_gate.shape, low),
            pltpu.VMEM(w_up.shape, low),
            dma((4,)),
            pltpu.VMEM((width, qkv_cols), low),
            pltpu.VMEM((share, columns), low),
            pltpu.VMEM((rows, width), jnp.float32),
            pltpu.VMEM((share, columns), jnp.float32),
            pltpu.VMEM(gate_sums.shape, low),
            pltpu.VMEM(gate_sums.shape, low),
            pltpu.VMEM(gate_sums.shape, low),
            pltpu.VMEM(up_parts.shape, low),
            pltpu.VMEM(up_parts.shape, low),
            dma,
            dma,
            dma((PLANE,)),
            dma((PLANE,)),
            dma((PLANE,)),
            dma((PLANE,)),
            dma,
            dma((2, lines)),
            dma((2, lines)),
            *reduce_scratch(lines, share, columns, low),
        ],
        compiler_params=pltpu.CompilerParams(collective_id=identity, vmem_limit_bytes=VMEM_LIMIT),
        name="finish",
    )(weights, normed, qkv_grad, gains, square, norm, up_parts, gate_sums, hidden_grad, tokens, w_gate, w_up)


def emit_kernel(joined, *refs):
    sem = refs[-1]
    count = (len(refs) - 2) // 2
    out = refs[count + 1 : -1]
    pairs = [(refs[i], out[i]) for i in range(count)]
    cut = refs[joined].shape[1]
    pairs[joined] = (refs[joined], out[joined].at[:, pl.ds(0, cut)])
    pairs.append((refs[count], out[joined].at[:, pl.ds(cut, refs[count].shape[1])]))
    copies = [pltpu.make_async_copy(src, dst, sem.at[i]) for i, (src, dst) in enumerate(pairs)]
    for copy in copies:
        copy.start()
    for copy in copies:
        copy.wait()


def emit(arrays, joined, rest):
    shapes = [array.shape for array in arrays]
    shapes[joined] = (shapes[joined][0], shapes[joined][1] + rest.shape[1])
    return pl.pallas_call(
        functools.partial(emit_kernel, joined),
        out_shape=[jax.ShapeDtypeStruct(shape, array.dtype) for shape, array in zip(shapes, arrays)],
        in_specs=[pl.BlockSpec(memory_space=pl.ANY)] * (len(arrays) + 1),
        out_specs=[pl.BlockSpec(memory_space=pltpu.VMEM)] * len(arrays),
        scratch_shapes=[pltpu.SemaphoreType.DMA((len(arrays) + 1,))],
        compiler_params=pltpu.CompilerParams(vmem_limit_bytes=VMEM_LIMIT),
        name="emit",
    )(*arrays, rest)


def plane_per_device(lines, *arrays):
    (
        tokens,
        lengths,
        deal,
        loss_mask,
        teacher,
        out_grad,
        attn_gain,
        w_query,
        w_key,
        w_value,
        w_out,
        ffn_gain,
        w_gate,
        w_up,
        w_down,
    ) = arrays
    devices = lines * PLANE
    width = tokens.shape[2]
    weight_rows = w_query.shape[0]
    scale = HD ** (-0.5)
    gain_rows = jnp.zeros((8, LANES), jnp.float32)
    gain_rows = gain_rows.at[0, :weight_rows].set(attn_gain.astype(jnp.float32))
    gain_rows = gain_rows.at[1, :weight_rows].set(ffn_gain.astype(jnp.float32))
    freq = rope_base ** (-(np.arange(HD // 2) * 2.0 / HD))
    freq = np.concatenate([freq, freq, np.zeros(LANES - HD)])[None].astype(np.float32)

    attended_low, normed_low, gains, cosine, sine, valid, attn_all, out_w, gate_up_w, qkv, probs = attend(
        scale,
        lines,
        w_query,
        w_key,
        w_value,
        w_gate,
        w_up,
        w_out,
        gain_rows,
        freq,
        loss_mask,
        deal,
        lengths,
        tokens[0],
        3,
    )
    attn_all = attn_all.reshape(devices * weight_rows, -1)
    gate_up_w = gate_up_w.reshape(devices * weight_rows, -1)

    result, square, norm, hidden_grad, branch_low, attended_grad, down_final, down_rest, gate_grad, up_grad = feed_forward(
        lines,
        out_w.reshape(width, width),
        attended_low,
        tokens[0],
        teacher[0],
        out_grad[0],
        valid,
        gains,
        gate_up_w,
        w_down,
        5,
    )
    gate_grad, up_grad = [grad.reshape(lines, PLANE * weight_rows, -1) for grad in (gate_grad, up_grad)]
    qkv_grad, out_final, gate_sums, down_more = attend_back(
        scale, lines, attended_grad, qkv, probs, (cosine, sine), attended_low, branch_low, gate_grad, down_rest, 9
    )

    input_grad, query_final, key_final, value_final, gate_final, up_final, gain_final, loss = finish(
        lines,
        attn_all,
        normed_low,
        qkv_grad,
        hidden_grad,
        tokens[0],
        gains,
        square,
        norm,
        w_gate,
        w_up,
        gate_sums,
        up_grad,
        11,
    )
    result, input_grad, query_final, key_final, value_final, out_final, gate_final, up_final, down_final = emit(
        (result, input_grad, query_final, key_final, value_final, out_final, gate_final, up_final, down_final),
        8,
        down_more,
    )
    return (
        result[None],
        loss.reshape(()),
        input_grad[None],
        gain_final[0, :weight_rows],
        query_final,
        key_final,
        value_final,
        out_final,
        gain_final[1, :weight_rows],
        gate_final,
        up_final,
        down_final,
    )


def suits_planes(mesh):
    sizes = dict(mesh.shape)
    return sizes["fsdp"] == 4 and sizes["ctx"] == KV


def solution(mesh):
    placed = (
        P("fsdp", "ctx", None),
        P("fsdp", None),
        P("fsdp", None),
        P("fsdp", "ctx"),
        P("fsdp", "ctx", None),
        P("fsdp", "ctx", None),
        P(("ctx", "fsdp")),
        P(("ctx", "fsdp"), None),
        P(("ctx", "fsdp"), None),
        P(("ctx", "fsdp"), None),
        P(("ctx", "fsdp"), None),
        P(("ctx", "fsdp")),
        P(("ctx", "fsdp"), None),
        P(("ctx", "fsdp"), None),
        P(("ctx", "fsdp"), None),
    )
    if suits_planes(mesh):
        per_device = functools.partial(plane_per_device, mesh.shape["ctx"] // ROWS_Y)
    else:
        per_device = ring_per_device
    return jax.shard_map(
        per_device,
        mesh=mesh,
        in_specs=placed,
        out_specs=(
            P("fsdp", "ctx", None),
            P(),
            P("fsdp", "ctx", None),
            P(("ctx", "fsdp")),
            P(("ctx", "fsdp"), None),
            P(("ctx", "fsdp"), None),
            P(("ctx", "fsdp"), None),
            P(("ctx", "fsdp"), None),
            P(("ctx", "fsdp")),
            P(("ctx", "fsdp"), None),
            P(("ctx", "fsdp"), None),
            P(("ctx", "fsdp"), None),
        ),
        check_vma=False,
    )
```

```python
import functools

import jax
import jax.numpy as jnp
import numpy as np
from jax import lax
from jax.experimental import pallas as pl
from jax.experimental.pallas import tpu as pltpu
from jax.sharding import PartitionSpec as P

HEADS = 16
KV = 8
HD = 96
NSEQ = 6


rope_base = 100000.0
epsilon = 1e-05
masked_score = -1e30


def shifted(value, axis, by):
    size = lax.axis_size(axis)
    return lax.ppermute(value, axis, [(i, (i + by) % size) for i in range(size)])


def rms_scale(values):
    return lax.rsqrt(jnp.mean(values * values, -1, keepdims=True) + epsilon)


def rotary_tables(inseq):
    freq = rope_base ** (-(jnp.arange(HD // 2, dtype=jnp.float32) * 2.0 / HD))
    angle = inseq.astype(jnp.float32)[:, None] * freq[None, :]
    return (jnp.cos(angle)[:, None, :], jnp.sin(angle)[:, None, :])


def rotary(values, cosine, sine):
    half = values.shape[-1] // 2
    first = values[..., :half]
    second = values[..., half:]
    return jnp.concatenate([first * cosine - second * sine, second * cosine + first * sine], -1)


def rotary_back(grads, cosine, sine):
    half = grads.shape[-1] // 2
    first = grads[..., :half]
    second = grads[..., half:]
    return jnp.concatenate([first * cosine + second * sine, second * cosine - first * sine], -1)


def transposed(left, right):
    return lax.dot_general(
        left, right, (((0,), (0,)), ((), ())), preferred_element_type=jnp.float32
    )


def against(left, right):
    return lax.dot_general(
        left, right, (((1,), (1,)), ((), ())), preferred_element_type=jnp.float32
    )


def permitted(query_place, query_seg, key_place, key_seg):
    same = (query_seg[:, None] == key_seg[None, :]) & (query_seg[:, None] < NSEQ)
    return same & (key_place[None, :] <= query_place[:, None]) | (
        key_place[None, :] == query_place[:, None]
    )


def ring_per_device(
    tokens,
    lengths,
    deal,
    loss_mask,
    teacher,
    out_grad,
    attn_gain,
    w_query,
    w_key,
    w_value,
    w_out,
    ffn_gain,
    w_gate,
    w_up,
    w_down,
):
    count_ctx = lax.axis_size("ctx")
    myself = lax.axis_index("ctx")
    tok_rows = tokens.shape[1]
    width = tokens.shape[2]
    half_block = tok_rows // 2
    groups = HEADS // KV
    scale = HD ** (-0.5)
    gain_one, query_w, key_w, value_w, out_w = (
        lax.all_gather(attn_gain, ("ctx", "fsdp"), axis=0, tiled=True),
        lax.all_gather(w_query, ("ctx", "fsdp"), axis=0, tiled=True),
        lax.all_gather(w_key, ("ctx", "fsdp"), axis=0, tiled=True),
        lax.all_gather(w_value, ("ctx", "fsdp"), axis=0, tiled=True),
        lax.all_gather(w_out, ("ctx", "fsdp"), axis=0, tiled=True),
    )
    gain_two, gate_w, up_w, down_w = (
        lax.all_gather(ffn_gain, ("ctx", "fsdp"), axis=0, tiled=True),
        lax.all_gather(w_gate, ("ctx", "fsdp"), axis=0, tiled=True),
        lax.all_gather(w_up, ("ctx", "fsdp"), axis=0, tiled=True),
        lax.all_gather(w_down, ("ctx", "fsdp"), axis=0, tiled=True),
    )
    dealt = jnp.arange(count_ctx * tok_rows, dtype=jnp.int32)
    local = dealt % tok_rows
    first = jnp.repeat(deal[0], tok_rows)
    block = jnp.where(local < half_block, first, 2 * count_ctx - 1 - first)
    places = block * half_block + local % half_block
    ends = jnp.cumsum(lengths[0])
    after = (places[:, None] >= ends[None, :]).astype(jnp.int32)
    seg_all = jnp.sum(after, 1)
    inseq_all = places - jnp.sum(after * lengths[0][None, :], 1)
    own_place = lax.dynamic_slice_in_dim(places, myself * tok_rows, tok_rows)
    own_seg = lax.dynamic_slice_in_dim(seg_all, myself * tok_rows, tok_rows)
    own_inseq = lax.dynamic_slice_in_dim(inseq_all, myself * tok_rows, tok_rows)
    cosine, sine = rotary_tables(own_inseq)
    inputs = tokens[0].astype(jnp.float32)
    scale_one = rms_scale(inputs)
    normed_one = inputs * scale_one
    gain_first = gain_one.astype(jnp.float32)
    normed_low = (normed_one * gain_first).astype(jnp.bfloat16)
    query_pre = jnp.dot(normed_low, query_w, preferred_element_type=jnp.float32).reshape(
        tok_rows, HEADS, HD
    )
    key_pre = jnp.dot(normed_low, key_w, preferred_element_type=jnp.float32).reshape(
        tok_rows, KV, HD
    )
    value_low = jnp.dot(normed_low, value_w, preferred_element_type=jnp.float32).astype(
        jnp.bfloat16
    )
    queries = rotary(query_pre, cosine, sine).astype(jnp.bfloat16).reshape(tok_rows, KV, groups, HD)
    keys = rotary(key_pre, cosine, sine).astype(jnp.bfloat16).reshape(tok_rows, KV * HD)

    def logits(key_block):
        return (
            jnp.einsum(
                "qcgd,kcd->cgqk",
                queries,
                key_block.reshape(-1, KV, HD),
                preferred_element_type=jnp.float32,
            )
            * scale
        )

    key_block = lax.all_gather(keys, "ctx", axis=0, tiled=True)
    value_block = lax.all_gather(value_low, "ctx", axis=0, tiled=True)
    allowed = permitted(own_place, own_seg, places, seg_all)
    top = jnp.full((KV, groups, tok_rows, 1), masked_score, jnp.float32)
    score = jnp.where(allowed, logits(key_block), masked_score)
    new_top = jnp.maximum(top, jnp.max(score, -1, keepdims=True))
    weight = jnp.where(allowed, jnp.exp(score - new_top), 0.0)
    summed = jnp.einsum(
        "cgqk,kcd->cgqd",
        weight.astype(jnp.bfloat16),
        value_block.reshape(-1, KV, HD),
        preferred_element_type=jnp.float32,
    )
    summed, top, total = (summed, new_top, jnp.sum(weight, -1, keepdims=True))
    attended = summed / total
    log_total = top + jnp.log(total)
    attended_low = (
        jnp.transpose(attended, (2, 0, 1, 3)).reshape(tok_rows, HEADS * HD).astype(jnp.bfloat16)
    )
    hidden = inputs + jnp.dot(attended_low, out_w, preferred_element_type=jnp.float32)
    scale_two = rms_scale(hidden)
    normed_two = hidden * scale_two
    gain_second = gain_two.astype(jnp.float32)
    ffn_low = (normed_two * gain_second).astype(jnp.bfloat16)
    gate = jnp.dot(ffn_low, gate_w, preferred_element_type=jnp.float32)
    up = jnp.dot(ffn_low, up_w, preferred_element_type=jnp.float32)
    sigmoid = jax.nn.sigmoid(gate)
    activated = gate * sigmoid
    mixed_low = (activated * up).astype(jnp.bfloat16)
    result = hidden + jnp.dot(mixed_low, down_w, preferred_element_type=jnp.float32)
    target = teacher[0].astype(jnp.float32)
    valid = (loss_mask[0] * (own_seg < NSEQ)).astype(jnp.float32)[:, None]
    differ = result - target
    square_sum, valid_count = lax.psum(
        (jnp.sum(valid * differ * differ), jnp.sum(valid)), ("ctx", "fsdp")
    )
    loss = square_sum / (valid_count * width)
    out_total = out_grad[0].astype(jnp.float32) + 2.0 * valid * differ / (valid_count * width)
    out_low = out_total.astype(jnp.bfloat16)
    down_grad = transposed(mixed_low, out_low)
    mixed_grad = against(out_low, down_w)
    silu_slope = sigmoid * (1.0 + gate * (1.0 - sigmoid))
    gate_low = (mixed_grad * up * silu_slope).astype(jnp.bfloat16)
    up_low = (mixed_grad * activated).astype(jnp.bfloat16)
    gate_grad = transposed(ffn_low, gate_low)
    up_grad = transposed(ffn_low, up_low)
    normed_grad = against(gate_low, gate_w) + against(up_low, up_w)
    gain_two_grad = jnp.sum(normed_grad * normed_two, 0)
    scaled_two = normed_grad * gain_second
    hidden_grad = out_total + scale_two * (
        scaled_two - normed_two * jnp.mean(scaled_two * normed_two, -1, keepdims=True)
    )
    ffn_final = (
        lax.psum_scatter(gain_two_grad, ("ctx", "fsdp"), scatter_dimension=0, tiled=True),
        lax.psum_scatter(gate_grad, ("ctx", "fsdp"), scatter_dimension=0, tiled=True),
        lax.psum_scatter(up_grad, ("ctx", "fsdp"), scatter_dimension=0, tiled=True),
        lax.psum_scatter(down_grad, ("ctx", "fsdp"), scatter_dimension=0, tiled=True),
    )
    branch_low = hidden_grad.astype(jnp.bfloat16)
    out_w_grad = transposed(attended_low, branch_low)
    attended_grad = against(branch_low, out_w).astype(jnp.bfloat16)
    grad_heads = jnp.transpose(attended_grad.reshape(tok_rows, KV, groups, HD), (1, 2, 0, 3))
    delta = jnp.sum(grad_heads.astype(jnp.float32) * attended, -1, keepdims=True)

    def cycle_step(step, state):
        key_block, value_block, key_acc, value_acc, query_acc = state
        source = (myself - step) % count_ctx
        allowed = permitted(
            own_place,
            own_seg,
            lax.dynamic_slice_in_dim(places, source * tok_rows, tok_rows),
            lax.dynamic_slice_in_dim(seg_all, source * tok_rows, tok_rows),
        )
        current_key = key_block
        current_value = value_block
        keys_three = current_key.reshape(tok_rows, KV, HD)
        values_three = current_value.reshape(tok_rows, KV, HD)
        prob = jnp.where(allowed, jnp.exp(logits(current_key) - log_total), 0.0)
        prob_grad = jnp.einsum(
            "cgqd,kcd->cgqk", grad_heads, values_three, preferred_element_type=jnp.float32
        )
        score_low = (prob * (prob_grad - delta)).astype(jnp.bfloat16)
        query_add = (
            jnp.einsum("cgqk,kcd->cgqd", score_low, keys_three, preferred_element_type=jnp.float32)
            * scale
        )
        key_add = (
            jnp.einsum(
                "cgqk,qcgd->kcd", score_low, queries, preferred_element_type=jnp.float32
            ).reshape(tok_rows, KV * HD)
            * scale
        )
        value_add = jnp.einsum(
            "cgqk,cgqd->kcd",
            prob.astype(jnp.bfloat16),
            grad_heads,
            preferred_element_type=jnp.float32,
        ).reshape(tok_rows, KV * HD)
        key_block, value_block = shifted((key_block, value_block), "ctx", 1)
        key_acc, value_acc = (
            shifted((key_acc + key_add).astype(jnp.bfloat16), "ctx", 1).astype(jnp.float32),
            shifted((value_acc + value_add).astype(jnp.bfloat16), "ctx", 1).astype(jnp.float32),
        )
        return (key_block, value_block, key_acc, value_acc, query_acc + query_add)

    cycle_start = (
        keys,
        value_low,
        jnp.zeros((tok_rows, KV * HD), jnp.float32),
        jnp.zeros((tok_rows, KV * HD), jnp.float32),
        jnp.zeros((KV, groups, tok_rows, HD), jnp.float32),
    )
    cycle_end = lax.fori_loop(0, count_ctx, cycle_step, cycle_start)
    key_acc = cycle_end[2]
    value_acc = cycle_end[3]
    query_acc = cycle_end[4]
    query_grad = jnp.transpose(query_acc, (2, 0, 1, 3)).reshape(tok_rows, HEADS, HD)
    query_low = (
        rotary_back(query_grad, cosine, sine).reshape(tok_rows, HEADS * HD).astype(jnp.bfloat16)
    )
    key_low = (
        rotary_back(key_acc.reshape(tok_rows, KV, HD), cosine, sine)
        .reshape(tok_rows, KV * HD)
        .astype(jnp.bfloat16)
    )
    value_grad_low = value_acc.astype(jnp.bfloat16)
    query_w_grad = transposed(normed_low, query_low)
    key_w_grad = transposed(normed_low, key_low)
    value_w_grad = transposed(normed_low, value_grad_low)
    normed_one_grad = (
        against(query_low, query_w) + against(key_low, key_w) + against(value_grad_low, value_w)
    )
    gain_one_grad = jnp.sum(normed_one_grad * normed_one, 0)
    scaled_one = normed_one_grad * gain_first
    input_grad = hidden_grad + scale_one * (
        scaled_one - normed_one * jnp.mean(scaled_one * normed_one, -1, keepdims=True)
    )
    attn_final = (
        lax.psum_scatter(gain_one_grad, ("ctx", "fsdp"), scatter_dimension=0, tiled=True),
        lax.psum_scatter(query_w_grad, ("ctx", "fsdp"), scatter_dimension=0, tiled=True),
        lax.psum_scatter(key_w_grad, ("ctx", "fsdp"), scatter_dimension=0, tiled=True),
        lax.psum_scatter(value_w_grad, ("ctx", "fsdp"), scatter_dimension=0, tiled=True),
        lax.psum_scatter(out_w_grad, ("ctx", "fsdp"), scatter_dimension=0, tiled=True),
    )
    return (
        result.astype(jnp.bfloat16)[None],
        loss,
        input_grad[None],
        attn_final[0],
        attn_final[1],
        attn_final[2],
        attn_final[3],
        attn_final[4],
        ffn_final[0],
        ffn_final[1],
        ffn_final[2],
        ffn_final[3],
    )


MESH = pl.DeviceIdType.MESH
ROWS_Y = 2
PLANE = 8
LANES = 128
VMEM_LIMIT = 60 * 2**20


def coordinates():
    ctx = lax.axis_index("ctx")
    fsdp = lax.axis_index("fsdp")
    return ctx // 2, ctx % 2, fsdp // 2, fsdp % 2


def device(z, y, x, c):
    return (z * 2 + y, x * 2 + c)


def greet(devices):
    barrier = pltpu.get_barrier_semaphore()
    for other in devices:
        pl.semaphore_signal(barrier, inc=1, device_id=other, device_id_type=MESH)
    pl.semaphore_wait(barrier, len(devices))


def remote(src, dst, send, recv, target):
    return pltpu.make_async_remote_copy(
        src_ref=src,
        dst_ref=dst,
        send_sem=send,
        recv_sem=recv,
        device_id=target,
        device_id_type=MESH,
    )


def transfers(sources, targets, sem):
    return [pltpu.make_async_copy(src, dst, sem.at[i]) for i, (src, dst) in enumerate(zip(sources, targets))]


def line_gather(place, lines, x_ref, slot, send, recv, here=None):
    z, y, x, c = place
    mine = None if here is None else pltpu.make_async_copy(x_ref, slot(z), here)
    ways = ((0, -1, device(z + 1, y, x, c)), (1, 1, device(z - 1, y, x, c)))

    def along(way, sign, to, s):
        zz = z + sign * (s - 1)
        return remote(x_ref if s == 1 else slot(zz), slot(zz), send.at[way, s], recv.at[way, s], to)

    def sends(sign, s):
        if sign < 0:
            return (z - (s - 1) >= 0) & (z + 1 < lines)
        return (z + (s - 1) < lines) & (z - 1 >= 0)

    def present(sign, s):
        return z - s >= 0 if sign < 0 else z + s < lines

    def start(s):
        for way, sign, to in ways:
            pl.when(sends(sign, s))(lambda way=way, sign=sign, to=to: along(way, sign, to, s).start())

    def begin():
        if mine is not None:
            mine.start()
        start(1)

    def pass_on(s):
        for way, sign, to in ways:
            pl.when(present(sign, s))(lambda way=way, sign=sign, to=to: along(way, sign, to, s).wait_recv())
        if s + 1 < lines:
            start(s + 1)

    def last():
        for s in range(1, lines):
            for way, sign, to in ways:
                pl.when(sends(sign, s))(lambda way=way, sign=sign, to=to, s=s: along(way, sign, to, s).wait_send())
        if mine is not None:
            mine.wait()

    return begin, pass_on, last


def line_reduce(place, lines, parts, up, down, send, recv):
    z, y, x, c = place
    ways = ((0, up, device(z + 1, y, x, c)), (1, down, device(z - 1, y, x, c)))

    def copy(way, t, own):
        _, sums, to = ways[way]
        src = parts.at[t] if own else sums.at[t]
        return remote(src, sums.at[t], send.at[way, t], recv.at[way, t], to)

    def begin():
        @pl.when(z == 0)
        def _():
            for t in range(lines - 1, 0, -1):
                copy(0, t, True).start()

        @pl.when(z == lines - 1)
        def _():
            for t in range(lines - 1):
                copy(1, t, True).start()

    def add_on(way, t):
        copy(way, t, False).wait_recv()
        add_rows(ways[way][1].at[t], parts.at[t])
        copy(way, t, False).start()

    def hop(moment):
        for t in range(lines):
            for zz in range(1, lines - 1):
                if zz < t and zz + (lines - 1 - t) == moment:
                    pl.when(z == zz)(functools.partial(add_on, 0, t))
                if zz > t and (lines - 1 - zz) + t == moment:
                    pl.when(z == zz)(functools.partial(add_on, 1, t))

    def last(write, step=32):
        for way, first in ((0, 0), (1, lines - 1)):

            @pl.when(z != first)
            def _():
                copy(way, z, False).wait_recv()

        def body(i, carry):
            at = pl.ds(pl.multiple_of(i * step, step), step)
            from_below = jnp.where(z > 0, up[z, at, :].astype(jnp.float32), 0.0)
            from_above = jnp.where(z < lines - 1, down[z, at, :].astype(jnp.float32), 0.0)
            write(i, parts[z, at, :].astype(jnp.float32) + from_below + from_above)
            return carry

        lax.fori_loop(0, parts.shape[1] // step, body, 0)
        for zz in range(lines):

            @pl.when(z == zz)
            def _():
                for t in range(lines):
                    if t > zz:
                        copy(0, t, zz == 0).wait_send()
                    if t < zz:
                        copy(1, t, zz == lines - 1).wait_send()

    return begin, hop, last


def column_cut(width):
    tiles = width // LANES
    return (tiles + 1) // 2 * LANES


def line_of(z, y, x, c, lines):
    return [device(lax.rem(z + k, lines), y, x, c) for k in range(1, lines)]


def reduce_plan(lines, prepare, p_ref, o_ref, held, corner_a, corner_b, from_side, from_over, along, send, recv):
    z, y, x, c = coordinates()
    parts = lines
    rows, width = held.shape[2], held.shape[3]
    cut = column_cut(width)
    first, second = pl.ds(0, cut), pl.ds(cut, width - cut)
    side, over, sibling = device(z, y, 1 - x, c), device(z, 1 - y, x, c), device(z, y, x, 1 - c)
    def given(part, yy, xx, cc):
        member = yy * 4 + xx * 2 + cc
        return p_ref.at[lax.rem(z + part + 1, lines), member]

    def make(part, kind, src, dst, to):
        return remote(src, dst, send.at[part, kind], recv.at[part, kind], to)

    lane = lambda part, yy, xx: held.at[part, yy * 2 + xx]

    def over_core(part):
        return [
            make(part, yy * 2 + xx, given(part, yy, xx, 1 - c), lane(part, yy, xx), sibling)
            for yy in range(2)
            for xx in range(2)
        ]

    def to_corner(part):
        return (
            make(part, 4, lane(part, 1 - y, 1 - x).at[:, first], corner_a.at[part], over),
            make(part, 5, lane(part, 1 - y, 1 - x).at[:, second], corner_b.at[part], side),
        )

    def to_neighbour(part, way):
        columns = (first, second)[way % 2]
        if way < 2:
            return make(part, 6 + way, lane(part, y, 1 - x).at[:, columns], from_side.at[part, :, columns], side)
        return make(part, 6 + way, lane(part, 1 - y, x).at[:, columns], from_over.at[part, :, columns], over)

    def along_z(part):
        to = lax.rem(z + part + 1, lines)
        return make(part, 10, lane(part, y, x), along.at[part], device(to, y, x, c))

    step = 16

    def add_core(part):
        for copy in over_core(part):
            copy.wait_recv()
        for yy, xx in ((1 - y, 1 - x), (y, 1 - x), (1 - y, x), (y, x)):
            mine, other = given(part, yy, xx, c), lane(part, yy, xx)

            def body(i, carry):
                at = pl.ds(pl.multiple_of(i * step, step), step)
                total = mine[at, :].astype(jnp.float32) + other[at, :].astype(jnp.float32)
                other[at, :] = total.astype(other.dtype)
                return carry

            lax.fori_loop(0, rows // step, body, 0)
        for copy in to_corner(part):
            copy.start()
        to_neighbour(part, 1).start()
        to_neighbour(part, 2).start()

    def add_corner(part):
        copies = to_corner(part)
        pairs = (
            (copies[0], lane(part, y, 1 - x), corner_a.at[part], first),
            (copies[1], lane(part, 1 - y, x), corner_b.at[part], second),
        )
        for copy, mine, other, columns in pairs:
            copy.wait_recv()

            def body(i, carry):
                at = pl.ds(pl.multiple_of(i * step, step), step)
                total = mine[at, columns].astype(jnp.float32) + other[at, :].astype(jnp.float32)
                mine[at, columns] = total.astype(mine.dtype)
                return carry

            lax.fori_loop(0, rows // step, body, 0)
        to_neighbour(part, 0).start()
        to_neighbour(part, 3).start()

    def add_neighbours(part):
        for way in range(4):
            to_neighbour(part, way).wait_recv()
        last = part == parts - 1
        mine = lane(part, y, x)

        def body(i, carry):
            at = pl.ds(pl.multiple_of(i * step, step), step)
            total = mine[at, :].astype(jnp.float32) + from_side[part, at, :].astype(jnp.float32)
            total += from_over[part, at, :].astype(jnp.float32)
            if last:
                o_ref[at, :] = total
            else:
                mine[at, :] = total.astype(mine.dtype)
            return carry

        lax.fori_loop(0, rows // step, body, 0)
        if not last:
            along_z(part).start()

    def ready(part):
        prepare(lax.rem(z + part + 1, lines))
        for copy in over_core(part):
            copy.start()

    kinds = (ready, add_core, add_corner, add_neighbours)

    def run(number):
        for lag, kind in enumerate(kinds):
            if 0 <= number - lag < parts:
                kind(number - lag)

    def last():
        for part in range(parts - 1):
            along_z(part).wait_recv()

        def body(i, carry):
            at = pl.ds(pl.multiple_of(i * step, step), step)
            total = o_ref[at, :]
            for part in range(parts - 1):
                total += along[part, at, :].astype(jnp.float32)
            o_ref[at, :] = total
            return carry

        lax.fori_loop(0, rows // step, body, 0)
        for part in range(parts - 1):
            along_z(part).wait_send()
        for part in range(parts):
            for copy in (*over_core(part), *to_corner(part), *(to_neighbour(part, way) for way in range(4))):
                copy.wait_send()

    return [functools.partial(run, number) for number in range(parts + len(kinds) - 1)], last


def reduce_scratch(lines, share, columns, low):
    cut = column_cut(columns)
    return [
        pltpu.VMEM((lines, PLANE, share, columns), low),
        pltpu.VMEM((lines, 4, share, columns), low),
        pltpu.VMEM((lines, share, cut), low),
        pltpu.VMEM((lines, share, columns - cut), low),
        pltpu.VMEM((lines, share, columns), low),
        pltpu.VMEM((lines, share, columns), low),
        pltpu.VMEM((lines - 1, share, columns), low),
        pltpu.SemaphoreType.DMA((lines, 11)),
        pltpu.SemaphoreType.DMA((lines, 11)),
    ]


def store_terms(p, block, start, value):
    members, share = p.shape[1:3]
    width = value.shape[1]
    p[block, :, :, start : start + width] = value.astype(p.dtype).reshape(members, share, width)


def halves(width):
    cut = column_cut(width)
    return pl.ds(0, cut), pl.ds(cut, width - cut)


class PlaneGather:
    def __init__(self, place, at, width, send, recv):
        z, y, x, c = place
        side, over, sibling = device(z, y, 1 - x, c), device(z, 1 - y, x, c), device(z, y, x, 1 - c)
        self.send, self.recv = send, recv
        own, next_x, next_y, corner = at(y, x), at(y, 1 - x), at(1 - y, x), at(1 - y, 1 - x)
        first, second = [lambda ref, of=of: ref.at[..., of] for of in halves(width)]
        self.table = (
            (first(own), side),
            (second(own), side),
            (first(own), over),
            (second(own), over),
            (own, sibling),
            (first(next_x), over),
            (second(next_y), side),
            (first(next_x), sibling),
            (second(next_x), sibling),
            (first(next_y), sibling),
            (second(next_y), sibling),
            (first(corner), sibling),
            (second(corner), sibling),
        )

    def copy(self, kind):
        ref, to = self.table[kind]
        return remote(ref, ref, self.send.at[kind], self.recv.at[kind], to)

    def begin(self):
        for kind in (0, 3, 4, 1, 2):
            self.copy(kind).start()

    def came(self, *kinds):
        for kind in kinds:
            self.copy(kind).wait_recv()

    def forward_on(self):
        for kind, onward in ((0, (5, 7)), (3, (6, 10)), (1, (8,)), (2, (9,))):
            self.came(kind)
            for other in onward:
                self.copy(other).start()

    def corner_on(self):
        for kind, onward in ((5, 11), (6, 12)):
            self.came(kind)
            self.copy(onward).start()

    def rest(self):
        self.came(4, *range(7, GATHER_KINDS))

    def drain(self):
        for kind in range(GATHER_KINDS):
            self.copy(kind).wait_send()


GATHER_KINDS = 13
REDUCE_KINDS = 10


def reduce_steps(place, at_rows, partial, held, corner_a, corner_b, from_side, from_over, send, recv):
    z, y, x, c = place
    side, over, sibling = device(z, y, 1 - x, c), device(z, 1 - y, x, c), device(z, y, x, 1 - c)
    first, second = halves(held.shape[-1])
    lane = lambda yy, xx: held.at[yy * 2 + xx, at_rows]
    next_x, next_y, corner = lane(y, 1 - x), lane(1 - y, x), lane(1 - y, 1 - x)

    def to_core(yy, xx):
        kind = yy * 2 + xx
        src = partial.at[yy * 4 + xx * 2 + 1 - c, at_rows]
        return remote(src, lane(yy, xx), send.at[kind], recv.at[kind], sibling)

    table = (
        (corner.at[:, first], corner_a.at[at_rows], over),
        (corner.at[:, second], corner_b.at[at_rows], side),
        (next_x.at[:, first], from_side.at[at_rows, first], side),
        (next_x.at[:, second], from_side.at[at_rows, second], side),
        (next_y.at[:, first], from_over.at[at_rows, first], over),
        (next_y.at[:, second], from_over.at[at_rows, second], over),
    )

    def copy(kind):
        src, dst, to = table[kind]
        return remote(src, dst, send.at[4 + kind], recv.at[4 + kind], to)

    return to_core, copy


def add_rows(target, other, columns=None, step=32):
    def body(i, carry):
        at = pl.ds(pl.multiple_of(i * step, step), step)
        mine = target[at, :] if columns is None else target[at, columns]
        total = (mine.astype(jnp.float32) + other[at, :].astype(jnp.float32)).astype(target.dtype)
        if columns is None:
            target[at, :] = total
        else:
            target[at, columns] = total
        return carry

    lax.fori_loop(0, other.shape[0] // step, body, 0)


def feed_forward_kernel(
    out_rows, attended, tokens, teacher_rows, out_grad_rows, valid, gains, gate_up_rows, down_rows,
    result_out, square, norm, hidden_grad, branch, attended_grad, down_final, down_out, gate_out, up_out,
    result, down_rest, gate_grad, up_grad, store_sem, out_w, gate_up_w, teacher, out_grad, down_w, down_up, down_down, normed_all, kept, mixed, grads_all, partial, held, corner_a, corner_b, from_side, from_over, hidden, total_grad, scales, squares,
    load_sem, here, line_send, line_recv, down_send, down_recv, gather_send, gather_recv, reduce_send, reduce_recv,
):
    place = coordinates()
    z, y, x, c = place
    width = tokens.shape[1]
    pairs = ((out_rows, out_w), (gate_up_rows, gate_up_w), (teacher_rows, teacher), (out_grad_rows, out_grad))
    loads = [pltpu.make_async_copy(src, dst, load_sem.at[i]) for i, (src, dst) in enumerate(pairs)]
    for load in loads:
        load.start()
    lines, units = down_w.shape[:2]
    greet([device(z, y, 1 - x, c), device(z, 1 - y, x, c), device(z, y, x, 1 - c)] + line_of(z, y, x, c, lines))
    rows = tokens.shape[0]
    share = lines * units
    first, second = halves(width)
    down_lines = [
        line_gather(
            place, lines, down_rows.at[:, of], lambda zz, of=of: down_w.at[zz, :, of],
            line_send.at[i], line_recv.at[i], here.at[i],
        )
        for i, of in enumerate((first, second))
    ]
    (begin_one, pass_one, last_one), (begin_two, pass_two, last_two) = down_lines
    begin_one()
    begin_two()
    mine = y * 4 + x * 2 + c
    chips = ((y, x), (y, 1 - x), (1 - y, x), (1 - y, 1 - x))

    gain = gains[1:2, :]
    count = jnp.sum(gains[2:3, :], -1, keepdims=True) / (width // (lines * PLANE))
    norm[...] = 2.0 / (count * width)
    loads[0].wait()
    hidden[...] = tokens[...].astype(jnp.float32) + jnp.dot(
        attended[...], out_w[...], preferred_element_type=jnp.float32
    )

    def norm_rows(at):
        values = hidden[at, :]
        scale = rms_scale(values)
        scales[at, :] = scale
        normed_all[mine, at, :] = (values * scale * gain[...]).astype(normed_all.dtype)

    parts = 2
    part_rows = rows // parts
    at_part = [pl.ds(part * part_rows, part_rows) for part in range(parts)]

    def of_part(part, body):
        by_rows(part_rows, lambda at: body(pl.ds(pl.multiple_of(part * part_rows + at.start, ROW_STEP), ROW_STEP)))

    class Phase(PlaneGather):
        def __init__(self, phase, part, whole):
            at_rows = at_part[part]
            self.part, self.at_rows = part, at_rows
            at = lambda yy, xx: whole.at[yy * 4 + xx * 2 + c, at_rows]
            super().__init__(place, at, width, gather_send.at[phase, part], gather_recv.at[phase, part])
            self.to_core, self.pass_on = reduce_steps(
                place, at_rows, partial, held, corner_a, corner_b, from_side, from_over,
                reduce_send.at[phase, part], reduce_recv.at[phase, part],
            )

        def join(self, yy, xx):
            self.to_core(yy, xx).wait_recv()
            add_rows(held.at[yy * 2 + xx, self.at_rows], partial.at[yy * 4 + xx * 2 + c, self.at_rows])

        def join_next(self, number):
            self.join(*chips[number])
            self.pass_on(2 + number).start()

        def join_corner(self):
            self.join(*chips[3])
            self.pass_on(0).start()
            self.pass_on(1).start()

        def add_corner(self):
            self.pass_on(0).wait_recv()
            add_rows(held.at[y * 2 + 1 - x, self.at_rows], corner_a.at[self.at_rows], first)
            self.pass_on(2).start()
            self.pass_on(1).wait_recv()
            add_rows(held.at[(1 - y) * 2 + x, self.at_rows], corner_b.at[self.at_rows], second)
            self.pass_on(5).start()

        def complete(self):
            for kind in (2, 3, 4, 5):
                self.pass_on(kind).wait_recv()
            for kind in range(6):
                self.pass_on(kind).wait_send()
            for yy, xx in chips:
                self.to_core(yy, xx).wait_send()

    def pair_of(number):
        yy, xx = chips[number]
        return pl.ds(yy * 4 + xx * 2, 2)

    one, two = [Phase(0, part, normed_all) for part in range(parts)]
    of_part(0, norm_rows)
    one.begin()
    of_part(1, norm_rows)

    def summed(at):
        total = held[y * 2 + x, at, :].astype(jnp.float32) + from_side[at, :].astype(jnp.float32)
        return total + from_over[at, :].astype(jnp.float32)

    def units_of(phase, number):
        where = (pair_of(number), phase.at_rows)
        both = jnp.dot(
            normed_all[where].reshape(rows, width), gate_up_w[...], preferred_element_type=jnp.float32
        )
        gate, up = both[:, :share], both[:, share:]
        sigmoid = 1.0 / (1.0 + jnp.exp(-gate))
        activated = gate * sigmoid
        slope = up * (sigmoid + activated * (1.0 - sigmoid))
        kept[(*where, slice(0, share))] = slope.astype(kept.dtype).reshape(2, part_rows, share)
        kept[(*where, slice(share, 2 * share))] = activated.astype(kept.dtype).reshape(2, part_rows, share)
        mixed[where] = (activated * up).astype(mixed.dtype).reshape(2, part_rows, share)

    def down_of(phase, number):
        where = (pair_of(number), phase.at_rows)
        out = jnp.dot(
            mixed[where].reshape(rows, share),
            down_w[...].reshape(share, width),
            preferred_element_type=jnp.float32,
        )
        partial[where] = out.astype(partial.dtype).reshape(2, part_rows, width)
        phase.to_core(*chips[number]).start()

    one.came(4)
    loads[1].wait()
    units_of(one, 0)
    pass_one(1)
    pass_two(1)
    one.forward_on()
    two.begin()
    for moment in range(2, lines - 1):
        pass_one(moment)
    one.came(7, 8)
    units_of(one, 1)
    for moment in range(2, lines - 1):
        pass_two(moment)
    one.came(9, 10)
    units_of(one, 2)
    pass_one(lines - 1)
    one.corner_on()
    two.came(4)
    units_of(two, 0)
    pass_two(lines - 1)
    last_one()
    last_two()
    two.forward_on()
    one.came(11, 12)
    units_of(one, 3)
    down_of(one, 1)
    two.came(7, 8)
    units_of(two, 1)
    down_of(one, 2)
    one.join_next(1)
    two.came(9, 10)
    units_of(two, 2)
    two.corner_on()
    down_of(one, 3)
    one.join_next(2)
    two.came(11, 12)
    units_of(two, 3)
    one.join_corner()
    down_of(two, 1)
    down_of(two, 2)
    two.join_next(1)
    down_of(one, 0)
    down_of(two, 3)
    two.join_next(2)
    one.join(*chips[0])
    one.add_corner()
    two.join_corner()
    down_of(two, 0)
    two.join(*chips[0])
    one.complete()
    loads[2].wait()
    loads[3].wait()

    def result_rows(at):
        values = hidden[at, :] + summed(at)
        result[at, :] = values.astype(result.dtype)
        differ = values - teacher[at, :].astype(jnp.float32)
        weighed = valid[at, :] * differ
        squares[at, :] = jnp.sum(weighed * differ, -1, keepdims=True)
        total = out_grad[at, :].astype(jnp.float32) + weighed * norm[...]
        total_grad[at, :] = total
        grads_all[mine, at, :] = total.astype(grads_all.dtype)

    def back_of(phase, number):
        where = (pair_of(number), phase.at_rows)
        mixed_grad = against(grads_all[where].reshape(rows, width), down_w[...].reshape(share, width))
        slope = kept[(*where, slice(0, share))].reshape(rows, share).astype(jnp.float32)
        activated = kept[(*where, slice(share, 2 * share))].reshape(rows, share).astype(jnp.float32)
        low_gate = (mixed_grad * slope).astype(kept.dtype)
        low_up = (mixed_grad * activated).astype(kept.dtype)
        kept[(*where, slice(0, share))] = low_gate.reshape(2, part_rows, share)
        kept[(*where, slice(share, 2 * share))] = low_up.reshape(2, part_rows, share)
        out = against(low_gate, gate_up_w[:, :share]) + against(low_up, gate_up_w[:, share:])
        partial[where] = out.astype(partial.dtype).reshape(2, part_rows, width)
        phase.to_core(*chips[number]).start()

    three, four = [Phase(1, part, grads_all) for part in range(parts)]
    of_part(0, result_rows)
    three.begin()
    two.add_corner()
    three.came(4)
    back_of(three, 0)
    two.complete()
    of_part(1, result_rows)
    square[...] = jnp.sum(squares[...], 0, keepdims=True)
    stores = transfers((result, down_rest, gate_grad, up_grad), (result_out, down_out, gate_out, up_out), store_sem)
    stores[0].start()
    three.forward_on()
    four.begin()
    three.came(7, 8)
    back_of(three, 1)
    three.came(9, 10)
    back_of(three, 2)
    three.join_next(1)
    four.came(4)
    back_of(four, 0)
    three.corner_on()
    three.join_next(2)
    three.came(11, 12)
    back_of(three, 3)
    four.forward_on()
    three.join_corner()
    four.came(7, 8)
    back_of(four, 1)
    three.join(*chips[0])
    four.came(9, 10)
    back_of(four, 2)
    four.join_next(1)
    four.corner_on()
    four.join_next(2)
    three.add_corner()
    four.came(11, 12)
    back_of(four, 3)
    four.join(*chips[0])
    four.join_corner()
    tokens_all = normed_all.shape[0] * rows
    block = 256

    def down_block(of, to):
        def run(i, carry):
            at = pl.ds(pl.multiple_of(i * block, block), block)
            left = mixed[:, :, at].reshape(tokens_all, block)
            grads = transposed(left, grads_all[:, :, of].reshape(tokens_all, of.size)).astype(to.dtype)
            per = block // units
            to[pl.ds(i * per, per)] = grads.reshape(per, units, of.size)
            return carry

        lax.fori_loop(0, share // block, run, 0)

    def both_block(i, carry):
        at = pl.ds(pl.multiple_of(i * block, block), block)
        left = normed_all[:, :, at].reshape(tokens_all, block)
        both = transposed(left, kept[...].reshape(tokens_all, 2 * share)).astype(gate_grad.dtype)
        gate_grad[at, :] = both[:, :share]
        up_grad[at, :] = both[:, share:]
        return carry

    down_parts = down_w.at[:, :, first]
    down_begin, down_hop, down_last = line_reduce(
        place, lines, down_parts, down_up, down_down, down_send, down_recv
    )
    down_block(first, down_parts)
    down_begin()
    down_block(second, down_rest)
    blocks = width // block
    third = blocks // 3
    lax.fori_loop(0, third, both_block, 0)
    three.complete()
    four.add_corner()
    down_hop(1)
    lax.fori_loop(third, 2 * third, both_block, 0)
    for moment in range(2, lines - 1):
        down_hop(moment)
    lax.fori_loop(2 * third, blocks, both_block, 0)
    for store in stores[1:]:
        store.start()

    def grad_rows(at):
        grads = summed(at)
        normed = hidden[at, :] * scales[at, :]
        scaled = grads * gain[...]
        values = total_grad[at, :] + scales[at, :] * (scaled - normed * jnp.mean(scaled * normed, -1, keepdims=True))
        hidden_grad[at, :] = values
        branch[at, :] = values.astype(branch.dtype)

    of_part(0, grad_rows)
    four.complete()
    of_part(1, grad_rows)
    attended_grad[...] = against(branch[...], out_w[...]).astype(attended_grad.dtype)


    def keep_down(i, sums):
        down_final[pl.ds(pl.multiple_of(i * 32, 32), 32), :] = sums

    down_last(keep_down)
    for phase in (one, two, three, four):
        phase.drain()
    for store in stores:
        store.wait()


def feed_forward(lines, out_rows, attended, tokens, teacher, out_grad, valid, gains, gate_up_w, down_rows, identity):
    rows, width = tokens.shape
    units = down_rows.shape[0]
    share = lines * units
    low = tokens.dtype
    shape = jax.ShapeDtypeStruct
    vmem, anywhere = pl.BlockSpec(memory_space=pltpu.VMEM), pl.BlockSpec(memory_space=pl.ANY)
    cut = column_cut(width)
    return pl.pallas_call(
        feed_forward_kernel,
        out_shape=[
            shape((rows, width), low),
            shape((1, 1), jnp.float32),
            shape((1, 1), jnp.float32),
            shape((rows, width), jnp.float32),
            shape((rows, width), low),
            shape((rows, width), low),
            shape((units, cut), jnp.float32),
            shape((lines, units, width - cut), low),
            shape((width, share), low),
            shape((width, share), low),
        ],
        in_specs=[anywhere, vmem, vmem, anywhere, anywhere, vmem, vmem, anywhere, anywhere],
        out_specs=[anywhere] + [vmem] * 6 + [anywhere] * 3,
        scratch_shapes=[
            pltpu.VMEM((rows, width), low),
            pltpu.VMEM((lines, units, width - cut), low),
            pltpu.VMEM((width, share), low),
            pltpu.VMEM((width, share), low),
            pltpu.SemaphoreType.DMA((4,)),
            pltpu.VMEM((width, width), low),
            pltpu.VMEM((width, 2 * share), low),
            pltpu.VMEM((rows, width), low),
            pltpu.VMEM((rows, width), low),
            pltpu.VMEM((lines, units, width), low),
            pltpu.VMEM((lines, units, cut), low),
            pltpu.VMEM((lines, units, cut), low),
            pltpu.VMEM((PLANE, rows, width), low),
            pltpu.VMEM((PLANE, rows, 2 * share), low),
            pltpu.VMEM((PLANE, rows, share), low),
            pltpu.VMEM((PLANE, rows, width), low),
            pltpu.VMEM((PLANE, rows, width), low),
            pltpu.VMEM((4, rows, width), low),
            pltpu.VMEM((rows, cut), low),
            pltpu.VMEM((rows, width - cut), low),
            pltpu.VMEM((rows, width), low),
            pltpu.VMEM((rows, width), low),
            pltpu.VMEM((rows, width), jnp.float32),
            pltpu.VMEM((rows, width), jnp.float32),
            pltpu.VMEM((rows, 1), jnp.float32),
            pltpu.VMEM((rows, 1), jnp.float32),
            pltpu.SemaphoreType.DMA((4,)),
            pltpu.SemaphoreType.DMA((2,)),
            pltpu.SemaphoreType.DMA((2, 2, lines)),
            pltpu.SemaphoreType.DMA((2, 2, lines)),
            pltpu.SemaphoreType.DMA((2, lines)),
            pltpu.SemaphoreType.DMA((2, lines)),
            pltpu.SemaphoreType.DMA((2, 2, GATHER_KINDS)),
            pltpu.SemaphoreType.DMA((2, 2, GATHER_KINDS)),
            pltpu.SemaphoreType.DMA((2, 2, REDUCE_KINDS)),
            pltpu.SemaphoreType.DMA((2, 2, REDUCE_KINDS)),
        ],
        compiler_params=pltpu.CompilerParams(collective_id=identity, vmem_limit_bytes=VMEM_LIMIT),
        cost_estimate=pl.CostEstimate(flops=40 * PLANE * rows * width * share // 2, bytes_accessed=30 * 2**20, transcendentals=0),
        name="feed_forward",
    )(out_rows, attended, tokens, teacher, out_grad, valid, gains, gate_up_w, down_rows)


HEAD_TILES = 3
ROW_STEP = 64


def by_rows(rows, body, step=ROW_STEP):
    def run(i, carry):
        body(pl.ds(pl.multiple_of(i * step, step), step))
        return carry

    lax.fori_loop(0, rows // step, run, 0)


def lanes_of(values):
    return lax.broadcasted_iota(jnp.int32, values.shape, len(values.shape) - 1)


def turned(tile, cosine, sine):
    half = HD // 2
    partner = jnp.where(lanes_of(tile) < half, -pltpu.roll(tile, LANES - half, 1), pltpu.roll(tile, half, 1))
    return tile * cosine + partner * sine


def packed_pair(first, second, even):
    lane = lanes_of(first)
    moved = pltpu.roll(second, HD, 1)
    full_even = jnp.where(lane < HD, first, moved)
    full_odd = jnp.where(lane < 32, pltpu.roll(first, 64, 1), pltpu.roll(second, 32, 1))
    return jnp.where(even, full_even, full_odd), jnp.where(even, moved, first)


def unpacked_pair(full, part, even):
    lane = lanes_of(full)
    zero = jnp.zeros_like(full)
    first_even = jnp.where(lane < HD, full, zero)
    second_even = jnp.where(lane < 32, pltpu.roll(full, 32, 1), jnp.where(lane < HD, pltpu.roll(part, 32, 1), zero))
    first_odd = jnp.where(lane < 64, part, jnp.where(lane < HD, pltpu.roll(full, 64, 1), zero))
    second_odd = jnp.where(lane < HD, pltpu.roll(full, HD, 1), zero)
    return jnp.where(even, first_even, first_odd), jnp.where(even, second_even, second_odd)


def keys_and_values(qkv, keys, values, count, rows):
    def body(src, carry):
        block = qkv[src].astype(jnp.float32)
        tiles = [block[:, i * LANES : (i + 1) * LANES] for i in range(HEAD_TILES)]
        lane = lanes_of(tiles[0])
        key = jnp.where(lane < HD, tiles[2], 0.0)
        value = jnp.where(lane < 64, pltpu.roll(tiles[1], 64, 1), pltpu.roll(tiles[2], HD, 1))
        value = jnp.where(lane < 32, pltpu.roll(tiles[0], 32, 1), value)
        value = jnp.where(lane < HD, value, 0.0)
        at = pl.ds(pl.multiple_of(src * rows, rows), rows)
        for half in range(2):
            keys[half, at, :] = key[half * rows : (half + 1) * rows].astype(keys.dtype)
            values[half, at, :] = value[half * rows : (half + 1) * rows].astype(values.dtype)
        return carry

    lax.fori_loop(0, count, body, 0)


def segment_of(lengths, place):
    start, end = jnp.zeros_like(place), 0
    for length in [lengths[0, j] for j in range(NSEQ)]:
        end = end + length
        start = start + jnp.where(place >= end, length, 0)
    return start, end


def side_by_side(heads):
    full, part = packed_pair(heads[0], heads[1], True)
    full_odd, part_odd = packed_pair(heads[2], heads[3], False)
    middle = jnp.where(lanes_of(part) < 64, part, pltpu.roll(part_odd, 64, 1))
    return full, middle, full_odd


def apart(ref, group):
    start = group * HEAD_TILES * LANES
    tiles = [ref[:, start + i * LANES : start + (i + 1) * LANES].astype(jnp.float32) for i in range(HEAD_TILES)]
    return unpacked_pair(tiles[0], tiles[1], True) + unpacked_pair(tiles[2], pltpu.roll(tiles[1], 64, 1), False)


def arrange_rows(rows_in, w_query, w_key, w_value, gain_rows, count):
    share = rows_in.shape[0]
    groups = HEADS // KV
    queries = [head for group in range(HEADS // 4) for head in apart(w_query, group)]
    keys = [head for group in range(KV // 4) for head in apart(w_key, group)]
    values = [head for group in range(KV // 4) for head in apart(w_value, group)]
    lane = lanes_of(keys[0])
    for head in range(KV):
        for number, tile in enumerate(queries[head * groups : (head + 1) * groups] + [keys[head]]):
            third = pltpu.roll(values[head], HD - 32 * number, 1)
            start = (head * HEAD_TILES + number) * LANES
            rows_in[:, start : start + LANES] = jnp.where(lane < HD, tile, third).astype(rows_in.dtype)
    row = lax.broadcasted_iota(jnp.int32, (LANES, LANES), 0)
    columns = jnp.where(row == 0, gain_rows[0:1, :], jnp.where(row == 1, gain_rows[1:2, :], 0.0))
    columns = jnp.where(row == 2, count, columns)
    rows_in[:, KV * HEAD_TILES * LANES :] = jnp.transpose(columns)[:share, :].astype(rows_in.dtype)


def attend_kernel(
    scale, lines, w_query, w_key, w_value, w_gate, w_up, out_rows, gain_rows, freq, mask, deal, lengths, tokens,
    attended, normed, gains, cosine, sine, valid, weights, out_w, unit_w, qkv_out, probs,
    rows_in, unit_rows, w, place_row, sent, qkv, keys, values, prob_blocks, o_sent, o_came,
    send, recv, o_send, o_recv, p_sem, q_sem, w_sem, w_line_send, w_line_recv, w_send, w_recv, w_here, g_send, g_recv, g_here,
    o_line_send, o_line_recv,
    u_send, u_recv, u_here, l_send, l_recv,
):
    z, y, x, c = coordinates()
    count = sent.shape[0]
    me = z * 2 + y
    even = y == 0
    rows, width = tokens.shape
    half_rows = rows // 2
    head_cols = HEAD_TILES * LANES
    to_device = lambda i: (i, x * 2 + c)
    peer = lambda k: lax.rem(me + k, count)

    member = y * 4 + x * 2 + c
    in_plane = lambda i: (z * 2 + i // 4, i % 4)
    unit_peer = lambda k: lax.rem(member + k, PLANE)
    others = [device(z, yy, xx, cc) for yy, xx, cc in ((y, 1 - x, c), (y, x, 1 - c), (y, 1 - x, 1 - c))]
    others += [device(z, 1 - y, xx, cc) for xx, cc in ((1 - x, c), (x, 1 - c), (1 - x, 1 - c))]
    units = w_gate.shape[1] // (lines * PLANE)
    for i in range(PLANE):
        for zz in range(lines):
            start = (zz * PLANE + i) * units
            unit_rows[i, :, zz * units : (zz + 1) * units] = w_gate[:, start : start + units]
            unit_rows[i, :, (lines + zz) * units : (lines + zz + 1) * units] = w_up[:, start : start + units]
    greet([to_device(peer(k)) for k in range(1, count)] + others)

    def unit_out(k):
        i = unit_peer(k)
        return remote(unit_rows.at[i], unit_w.at[z, member], u_send.at[k], u_recv.at[k], in_plane(i))

    unit_own = pltpu.make_async_copy(unit_rows.at[member], unit_w.at[z, member], u_here)
    unit_own.start()
    columns = rows_in.shape[1]
    line_gathers, plane_gathers = [], []
    for part, of in enumerate(halves(columns)):
        line_gathers.append(
            line_gather(
                (z, y, x, c), lines, rows_in.at[:, of], lambda zz, of=of: w.at[zz, member, :, of],
                w_line_send.at[part], w_line_recv.at[part], w_here.at[part],
            )
        )
        plane_gathers.append(
            PlaneGather(
                (z, y, x, c), lambda yy, xx, of=of: w.at[:, yy * 4 + xx * 2 + c, :, of], of.size,
                w_send.at[part], w_recv.at[part],
            )
        )
    (one_begin, one_pass, one_last), (two_begin, two_pass, two_last) = line_gathers
    one, two = plane_gathers
    out_begin, out_pass, out_last = line_gather(
        (z, y, x, c), lines, out_rows, lambda zz: out_w.at[zz, member], o_line_send, o_line_recv, g_here
    )
    out_gather = PlaneGather(
        (z, y, x, c), lambda yy, xx: out_w.at[:, yy * 4 + xx * 2 + c], out_rows.shape[1], g_send, g_recv
    )
    line_begin, line_pass, line_last = line_gather(
        (z, y, x, c), lines, unit_w.at[z], lambda zz: unit_w.at[zz], l_send, l_recv
    )
    for k in range(1, PLANE):
        unit_out(k).start()
    first_block = deal[0, me]
    total = functools.reduce(lambda a, b: a + b, [lengths[0, j] for j in range(NSEQ)])
    token = lax.broadcasted_iota(jnp.int32, (1, rows), 1)
    in_pack = jnp.where(token < half_rows, first_block * half_rows, (2 * count - 2 - first_block) * half_rows) + token
    counted = jnp.where(in_pack < total, mask[...].astype(jnp.float32), 0.0)
    arrange_rows(rows_in, w_query, w_key, w_value, gain_rows, jnp.sum(counted, -1, keepdims=True))
    one_begin()
    valid[...] = jnp.transpose(jnp.broadcast_to(counted, (LANES, rows)))[:, :1]
    token = lax.broadcasted_iota(jnp.int32, (rows, 1), 0)
    in_pack = jnp.where(token < half_rows, first_block * half_rows, (2 * count - 2 - first_block) * half_rows) + token
    angle = (in_pack - segment_of(lengths, in_pack)[0]).astype(jnp.float32) * freq[...]
    cosine[...] = jnp.cos(angle)
    sine[...] = jnp.sin(angle)
    one_pass(1)
    two_begin()
    for moment in range(2, lines):
        one_pass(moment)
        two_pass(moment - 1)
    one_last()
    one.begin()
    two_pass(lines - 1)
    two_last()
    unit_own.wait()
    for k in range(1, PLANE):
        unit_out(k).wait_recv()
    line_begin()
    out_begin()
    one.forward_on()
    two.begin()
    for moment in range(1, lines - 1):
        out_pass(moment)
    one.corner_on()
    out_pass(lines - 1)
    out_last()
    two.forward_on()
    line_pass(1)
    one.rest()
    two.corner_on()
    two.rest()
    keep_weights = pltpu.make_async_copy(w, weights, w_sem)
    keep_weights.start()

    def columns_of(start, size):
        return w[:, :, :, pl.ds(start, size)].reshape(width, size)

    extras = columns_of(count * head_cols, LANES)
    gains[...] = jnp.transpose(extras.astype(jnp.float32))[: gains.shape[0], :]
    gain = gains[0:1, :]

    def norm_rows(at):
        values_at = tokens[at, :].astype(jnp.float32)
        normed[at, :] = (values_at * rms_scale(values_at) * gain).astype(normed.dtype)

    by_rows(rows, norm_rows)

    def out(k):
        return remote(sent.at[peer(k)], qkv.at[me], send.at[k], recv.at[k], to_device(peer(k)))

    def project(k, carry):
        i = peer(k)
        columns = columns_of(pl.multiple_of(i * head_cols, LANES), head_cols)
        both = jnp.dot(normed[...], columns, preferred_element_type=jnp.float32)
        for tile in range(HEAD_TILES):
            at = slice(tile * LANES, (tile + 1) * LANES)
            sent[i, :, at] = turned(both[:, at], cosine[...], sine[...]).astype(sent.dtype)

        @pl.when(k < count)
        def _():
            out(k).start()

        return carry

    lax.fori_loop(1, count + 1, project, 0)
    out_gather.begin()
    line_pass(2)
    qkv[me] = sent[me]
    for src in range(count):
        columns = slice(src * half_rows, (src + 1) * half_rows)
        steps = lax.broadcasted_iota(jnp.int32, (1, half_rows), 1)
        place_row[0, :, columns] = deal[0, src] * half_rows + steps
        place_row[1, :, columns] = (2 * count - 1 - deal[0, src]) * half_rows + steps

    def arrive(k, carry):
        out(k).wait_recv()
        return carry

    out_gather.forward_on()
    out_gather.corner_on()
    lax.fori_loop(1, count, arrive, 0)
    keep_qkv = pltpu.make_async_copy(qkv, qkv_out, q_sem)
    keep_qkv.start()
    keys_and_values(qkv, keys, values, count, half_rows)

    def back(k):
        return remote(o_sent.at[peer(k)], o_came.at[me], o_send.at[k], o_recv.at[k], to_device(peer(k)))

    def keep(src, half):
        return pltpu.make_async_copy(prob_blocks.at[src, half], probs.at[src, half], p_sem.at[src, half])

    def attend(k, carry):
        src = peer(k)
        halves_out = []
        for half in range(2):
            at = pl.ds(half * half_rows, half_rows)
            queries = jnp.concatenate([qkv[src, at, :LANES], qkv[src, at, LANES : 2 * LANES]], 0)
            score = against(queries, keys[half]) * scale
            first = deal[0, src]
            block = first if half == 0 else 2 * count - 1 - first
            own = block * half_rows + lax.broadcasted_iota(jnp.int32, (half_rows, 1), 0)
            start, end = segment_of(lengths, own)
            lowest = jnp.where(own < end, start, own)
            place = place_row[half]
            allowed = (place >= lowest) & (place <= own)
            bias = jnp.where(allowed, 0.0, masked_score)
            score = score + jnp.concatenate([bias, bias], 0)
            top = jnp.max(score, -1, keepdims=True)
            weight = jnp.exp(score - top)
            total = jnp.sum(weight, -1, keepdims=True)
            low = (weight * (1.0 / total)).astype(prob_blocks.dtype)
            prob_blocks[src, half] = low
            keep(src, half).start()
            summed = jnp.dot(low, values[half], preferred_element_type=jnp.float32)
            full, part = packed_pair(summed[:half_rows], summed[half_rows:], even)
            o_sent[src, at, :] = full.astype(o_sent.dtype)
            halves_out.append(part)
        lane = lanes_of(halves_out[0])
        part = jnp.where(lane < 64, halves_out[0], pltpu.roll(halves_out[1], 64, 1))
        o_sent[src, pl.ds(rows, half_rows), :] = part.astype(o_sent.dtype)

        @pl.when(k < count)
        def _():
            back(k).start()

        return carry

    lax.fori_loop(1, count + 1, attend, 0)
    o_came[me] = o_sent[me]

    def return_arrive(k, carry):
        back(k).wait_recv()
        return carry

    lax.fori_loop(1, count, return_arrive, 0)
    for pair in range(count // 2):
        at = pair * head_cols
        attended[:, at : at + LANES] = o_came[2 * pair, :rows, :]
        attended[:, at + 2 * LANES : at + 3 * LANES] = o_came[2 * pair + 1, :rows, :]
        one = o_came[2 * pair, rows:, :].astype(jnp.float32)
        two = o_came[2 * pair + 1, rows:, :].astype(jnp.float32)
        lane = lanes_of(one)
        middle = slice(at + LANES, at + 2 * LANES)
        attended[:half_rows, middle] = jnp.where(lane < 64, one, pltpu.roll(two, 64, 1)).astype(attended.dtype)
        attended[half_rows:, middle] = jnp.where(lane < 64, pltpu.roll(one, 64, 1), two).astype(attended.dtype)

    def drain(k, carry):
        out(k).wait_send()
        back(k).wait_send()
        return carry

    lax.fori_loop(1, count, drain, 0)

    def drain_probs(src, carry):
        keep(src, 0).wait()
        keep(src, 1).wait()
        return carry

    lax.fori_loop(0, count, drain_probs, 0)
    keep_qkv.wait()
    out_gather.rest()
    for gather in (out_gather, *plane_gathers):
        gather.drain()
    for moment in range(3, lines):
        line_pass(moment)
    line_last()
    for k in range(1, PLANE):
        unit_out(k).wait_send()
    keep_weights.wait()


def attend(scale, lines, w_query, w_key, w_value, w_gate, w_up, out_rows, gain_rows, freq, mask, deal, lengths, tokens, identity):
    rows, width = tokens.shape
    share, units = out_rows.shape[0], w_gate.shape[1] // PLANE
    count = KV
    columns = count * HEAD_TILES * LANES + LANES
    half_rows = rows // 2
    half = count * half_rows
    head_cols = HEAD_TILES * LANES
    low = tokens.dtype
    shape = jax.ShapeDtypeStruct
    vmem, anywhere = pl.BlockSpec(memory_space=pltpu.VMEM), pl.BlockSpec(memory_space=pl.ANY)
    smem = pl.BlockSpec(memory_space=pltpu.SMEM)
    dma = pltpu.SemaphoreType.DMA
    return pl.pallas_call(
        functools.partial(attend_kernel, scale, lines),
        out_shape=[
            shape((rows, width), low),
            shape((rows, width), low),
            shape((8, width), jnp.float32),
            shape((rows, LANES), jnp.float32),
            shape((rows, LANES), jnp.float32),
            shape((rows, 1), jnp.float32),
            shape((lines, PLANE, share, columns), low),
            shape((lines, PLANE) + out_rows.shape, low),
            shape((lines, PLANE, share, 2 * units), low),
            shape((count, rows, head_cols), low),
            shape((count, 2, rows, half), low),
        ],
        in_specs=[vmem] * 5 + [anywhere] + [vmem] * 3 + [smem, smem, vmem],
        out_specs=[vmem] * 6 + [anywhere] * 5,
        scratch_shapes=[
            pltpu.VMEM((share, columns), low),
            pltpu.VMEM((PLANE, share, 2 * units), low),
            pltpu.VMEM((lines, PLANE, share, columns), low),
            pltpu.VMEM((2, 1, half), jnp.int32),
            pltpu.VMEM((count, rows, head_cols), low),
            pltpu.VMEM((count, rows, head_cols), low),
            pltpu.VMEM((2, half, LANES), low),
            pltpu.VMEM((2, half, LANES), low),
            pltpu.VMEM((count, 2, rows, half), low),
            pltpu.VMEM((count, rows + half_rows, LANES), low),
            pltpu.VMEM((count, rows + half_rows, LANES), low),
            dma((count,)),
            dma((count,)),
            dma((count,)),
            dma((count,)),
            dma((count, 2)),
            dma,
            dma,
            dma((2, 2, lines)),
            dma((2, 2, lines)),
            dma((2, GATHER_KINDS)),
            dma((2, GATHER_KINDS)),
            dma((2,)),
            dma((GATHER_KINDS,)),
            dma((GATHER_KINDS,)),
            dma,
            dma((2, lines)),
            dma((2, lines)),
            dma((PLANE,)),
            dma((PLANE,)),
            dma,
            dma((2, lines)),
            dma((2, lines)),
        ],
        compiler_params=pltpu.CompilerParams(collective_id=identity, vmem_limit_bytes=VMEM_LIMIT),
        name="attend",
    )(w_query, w_key, w_value, w_gate, w_up, out_rows, gain_rows, freq, mask, deal, lengths, tokens)


def attend_back_kernel(
    scale, lines, attended_grad, probs, cosine, sine, qkv_in, attended_in, branch_in, gate_in, down_in,
    qkv_grad, out_final, gate_sums, down_final,
    qkv, attended, branch, gate_parts, down_parts, in_sem,
    sent, came, keys, values, prob_blocks, dk_sum, dv_sum, back_sent, back_came,
    send, recv, back_send, back_recv, p_sem, up, down, l_send, l_recv, down_up, down_down, d_send, d_recv, p, *reducing,
):
    z, y, x, c = coordinates()
    count = sent.shape[0]
    me = z * 2 + y
    even = y == 0
    rows, width = attended_grad.shape
    half_rows = rows // 2
    head_cols = HEAD_TILES * LANES
    to_device = lambda i: (i, x * 2 + c)
    peer = lambda k: lax.rem(me + k, count)
    source = lambda k: lax.rem(me + count - k, count)

    loads = transfers(
        (attended_in, branch_in, qkv_in, gate_in, down_in), (attended, branch, qkv, gate_parts, down_parts), in_sem
    )
    for load_in in loads:
        load_in.start()

    def load(src, half):
        return pltpu.make_async_copy(probs.at[src, half], prob_blocks.at[src, half], p_sem.at[src, half])

    def load_start(k, carry):
        load(source(k), 0).start()
        load(source(k), 1).start()
        return carry

    lax.fori_loop(0, count, load_start, 0)
    greet([to_device(peer(k)) for k in range(1, count)] + [device(z, y, 1 - x, c), device(z, y, x, 1 - c)])
    members, share = p.shape[1:3]

    def prepare(block):
        at = pl.ds(pl.multiple_of(block * members * share, LANES), members * share)
        store_terms(p, block, 0, transposed(attended[:, at], branch[...]))

    reduce_stages, reduce_last = reduce_plan(lines, prepare, p, out_final, *reducing)
    line_begin, line_hop, line_last = line_reduce((z, y, x, c), lines, gate_parts, up, down, l_send, l_recv)
    down_begin, down_hop, down_last = line_reduce((z, y, x, c), lines, down_parts, down_up, down_down, d_send, d_recv)
    for pair in range(count // 2):
        at = pair * head_cols
        sent[2 * pair, :rows, :] = attended_grad[:, at : at + LANES]
        sent[2 * pair + 1, :rows, :] = attended_grad[:, at + 2 * LANES : at + 3 * LANES]
        middle = attended_grad[:, at + LANES : at + 2 * LANES].astype(jnp.float32)
        one, two = middle[:half_rows], middle[half_rows:]
        lane = lanes_of(one)
        sent[2 * pair, rows:, :] = jnp.where(lane < 64, one, pltpu.roll(two, 64, 1)).astype(sent.dtype)
        sent[2 * pair + 1, rows:, :] = jnp.where(lane < 64, pltpu.roll(one, 64, 1), two).astype(sent.dtype)

    def out(k):
        return remote(sent.at[peer(k)], came.at[me], send.at[k], recv.at[k], to_device(peer(k)))

    def begin(k, carry):
        out(k).start()
        return carry

    lax.fori_loop(1, count, begin, 0)
    for load_in in loads[:2]:
        load_in.wait()
    reduce_stages[0]()
    came[me] = sent[me]
    for load_in in loads[2:]:
        load_in.wait()
    keys_and_values(qkv, keys, values, count, half_rows)
    dk_sum[...] = jnp.zeros_like(dk_sum)
    dv_sum[...] = jnp.zeros_like(dv_sum)

    def pack(src, kind, at, first, second):
        full, part = packed_pair(first, second, even)
        back_sent[src, kind, at, :] = full.astype(back_sent.dtype)
        return part

    def pack_parts(src, kind, parts):
        part = jnp.where(lanes_of(parts[0]) < 64, parts[0], pltpu.roll(parts[1], 64, 1))
        back_sent[src, kind, pl.ds(rows, half_rows), :] = part.astype(back_sent.dtype)

    def back(kind, k):
        to = source(k) if kind == 0 else peer(k)
        return remote(
            back_sent.at[to, kind], back_came.at[me, kind], back_send.at[kind, k], back_recv.at[kind, k], to_device(to)
        )

    def grads(k, carry):
        src = source(k)

        @pl.when(k > 0)
        def _():
            out(k).wait_recv()

        parts = []
        for half in range(2):
            at = pl.ds(half * half_rows, half_rows)
            full = came[src, at, :].astype(jnp.float32)
            part = came[src, pl.ds(rows, half_rows), :].astype(jnp.float32)
            if half:
                part = pltpu.roll(part, 64, 1)
            pair = jnp.concatenate(unpacked_pair(full, part, even), 0).astype(came.dtype)
            queries = jnp.concatenate([qkv[src, at, :LANES], qkv[src, at, LANES : 2 * LANES]], 0)
            load(src, half).wait()
            low = prob_blocks[src, half]
            prob = low.astype(jnp.float32)
            prob_grad = against(pair, values[half])
            delta = jnp.sum(prob * prob_grad, -1, keepdims=True)
            score_low = (prob * (prob_grad - delta)).astype(low.dtype)
            dq = jnp.dot(score_low, keys[half], preferred_element_type=jnp.float32) * scale
            parts.append(pack(src, 0, at, dq[:half_rows], dq[half_rows:]))
            dk_sum[half] += transposed(score_low, queries)
            dv_sum[half] += transposed(low, pair)
        pack_parts(src, 0, parts)

        @pl.when(k > 0)
        def _():
            back(0, k).start()

        pl.when(k == 2)(line_begin)
        pl.when(k == 5)(down_begin)
        for number in range(1, len(reduce_stages)):
            pl.when(k == number)(reduce_stages[number])
        return carry

    lax.fori_loop(0, count, grads, 0)

    def finish(k, carry):
        src = peer(k)
        in_half = pl.ds(pl.multiple_of(src * half_rows, half_rows), half_rows)
        parts = []
        for half in range(2):
            at = pl.ds(half * half_rows, half_rows)
            parts.append(pack(src, 1, at, dk_sum[half, in_half, :] * scale, dv_sum[half, in_half, :]))
        pack_parts(src, 1, parts)

        @pl.when(k < count)
        def _():
            back(1, k).start()

        return carry

    lax.fori_loop(1, count + 1, finish, 0)
    for moment in range(1, lines - 1):
        line_hop(moment)
        down_hop(moment)
    reduce_last()
    back_came[me] = back_sent[me]

    def turn_back(k, carry):
        src = source(k)
        src_even = lax.rem(src, 2) == 0

        @pl.when(k > 0)
        def _():
            back(0, count - k).wait_recv()
            back(1, k).wait_recv()

        for half in range(2):
            at = pl.ds(half * half_rows, half_rows)
            heads = []
            for kind in range(2):
                full = back_came[src, kind, at, :].astype(jnp.float32)
                part = back_came[src, kind, pl.ds(rows, half_rows), :].astype(jnp.float32)
                if half:
                    part = pltpu.roll(part, 64, 1)
                heads.extend(unpacked_pair(full, part, src_even))
            dv = heads.pop()
            lane = lanes_of(dv)
            for tile in range(HEAD_TILES):
                turned_at = turned(heads[tile], cosine[at, :], -sine[at, :])
                joined = jnp.where(lane < HD, turned_at, pltpu.roll(dv, HD - 32 * tile, 1))
                to = pl.ds(pl.multiple_of(src * head_cols + tile * LANES, LANES), LANES)
                qkv_grad[at, to] = joined.astype(qkv_grad.dtype)
        return carry

    lax.fori_loop(0, count, turn_back, 0)

    def keep_sums(i, sums):
        gate_sums[i] = sums.astype(gate_sums.dtype)

    line_last(keep_sums, gate_sums.shape[1])

    def keep_down(i, sums):
        down_final[pl.ds(pl.multiple_of(i * 32, 32), 32), :] = sums

    down_last(keep_down)

    def drain(k, carry):
        out(k).wait_send()
        back(0, k).wait_send()
        back(1, k).wait_send()
        return carry

    lax.fori_loop(1, count, drain, 0)


def attend_back(scale, lines, attended_grad, qkv, probs, tables, attended, branch, gate_parts, down_parts, identity):
    rows, width = attended_grad.shape
    count, _, head_cols = qkv.shape
    half = probs.shape[-1]
    half_rows = rows // 2
    share = width // (lines * PLANE)
    low = attended_grad.dtype
    vmem, anywhere = pl.BlockSpec(memory_space=pltpu.VMEM), pl.BlockSpec(memory_space=pl.ANY)
    dma = pltpu.SemaphoreType.DMA
    return pl.pallas_call(
        functools.partial(attend_back_kernel, scale, lines),
        out_shape=[
            jax.ShapeDtypeStruct((rows, count * head_cols), low),
            jax.ShapeDtypeStruct((share, width), jnp.float32),
            jax.ShapeDtypeStruct((PLANE, share, gate_parts.shape[2]), low),
            jax.ShapeDtypeStruct(down_parts.shape[1:], jnp.float32),
        ],
        in_specs=[vmem, anywhere, vmem, vmem] + [anywhere] * 5,
        out_specs=[vmem] * 4,
        scratch_shapes=[
            pltpu.VMEM(qkv.shape, low),
            pltpu.VMEM(attended.shape, low),
            pltpu.VMEM(branch.shape, low),
            pltpu.VMEM(gate_parts.shape, low),
            pltpu.VMEM(down_parts.shape, low),
            dma((5,)),
            pltpu.VMEM((count, rows + half_rows, LANES), low),
            pltpu.VMEM((count, rows + half_rows, LANES), low),
            pltpu.VMEM((2, half, LANES), low),
            pltpu.VMEM((2, half, LANES), low),
            pltpu.VMEM((count, 2, rows, half), low),
            pltpu.VMEM((2, half, LANES), jnp.float32),
            pltpu.VMEM((2, half, LANES), jnp.float32),
            pltpu.VMEM((count, 2, rows + half_rows, LANES), low),
            pltpu.VMEM((count, 2, rows + half_rows, LANES), low),
            dma((count,)),
            dma((count,)),
            dma((2, count)),
            dma((2, count)),
            dma((count, 2)),
            pltpu.VMEM(gate_parts.shape, low),
            pltpu.VMEM(gate_parts.shape, low),
            dma((2, lines)),
            dma((2, lines)),
            pltpu.VMEM(down_parts.shape, low),
            pltpu.VMEM(down_parts.shape, low),
            dma((2, lines)),
            dma((2, lines)),
            *reduce_scratch(lines, share, width, low),
        ],
        compiler_params=pltpu.CompilerParams(collective_id=identity, vmem_limit_bytes=VMEM_LIMIT),
        name="attend_back",
    )(attended_grad, probs, *tables, qkv, attended, branch, gate_parts, down_parts)


def finish_kernel(
    weights, normed, qkv_grad, gains, square, norm, up_parts, gate_sums, hidden_in, tokens_in, gate_in, up_in,
    input_grad, query_final, key_final, value_final, gate_final, up_final, gain_final, loss,
    hidden_grad, tokens, w_gate, w_up, in_sem, w, own_rows, normed_grad, final, up_sums, gate_came, up_came, line_up, line_down,
    w_sem, own_sem, gate_send, gate_recv, up_send, up_recv, here, l_send, l_recv, p, *reducing,
):
    z, y, x, c = coordinates()
    lines, members, share = p.shape[:3]
    rows, width = tokens.shape
    qkv_cols = qkv_grad.shape[1]
    low = normed.dtype
    load = pltpu.make_async_copy(weights.at[:, pl.ds(0, qkv_cols)], w, w_sem)
    load.start()
    loads = transfers((hidden_in, tokens_in, gate_in, up_in), (hidden_grad, tokens, w_gate, w_up), in_sem)
    for load_in in loads:
        load_in.start()
    number = (z * 2 + y) * 4 + x * 2 + c
    own_at = pl.ds(pl.multiple_of(number * share, 16), share)
    load_own = pltpu.make_async_copy(weights.at[own_at, :], own_rows, own_sem)
    load_own.start()
    me = y * 4 + x * 2 + c
    peer = lambda k: lax.rem(me + k, members)
    member = lambda i: (z * 2 + i // 4, i % 4)
    greet([member(peer(k)) for k in range(1, members)] + line_of(z, y, x, c, lines))

    def out(kind, k):
        src, came, send, recv = (
            (gate_sums, gate_came, gate_send, gate_recv),
            (up_sums, up_came, up_send, up_recv),
        )[kind]
        return remote(src.at[peer(k)], came.at[me], send.at[k], recv.at[k], member(peer(k)))

    gate_own = pltpu.make_async_copy(gate_sums.at[me], gate_came.at[me], here)
    gate_own.start()
    for k in range(1, members):
        out(0, k).start()
    line_begin, line_hop, line_last = line_reduce((z, y, x, c), lines, up_parts, line_up, line_down, l_send, l_recv)
    line_begin()

    def keep_up(i, sums):
        up_sums[i] = sums.astype(up_sums.dtype)

    devices = lines * PLANE
    place = lax.broadcasted_iota(jnp.int32, (1, LANES), 1) - number
    rest = square[...]
    loss_terms = jnp.zeros((1, LANES), jnp.float32)
    for term in range(3):
        top = rest.astype(low).astype(jnp.float32)
        loss_terms = loss_terms + jnp.where(place == term * devices, top, 0.0)
        rest = rest - top

    def prepare(block):
        at = pl.ds(pl.multiple_of(block * members * share, LANES), members * share)
        left = normed[:, at]
        chunk = qkv_cols // 2
        for start in range(0, qkv_cols, chunk):
            store_terms(p, block, start, transposed(left, qkv_grad[:, start : start + chunk]))
        store_terms(p, block, qkv_cols, jnp.broadcast_to(loss_terms, (members * share, LANES)))

    stages, last = reduce_plan(lines, prepare, p, final, *reducing)

    def grad_rows(at):
        values = tokens[at, :].astype(jnp.float32)
        scale = rms_scale(values)
        unit = values * scale
        scaled = normed_grad[at, :] * gains[0:1, :]
        input_grad[at, :] = hidden_grad[at, :] + scale * (
            scaled - unit * jnp.mean(scaled * unit, -1, keepdims=True)
        )

    block = rows // lines
    for index, stage in enumerate(stages):
        if index == 2:
            load.wait()
            for load_in in loads:
                load_in.wait()
        if 2 <= index < lines:
            line_hop(index - 1)
        if index == 1 + lines:
            line_last(keep_up, share)
            for k in range(1, members):
                out(1, k).start()
        stage()
        if 2 <= index < 2 + lines:
            at = slice((index - 2) * block, (index - 1) * block)
            normed_grad[at, :] = against(qkv_grad[at, :], w[...])
        if index == 2 + lines:
            by_rows(rows, grad_rows)
    up_came[me] = up_sums[me]
    gate_own.wait()
    for kind in range(2):
        for k in range(1, members):
            out(kind, k).wait_recv()
    units = gate_came.shape[2] // lines
    for i in range(members):
        for zz in range(lines):
            to = slice((zz * members + i) * units, (zz * members + i + 1) * units)
            of = slice(zz * units, (zz + 1) * units)
            gate_final[:, to] = gate_came[i, :, of].astype(jnp.float32)
            up_final[:, to] = up_came[i, :, of].astype(jnp.float32)
    last()

    def tile(head, number):
        start = (head * HEAD_TILES + number) * LANES
        return final[:, start : start + LANES]

    def put(ref, group, heads):
        for number, value in enumerate(side_by_side(heads)):
            start = (group * HEAD_TILES + number) * LANES
            ref[:, start : start + LANES] = value

    for pair in range(KV // 2):
        put(query_final, pair, [tile(2 * pair + i, j) for i in range(2) for j in range(2)])
    for group in range(KV // 4):
        heads = [4 * group + i for i in range(4)]
        put(key_final, group, [tile(head, 2) for head in heads])
        parts = []
        for head in heads:
            thirds = [pltpu.roll(tile(head, number), 32 * (number + 1), 1) for number in range(HEAD_TILES)]
            in_tile = lanes_of(thirds[0])
            parts.append(jnp.where(in_tile < 32, thirds[0], jnp.where(in_tile < 64, thirds[1], thirds[2])))
        put(value_final, group, parts)

    load_own.wait()
    own_gains = own_rows[:, qkv_cols:].astype(jnp.float32)

    def product(grads, weights_of, width_of):
        sums = jnp.zeros((share, 1), jnp.float32)
        for start in range(0, width_of, 4 * LANES):
            at = slice(start, start + 4 * LANES)
            sums += jnp.sum(grads[:, at] * weights_of[:, at].astype(jnp.float32), -1, keepdims=True)
        return sums

    units_all = w_gate.shape[1]
    first_gain = product(final, own_rows, qkv_cols) / own_gains[:, 0:1]
    second_gain = product(gate_final, w_gate, units_all) + product(up_final, w_up, units_all)
    second_gain = second_gain / own_gains[:, 1:2]
    columns = lax.broadcasted_iota(jnp.int32, (share, LANES), 1)
    both_gains = jnp.where(columns == 0, first_gain, jnp.where(columns == 1, second_gain, 0.0))
    both_gains = jnp.concatenate([both_gains, jnp.zeros((LANES - share, LANES), jnp.float32)], 0)
    gain_final[...] = jnp.transpose(both_gains)[:8, :]
    tail = final[:, qkv_cols:]
    of_loss = lax.broadcasted_iota(jnp.int32, (1, LANES), 1) < 3 * devices
    loss[...] = jnp.sum(jnp.where(of_loss, tail[:1, :], 0.0), -1, keepdims=True) * (0.5 * norm[...])
    for kind in range(2):
        for k in range(1, members):
            out(kind, k).wait_send()


def finish(
    lines, weights, normed, qkv_grad, hidden_grad, tokens, gains, square, norm, w_gate, w_up, gate_sums, up_parts, identity
):
    rows, width = tokens.shape
    qkv_cols = qkv_grad.shape[1]
    share = weights.shape[0] // (lines * PLANE)
    columns = weights.shape[1]
    units_all = w_gate.shape[1]
    low = tokens.dtype
    vmem, anywhere = pl.BlockSpec(memory_space=pltpu.VMEM), pl.BlockSpec(memory_space=pl.ANY)
    dma = pltpu.SemaphoreType.DMA
    shapes = [
        (rows, width),
        (share, width),
        (share, KV * HD),
        (share, KV * HD),
        (share, units_all),
        (share, units_all),
        (8, LANES),
        (1, 1),
    ]
    return pl.pallas_call(
        finish_kernel,
        out_shape=[jax.ShapeDtypeStruct(shape, jnp.float32) for shape in shapes],
        in_specs=[anywhere] + [vmem] * 6 + [anywhere] * 5,
        out_specs=[vmem] * len(shapes),
        scratch_shapes=[
            pltpu.VMEM(hidden_grad.shape, jnp.float32),
            pltpu.VMEM(tokens.shape, low),
            pltpu.VMEM(w_gate.shape, low),
            pltpu.VMEM(w_up.shape, low),
            dma((4,)),
            pltpu.VMEM((width, qkv_cols), low),
            pltpu.VMEM((share, columns), low),
            pltpu.VMEM((rows, width), jnp.float32),
            pltpu.VMEM((share, columns), jnp.float32),
            pltpu.VMEM(gate_sums.shape, low),
            pltpu.VMEM(gate_sums.shape, low),
            pltpu.VMEM(gate_sums.shape, low),
            pltpu.VMEM(up_parts.shape, low),
            pltpu.VMEM(up_parts.shape, low),
            dma,
            dma,
            dma((PLANE,)),
            dma((PLANE,)),
            dma((PLANE,)),
            dma((PLANE,)),
            dma,
            dma((2, lines)),
            dma((2, lines)),
            *reduce_scratch(lines, share, columns, low),
        ],
        compiler_params=pltpu.CompilerParams(collective_id=identity, vmem_limit_bytes=VMEM_LIMIT),
        name="finish",
    )(weights, normed, qkv_grad, gains, square, norm, up_parts, gate_sums, hidden_grad, tokens, w_gate, w_up)


def emit_kernel(joined, *refs):
    sem = refs[-1]
    count = (len(refs) - 2) // 2
    out = refs[count + 1 : -1]
    pairs = [(refs[i], out[i]) for i in range(count)]
    cut = refs[joined].shape[1]
    pairs[joined] = (refs[joined], out[joined].at[:, pl.ds(0, cut)])
    pairs.append((refs[count], out[joined].at[:, pl.ds(cut, refs[count].shape[1])]))
    copies = [pltpu.make_async_copy(src, dst, sem.at[i]) for i, (src, dst) in enumerate(pairs)]
    for copy in copies:
        copy.start()
    for copy in copies:
        copy.wait()


def emit(arrays, joined, rest):
    shapes = [array.shape for array in arrays]
    shapes[joined] = (shapes[joined][0], shapes[joined][1] + rest.shape[1])
    return pl.pallas_call(
        functools.partial(emit_kernel, joined),
        out_shape=[jax.ShapeDtypeStruct(shape, array.dtype) for shape, array in zip(shapes, arrays)],
        in_specs=[pl.BlockSpec(memory_space=pl.ANY)] * (len(arrays) + 1),
        out_specs=[pl.BlockSpec(memory_space=pltpu.VMEM)] * len(arrays),
        scratch_shapes=[pltpu.SemaphoreType.DMA((len(arrays) + 1,))],
        compiler_params=pltpu.CompilerParams(vmem_limit_bytes=VMEM_LIMIT),
        name="emit",
    )(*arrays, rest)


def plane_per_device(lines, *arrays):
    (
        tokens,
        lengths,
        deal,
        loss_mask,
        teacher,
        out_grad,
        attn_gain,
        w_query,
        w_key,
        w_value,
        w_out,
        ffn_gain,
        w_gate,
        w_up,
        w_down,
    ) = arrays
    devices = lines * PLANE
    width = tokens.shape[2]
    weight_rows = w_query.shape[0]
    scale = HD ** (-0.5)
    gain_rows = jnp.zeros((8, LANES), jnp.float32)
    gain_rows = gain_rows.at[0, :weight_rows].set(attn_gain.astype(jnp.float32))
    gain_rows = gain_rows.at[1, :weight_rows].set(ffn_gain.astype(jnp.float32))
    freq = rope_base ** (-(np.arange(HD // 2) * 2.0 / HD))
    freq = np.concatenate([freq, freq, np.zeros(LANES - HD)])[None].astype(np.float32)

    attended_low, normed_low, gains, cosine, sine, valid, attn_all, out_w, gate_up_w, qkv, probs = attend(
        scale,
        lines,
        w_query,
        w_key,
        w_value,
        w_gate,
        w_up,
        w_out,
        gain_rows,
        freq,
        loss_mask,
        deal,
        lengths,
        tokens[0],
        3,
    )
    attn_all = attn_all.reshape(devices * weight_rows, -1)
    gate_up_w = gate_up_w.reshape(devices * weight_rows, -1)

    result, square, norm, hidden_grad, branch_low, attended_grad, down_final, down_rest, gate_grad, up_grad = feed_forward(
        lines,
        out_w.reshape(width, width),
        attended_low,
        tokens[0],
        teacher[0],
        out_grad[0],
        valid,
        gains,
        gate_up_w,
        w_down,
        5,
    )
    gate_grad, up_grad = [grad.reshape(lines, PLANE * weight_rows, -1) for grad in (gate_grad, up_grad)]
    qkv_grad, out_final, gate_sums, down_more = attend_back(
        scale, lines, attended_grad, qkv, probs, (cosine, sine), attended_low, branch_low, gate_grad, down_rest, 9
    )

    input_grad, query_final, key_final, value_final, gate_final, up_final, gain_final, loss = finish(
        lines,
        attn_all,
        normed_low,
        qkv_grad,
        hidden_grad,
        tokens[0],
        gains,
        square,
        norm,
        w_gate,
        w_up,
        gate_sums,
        up_grad,
        11,
    )
    result, input_grad, query_final, key_final, value_final, out_final, gate_final, up_final, down_final = emit(
        (result, input_grad, query_final, key_final, value_final, out_final, gate_final, up_final, down_final),
        8,
        down_more,
    )
    return (
        result[None],
        loss.reshape(()),
        input_grad[None],
        gain_final[0, :weight_rows],
        query_final,
        key_final,
        value_final,
        out_final,
        gain_final[1, :weight_rows],
        gate_final,
        up_final,
        down_final,
    )


def suits_planes(mesh):
    sizes = dict(mesh.shape)
    return sizes["fsdp"] == 4 and sizes["ctx"] == KV


def solution(mesh):
    placed = (
        P("fsdp", "ctx", None),
        P("fsdp", None),
        P("fsdp", None),
        P("fsdp", "ctx"),
        P("fsdp", "ctx", None),
        P("fsdp", "ctx", None),
        P(("ctx", "fsdp")),
        P(("ctx", "fsdp"), None),
        P(("ctx", "fsdp"), None),
        P(("ctx", "fsdp"), None),
        P(("ctx", "fsdp"), None),
        P(("ctx", "fsdp")),
        P(("ctx", "fsdp"), None),
        P(("ctx", "fsdp"), None),
        P(("ctx", "fsdp"), None),
    )
    if suits_planes(mesh):
        per_device = functools.partial(plane_per_device, mesh.shape["ctx"] // ROWS_Y)
    else:
        per_device = ring_per_device
    return jax.shard_map(
        per_device,
        mesh=mesh,
        in_specs=placed,
        out_specs=(
            P("fsdp", "ctx", None),
            P(),
            P("fsdp", "ctx", None),
            P(("ctx", "fsdp")),
            P(("ctx", "fsdp"), None),
            P(("ctx", "fsdp"), None),
            P(("ctx", "fsdp"), None),
            P(("ctx", "fsdp"), None),
            P(("ctx", "fsdp")),
            P(("ctx", "fsdp"), None),
            P(("ctx", "fsdp"), None),
            P(("ctx", "fsdp"), None),
        ),
        check_vma=False,
    )
```

```python
import functools

import jax
import jax.numpy as jnp
import numpy as np
from jax import lax
from jax.experimental import pallas as pl
from jax.experimental.pallas import tpu as pltpu
from jax.sharding import PartitionSpec as P

HEADS = 16
KV = 8
HD = 96
NSEQ = 6


rope_base = 100000.0
epsilon = 1e-05
masked_score = -1e30


def shifted(value, axis, by):
    size = lax.axis_size(axis)
    return lax.ppermute(value, axis, [(i, (i + by) % size) for i in range(size)])


def rms_scale(values):
    return lax.rsqrt(jnp.mean(values * values, -1, keepdims=True) + epsilon)


def rotary_tables(inseq):
    freq = rope_base ** (-(jnp.arange(HD // 2, dtype=jnp.float32) * 2.0 / HD))
    angle = inseq.astype(jnp.float32)[:, None] * freq[None, :]
    return (jnp.cos(angle)[:, None, :], jnp.sin(angle)[:, None, :])


def rotary(values, cosine, sine):
    half = values.shape[-1] // 2
    first = values[..., :half]
    second = values[..., half:]
    return jnp.concatenate([first * cosine - second * sine, second * cosine + first * sine], -1)


def rotary_back(grads, cosine, sine):
    half = grads.shape[-1] // 2
    first = grads[..., :half]
    second = grads[..., half:]
    return jnp.concatenate([first * cosine + second * sine, second * cosine - first * sine], -1)


def transposed(left, right):
    return lax.dot_general(
        left, right, (((0,), (0,)), ((), ())), preferred_element_type=jnp.float32
    )


def against(left, right):
    return lax.dot_general(
        left, right, (((1,), (1,)), ((), ())), preferred_element_type=jnp.float32
    )


def permitted(query_place, query_seg, key_place, key_seg):
    same = (query_seg[:, None] == key_seg[None, :]) & (query_seg[:, None] < NSEQ)
    return same & (key_place[None, :] <= query_place[:, None]) | (
        key_place[None, :] == query_place[:, None]
    )


def ring_per_device(
    tokens,
    lengths,
    deal,
    loss_mask,
    teacher,
    out_grad,
    attn_gain,
    w_query,
    w_key,
    w_value,
    w_out,
    ffn_gain,
    w_gate,
    w_up,
    w_down,
):
    count_ctx = lax.axis_size("ctx")
    myself = lax.axis_index("ctx")
    tok_rows = tokens.shape[1]
    width = tokens.shape[2]
    half_block = tok_rows // 2
    groups = HEADS // KV
    scale = HD ** (-0.5)
    gain_one, query_w, key_w, value_w, out_w = (
        lax.all_gather(attn_gain, ("ctx", "fsdp"), axis=0, tiled=True),
        lax.all_gather(w_query, ("ctx", "fsdp"), axis=0, tiled=True),
        lax.all_gather(w_key, ("ctx", "fsdp"), axis=0, tiled=True),
        lax.all_gather(w_value, ("ctx", "fsdp"), axis=0, tiled=True),
        lax.all_gather(w_out, ("ctx", "fsdp"), axis=0, tiled=True),
    )
    gain_two, gate_w, up_w, down_w = (
        lax.all_gather(ffn_gain, ("ctx", "fsdp"), axis=0, tiled=True),
        lax.all_gather(w_gate, ("ctx", "fsdp"), axis=0, tiled=True),
        lax.all_gather(w_up, ("ctx", "fsdp"), axis=0, tiled=True),
        lax.all_gather(w_down, ("ctx", "fsdp"), axis=0, tiled=True),
    )
    dealt = jnp.arange(count_ctx * tok_rows, dtype=jnp.int32)
    local = dealt % tok_rows
    first = jnp.repeat(deal[0], tok_rows)
    block = jnp.where(local < half_block, first, 2 * count_ctx - 1 - first)
    places = block * half_block + local % half_block
    ends = jnp.cumsum(lengths[0])
    after = (places[:, None] >= ends[None, :]).astype(jnp.int32)
    seg_all = jnp.sum(after, 1)
    inseq_all = places - jnp.sum(after * lengths[0][None, :], 1)
    own_place = lax.dynamic_slice_in_dim(places, myself * tok_rows, tok_rows)
    own_seg = lax.dynamic_slice_in_dim(seg_all, myself * tok_rows, tok_rows)
    own_inseq = lax.dynamic_slice_in_dim(inseq_all, myself * tok_rows, tok_rows)
    cosine, sine = rotary_tables(own_inseq)
    inputs = tokens[0].astype(jnp.float32)
    scale_one = rms_scale(inputs)
    normed_one = inputs * scale_one
    gain_first = gain_one.astype(jnp.float32)
    normed_low = (normed_one * gain_first).astype(jnp.bfloat16)
    query_pre = jnp.dot(normed_low, query_w, preferred_element_type=jnp.float32).reshape(
        tok_rows, HEADS, HD
    )
    key_pre = jnp.dot(normed_low, key_w, preferred_element_type=jnp.float32).reshape(
        tok_rows, KV, HD
    )
    value_low = jnp.dot(normed_low, value_w, preferred_element_type=jnp.float32).astype(
        jnp.bfloat16
    )
    queries = rotary(query_pre, cosine, sine).astype(jnp.bfloat16).reshape(tok_rows, KV, groups, HD)
    keys = rotary(key_pre, cosine, sine).astype(jnp.bfloat16).reshape(tok_rows, KV * HD)

    def logits(key_block):
        return (
            jnp.einsum(
                "qcgd,kcd->cgqk",
                queries,
                key_block.reshape(-1, KV, HD),
                preferred_element_type=jnp.float32,
            )
            * scale
        )

    key_block = lax.all_gather(keys, "ctx", axis=0, tiled=True)
    value_block = lax.all_gather(value_low, "ctx", axis=0, tiled=True)
    allowed = permitted(own_place, own_seg, places, seg_all)
    top = jnp.full((KV, groups, tok_rows, 1), masked_score, jnp.float32)
    score = jnp.where(allowed, logits(key_block), masked_score)
    new_top = jnp.maximum(top, jnp.max(score, -1, keepdims=True))
    weight = jnp.where(allowed, jnp.exp(score - new_top), 0.0)
    summed = jnp.einsum(
        "cgqk,kcd->cgqd",
        weight.astype(jnp.bfloat16),
        value_block.reshape(-1, KV, HD),
        preferred_element_type=jnp.float32,
    )
    summed, top, total = (summed, new_top, jnp.sum(weight, -1, keepdims=True))
    attended = summed / total
    log_total = top + jnp.log(total)
    attended_low = (
        jnp.transpose(attended, (2, 0, 1, 3)).reshape(tok_rows, HEADS * HD).astype(jnp.bfloat16)
    )
    hidden = inputs + jnp.dot(attended_low, out_w, preferred_element_type=jnp.float32)
    scale_two = rms_scale(hidden)
    normed_two = hidden * scale_two
    gain_second = gain_two.astype(jnp.float32)
    ffn_low = (normed_two * gain_second).astype(jnp.bfloat16)
    gate = jnp.dot(ffn_low, gate_w, preferred_element_type=jnp.float32)
    up = jnp.dot(ffn_low, up_w, preferred_element_type=jnp.float32)
    sigmoid = jax.nn.sigmoid(gate)
    activated = gate * sigmoid
    mixed_low = (activated * up).astype(jnp.bfloat16)
    result = hidden + jnp.dot(mixed_low, down_w, preferred_element_type=jnp.float32)
    target = teacher[0].astype(jnp.float32)
    valid = (loss_mask[0] * (own_seg < NSEQ)).astype(jnp.float32)[:, None]
    differ = result - target
    square_sum, valid_count = lax.psum(
        (jnp.sum(valid * differ * differ), jnp.sum(valid)), ("ctx", "fsdp")
    )
    loss = square_sum / (valid_count * width)
    out_total = out_grad[0].astype(jnp.float32) + 2.0 * valid * differ / (valid_count * width)
    out_low = out_total.astype(jnp.bfloat16)
    down_grad = transposed(mixed_low, out_low)
    mixed_grad = against(out_low, down_w)
    silu_slope = sigmoid * (1.0 + gate * (1.0 - sigmoid))
    gate_low = (mixed_grad * up * silu_slope).astype(jnp.bfloat16)
    up_low = (mixed_grad * activated).astype(jnp.bfloat16)
    gate_grad = transposed(ffn_low, gate_low)
    up_grad = transposed(ffn_low, up_low)
    normed_grad = against(gate_low, gate_w) + against(up_low, up_w)
    gain_two_grad = jnp.sum(normed_grad * normed_two, 0)
    scaled_two = normed_grad * gain_second
    hidden_grad = out_total + scale_two * (
        scaled_two - normed_two * jnp.mean(scaled_two * normed_two, -1, keepdims=True)
    )
    ffn_final = (
        lax.psum_scatter(gain_two_grad, ("ctx", "fsdp"), scatter_dimension=0, tiled=True),
        lax.psum_scatter(gate_grad, ("ctx", "fsdp"), scatter_dimension=0, tiled=True),
        lax.psum_scatter(up_grad, ("ctx", "fsdp"), scatter_dimension=0, tiled=True),
        lax.psum_scatter(down_grad, ("ctx", "fsdp"), scatter_dimension=0, tiled=True),
    )
    branch_low = hidden_grad.astype(jnp.bfloat16)
    out_w_grad = transposed(attended_low, branch_low)
    attended_grad = against(branch_low, out_w).astype(jnp.bfloat16)
    grad_heads = jnp.transpose(attended_grad.reshape(tok_rows, KV, groups, HD), (1, 2, 0, 3))
    delta = jnp.sum(grad_heads.astype(jnp.float32) * attended, -1, keepdims=True)

    def cycle_step(step, state):
        key_block, value_block, key_acc, value_acc, query_acc = state
        source = (myself - step) % count_ctx
        allowed = permitted(
            own_place,
            own_seg,
            lax.dynamic_slice_in_dim(places, source * tok_rows, tok_rows),
            lax.dynamic_slice_in_dim(seg_all, source * tok_rows, tok_rows),
        )
        current_key = key_block
        current_value = value_block
        keys_three = current_key.reshape(tok_rows, KV, HD)
        values_three = current_value.reshape(tok_rows, KV, HD)
        prob = jnp.where(allowed, jnp.exp(logits(current_key) - log_total), 0.0)
        prob_grad = jnp.einsum(
            "cgqd,kcd->cgqk", grad_heads, values_three, preferred_element_type=jnp.float32
        )
        score_low = (prob * (prob_grad - delta)).astype(jnp.bfloat16)
        query_add = (
            jnp.einsum("cgqk,kcd->cgqd", score_low, keys_three, preferred_element_type=jnp.float32)
            * scale
        )
        key_add = (
            jnp.einsum(
                "cgqk,qcgd->kcd", score_low, queries, preferred_element_type=jnp.float32
            ).reshape(tok_rows, KV * HD)
            * scale
        )
        value_add = jnp.einsum(
            "cgqk,cgqd->kcd",
            prob.astype(jnp.bfloat16),
            grad_heads,
            preferred_element_type=jnp.float32,
        ).reshape(tok_rows, KV * HD)
        key_block, value_block = shifted((key_block, value_block), "ctx", 1)
        key_acc, value_acc = (
            shifted((key_acc + key_add).astype(jnp.bfloat16), "ctx", 1).astype(jnp.float32),
            shifted((value_acc + value_add).astype(jnp.bfloat16), "ctx", 1).astype(jnp.float32),
        )
        return (key_block, value_block, key_acc, value_acc, query_acc + query_add)

    cycle_start = (
        keys,
        value_low,
        jnp.zeros((tok_rows, KV * HD), jnp.float32),
        jnp.zeros((tok_rows, KV * HD), jnp.float32),
        jnp.zeros((KV, groups, tok_rows, HD), jnp.float32),
    )
    cycle_end = lax.fori_loop(0, count_ctx, cycle_step, cycle_start)
    key_acc = cycle_end[2]
    value_acc = cycle_end[3]
    query_acc = cycle_end[4]
    query_grad = jnp.transpose(query_acc, (2, 0, 1, 3)).reshape(tok_rows, HEADS, HD)
    query_low = (
        rotary_back(query_grad, cosine, sine).reshape(tok_rows, HEADS * HD).astype(jnp.bfloat16)
    )
    key_low = (
        rotary_back(key_acc.reshape(tok_rows, KV, HD), cosine, sine)
        .reshape(tok_rows, KV * HD)
        .astype(jnp.bfloat16)
    )
    value_grad_low = value_acc.astype(jnp.bfloat16)
    query_w_grad = transposed(normed_low, query_low)
    key_w_grad = transposed(normed_low, key_low)
    value_w_grad = transposed(normed_low, value_grad_low)
    normed_one_grad = (
        against(query_low, query_w) + against(key_low, key_w) + against(value_grad_low, value_w)
    )
    gain_one_grad = jnp.sum(normed_one_grad * normed_one, 0)
    scaled_one = normed_one_grad * gain_first
    input_grad = hidden_grad + scale_one * (
        scaled_one - normed_one * jnp.mean(scaled_one * normed_one, -1, keepdims=True)
    )
    attn_final = (
        lax.psum_scatter(gain_one_grad, ("ctx", "fsdp"), scatter_dimension=0, tiled=True),
        lax.psum_scatter(query_w_grad, ("ctx", "fsdp"), scatter_dimension=0, tiled=True),
        lax.psum_scatter(key_w_grad, ("ctx", "fsdp"), scatter_dimension=0, tiled=True),
        lax.psum_scatter(value_w_grad, ("ctx", "fsdp"), scatter_dimension=0, tiled=True),
        lax.psum_scatter(out_w_grad, ("ctx", "fsdp"), scatter_dimension=0, tiled=True),
    )
    return (
        result.astype(jnp.bfloat16)[None],
        loss,
        input_grad[None],
        attn_final[0],
        attn_final[1],
        attn_final[2],
        attn_final[3],
        attn_final[4],
        ffn_final[0],
        ffn_final[1],
        ffn_final[2],
        ffn_final[3],
    )


MESH = pl.DeviceIdType.MESH
ROWS_Y = 2
PLANE = 8
LANES = 128
VMEM_LIMIT = 60 * 2**20


def coordinates():
    ctx = lax.axis_index("ctx")
    fsdp = lax.axis_index("fsdp")
    return ctx // 2, ctx % 2, fsdp // 2, fsdp % 2


def device(z, y, x, c):
    return (z * 2 + y, x * 2 + c)


def greet(devices):
    barrier = pltpu.get_barrier_semaphore()
    for other in devices:
        pl.semaphore_signal(barrier, inc=1, device_id=other, device_id_type=MESH)
    pl.semaphore_wait(barrier, len(devices))


def remote(src, dst, send, recv, target):
    return pltpu.make_async_remote_copy(
        src_ref=src,
        dst_ref=dst,
        send_sem=send,
        recv_sem=recv,
        device_id=target,
        device_id_type=MESH,
    )


def transfers(sources, targets, sem):
    return [pltpu.make_async_copy(src, dst, sem.at[i]) for i, (src, dst) in enumerate(zip(sources, targets))]


def line_gather(place, lines, x_ref, slot, send, recv, here=None):
    z, y, x, c = place
    mine = None if here is None else pltpu.make_async_copy(x_ref, slot(z), here)
    ways = ((0, -1, device(z + 1, y, x, c)), (1, 1, device(z - 1, y, x, c)))

    def along(way, sign, to, s):
        zz = z + sign * (s - 1)
        return remote(x_ref if s == 1 else slot(zz), slot(zz), send.at[way, s], recv.at[way, s], to)

    def sends(sign, s):
        if sign < 0:
            return (z - (s - 1) >= 0) & (z + 1 < lines)
        return (z + (s - 1) < lines) & (z - 1 >= 0)

    def present(sign, s):
        return z - s >= 0 if sign < 0 else z + s < lines

    def start(s):
        for way, sign, to in ways:
            pl.when(sends(sign, s))(lambda way=way, sign=sign, to=to: along(way, sign, to, s).start())

    def begin():
        if mine is not None:
            mine.start()
        start(1)

    def pass_on(s):
        for way, sign, to in ways:
            pl.when(present(sign, s))(lambda way=way, sign=sign, to=to: along(way, sign, to, s).wait_recv())
        if s + 1 < lines:
            start(s + 1)

    def last():
        for s in range(1, lines):
            for way, sign, to in ways:
                pl.when(sends(sign, s))(lambda way=way, sign=sign, to=to, s=s: along(way, sign, to, s).wait_send())
        if mine is not None:
            mine.wait()

    return begin, pass_on, last


def line_reduce(place, lines, parts, up, down, send, recv):
    z, y, x, c = place
    ways = ((0, up, device(z + 1, y, x, c)), (1, down, device(z - 1, y, x, c)))

    def copy(way, t, own):
        _, sums, to = ways[way]
        src = parts.at[t] if own else sums.at[t]
        return remote(src, sums.at[t], send.at[way, t], recv.at[way, t], to)

    def begin():
        @pl.when(z == 0)
        def _():
            for t in range(lines - 1, 0, -1):
                copy(0, t, True).start()

        @pl.when(z == lines - 1)
        def _():
            for t in range(lines - 1):
                copy(1, t, True).start()

    def add_on(way, t):
        copy(way, t, False).wait_recv()
        add_rows(ways[way][1].at[t], parts.at[t])
        copy(way, t, False).start()

    def hop(moment):
        for t in range(lines):
            for zz in range(1, lines - 1):
                if zz < t and zz + (lines - 1 - t) == moment:
                    pl.when(z == zz)(functools.partial(add_on, 0, t))
                if zz > t and (lines - 1 - zz) + t == moment:
                    pl.when(z == zz)(functools.partial(add_on, 1, t))

    def last(write, step=32):
        for way, first in ((0, 0), (1, lines - 1)):

            @pl.when(z != first)
            def _():
                copy(way, z, False).wait_recv()

        def body(i, carry):
            at = pl.ds(pl.multiple_of(i * step, step), step)
            from_below = jnp.where(z > 0, up[z, at, :].astype(jnp.float32), 0.0)
            from_above = jnp.where(z < lines - 1, down[z, at, :].astype(jnp.float32), 0.0)
            write(i, parts[z, at, :].astype(jnp.float32) + from_below + from_above)
            return carry

        lax.fori_loop(0, parts.shape[1] // step, body, 0)
        for zz in range(lines):

            @pl.when(z == zz)
            def _():
                for t in range(lines):
                    if t > zz:
                        copy(0, t, zz == 0).wait_send()
                    if t < zz:
                        copy(1, t, zz == lines - 1).wait_send()

    return begin, hop, last


def column_cut(width):
    tiles = width // LANES
    return (tiles + 1) // 2 * LANES


def line_of(z, y, x, c, lines):
    return [device(lax.rem(z + k, lines), y, x, c) for k in range(1, lines)]


def reduce_plan(lines, prepare, p_ref, o_ref, held, corner_a, corner_b, from_side, from_over, along, send, recv):
    z, y, x, c = coordinates()
    parts = lines
    rows, width = held.shape[2], held.shape[3]
    cut = column_cut(width)
    first, second = pl.ds(0, cut), pl.ds(cut, width - cut)
    side, over, sibling = device(z, y, 1 - x, c), device(z, 1 - y, x, c), device(z, y, x, 1 - c)
    def given(part, yy, xx, cc):
        member = yy * 4 + xx * 2 + cc
        return p_ref.at[lax.rem(z + part + 1, lines), member]

    def make(part, kind, src, dst, to):
        return remote(src, dst, send.at[part, kind], recv.at[part, kind], to)

    lane = lambda part, yy, xx: held.at[part, yy * 2 + xx]

    def over_core(part):
        return [
            make(part, yy * 2 + xx, given(part, yy, xx, 1 - c), lane(part, yy, xx), sibling)
            for yy in range(2)
            for xx in range(2)
        ]

    def to_corner(part):
        return (
            make(part, 4, lane(part, 1 - y, 1 - x).at[:, first], corner_a.at[part], over),
            make(part, 5, lane(part, 1 - y, 1 - x).at[:, second], corner_b.at[part], side),
        )

    def to_neighbour(part, way):
        columns = (first, second)[way % 2]
        if way < 2:
            return make(part, 6 + way, lane(part, y, 1 - x).at[:, columns], from_side.at[part, :, columns], side)
        return make(part, 6 + way, lane(part, 1 - y, x).at[:, columns], from_over.at[part, :, columns], over)

    def along_z(part):
        to = lax.rem(z + part + 1, lines)
        return make(part, 10, lane(part, y, x), along.at[part], device(to, y, x, c))

    step = 16

    def add_core(part):
        for copy in over_core(part):
            copy.wait_recv()
        for yy, xx in ((1 - y, 1 - x), (y, 1 - x), (1 - y, x), (y, x)):
            mine, other = given(part, yy, xx, c), lane(part, yy, xx)

            def body(i, carry):
                at = pl.ds(pl.multiple_of(i * step, step), step)
                total = mine[at, :].astype(jnp.float32) + other[at, :].astype(jnp.float32)
                other[at, :] = total.astype(other.dtype)
                return carry

            lax.fori_loop(0, rows // step, body, 0)
        for copy in to_corner(part):
            copy.start()
        to_neighbour(part, 1).start()
        to_neighbour(part, 2).start()

    def add_corner(part):
        copies = to_corner(part)
        pairs = (
            (copies[0], lane(part, y, 1 - x), corner_a.at[part], first),
            (copies[1], lane(part, 1 - y, x), corner_b.at[part], second),
        )
        for copy, mine, other, columns in pairs:
            copy.wait_recv()

            def body(i, carry):
                at = pl.ds(pl.multiple_of(i * step, step), step)
                total = mine[at, columns].astype(jnp.float32) + other[at, :].astype(jnp.float32)
                mine[at, columns] = total.astype(mine.dtype)
                return carry

            lax.fori_loop(0, rows // step, body, 0)
        to_neighbour(part, 0).start()
        to_neighbour(part, 3).start()

    def add_neighbours(part):
        for way in range(4):
            to_neighbour(part, way).wait_recv()
        last = part == parts - 1
        mine = lane(part, y, x)

        def body(i, carry):
            at = pl.ds(pl.multiple_of(i * step, step), step)
            total = mine[at, :].astype(jnp.float32) + from_side[part, at, :].astype(jnp.float32)
            total += from_over[part, at, :].astype(jnp.float32)
            if last:
                o_ref[at, :] = total
            else:
                mine[at, :] = total.astype(mine.dtype)
            return carry

        lax.fori_loop(0, rows // step, body, 0)
        if not last:
            along_z(part).start()

    def ready(part):
        prepare(lax.rem(z + part + 1, lines))
        for copy in over_core(part):
            copy.start()

    kinds = (ready, add_core, add_corner, add_neighbours)

    def run(number):
        for lag, kind in enumerate(kinds):
            if 0 <= number - lag < parts:
                kind(number - lag)

    def last():
        for part in range(parts - 1):
            along_z(part).wait_recv()

        def body(i, carry):
            at = pl.ds(pl.multiple_of(i * step, step), step)
            total = o_ref[at, :]
            for part in range(parts - 1):
                total += along[part, at, :].astype(jnp.float32)
            o_ref[at, :] = total
            return carry

        lax.fori_loop(0, rows // step, body, 0)
        for part in range(parts - 1):
            along_z(part).wait_send()
        for part in range(parts):
            for copy in (*over_core(part), *to_corner(part), *(to_neighbour(part, way) for way in range(4))):
                copy.wait_send()

    return [functools.partial(run, number) for number in range(parts + len(kinds) - 1)], last


def reduce_scratch(lines, share, columns, low):
    cut = column_cut(columns)
    return [
        pltpu.VMEM((lines, PLANE, share, columns), low),
        pltpu.VMEM((lines, 4, share, columns), low),
        pltpu.VMEM((lines, share, cut), low),
        pltpu.VMEM((lines, share, columns - cut), low),
        pltpu.VMEM((lines, share, columns), low),
        pltpu.VMEM((lines, share, columns), low),
        pltpu.VMEM((lines - 1, share, columns), low),
        pltpu.SemaphoreType.DMA((lines, 11)),
        pltpu.SemaphoreType.DMA((lines, 11)),
    ]


def store_terms(p, block, start, value):
    members, share = p.shape[1:3]
    width = value.shape[1]
    p[block, :, :, start : start + width] = value.astype(p.dtype).reshape(members, share, width)


def halves(width):
    cut = column_cut(width)
    return pl.ds(0, cut), pl.ds(cut, width - cut)


class PlaneGather:
    def __init__(self, place, at, width, send, recv):
        z, y, x, c = place
        side, over, sibling = device(z, y, 1 - x, c), device(z, 1 - y, x, c), device(z, y, x, 1 - c)
        self.send, self.recv = send, recv
        own, next_x, next_y, corner = at(y, x), at(y, 1 - x), at(1 - y, x), at(1 - y, 1 - x)
        first, second = [lambda ref, of=of: ref.at[..., of] for of in halves(width)]
        self.table = (
            (first(own), side),
            (second(own), side),
            (first(own), over),
            (second(own), over),
            (own, sibling),
            (first(next_x), over),
            (second(next_y), side),
            (first(next_x), sibling),
            (second(next_x), sibling),
            (first(next_y), sibling),
            (second(next_y), sibling),
            (first(corner), sibling),
            (second(corner), sibling),
        )

    def copy(self, kind):
        ref, to = self.table[kind]
        return remote(ref, ref, self.send.at[kind], self.recv.at[kind], to)

    def begin(self):
        for kind in (0, 3, 4, 1, 2):
            self.copy(kind).start()

    def came(self, *kinds):
        for kind in kinds:
            self.copy(kind).wait_recv()

    def forward_on(self):
        for kind, onward in ((0, (5, 7)), (3, (6, 10)), (1, (8,)), (2, (9,))):
            self.came(kind)
            for other in onward:
                self.copy(other).start()

    def corner_on(self):
        for kind, onward in ((5, 11), (6, 12)):
            self.came(kind)
            self.copy(onward).start()

    def rest(self):
        self.came(4, *range(7, GATHER_KINDS))

    def drain(self):
        for kind in range(GATHER_KINDS):
            self.copy(kind).wait_send()


GATHER_KINDS = 13
REDUCE_KINDS = 10


def reduce_steps(place, at_rows, partial, held, corner_a, corner_b, from_side, from_over, send, recv):
    z, y, x, c = place
    side, over, sibling = device(z, y, 1 - x, c), device(z, 1 - y, x, c), device(z, y, x, 1 - c)
    first, second = halves(held.shape[-1])
    lane = lambda yy, xx: held.at[yy * 2 + xx, at_rows]
    next_x, next_y, corner = lane(y, 1 - x), lane(1 - y, x), lane(1 - y, 1 - x)

    def to_core(yy, xx):
        kind = yy * 2 + xx
        src = partial.at[yy * 4 + xx * 2 + 1 - c, at_rows]
        return remote(src, lane(yy, xx), send.at[kind], recv.at[kind], sibling)

    table = (
        (corner.at[:, first], corner_a.at[at_rows], over),
        (corner.at[:, second], corner_b.at[at_rows], side),
        (next_x.at[:, first], from_side.at[at_rows, first], side),
        (next_x.at[:, second], from_side.at[at_rows, second], side),
        (next_y.at[:, first], from_over.at[at_rows, first], over),
        (next_y.at[:, second], from_over.at[at_rows, second], over),
    )

    def copy(kind):
        src, dst, to = table[kind]
        return remote(src, dst, send.at[4 + kind], recv.at[4 + kind], to)

    return to_core, copy


def add_rows(target, other, columns=None, step=32):
    def body(i, carry):
        at = pl.ds(pl.multiple_of(i * step, step), step)
        mine = target[at, :] if columns is None else target[at, columns]
        total = (mine.astype(jnp.float32) + other[at, :].astype(jnp.float32)).astype(target.dtype)
        if columns is None:
            target[at, :] = total
        else:
            target[at, columns] = total
        return carry

    lax.fori_loop(0, other.shape[0] // step, body, 0)


def feed_forward_kernel(
    out_rows, attended, tokens, teacher_rows, out_grad_rows, valid, gains, gate_up_rows, down_rows,
    result_out, square, norm, hidden_grad, branch, attended_grad, down_final, down_out, gate_out, up_out,
    result, down_rest, gate_grad, up_grad, store_sem, out_w, gate_up_w, teacher, out_grad, down_w, down_up, down_down, normed_all, kept, mixed, grads_all, partial, held, corner_a, corner_b, from_side, from_over, hidden, total_grad, scales, squares,
    load_sem, here, line_send, line_recv, down_send, down_recv, gather_send, gather_recv, reduce_send, reduce_recv,
):
    place = coordinates()
    z, y, x, c = place
    width = tokens.shape[1]
    pairs = ((out_rows, out_w), (gate_up_rows, gate_up_w), (teacher_rows, teacher), (out_grad_rows, out_grad))
    loads = [pltpu.make_async_copy(src, dst, load_sem.at[i]) for i, (src, dst) in enumerate(pairs)]
    for load in loads:
        load.start()
    lines, units = down_w.shape[:2]
    greet([device(z, y, 1 - x, c), device(z, 1 - y, x, c), device(z, y, x, 1 - c)] + line_of(z, y, x, c, lines))
    rows = tokens.shape[0]
    share = lines * units
    first, second = halves(width)
    down_lines = [
        line_gather(
            place, lines, down_rows.at[:, of], lambda zz, of=of: down_w.at[zz, :, of],
            line_send.at[i], line_recv.at[i], here.at[i],
        )
        for i, of in enumerate((first, second))
    ]
    (begin_one, pass_one, last_one), (begin_two, pass_two, last_two) = down_lines
    begin_one()
    begin_two()
    mine = y * 4 + x * 2 + c
    chips = ((y, x), (y, 1 - x), (1 - y, x), (1 - y, 1 - x))

    gain = gains[1:2, :]
    count = jnp.sum(gains[2:3, :], -1, keepdims=True) / (width // (lines * PLANE))
    norm[...] = 2.0 / (count * width)
    loads[0].wait()
    def hidden_rows(at):
        product = jnp.dot(attended[at, :], out_w[...], preferred_element_type=jnp.float32)
        hidden[at, :] = tokens[at, :].astype(jnp.float32) + product

    def norm_rows(at):
        values = hidden[at, :]
        scale = rms_scale(values)
        scales[at, :] = scale
        normed_all[mine, at, :] = (values * scale * gain[...]).astype(normed_all.dtype)

    parts = 2
    part_rows = rows // parts
    at_part = [pl.ds(part * part_rows, part_rows) for part in range(parts)]

    def of_part(part, body):
        by_rows(part_rows, lambda at: body(pl.ds(pl.multiple_of(part * part_rows + at.start, ROW_STEP), ROW_STEP)))

    class Phase(PlaneGather):
        def __init__(self, phase, part, whole):
            at_rows = at_part[part]
            self.part, self.at_rows = part, at_rows
            at = lambda yy, xx: whole.at[yy * 4 + xx * 2 + c, at_rows]
            super().__init__(place, at, width, gather_send.at[phase, part], gather_recv.at[phase, part])
            self.to_core, self.pass_on = reduce_steps(
                place, at_rows, partial, held, corner_a, corner_b, from_side, from_over,
                reduce_send.at[phase, part], reduce_recv.at[phase, part],
            )

        def join(self, yy, xx):
            self.to_core(yy, xx).wait_recv()
            add_rows(held.at[yy * 2 + xx, self.at_rows], partial.at[yy * 4 + xx * 2 + c, self.at_rows])

        def join_next(self, number):
            self.join(*chips[number])
            self.pass_on(2 + number).start()

        def join_corner(self):
            self.join(*chips[3])
            self.pass_on(0).start()
            self.pass_on(1).start()

        def add_corner(self):
            self.pass_on(0).wait_recv()
            add_rows(held.at[y * 2 + 1 - x, self.at_rows], corner_a.at[self.at_rows], first)
            self.pass_on(2).start()
            self.pass_on(1).wait_recv()
            add_rows(held.at[(1 - y) * 2 + x, self.at_rows], corner_b.at[self.at_rows], second)
            self.pass_on(5).start()

        def complete(self):
            for kind in (2, 3, 4, 5):
                self.pass_on(kind).wait_recv()
            for kind in range(6):
                self.pass_on(kind).wait_send()
            for yy, xx in chips:
                self.to_core(yy, xx).wait_send()

    def pair_of(number):
        yy, xx = chips[number]
        return pl.ds(yy * 4 + xx * 2, 2)

    one, two = [Phase(0, part, normed_all) for part in range(parts)]
    hidden_rows(at_part[0])
    of_part(0, norm_rows)
    one.begin()
    hidden_rows(at_part[1])
    of_part(1, norm_rows)

    def summed(at):
        total = held[y * 2 + x, at, :].astype(jnp.float32) + from_side[at, :].astype(jnp.float32)
        return total + from_over[at, :].astype(jnp.float32)

    def units_of(phase, number):
        where = (pair_of(number), phase.at_rows)
        both = jnp.dot(
            normed_all[where].reshape(rows, width), gate_up_w[...], preferred_element_type=jnp.float32
        )
        gate, up = both[:, :share], both[:, share:]
        sigmoid = 1.0 / (1.0 + jnp.exp(-gate))
        activated = gate * sigmoid
        slope = up * (sigmoid + activated * (1.0 - sigmoid))
        kept[(*where, slice(0, share))] = slope.astype(kept.dtype).reshape(2, part_rows, share)
        kept[(*where, slice(share, 2 * share))] = activated.astype(kept.dtype).reshape(2, part_rows, share)
        mixed[where] = (activated * up).astype(mixed.dtype).reshape(2, part_rows, share)

    def down_of(phase, number):
        where = (pair_of(number), phase.at_rows)
        out = jnp.dot(
            mixed[where].reshape(rows, share),
            down_w[...].reshape(share, width),
            preferred_element_type=jnp.float32,
        )
        partial[where] = out.astype(partial.dtype).reshape(2, part_rows, width)
        phase.to_core(*chips[number]).start()

    one.came(4)
    loads[1].wait()
    units_of(one, 0)
    pass_one(1)
    pass_two(1)
    one.forward_on()
    two.begin()
    for moment in range(2, lines - 1):
        pass_one(moment)
    one.came(7, 8)
    units_of(one, 1)
    for moment in range(2, lines - 1):
        pass_two(moment)
    one.came(9, 10)
    units_of(one, 2)
    pass_one(lines - 1)
    one.corner_on()
    two.came(4)
    units_of(two, 0)
    pass_two(lines - 1)
    last_one()
    last_two()
    two.forward_on()
    one.came(11, 12)
    units_of(one, 3)
    down_of(one, 1)
    two.came(7, 8)
    units_of(two, 1)
    down_of(one, 2)
    one.join_next(1)
    two.came(9, 10)
    units_of(two, 2)
    two.corner_on()
    down_of(one, 3)
    one.join_next(2)
    two.came(11, 12)
    units_of(two, 3)
    one.join_corner()
    down_of(two, 1)
    down_of(two, 2)
    two.join_next(1)
    down_of(one, 0)
    down_of(two, 3)
    two.join_next(2)
    one.join(*chips[0])
    one.add_corner()
    two.join_corner()
    down_of(two, 0)
    two.join(*chips[0])
    one.complete()
    loads[2].wait()
    loads[3].wait()

    def result_rows(at):
        values = hidden[at, :] + summed(at)
        result[at, :] = values.astype(result.dtype)
        differ = values - teacher[at, :].astype(jnp.float32)
        weighed = valid[at, :] * differ
        squares[at, :] = jnp.sum(weighed * differ, -1, keepdims=True)
        total = out_grad[at, :].astype(jnp.float32) + weighed * norm[...]
        total_grad[at, :] = total
        grads_all[mine, at, :] = total.astype(grads_all.dtype)

    def back_of(phase, number):
        where = (pair_of(number), phase.at_rows)
        mixed_grad = against(grads_all[where].reshape(rows, width), down_w[...].reshape(share, width))
        slope = kept[(*where, slice(0, share))].reshape(rows, share).astype(jnp.float32)
        activated = kept[(*where, slice(share, 2 * share))].reshape(rows, share).astype(jnp.float32)
        low_gate = (mixed_grad * slope).astype(kept.dtype)
        low_up = (mixed_grad * activated).astype(kept.dtype)
        kept[(*where, slice(0, share))] = low_gate.reshape(2, part_rows, share)
        kept[(*where, slice(share, 2 * share))] = low_up.reshape(2, part_rows, share)
        out = against(low_gate, gate_up_w[:, :share]) + against(low_up, gate_up_w[:, share:])
        partial[where] = out.astype(partial.dtype).reshape(2, part_rows, width)
        phase.to_core(*chips[number]).start()

    three, four = [Phase(1, part, grads_all) for part in range(parts)]
    of_part(0, result_rows)
    three.begin()
    two.add_corner()
    three.came(4)
    back_of(three, 0)
    two.complete()
    of_part(1, result_rows)
    square[...] = jnp.sum(squares[...], 0, keepdims=True)
    stores = transfers((result, down_rest, gate_grad, up_grad), (result_out, down_out, gate_out, up_out), store_sem)
    stores[0].start()
    three.forward_on()
    four.begin()
    three.came(7, 8)
    back_of(three, 1)
    three.came(9, 10)
    back_of(three, 2)
    three.join_next(1)
    four.came(4)
    back_of(four, 0)
    three.corner_on()
    three.join_next(2)
    three.came(11, 12)
    back_of(three, 3)
    four.forward_on()
    three.join_corner()
    four.came(7, 8)
    back_of(four, 1)
    three.join(*chips[0])
    four.came(9, 10)
    back_of(four, 2)
    four.join_next(1)
    four.corner_on()
    four.join_next(2)
    three.add_corner()
    four.came(11, 12)
    back_of(four, 3)
    four.join(*chips[0])
    four.join_corner()
    tokens_all = normed_all.shape[0] * rows
    block = 256

    def down_block(of, to):
        def run(i, carry):
            at = pl.ds(pl.multiple_of(i * block, block), block)
            left = mixed[:, :, at].reshape(tokens_all, block)
            grads = transposed(left, grads_all[:, :, of].reshape(tokens_all, of.size)).astype(to.dtype)
            per = block // units
            to[pl.ds(i * per, per)] = grads.reshape(per, units, of.size)
            return carry

        lax.fori_loop(0, share // block, run, 0)

    def both_block(i, carry):
        at = pl.ds(pl.multiple_of(i * block, block), block)
        left = normed_all[:, :, at].reshape(tokens_all, block)
        both = transposed(left, kept[...].reshape(tokens_all, 2 * share)).astype(gate_grad.dtype)
        gate_grad[at, :] = both[:, :share]
        up_grad[at, :] = both[:, share:]
        return carry

    down_parts = down_w.at[:, :, first]
    down_begin, down_hop, down_last = line_reduce(
        place, lines, down_parts, down_up, down_down, down_send, down_recv
    )
    down_block(first, down_parts)
    down_begin()
    down_block(second, down_rest)
    blocks = width // block
    third = blocks // 3
    lax.fori_loop(0, third, both_block, 0)
    three.complete()
    four.add_corner()
    down_hop(1)
    lax.fori_loop(third, 2 * third, both_block, 0)
    for moment in range(2, lines - 1):
        down_hop(moment)
    lax.fori_loop(2 * third, blocks, both_block, 0)
    for store in stores[1:]:
        store.start()

    def grad_rows(at):
        grads = summed(at)
        normed = hidden[at, :] * scales[at, :]
        scaled = grads * gain[...]
        values = total_grad[at, :] + scales[at, :] * (scaled - normed * jnp.mean(scaled * normed, -1, keepdims=True))
        hidden_grad[at, :] = values
        branch[at, :] = values.astype(branch.dtype)

    def attended_rows(at):
        attended_grad[at, :] = against(branch[at, :], out_w[...]).astype(attended_grad.dtype)

    of_part(0, grad_rows)
    attended_rows(at_part[0])
    four.complete()
    of_part(1, grad_rows)
    attended_rows(at_part[1])


    def keep_down(i, sums):
        down_final[pl.ds(pl.multiple_of(i * 32, 32), 32), :] = sums

    down_last(keep_down)
    for phase in (one, two, three, four):
        phase.drain()
    for store in stores:
        store.wait()


def feed_forward(lines, out_rows, attended, tokens, teacher, out_grad, valid, gains, gate_up_w, down_rows, identity):
    rows, width = tokens.shape
    units = down_rows.shape[0]
    share = lines * units
    low = tokens.dtype
    shape = jax.ShapeDtypeStruct
    vmem, anywhere = pl.BlockSpec(memory_space=pltpu.VMEM), pl.BlockSpec(memory_space=pl.ANY)
    cut = column_cut(width)
    return pl.pallas_call(
        feed_forward_kernel,
        out_shape=[
            shape((rows, width), low),
            shape((1, 1), jnp.float32),
            shape((1, 1), jnp.float32),
            shape((rows, width), jnp.float32),
            shape((rows, width), low),
            shape((rows, width), low),
            shape((units, cut), jnp.float32),
            shape((lines, units, width - cut), low),
            shape((width, share), low),
            shape((width, share), low),
        ],
        in_specs=[anywhere, vmem, vmem, anywhere, anywhere, vmem, vmem, anywhere, anywhere],
        out_specs=[anywhere] + [vmem] * 6 + [anywhere] * 3,
        scratch_shapes=[
            pltpu.VMEM((rows, width), low),
            pltpu.VMEM((lines, units, width - cut), low),
            pltpu.VMEM((width, share), low),
            pltpu.VMEM((width, share), low),
            pltpu.SemaphoreType.DMA((4,)),
            pltpu.VMEM((width, width), low),
            pltpu.VMEM((width, 2 * share), low),
            pltpu.VMEM((rows, width), low),
            pltpu.VMEM((rows, width), low),
            pltpu.VMEM((lines, units, width), low),
            pltpu.VMEM((lines, units, cut), low),
            pltpu.VMEM((lines, units, cut), low),
            pltpu.VMEM((PLANE, rows, width), low),
            pltpu.VMEM((PLANE, rows, 2 * share), low),
            pltpu.VMEM((PLANE, rows, share), low),
            pltpu.VMEM((PLANE, rows, width), low),
            pltpu.VMEM((PLANE, rows, width), low),
            pltpu.VMEM((4, rows, width), low),
            pltpu.VMEM((rows, cut), low),
            pltpu.VMEM((rows, width - cut), low),
            pltpu.VMEM((rows, width), low),
            pltpu.VMEM((rows, width), low),
            pltpu.VMEM((rows, width), jnp.float32),
            pltpu.VMEM((rows, width), jnp.float32),
            pltpu.VMEM((rows, 1), jnp.float32),
            pltpu.VMEM((rows, 1), jnp.float32),
            pltpu.SemaphoreType.DMA((4,)),
            pltpu.SemaphoreType.DMA((2,)),
            pltpu.SemaphoreType.DMA((2, 2, lines)),
            pltpu.SemaphoreType.DMA((2, 2, lines)),
            pltpu.SemaphoreType.DMA((2, lines)),
            pltpu.SemaphoreType.DMA((2, lines)),
            pltpu.SemaphoreType.DMA((2, 2, GATHER_KINDS)),
            pltpu.SemaphoreType.DMA((2, 2, GATHER_KINDS)),
            pltpu.SemaphoreType.DMA((2, 2, REDUCE_KINDS)),
            pltpu.SemaphoreType.DMA((2, 2, REDUCE_KINDS)),
        ],
        compiler_params=pltpu.CompilerParams(collective_id=identity, vmem_limit_bytes=VMEM_LIMIT),
        cost_estimate=pl.CostEstimate(flops=40 * PLANE * rows * width * share // 2, bytes_accessed=30 * 2**20, transcendentals=0),
        name="feed_forward",
    )(out_rows, attended, tokens, teacher, out_grad, valid, gains, gate_up_w, down_rows)


HEAD_TILES = 3
ROW_STEP = 64


def by_rows(rows, body, step=ROW_STEP):
    def run(i, carry):
        body(pl.ds(pl.multiple_of(i * step, step), step))
        return carry

    lax.fori_loop(0, rows // step, run, 0)


def lanes_of(values):
    return lax.broadcasted_iota(jnp.int32, values.shape, len(values.shape) - 1)


def turned(tile, cosine, sine):
    half = HD // 2
    partner = jnp.where(lanes_of(tile) < half, -pltpu.roll(tile, LANES - half, 1), pltpu.roll(tile, half, 1))
    return tile * cosine + partner * sine


def packed_pair(first, second, even):
    lane = lanes_of(first)
    moved = pltpu.roll(second, HD, 1)
    full_even = jnp.where(lane < HD, first, moved)
    full_odd = jnp.where(lane < 32, pltpu.roll(first, 64, 1), pltpu.roll(second, 32, 1))
    return jnp.where(even, full_even, full_odd), jnp.where(even, moved, first)


def unpacked_pair(full, part, even):
    lane = lanes_of(full)
    zero = jnp.zeros_like(full)
    first_even = jnp.where(lane < HD, full, zero)
    second_even = jnp.where(lane < 32, pltpu.roll(full, 32, 1), jnp.where(lane < HD, pltpu.roll(part, 32, 1), zero))
    first_odd = jnp.where(lane < 64, part, jnp.where(lane < HD, pltpu.roll(full, 64, 1), zero))
    second_odd = jnp.where(lane < HD, pltpu.roll(full, HD, 1), zero)
    return jnp.where(even, first_even, first_odd), jnp.where(even, second_even, second_odd)


def keys_and_values(qkv, keys, values, count, rows):
    def body(src, carry):
        block = qkv[src].astype(jnp.float32)
        tiles = [block[:, i * LANES : (i + 1) * LANES] for i in range(HEAD_TILES)]
        lane = lanes_of(tiles[0])
        key = jnp.where(lane < HD, tiles[2], 0.0)
        value = jnp.where(lane < 64, pltpu.roll(tiles[1], 64, 1), pltpu.roll(tiles[2], HD, 1))
        value = jnp.where(lane < 32, pltpu.roll(tiles[0], 32, 1), value)
        value = jnp.where(lane < HD, value, 0.0)
        at = pl.ds(pl.multiple_of(src * rows, rows), rows)
        for half in range(2):
            keys[half, at, :] = key[half * rows : (half + 1) * rows].astype(keys.dtype)
            values[half, at, :] = value[half * rows : (half + 1) * rows].astype(values.dtype)
        return carry

    lax.fori_loop(0, count, body, 0)


def segment_of(lengths, place):
    start, end = jnp.zeros_like(place), 0
    for length in [lengths[0, j] for j in range(NSEQ)]:
        end = end + length
        start = start + jnp.where(place >= end, length, 0)
    return start, end


def side_by_side(heads):
    full, part = packed_pair(heads[0], heads[1], True)
    full_odd, part_odd = packed_pair(heads[2], heads[3], False)
    middle = jnp.where(lanes_of(part) < 64, part, pltpu.roll(part_odd, 64, 1))
    return full, middle, full_odd


def apart(ref, group):
    start = group * HEAD_TILES * LANES
    tiles = [ref[:, start + i * LANES : start + (i + 1) * LANES].astype(jnp.float32) for i in range(HEAD_TILES)]
    return unpacked_pair(tiles[0], tiles[1], True) + unpacked_pair(tiles[2], pltpu.roll(tiles[1], 64, 1), False)


def arrange_rows(rows_in, w_query, w_key, w_value, gain_rows, count):
    share = rows_in.shape[0]
    groups = HEADS // KV
    queries = [head for group in range(HEADS // 4) for head in apart(w_query, group)]
    keys = [head for group in range(KV // 4) for head in apart(w_key, group)]
    values = [head for group in range(KV // 4) for head in apart(w_value, group)]
    lane = lanes_of(keys[0])
    for head in range(KV):
        for number, tile in enumerate(queries[head * groups : (head + 1) * groups] + [keys[head]]):
            third = pltpu.roll(values[head], HD - 32 * number, 1)
            start = (head * HEAD_TILES + number) * LANES
            rows_in[:, start : start + LANES] = jnp.where(lane < HD, tile, third).astype(rows_in.dtype)
    row = lax.broadcasted_iota(jnp.int32, (LANES, LANES), 0)
    columns = jnp.where(row == 0, gain_rows[0:1, :], jnp.where(row == 1, gain_rows[1:2, :], 0.0))
    columns = jnp.where(row == 2, count, columns)
    rows_in[:, KV * HEAD_TILES * LANES :] = jnp.transpose(columns)[:share, :].astype(rows_in.dtype)


def attend_kernel(
    scale, lines, w_query, w_key, w_value, w_gate, w_up, out_rows, gain_rows, freq, mask, deal, lengths, tokens,
    attended, normed, gains, cosine, sine, valid, weights, out_w, unit_w, qkv_out, probs,
    rows_in, unit_rows, w, place_row, sent, qkv, keys, values, prob_blocks, o_sent, o_came,
    send, recv, o_send, o_recv, p_sem, q_sem, w_sem, w_line_send, w_line_recv, w_send, w_recv, w_here, g_send, g_recv, g_here,
    o_line_send, o_line_recv,
    u_send, u_recv, u_here, l_send, l_recv,
):
    z, y, x, c = coordinates()
    count = sent.shape[0]
    me = z * 2 + y
    even = y == 0
    rows, width = tokens.shape
    half_rows = rows // 2
    head_cols = HEAD_TILES * LANES
    to_device = lambda i: (i, x * 2 + c)
    peer = lambda k: lax.rem(me + k, count)

    member = y * 4 + x * 2 + c
    in_plane = lambda i: (z * 2 + i // 4, i % 4)
    unit_peer = lambda k: lax.rem(member + k, PLANE)
    others = [device(z, yy, xx, cc) for yy, xx, cc in ((y, 1 - x, c), (y, x, 1 - c), (y, 1 - x, 1 - c))]
    others += [device(z, 1 - y, xx, cc) for xx, cc in ((1 - x, c), (x, 1 - c), (1 - x, 1 - c))]
    units = w_gate.shape[1] // (lines * PLANE)
    for i in range(PLANE):
        for zz in range(lines):
            start = (zz * PLANE + i) * units
            unit_rows[i, :, zz * units : (zz + 1) * units] = w_gate[:, start : start + units]
            unit_rows[i, :, (lines + zz) * units : (lines + zz + 1) * units] = w_up[:, start : start + units]
    greet([to_device(peer(k)) for k in range(1, count)] + others)

    def unit_out(k):
        i = unit_peer(k)
        return remote(unit_rows.at[i], unit_w.at[z, member], u_send.at[k], u_recv.at[k], in_plane(i))

    unit_own = pltpu.make_async_copy(unit_rows.at[member], unit_w.at[z, member], u_here)
    unit_own.start()
    columns = rows_in.shape[1]
    line_gathers, plane_gathers = [], []
    for part, of in enumerate(halves(columns)):
        line_gathers.append(
            line_gather(
                (z, y, x, c), lines, rows_in.at[:, of], lambda zz, of=of: w.at[zz, member, :, of],
                w_line_send.at[part], w_line_recv.at[part], w_here.at[part],
            )
        )
        plane_gathers.append(
            PlaneGather(
                (z, y, x, c), lambda yy, xx, of=of: w.at[:, yy * 4 + xx * 2 + c, :, of], of.size,
                w_send.at[part], w_recv.at[part],
            )
        )
    (one_begin, one_pass, one_last), (two_begin, two_pass, two_last) = line_gathers
    one, two = plane_gathers
    out_begin, out_pass, out_last = line_gather(
        (z, y, x, c), lines, out_rows, lambda zz: out_w.at[zz, member], o_line_send, o_line_recv, g_here
    )
    out_gather = PlaneGather(
        (z, y, x, c), lambda yy, xx: out_w.at[:, yy * 4 + xx * 2 + c], out_rows.shape[1], g_send, g_recv
    )
    line_begin, line_pass, line_last = line_gather(
        (z, y, x, c), lines, unit_w.at[z], lambda zz: unit_w.at[zz], l_send, l_recv
    )
    for k in range(1, PLANE):
        unit_out(k).start()
    first_block = deal[0, me]
    total = functools.reduce(lambda a, b: a + b, [lengths[0, j] for j in range(NSEQ)])
    token = lax.broadcasted_iota(jnp.int32, (1, rows), 1)
    in_pack = jnp.where(token < half_rows, first_block * half_rows, (2 * count - 2 - first_block) * half_rows) + token
    counted = jnp.where(in_pack < total, mask[...].astype(jnp.float32), 0.0)
    arrange_rows(rows_in, w_query, w_key, w_value, gain_rows, jnp.sum(counted, -1, keepdims=True))
    one_begin()
    valid[...] = jnp.transpose(jnp.broadcast_to(counted, (LANES, rows)))[:, :1]
    token = lax.broadcasted_iota(jnp.int32, (rows, 1), 0)
    in_pack = jnp.where(token < half_rows, first_block * half_rows, (2 * count - 2 - first_block) * half_rows) + token
    angle = (in_pack - segment_of(lengths, in_pack)[0]).astype(jnp.float32) * freq[...]
    cosine[...] = jnp.cos(angle)
    sine[...] = jnp.sin(angle)
    one_pass(1)
    two_begin()
    for moment in range(2, lines):
        one_pass(moment)
        two_pass(moment - 1)
    one_last()
    one.begin()
    two_pass(lines - 1)
    two_last()
    unit_own.wait()
    for k in range(1, PLANE):
        unit_out(k).wait_recv()
    line_begin()
    out_begin()
    one.forward_on()
    two.begin()
    for moment in range(1, lines - 1):
        out_pass(moment)
    one.corner_on()
    out_pass(lines - 1)
    out_last()
    two.forward_on()
    line_pass(1)
    one.rest()
    two.corner_on()
    two.rest()
    keep_weights = pltpu.make_async_copy(w, weights, w_sem)
    keep_weights.start()

    def columns_of(start, size):
        return w[:, :, :, pl.ds(start, size)].reshape(width, size)

    extras = columns_of(count * head_cols, LANES)
    gains[...] = jnp.transpose(extras.astype(jnp.float32))[: gains.shape[0], :]
    gain = gains[0:1, :]

    def norm_rows(at):
        values_at = tokens[at, :].astype(jnp.float32)
        normed[at, :] = (values_at * rms_scale(values_at) * gain).astype(normed.dtype)

    by_rows(rows, norm_rows)

    def out(k):
        return remote(sent.at[peer(k)], qkv.at[me], send.at[k], recv.at[k], to_device(peer(k)))

    def project(k, carry):
        i = peer(k)
        columns = columns_of(pl.multiple_of(i * head_cols, LANES), head_cols)
        both = jnp.dot(normed[...], columns, preferred_element_type=jnp.float32)
        for tile in range(HEAD_TILES):
            at = slice(tile * LANES, (tile + 1) * LANES)
            sent[i, :, at] = turned(both[:, at], cosine[...], sine[...]).astype(sent.dtype)

        @pl.when(k < count)
        def _():
            out(k).start()

        return carry

    lax.fori_loop(1, count + 1, project, 0)
    out_gather.begin()
    line_pass(2)
    qkv[me] = sent[me]
    for src in range(count):
        columns = slice(src * half_rows, (src + 1) * half_rows)
        steps = lax.broadcasted_iota(jnp.int32, (1, half_rows), 1)
        place_row[0, :, columns] = deal[0, src] * half_rows + steps
        place_row[1, :, columns] = (2 * count - 1 - deal[0, src]) * half_rows + steps

    def arrive(k, carry):
        out(k).wait_recv()
        return carry

    out_gather.forward_on()
    out_gather.corner_on()
    lax.fori_loop(1, count, arrive, 0)
    keep_qkv = pltpu.make_async_copy(qkv, qkv_out, q_sem)
    keep_qkv.start()
    keys_and_values(qkv, keys, values, count, half_rows)

    def back(k):
        return remote(o_sent.at[peer(k)], o_came.at[me], o_send.at[k], o_recv.at[k], to_device(peer(k)))

    def keep(src, half):
        return pltpu.make_async_copy(prob_blocks.at[src, half], probs.at[src, half], p_sem.at[src, half])

    def attend(k, carry):
        src = peer(k)
        halves_out = []
        for half in range(2):
            at = pl.ds(half * half_rows, half_rows)
            queries = jnp.concatenate([qkv[src, at, :LANES], qkv[src, at, LANES : 2 * LANES]], 0)
            score = against(queries, keys[half]) * scale
            first = deal[0, src]
            block = first if half == 0 else 2 * count - 1 - first
            own = block * half_rows + lax.broadcasted_iota(jnp.int32, (half_rows, 1), 0)
            start, end = segment_of(lengths, own)
            lowest = jnp.where(own < end, start, own)
            place = place_row[half]
            allowed = (place >= lowest) & (place <= own)
            bias = jnp.where(allowed, 0.0, masked_score)
            score = score + jnp.concatenate([bias, bias], 0)
            top = jnp.max(score, -1, keepdims=True)
            weight = jnp.exp(score - top)
            total = jnp.sum(weight, -1, keepdims=True)
            low = (weight * (1.0 / total)).astype(prob_blocks.dtype)
            prob_blocks[src, half] = low
            keep(src, half).start()
            summed = jnp.dot(low, values[half], preferred_element_type=jnp.float32)
            full, part = packed_pair(summed[:half_rows], summed[half_rows:], even)
            o_sent[src, at, :] = full.astype(o_sent.dtype)
            halves_out.append(part)
        lane = lanes_of(halves_out[0])
        part = jnp.where(lane < 64, halves_out[0], pltpu.roll(halves_out[1], 64, 1))
        o_sent[src, pl.ds(rows, half_rows), :] = part.astype(o_sent.dtype)

        @pl.when(k < count)
        def _():
            back(k).start()

        return carry

    lax.fori_loop(1, count + 1, attend, 0)
    o_came[me] = o_sent[me]

    def return_arrive(k, carry):
        back(k).wait_recv()
        return carry

    lax.fori_loop(1, count, return_arrive, 0)
    for pair in range(count // 2):
        at = pair * head_cols
        attended[:, at : at + LANES] = o_came[2 * pair, :rows, :]
        attended[:, at + 2 * LANES : at + 3 * LANES] = o_came[2 * pair + 1, :rows, :]
        one = o_came[2 * pair, rows:, :].astype(jnp.float32)
        two = o_came[2 * pair + 1, rows:, :].astype(jnp.float32)
        lane = lanes_of(one)
        middle = slice(at + LANES, at + 2 * LANES)
        attended[:half_rows, middle] = jnp.where(lane < 64, one, pltpu.roll(two, 64, 1)).astype(attended.dtype)
        attended[half_rows:, middle] = jnp.where(lane < 64, pltpu.roll(one, 64, 1), two).astype(attended.dtype)

    def drain(k, carry):
        out(k).wait_send()
        back(k).wait_send()
        return carry

    lax.fori_loop(1, count, drain, 0)

    def drain_probs(src, carry):
        keep(src, 0).wait()
        keep(src, 1).wait()
        return carry

    lax.fori_loop(0, count, drain_probs, 0)
    keep_qkv.wait()
    out_gather.rest()
    for gather in (out_gather, *plane_gathers):
        gather.drain()
    for moment in range(3, lines):
        line_pass(moment)
    line_last()
    for k in range(1, PLANE):
        unit_out(k).wait_send()
    keep_weights.wait()


def attend(scale, lines, w_query, w_key, w_value, w_gate, w_up, out_rows, gain_rows, freq, mask, deal, lengths, tokens, identity):
    rows, width = tokens.shape
    share, units = out_rows.shape[0], w_gate.shape[1] // PLANE
    count = KV
    columns = count * HEAD_TILES * LANES + LANES
    half_rows = rows // 2
    half = count * half_rows
    head_cols = HEAD_TILES * LANES
    low = tokens.dtype
    shape = jax.ShapeDtypeStruct
    vmem, anywhere = pl.BlockSpec(memory_space=pltpu.VMEM), pl.BlockSpec(memory_space=pl.ANY)
    smem = pl.BlockSpec(memory_space=pltpu.SMEM)
    dma = pltpu.SemaphoreType.DMA
    return pl.pallas_call(
        functools.partial(attend_kernel, scale, lines),
        out_shape=[
            shape((rows, width), low),
            shape((rows, width), low),
            shape((8, width), jnp.float32),
            shape((rows, LANES), jnp.float32),
            shape((rows, LANES), jnp.float32),
            shape((rows, 1), jnp.float32),
            shape((lines, PLANE, share, columns), low),
            shape((lines, PLANE) + out_rows.shape, low),
            shape((lines, PLANE, share, 2 * units), low),
            shape((count, rows, head_cols), low),
            shape((count, 2, rows, half), low),
        ],
        in_specs=[vmem] * 5 + [anywhere] + [vmem] * 3 + [smem, smem, vmem],
        out_specs=[vmem] * 6 + [anywhere] * 5,
        scratch_shapes=[
            pltpu.VMEM((share, columns), low),
            pltpu.VMEM((PLANE, share, 2 * units), low),
            pltpu.VMEM((lines, PLANE, share, columns), low),
            pltpu.VMEM((2, 1, half), jnp.int32),
            pltpu.VMEM((count, rows, head_cols), low),
            pltpu.VMEM((count, rows, head_cols), low),
            pltpu.VMEM((2, half, LANES), low),
            pltpu.VMEM((2, half, LANES), low),
            pltpu.VMEM((count, 2, rows, half), low),
            pltpu.VMEM((count, rows + half_rows, LANES), low),
            pltpu.VMEM((count, rows + half_rows, LANES), low),
            dma((count,)),
            dma((count,)),
            dma((count,)),
            dma((count,)),
            dma((count, 2)),
            dma,
            dma,
            dma((2, 2, lines)),
            dma((2, 2, lines)),
            dma((2, GATHER_KINDS)),
            dma((2, GATHER_KINDS)),
            dma((2,)),
            dma((GATHER_KINDS,)),
            dma((GATHER_KINDS,)),
            dma,
            dma((2, lines)),
            dma((2, lines)),
            dma((PLANE,)),
            dma((PLANE,)),
            dma,
            dma((2, lines)),
            dma((2, lines)),
        ],
        compiler_params=pltpu.CompilerParams(collective_id=identity, vmem_limit_bytes=VMEM_LIMIT),
        name="attend",
    )(w_query, w_key, w_value, w_gate, w_up, out_rows, gain_rows, freq, mask, deal, lengths, tokens)


def attend_back_kernel(
    scale, lines, attended_grad, probs, cosine, sine, qkv_in, attended_in, branch_in, gate_in, down_in,
    qkv_grad, out_final, gate_sums, down_final,
    qkv, attended, branch, gate_parts, down_parts, in_sem,
    sent, came, keys, values, prob_blocks, dk_sum, dv_sum, back_sent, back_came,
    send, recv, back_send, back_recv, p_sem, up, down, l_send, l_recv, down_up, down_down, d_send, d_recv, p, *reducing,
):
    z, y, x, c = coordinates()
    count = sent.shape[0]
    me = z * 2 + y
    even = y == 0
    rows, width = attended_grad.shape
    half_rows = rows // 2
    head_cols = HEAD_TILES * LANES
    to_device = lambda i: (i, x * 2 + c)
    peer = lambda k: lax.rem(me + k, count)
    source = lambda k: lax.rem(me + count - k, count)

    loads = transfers(
        (attended_in, branch_in, qkv_in, gate_in, down_in), (attended, branch, qkv, gate_parts, down_parts), in_sem
    )
    for load_in in loads:
        load_in.start()

    def load(src, half):
        return pltpu.make_async_copy(probs.at[src, half], prob_blocks.at[src, half], p_sem.at[src, half])

    def load_start(k, carry):
        load(source(k), 0).start()
        load(source(k), 1).start()
        return carry

    lax.fori_loop(0, count, load_start, 0)
    greet([to_device(peer(k)) for k in range(1, count)] + [device(z, y, 1 - x, c), device(z, y, x, 1 - c)])
    members, share = p.shape[1:3]

    def prepare(block):
        at = pl.ds(pl.multiple_of(block * members * share, LANES), members * share)
        store_terms(p, block, 0, transposed(attended[:, at], branch[...]))

    reduce_stages, reduce_last = reduce_plan(lines, prepare, p, out_final, *reducing)
    line_begin, line_hop, line_last = line_reduce((z, y, x, c), lines, gate_parts, up, down, l_send, l_recv)
    down_begin, down_hop, down_last = line_reduce((z, y, x, c), lines, down_parts, down_up, down_down, d_send, d_recv)
    for pair in range(count // 2):
        at = pair * head_cols
        sent[2 * pair, :rows, :] = attended_grad[:, at : at + LANES]
        sent[2 * pair + 1, :rows, :] = attended_grad[:, at + 2 * LANES : at + 3 * LANES]
        middle = attended_grad[:, at + LANES : at + 2 * LANES].astype(jnp.float32)
        one, two = middle[:half_rows], middle[half_rows:]
        lane = lanes_of(one)
        sent[2 * pair, rows:, :] = jnp.where(lane < 64, one, pltpu.roll(two, 64, 1)).astype(sent.dtype)
        sent[2 * pair + 1, rows:, :] = jnp.where(lane < 64, pltpu.roll(one, 64, 1), two).astype(sent.dtype)

    def out(k):
        return remote(sent.at[peer(k)], came.at[me], send.at[k], recv.at[k], to_device(peer(k)))

    def begin(k, carry):
        out(k).start()
        return carry

    lax.fori_loop(1, count, begin, 0)
    for load_in in loads[:2]:
        load_in.wait()
    reduce_stages[0]()
    came[me] = sent[me]
    for load_in in loads[2:]:
        load_in.wait()
    keys_and_values(qkv, keys, values, count, half_rows)
    dk_sum[...] = jnp.zeros_like(dk_sum)
    dv_sum[...] = jnp.zeros_like(dv_sum)

    def pack(src, kind, at, first, second):
        full, part = packed_pair(first, second, even)
        back_sent[src, kind, at, :] = full.astype(back_sent.dtype)
        return part

    def pack_parts(src, kind, parts):
        part = jnp.where(lanes_of(parts[0]) < 64, parts[0], pltpu.roll(parts[1], 64, 1))
        back_sent[src, kind, pl.ds(rows, half_rows), :] = part.astype(back_sent.dtype)

    def back(kind, k):
        to = source(k) if kind == 0 else peer(k)
        return remote(
            back_sent.at[to, kind], back_came.at[me, kind], back_send.at[kind, k], back_recv.at[kind, k], to_device(to)
        )

    def grads(k, carry):
        src = source(k)

        @pl.when(k > 0)
        def _():
            out(k).wait_recv()

        parts = []
        for half in range(2):
            at = pl.ds(half * half_rows, half_rows)
            full = came[src, at, :].astype(jnp.float32)
            part = came[src, pl.ds(rows, half_rows), :].astype(jnp.float32)
            if half:
                part = pltpu.roll(part, 64, 1)
            pair = jnp.concatenate(unpacked_pair(full, part, even), 0).astype(came.dtype)
            queries = jnp.concatenate([qkv[src, at, :LANES], qkv[src, at, LANES : 2 * LANES]], 0)
            load(src, half).wait()
            low = prob_blocks[src, half]
            prob = low.astype(jnp.float32)
            prob_grad = against(pair, values[half])
            delta = jnp.sum(prob * prob_grad, -1, keepdims=True)
            score_low = (prob * (prob_grad - delta)).astype(low.dtype)
            dq = jnp.dot(score_low, keys[half], preferred_element_type=jnp.float32) * scale
            parts.append(pack(src, 0, at, dq[:half_rows], dq[half_rows:]))
            dk_sum[half] += transposed(score_low, queries)
            dv_sum[half] += transposed(low, pair)
        pack_parts(src, 0, parts)

        @pl.when(k > 0)
        def _():
            back(0, k).start()

        pl.when(k == 2)(line_begin)
        pl.when(k == 5)(down_begin)
        for number in range(1, len(reduce_stages)):
            pl.when(k == number)(reduce_stages[number])
        return carry

    lax.fori_loop(0, count, grads, 0)

    def finish(k, carry):
        src = peer(k)
        in_half = pl.ds(pl.multiple_of(src * half_rows, half_rows), half_rows)
        parts = []
        for half in range(2):
            at = pl.ds(half * half_rows, half_rows)
            parts.append(pack(src, 1, at, dk_sum[half, in_half, :] * scale, dv_sum[half, in_half, :]))
        pack_parts(src, 1, parts)

        @pl.when(k < count)
        def _():
            back(1, k).start()

        return carry

    lax.fori_loop(1, count + 1, finish, 0)
    for moment in range(1, lines - 1):
        line_hop(moment)
        down_hop(moment)
    reduce_last()
    back_came[me] = back_sent[me]

    def turn_back(k, carry):
        src = source(k)
        src_even = lax.rem(src, 2) == 0

        @pl.when(k > 0)
        def _():
            back(0, count - k).wait_recv()
            back(1, k).wait_recv()

        for half in range(2):
            at = pl.ds(half * half_rows, half_rows)
            heads = []
            for kind in range(2):
                full = back_came[src, kind, at, :].astype(jnp.float32)
                part = back_came[src, kind, pl.ds(rows, half_rows), :].astype(jnp.float32)
                if half:
                    part = pltpu.roll(part, 64, 1)
                heads.extend(unpacked_pair(full, part, src_even))
            dv = heads.pop()
            lane = lanes_of(dv)
            for tile in range(HEAD_TILES):
                turned_at = turned(heads[tile], cosine[at, :], -sine[at, :])
                joined = jnp.where(lane < HD, turned_at, pltpu.roll(dv, HD - 32 * tile, 1))
                to = pl.ds(pl.multiple_of(src * head_cols + tile * LANES, LANES), LANES)
                qkv_grad[at, to] = joined.astype(qkv_grad.dtype)
        return carry

    lax.fori_loop(0, count, turn_back, 0)

    def keep_sums(i, sums):
        gate_sums[i] = sums.astype(gate_sums.dtype)

    line_last(keep_sums, gate_sums.shape[1])

    def keep_down(i, sums):
        down_final[pl.ds(pl.multiple_of(i * 32, 32), 32), :] = sums

    down_last(keep_down)

    def drain(k, carry):
        out(k).wait_send()
        back(0, k).wait_send()
        back(1, k).wait_send()
        return carry

    lax.fori_loop(1, count, drain, 0)


def attend_back(scale, lines, attended_grad, qkv, probs, tables, attended, branch, gate_parts, down_parts, identity):
    rows, width = attended_grad.shape
    count, _, head_cols = qkv.shape
    half = probs.shape[-1]
    half_rows = rows // 2
    share = width // (lines * PLANE)
    low = attended_grad.dtype
    vmem, anywhere = pl.BlockSpec(memory_space=pltpu.VMEM), pl.BlockSpec(memory_space=pl.ANY)
    dma = pltpu.SemaphoreType.DMA
    return pl.pallas_call(
        functools.partial(attend_back_kernel, scale, lines),
        out_shape=[
            jax.ShapeDtypeStruct((rows, count * head_cols), low),
            jax.ShapeDtypeStruct((share, width), jnp.float32),
            jax.ShapeDtypeStruct((PLANE, share, gate_parts.shape[2]), low),
            jax.ShapeDtypeStruct(down_parts.shape[1:], jnp.float32),
        ],
        in_specs=[vmem, anywhere, vmem, vmem] + [anywhere] * 5,
        out_specs=[vmem] * 4,
        scratch_shapes=[
            pltpu.VMEM(qkv.shape, low),
            pltpu.VMEM(attended.shape, low),
            pltpu.VMEM(branch.shape, low),
            pltpu.VMEM(gate_parts.shape, low),
            pltpu.VMEM(down_parts.shape, low),
            dma((5,)),
            pltpu.VMEM((count, rows + half_rows, LANES), low),
            pltpu.VMEM((count, rows + half_rows, LANES), low),
            pltpu.VMEM((2, half, LANES), low),
            pltpu.VMEM((2, half, LANES), low),
            pltpu.VMEM((count, 2, rows, half), low),
            pltpu.VMEM((2, half, LANES), jnp.float32),
            pltpu.VMEM((2, half, LANES), jnp.float32),
            pltpu.VMEM((count, 2, rows + half_rows, LANES), low),
            pltpu.VMEM((count, 2, rows + half_rows, LANES), low),
            dma((count,)),
            dma((count,)),
            dma((2, count)),
            dma((2, count)),
            dma((count, 2)),
            pltpu.VMEM(gate_parts.shape, low),
            pltpu.VMEM(gate_parts.shape, low),
            dma((2, lines)),
            dma((2, lines)),
            pltpu.VMEM(down_parts.shape, low),
            pltpu.VMEM(down_parts.shape, low),
            dma((2, lines)),
            dma((2, lines)),
            *reduce_scratch(lines, share, width, low),
        ],
        compiler_params=pltpu.CompilerParams(collective_id=identity, vmem_limit_bytes=VMEM_LIMIT),
        name="attend_back",
    )(attended_grad, probs, *tables, qkv, attended, branch, gate_parts, down_parts)


def finish_kernel(
    weights, normed, qkv_grad, gains, square, norm, up_parts, gate_sums, hidden_in, tokens_in, gate_in, up_in,
    input_grad, query_final, key_final, value_final, gate_final, up_final, gain_final, loss,
    hidden_grad, tokens, w_gate, w_up, in_sem, w, own_rows, normed_grad, final, up_sums, gate_came, up_came, line_up, line_down,
    w_sem, own_sem, gate_send, gate_recv, up_send, up_recv, here, l_send, l_recv, p, *reducing,
):
    z, y, x, c = coordinates()
    lines, members, share = p.shape[:3]
    rows, width = tokens.shape
    qkv_cols = qkv_grad.shape[1]
    low = normed.dtype
    load = pltpu.make_async_copy(weights.at[:, pl.ds(0, qkv_cols)], w, w_sem)
    load.start()
    loads = transfers((hidden_in, tokens_in, gate_in, up_in), (hidden_grad, tokens, w_gate, w_up), in_sem)
    for load_in in loads:
        load_in.start()
    number = (z * 2 + y) * 4 + x * 2 + c
    own_at = pl.ds(pl.multiple_of(number * share, 16), share)
    load_own = pltpu.make_async_copy(weights.at[own_at, :], own_rows, own_sem)
    load_own.start()
    me = y * 4 + x * 2 + c
    peer = lambda k: lax.rem(me + k, members)
    member = lambda i: (z * 2 + i // 4, i % 4)
    greet([member(peer(k)) for k in range(1, members)] + line_of(z, y, x, c, lines))

    def out(kind, k):
        src, came, send, recv = (
            (gate_sums, gate_came, gate_send, gate_recv),
            (up_sums, up_came, up_send, up_recv),
        )[kind]
        return remote(src.at[peer(k)], came.at[me], send.at[k], recv.at[k], member(peer(k)))

    gate_own = pltpu.make_async_copy(gate_sums.at[me], gate_came.at[me], here)
    gate_own.start()
    for k in range(1, members):
        out(0, k).start()
    line_begin, line_hop, line_last = line_reduce((z, y, x, c), lines, up_parts, line_up, line_down, l_send, l_recv)
    line_begin()

    def keep_up(i, sums):
        up_sums[i] = sums.astype(up_sums.dtype)

    devices = lines * PLANE
    place = lax.broadcasted_iota(jnp.int32, (1, LANES), 1) - number
    rest = square[...]
    loss_terms = jnp.zeros((1, LANES), jnp.float32)
    for term in range(3):
        top = rest.astype(low).astype(jnp.float32)
        loss_terms = loss_terms + jnp.where(place == term * devices, top, 0.0)
        rest = rest - top

    def prepare(block):
        at = pl.ds(pl.multiple_of(block * members * share, LANES), members * share)
        left = normed[:, at]
        chunk = qkv_cols // 2
        for start in range(0, qkv_cols, chunk):
            store_terms(p, block, start, transposed(left, qkv_grad[:, start : start + chunk]))
        store_terms(p, block, qkv_cols, jnp.broadcast_to(loss_terms, (members * share, LANES)))

    stages, last = reduce_plan(lines, prepare, p, final, *reducing)

    def grad_rows(at):
        values = tokens[at, :].astype(jnp.float32)
        scale = rms_scale(values)
        unit = values * scale
        scaled = normed_grad[at, :] * gains[0:1, :]
        input_grad[at, :] = hidden_grad[at, :] + scale * (
            scaled - unit * jnp.mean(scaled * unit, -1, keepdims=True)
        )

    block = rows // lines
    for index, stage in enumerate(stages):
        if index == 2:
            load.wait()
            for load_in in loads:
                load_in.wait()
        if 2 <= index < lines:
            line_hop(index - 1)
        if index == 1 + lines:
            line_last(keep_up, share)
            for k in range(1, members):
                out(1, k).start()
        stage()
        if 2 <= index < 2 + lines:
            at = slice((index - 2) * block, (index - 1) * block)
            normed_grad[at, :] = against(qkv_grad[at, :], w[...])
        if index == 2 + lines:
            by_rows(rows, grad_rows)
    up_came[me] = up_sums[me]
    gate_own.wait()
    for kind in range(2):
        for k in range(1, members):
            out(kind, k).wait_recv()
    units = gate_came.shape[2] // lines
    for i in range(members):
        for zz in range(lines):
            to = slice((zz * members + i) * units, (zz * members + i + 1) * units)
            of = slice(zz * units, (zz + 1) * units)
            gate_final[:, to] = gate_came[i, :, of].astype(jnp.float32)
            up_final[:, to] = up_came[i, :, of].astype(jnp.float32)
    last()

    def tile(head, number):
        start = (head * HEAD_TILES + number) * LANES
        return final[:, start : start + LANES]

    def put(ref, group, heads):
        for number, value in enumerate(side_by_side(heads)):
            start = (group * HEAD_TILES + number) * LANES
            ref[:, start : start + LANES] = value

    for pair in range(KV // 2):
        put(query_final, pair, [tile(2 * pair + i, j) for i in range(2) for j in range(2)])
    for group in range(KV // 4):
        heads = [4 * group + i for i in range(4)]
        put(key_final, group, [tile(head, 2) for head in heads])
        parts = []
        for head in heads:
            thirds = [pltpu.roll(tile(head, number), 32 * (number + 1), 1) for number in range(HEAD_TILES)]
            in_tile = lanes_of(thirds[0])
            parts.append(jnp.where(in_tile < 32, thirds[0], jnp.where(in_tile < 64, thirds[1], thirds[2])))
        put(value_final, group, parts)

    load_own.wait()
    own_gains = own_rows[:, qkv_cols:].astype(jnp.float32)

    def product(grads, weights_of, width_of):
        sums = jnp.zeros((share, 1), jnp.float32)
        for start in range(0, width_of, 4 * LANES):
            at = slice(start, start + 4 * LANES)
            sums += jnp.sum(grads[:, at] * weights_of[:, at].astype(jnp.float32), -1, keepdims=True)
        return sums

    units_all = w_gate.shape[1]
    first_gain = product(final, own_rows, qkv_cols) / own_gains[:, 0:1]
    second_gain = product(gate_final, w_gate, units_all) + product(up_final, w_up, units_all)
    second_gain = second_gain / own_gains[:, 1:2]
    columns = lax.broadcasted_iota(jnp.int32, (share, LANES), 1)
    both_gains = jnp.where(columns == 0, first_gain, jnp.where(columns == 1, second_gain, 0.0))
    both_gains = jnp.concatenate([both_gains, jnp.zeros((LANES - share, LANES), jnp.float32)], 0)
    gain_final[...] = jnp.transpose(both_gains)[:8, :]
    tail = final[:, qkv_cols:]
    of_loss = lax.broadcasted_iota(jnp.int32, (1, LANES), 1) < 3 * devices
    loss[...] = jnp.sum(jnp.where(of_loss, tail[:1, :], 0.0), -1, keepdims=True) * (0.5 * norm[...])
    for kind in range(2):
        for k in range(1, members):
            out(kind, k).wait_send()


def finish(
    lines, weights, normed, qkv_grad, hidden_grad, tokens, gains, square, norm, w_gate, w_up, gate_sums, up_parts, identity
):
    rows, width = tokens.shape
    qkv_cols = qkv_grad.shape[1]
    share = weights.shape[0] // (lines * PLANE)
    columns = weights.shape[1]
    units_all = w_gate.shape[1]
    low = tokens.dtype
    vmem, anywhere = pl.BlockSpec(memory_space=pltpu.VMEM), pl.BlockSpec(memory_space=pl.ANY)
    dma = pltpu.SemaphoreType.DMA
    shapes = [
        (rows, width),
        (share, width),
        (share, KV * HD),
        (share, KV * HD),
        (share, units_all),
        (share, units_all),
        (8, LANES),
        (1, 1),
    ]
    return pl.pallas_call(
        finish_kernel,
        out_shape=[jax.ShapeDtypeStruct(shape, jnp.float32) for shape in shapes],
        in_specs=[anywhere] + [vmem] * 6 + [anywhere] * 5,
        out_specs=[vmem] * len(shapes),
        scratch_shapes=[
            pltpu.VMEM(hidden_grad.shape, jnp.float32),
            pltpu.VMEM(tokens.shape, low),
            pltpu.VMEM(w_gate.shape, low),
            pltpu.VMEM(w_up.shape, low),
            dma((4,)),
            pltpu.VMEM((width, qkv_cols), low),
            pltpu.VMEM((share, columns), low),
            pltpu.VMEM((rows, width), jnp.float32),
            pltpu.VMEM((share, columns), jnp.float32),
            pltpu.VMEM(gate_sums.shape, low),
            pltpu.VMEM(gate_sums.shape, low),
            pltpu.VMEM(gate_sums.shape, low),
            pltpu.VMEM(up_parts.shape, low),
            pltpu.VMEM(up_parts.shape, low),
            dma,
            dma,
            dma((PLANE,)),
            dma((PLANE,)),
            dma((PLANE,)),
            dma((PLANE,)),
            dma,
            dma((2, lines)),
            dma((2, lines)),
            *reduce_scratch(lines, share, columns, low),
        ],
        compiler_params=pltpu.CompilerParams(collective_id=identity, vmem_limit_bytes=VMEM_LIMIT),
        name="finish",
    )(weights, normed, qkv_grad, gains, square, norm, up_parts, gate_sums, hidden_grad, tokens, w_gate, w_up)


def emit_kernel(joined, *refs):
    sem = refs[-1]
    count = (len(refs) - 2) // 2
    out = refs[count + 1 : -1]
    pairs = [(refs[i], out[i]) for i in range(count)]
    cut = refs[joined].shape[1]
    pairs[joined] = (refs[joined], out[joined].at[:, pl.ds(0, cut)])
    pairs.append((refs[count], out[joined].at[:, pl.ds(cut, refs[count].shape[1])]))
    copies = [pltpu.make_async_copy(src, dst, sem.at[i]) for i, (src, dst) in enumerate(pairs)]
    for copy in copies:
        copy.start()
    for copy in copies:
        copy.wait()


def emit(arrays, joined, rest):
    shapes = [array.shape for array in arrays]
    shapes[joined] = (shapes[joined][0], shapes[joined][1] + rest.shape[1])
    return pl.pallas_call(
        functools.partial(emit_kernel, joined),
        out_shape=[jax.ShapeDtypeStruct(shape, array.dtype) for shape, array in zip(shapes, arrays)],
        in_specs=[pl.BlockSpec(memory_space=pl.ANY)] * (len(arrays) + 1),
        out_specs=[pl.BlockSpec(memory_space=pltpu.VMEM)] * len(arrays),
        scratch_shapes=[pltpu.SemaphoreType.DMA((len(arrays) + 1,))],
        compiler_params=pltpu.CompilerParams(vmem_limit_bytes=VMEM_LIMIT),
        name="emit",
    )(*arrays, rest)


def plane_per_device(lines, *arrays):
    (
        tokens,
        lengths,
        deal,
        loss_mask,
        teacher,
        out_grad,
        attn_gain,
        w_query,
        w_key,
        w_value,
        w_out,
        ffn_gain,
        w_gate,
        w_up,
        w_down,
    ) = arrays
    devices = lines * PLANE
    width = tokens.shape[2]
    weight_rows = w_query.shape[0]
    scale = HD ** (-0.5)
    gain_rows = jnp.zeros((8, LANES), jnp.float32)
    gain_rows = gain_rows.at[0, :weight_rows].set(attn_gain.astype(jnp.float32))
    gain_rows = gain_rows.at[1, :weight_rows].set(ffn_gain.astype(jnp.float32))
    freq = rope_base ** (-(np.arange(HD // 2) * 2.0 / HD))
    freq = np.concatenate([freq, freq, np.zeros(LANES - HD)])[None].astype(np.float32)

    attended_low, normed_low, gains, cosine, sine, valid, attn_all, out_w, gate_up_w, qkv, probs = attend(
        scale,
        lines,
        w_query,
        w_key,
        w_value,
        w_gate,
        w_up,
        w_out,
        gain_rows,
        freq,
        loss_mask,
        deal,
        lengths,
        tokens[0],
        3,
    )
    attn_all = attn_all.reshape(devices * weight_rows, -1)
    gate_up_w = gate_up_w.reshape(devices * weight_rows, -1)

    result, square, norm, hidden_grad, branch_low, attended_grad, down_final, down_rest, gate_grad, up_grad = feed_forward(
        lines,
        out_w.reshape(width, width),
        attended_low,
        tokens[0],
        teacher[0],
        out_grad[0],
        valid,
        gains,
        gate_up_w,
        w_down,
        5,
    )
    gate_grad, up_grad = [grad.reshape(lines, PLANE * weight_rows, -1) for grad in (gate_grad, up_grad)]
    qkv_grad, out_final, gate_sums, down_more = attend_back(
        scale, lines, attended_grad, qkv, probs, (cosine, sine), attended_low, branch_low, gate_grad, down_rest, 9
    )

    input_grad, query_final, key_final, value_final, gate_final, up_final, gain_final, loss = finish(
        lines,
        attn_all,
        normed_low,
        qkv_grad,
        hidden_grad,
        tokens[0],
        gains,
        square,
        norm,
        w_gate,
        w_up,
        gate_sums,
        up_grad,
        11,
    )
    result, input_grad, query_final, key_final, value_final, out_final, gate_final, up_final, down_final = emit(
        (result, input_grad, query_final, key_final, value_final, out_final, gate_final, up_final, down_final),
        8,
        down_more,
    )
    return (
        result[None],
        loss.reshape(()),
        input_grad[None],
        gain_final[0, :weight_rows],
        query_final,
        key_final,
        value_final,
        out_final,
        gain_final[1, :weight_rows],
        gate_final,
        up_final,
        down_final,
    )


def suits_planes(mesh):
    sizes = dict(mesh.shape)
    return sizes["fsdp"] == 4 and sizes["ctx"] == KV


def solution(mesh):
    placed = (
        P("fsdp", "ctx", None),
        P("fsdp", None),
        P("fsdp", None),
        P("fsdp", "ctx"),
        P("fsdp", "ctx", None),
        P("fsdp", "ctx", None),
        P(("ctx", "fsdp")),
        P(("ctx", "fsdp"), None),
        P(("ctx", "fsdp"), None),
        P(("ctx", "fsdp"), None),
        P(("ctx", "fsdp"), None),
        P(("ctx", "fsdp")),
        P(("ctx", "fsdp"), None),
        P(("ctx", "fsdp"), None),
        P(("ctx", "fsdp"), None),
    )
    if suits_planes(mesh):
        per_device = functools.partial(plane_per_device, mesh.shape["ctx"] // ROWS_Y)
    else:
        per_device = ring_per_device
    return jax.shard_map(
        per_device,
        mesh=mesh,
        in_specs=placed,
        out_specs=(
            P("fsdp", "ctx", None),
            P(),
            P("fsdp", "ctx", None),
            P(("ctx", "fsdp")),
            P(("ctx", "fsdp"), None),
            P(("ctx", "fsdp"), None),
            P(("ctx", "fsdp"), None),
            P(("ctx", "fsdp"), None),
            P(("ctx", "fsdp")),
            P(("ctx", "fsdp"), None),
            P(("ctx", "fsdp"), None),
            P(("ctx", "fsdp"), None),
        ),
        check_vma=False,
    )
```

```python
import functools

import jax
import jax.numpy as jnp
import numpy as np
from jax import lax
from jax.experimental import pallas as pl
from jax.experimental.pallas import tpu as pltpu
from jax.sharding import PartitionSpec as P

HEADS = 16
KV = 8
HD = 96
NSEQ = 6


rope_base = 100000.0
epsilon = 1e-05
masked_score = -1e30


def shifted(value, axis, by):
    size = lax.axis_size(axis)
    return lax.ppermute(value, axis, [(i, (i + by) % size) for i in range(size)])


def rms_scale(values):
    return lax.rsqrt(jnp.mean(values * values, -1, keepdims=True) + epsilon)


def rotary_tables(inseq):
    freq = rope_base ** (-(jnp.arange(HD // 2, dtype=jnp.float32) * 2.0 / HD))
    angle = inseq.astype(jnp.float32)[:, None] * freq[None, :]
    return (jnp.cos(angle)[:, None, :], jnp.sin(angle)[:, None, :])


def rotary(values, cosine, sine):
    half = values.shape[-1] // 2
    first = values[..., :half]
    second = values[..., half:]
    return jnp.concatenate([first * cosine - second * sine, second * cosine + first * sine], -1)


def rotary_back(grads, cosine, sine):
    half = grads.shape[-1] // 2
    first = grads[..., :half]
    second = grads[..., half:]
    return jnp.concatenate([first * cosine + second * sine, second * cosine - first * sine], -1)


def transposed(left, right):
    return lax.dot_general(
        left, right, (((0,), (0,)), ((), ())), preferred_element_type=jnp.float32
    )


def against(left, right):
    return lax.dot_general(
        left, right, (((1,), (1,)), ((), ())), preferred_element_type=jnp.float32
    )


def permitted(query_place, query_seg, key_place, key_seg):
    same = (query_seg[:, None] == key_seg[None, :]) & (query_seg[:, None] < NSEQ)
    return same & (key_place[None, :] <= query_place[:, None]) | (
        key_place[None, :] == query_place[:, None]
    )


def ring_per_device(
    tokens,
    lengths,
    deal,
    loss_mask,
    teacher,
    out_grad,
    attn_gain,
    w_query,
    w_key,
    w_value,
    w_out,
    ffn_gain,
    w_gate,
    w_up,
    w_down,
):
    count_ctx = lax.axis_size("ctx")
    myself = lax.axis_index("ctx")
    tok_rows = tokens.shape[1]
    width = tokens.shape[2]
    half_block = tok_rows // 2
    groups = HEADS // KV
    scale = HD ** (-0.5)
    gain_one, query_w, key_w, value_w, out_w = (
        lax.all_gather(attn_gain, ("ctx", "fsdp"), axis=0, tiled=True),
        lax.all_gather(w_query, ("ctx", "fsdp"), axis=0, tiled=True),
        lax.all_gather(w_key, ("ctx", "fsdp"), axis=0, tiled=True),
        lax.all_gather(w_value, ("ctx", "fsdp"), axis=0, tiled=True),
        lax.all_gather(w_out, ("ctx", "fsdp"), axis=0, tiled=True),
    )
    gain_two, gate_w, up_w, down_w = (
        lax.all_gather(ffn_gain, ("ctx", "fsdp"), axis=0, tiled=True),
        lax.all_gather(w_gate, ("ctx", "fsdp"), axis=0, tiled=True),
        lax.all_gather(w_up, ("ctx", "fsdp"), axis=0, tiled=True),
        lax.all_gather(w_down, ("ctx", "fsdp"), axis=0, tiled=True),
    )
    dealt = jnp.arange(count_ctx * tok_rows, dtype=jnp.int32)
    local = dealt % tok_rows
    first = jnp.repeat(deal[0], tok_rows)
    block = jnp.where(local < half_block, first, 2 * count_ctx - 1 - first)
    places = block * half_block + local % half_block
    ends = jnp.cumsum(lengths[0])
    after = (places[:, None] >= ends[None, :]).astype(jnp.int32)
    seg_all = jnp.sum(after, 1)
    inseq_all = places - jnp.sum(after * lengths[0][None, :], 1)
    own_place = lax.dynamic_slice_in_dim(places, myself * tok_rows, tok_rows)
    own_seg = lax.dynamic_slice_in_dim(seg_all, myself * tok_rows, tok_rows)
    own_inseq = lax.dynamic_slice_in_dim(inseq_all, myself * tok_rows, tok_rows)
    cosine, sine = rotary_tables(own_inseq)
    inputs = tokens[0].astype(jnp.float32)
    scale_one = rms_scale(inputs)
    normed_one = inputs * scale_one
    gain_first = gain_one.astype(jnp.float32)
    normed_low = (normed_one * gain_first).astype(jnp.bfloat16)
    query_pre = jnp.dot(normed_low, query_w, preferred_element_type=jnp.float32).reshape(
        tok_rows, HEADS, HD
    )
    key_pre = jnp.dot(normed_low, key_w, preferred_element_type=jnp.float32).reshape(
        tok_rows, KV, HD
    )
    value_low = jnp.dot(normed_low, value_w, preferred_element_type=jnp.float32).astype(
        jnp.bfloat16
    )
    queries = rotary(query_pre, cosine, sine).astype(jnp.bfloat16).reshape(tok_rows, KV, groups, HD)
    keys = rotary(key_pre, cosine, sine).astype(jnp.bfloat16).reshape(tok_rows, KV * HD)

    def logits(key_block):
        return (
            jnp.einsum(
                "qcgd,kcd->cgqk",
                queries,
                key_block.reshape(-1, KV, HD),
                preferred_element_type=jnp.float32,
            )
            * scale
        )

    key_block = lax.all_gather(keys, "ctx", axis=0, tiled=True)
    value_block = lax.all_gather(value_low, "ctx", axis=0, tiled=True)
    allowed = permitted(own_place, own_seg, places, seg_all)
    top = jnp.full((KV, groups, tok_rows, 1), masked_score, jnp.float32)
    score = jnp.where(allowed, logits(key_block), masked_score)
    new_top = jnp.maximum(top, jnp.max(score, -1, keepdims=True))
    weight = jnp.where(allowed, jnp.exp(score - new_top), 0.0)
    summed = jnp.einsum(
        "cgqk,kcd->cgqd",
        weight.astype(jnp.bfloat16),
        value_block.reshape(-1, KV, HD),
        preferred_element_type=jnp.float32,
    )
    summed, top, total = (summed, new_top, jnp.sum(weight, -1, keepdims=True))
    attended = summed / total
    log_total = top + jnp.log(total)
    attended_low = (
        jnp.transpose(attended, (2, 0, 1, 3)).reshape(tok_rows, HEADS * HD).astype(jnp.bfloat16)
    )
    hidden = inputs + jnp.dot(attended_low, out_w, preferred_element_type=jnp.float32)
    scale_two = rms_scale(hidden)
    normed_two = hidden * scale_two
    gain_second = gain_two.astype(jnp.float32)
    ffn_low = (normed_two * gain_second).astype(jnp.bfloat16)
    gate = jnp.dot(ffn_low, gate_w, preferred_element_type=jnp.float32)
    up = jnp.dot(ffn_low, up_w, preferred_element_type=jnp.float32)
    sigmoid = jax.nn.sigmoid(gate)
    activated = gate * sigmoid
    mixed_low = (activated * up).astype(jnp.bfloat16)
    result = hidden + jnp.dot(mixed_low, down_w, preferred_element_type=jnp.float32)
    target = teacher[0].astype(jnp.float32)
    valid = (loss_mask[0] * (own_seg < NSEQ)).astype(jnp.float32)[:, None]
    differ = result - target
    square_sum, valid_count = lax.psum(
        (jnp.sum(valid * differ * differ), jnp.sum(valid)), ("ctx", "fsdp")
    )
    loss = square_sum / (valid_count * width)
    out_total = out_grad[0].astype(jnp.float32) + 2.0 * valid * differ / (valid_count * width)
    out_low = out_total.astype(jnp.bfloat16)
    down_grad = transposed(mixed_low, out_low)
    mixed_grad = against(out_low, down_w)
    silu_slope = sigmoid * (1.0 + gate * (1.0 - sigmoid))
    gate_low = (mixed_grad * up * silu_slope).astype(jnp.bfloat16)
    up_low = (mixed_grad * activated).astype(jnp.bfloat16)
    gate_grad = transposed(ffn_low, gate_low)
    up_grad = transposed(ffn_low, up_low)
    normed_grad = against(gate_low, gate_w) + against(up_low, up_w)
    gain_two_grad = jnp.sum(normed_grad * normed_two, 0)
    scaled_two = normed_grad * gain_second
    hidden_grad = out_total + scale_two * (
        scaled_two - normed_two * jnp.mean(scaled_two * normed_two, -1, keepdims=True)
    )
    ffn_final = (
        lax.psum_scatter(gain_two_grad, ("ctx", "fsdp"), scatter_dimension=0, tiled=True),
        lax.psum_scatter(gate_grad, ("ctx", "fsdp"), scatter_dimension=0, tiled=True),
        lax.psum_scatter(up_grad, ("ctx", "fsdp"), scatter_dimension=0, tiled=True),
        lax.psum_scatter(down_grad, ("ctx", "fsdp"), scatter_dimension=0, tiled=True),
    )
    branch_low = hidden_grad.astype(jnp.bfloat16)
    out_w_grad = transposed(attended_low, branch_low)
    attended_grad = against(branch_low, out_w).astype(jnp.bfloat16)
    grad_heads = jnp.transpose(attended_grad.reshape(tok_rows, KV, groups, HD), (1, 2, 0, 3))
    delta = jnp.sum(grad_heads.astype(jnp.float32) * attended, -1, keepdims=True)

    def cycle_step(step, state):
        key_block, value_block, key_acc, value_acc, query_acc = state
        source = (myself - step) % count_ctx
        allowed = permitted(
            own_place,
            own_seg,
            lax.dynamic_slice_in_dim(places, source * tok_rows, tok_rows),
            lax.dynamic_slice_in_dim(seg_all, source * tok_rows, tok_rows),
        )
        current_key = key_block
        current_value = value_block
        keys_three = current_key.reshape(tok_rows, KV, HD)
        values_three = current_value.reshape(tok_rows, KV, HD)
        prob = jnp.where(allowed, jnp.exp(logits(current_key) - log_total), 0.0)
        prob_grad = jnp.einsum(
            "cgqd,kcd->cgqk", grad_heads, values_three, preferred_element_type=jnp.float32
        )
        score_low = (prob * (prob_grad - delta)).astype(jnp.bfloat16)
        query_add = (
            jnp.einsum("cgqk,kcd->cgqd", score_low, keys_three, preferred_element_type=jnp.float32)
            * scale
        )
        key_add = (
            jnp.einsum(
                "cgqk,qcgd->kcd", score_low, queries, preferred_element_type=jnp.float32
            ).reshape(tok_rows, KV * HD)
            * scale
        )
        value_add = jnp.einsum(
            "cgqk,cgqd->kcd",
            prob.astype(jnp.bfloat16),
            grad_heads,
            preferred_element_type=jnp.float32,
        ).reshape(tok_rows, KV * HD)
        key_block, value_block = shifted((key_block, value_block), "ctx", 1)
        key_acc, value_acc = (
            shifted((key_acc + key_add).astype(jnp.bfloat16), "ctx", 1).astype(jnp.float32),
            shifted((value_acc + value_add).astype(jnp.bfloat16), "ctx", 1).astype(jnp.float32),
        )
        return (key_block, value_block, key_acc, value_acc, query_acc + query_add)

    cycle_start = (
        keys,
        value_low,
        jnp.zeros((tok_rows, KV * HD), jnp.float32),
        jnp.zeros((tok_rows, KV * HD), jnp.float32),
        jnp.zeros((KV, groups, tok_rows, HD), jnp.float32),
    )
    cycle_end = lax.fori_loop(0, count_ctx, cycle_step, cycle_start)
    key_acc = cycle_end[2]
    value_acc = cycle_end[3]
    query_acc = cycle_end[4]
    query_grad = jnp.transpose(query_acc, (2, 0, 1, 3)).reshape(tok_rows, HEADS, HD)
    query_low = (
        rotary_back(query_grad, cosine, sine).reshape(tok_rows, HEADS * HD).astype(jnp.bfloat16)
    )
    key_low = (
        rotary_back(key_acc.reshape(tok_rows, KV, HD), cosine, sine)
        .reshape(tok_rows, KV * HD)
        .astype(jnp.bfloat16)
    )
    value_grad_low = value_acc.astype(jnp.bfloat16)
    query_w_grad = transposed(normed_low, query_low)
    key_w_grad = transposed(normed_low, key_low)
    value_w_grad = transposed(normed_low, value_grad_low)
    normed_one_grad = (
        against(query_low, query_w) + against(key_low, key_w) + against(value_grad_low, value_w)
    )
    gain_one_grad = jnp.sum(normed_one_grad * normed_one, 0)
    scaled_one = normed_one_grad * gain_first
    input_grad = hidden_grad + scale_one * (
        scaled_one - normed_one * jnp.mean(scaled_one * normed_one, -1, keepdims=True)
    )
    attn_final = (
        lax.psum_scatter(gain_one_grad, ("ctx", "fsdp"), scatter_dimension=0, tiled=True),
        lax.psum_scatter(query_w_grad, ("ctx", "fsdp"), scatter_dimension=0, tiled=True),
        lax.psum_scatter(key_w_grad, ("ctx", "fsdp"), scatter_dimension=0, tiled=True),
        lax.psum_scatter(value_w_grad, ("ctx", "fsdp"), scatter_dimension=0, tiled=True),
        lax.psum_scatter(out_w_grad, ("ctx", "fsdp"), scatter_dimension=0, tiled=True),
    )
    return (
        result.astype(jnp.bfloat16)[None],
        loss,
        input_grad[None],
        attn_final[0],
        attn_final[1],
        attn_final[2],
        attn_final[3],
        attn_final[4],
        ffn_final[0],
        ffn_final[1],
        ffn_final[2],
        ffn_final[3],
    )


MESH = pl.DeviceIdType.MESH
ROWS_Y = 2
PLANE = 8
LANES = 128
VMEM_LIMIT = 60 * 2**20


def coordinates():
    ctx = lax.axis_index("ctx")
    fsdp = lax.axis_index("fsdp")
    return ctx // 2, ctx % 2, fsdp // 2, fsdp % 2


def device(z, y, x, c):
    return (z * 2 + y, x * 2 + c)


def greet(devices):
    barrier = pltpu.get_barrier_semaphore()
    for other in devices:
        pl.semaphore_signal(barrier, inc=1, device_id=other, device_id_type=MESH)
    pl.semaphore_wait(barrier, len(devices))


def remote(src, dst, send, recv, target):
    return pltpu.make_async_remote_copy(
        src_ref=src,
        dst_ref=dst,
        send_sem=send,
        recv_sem=recv,
        device_id=target,
        device_id_type=MESH,
    )


def transfers(sources, targets, sem):
    return [pltpu.make_async_copy(src, dst, sem.at[i]) for i, (src, dst) in enumerate(zip(sources, targets))]


def line_gather(place, lines, x_ref, slot, send, recv, here=None):
    z, y, x, c = place
    mine = None if here is None else pltpu.make_async_copy(x_ref, slot(z), here)
    ways = ((0, -1, device(z + 1, y, x, c)), (1, 1, device(z - 1, y, x, c)))

    def along(way, sign, to, s):
        zz = z + sign * (s - 1)
        return remote(x_ref if s == 1 else slot(zz), slot(zz), send.at[way, s], recv.at[way, s], to)

    def sends(sign, s):
        if sign < 0:
            return (z - (s - 1) >= 0) & (z + 1 < lines)
        return (z + (s - 1) < lines) & (z - 1 >= 0)

    def present(sign, s):
        return z - s >= 0 if sign < 0 else z + s < lines

    def start(s):
        for way, sign, to in ways:
            pl.when(sends(sign, s))(lambda way=way, sign=sign, to=to: along(way, sign, to, s).start())

    def begin():
        if mine is not None:
            mine.start()
        start(1)

    def pass_on(s):
        for way, sign, to in ways:
            pl.when(present(sign, s))(lambda way=way, sign=sign, to=to: along(way, sign, to, s).wait_recv())
        if s + 1 < lines:
            start(s + 1)

    def last():
        for s in range(1, lines):
            for way, sign, to in ways:
                pl.when(sends(sign, s))(lambda way=way, sign=sign, to=to, s=s: along(way, sign, to, s).wait_send())
        if mine is not None:
            mine.wait()

    return begin, pass_on, last


def line_reduce(place, lines, parts, up, down, send, recv):
    z, y, x, c = place
    ways = ((0, up, device(z + 1, y, x, c)), (1, down, device(z - 1, y, x, c)))

    def copy(way, t, own):
        _, sums, to = ways[way]
        src = parts.at[t] if own else sums.at[t]
        return remote(src, sums.at[t], send.at[way, t], recv.at[way, t], to)

    def begin():
        @pl.when(z == 0)
        def _():
            for t in range(lines - 1, 0, -1):
                copy(0, t, True).start()

        @pl.when(z == lines - 1)
        def _():
            for t in range(lines - 1):
                copy(1, t, True).start()

    def add_on(way, t):
        copy(way, t, False).wait_recv()
        add_rows(ways[way][1].at[t], parts.at[t])
        copy(way, t, False).start()

    def hop(moment):
        for t in range(lines):
            for zz in range(1, lines - 1):
                if zz < t and zz + (lines - 1 - t) == moment:
                    pl.when(z == zz)(functools.partial(add_on, 0, t))
                if zz > t and (lines - 1 - zz) + t == moment:
                    pl.when(z == zz)(functools.partial(add_on, 1, t))

    def last(write, step=32):
        for way, first in ((0, 0), (1, lines - 1)):

            @pl.when(z != first)
            def _():
                copy(way, z, False).wait_recv()

        def body(i, carry):
            at = pl.ds(pl.multiple_of(i * step, step), step)
            from_below = jnp.where(z > 0, up[z, at, :].astype(jnp.float32), 0.0)
            from_above = jnp.where(z < lines - 1, down[z, at, :].astype(jnp.float32), 0.0)
            write(i, parts[z, at, :].astype(jnp.float32) + from_below + from_above)
            return carry

        lax.fori_loop(0, parts.shape[1] // step, body, 0)
        for zz in range(lines):

            @pl.when(z == zz)
            def _():
                for t in range(lines):
                    if t > zz:
                        copy(0, t, zz == 0).wait_send()
                    if t < zz:
                        copy(1, t, zz == lines - 1).wait_send()

    return begin, hop, last


def column_cut(width):
    tiles = width // LANES
    return (tiles + 1) // 2 * LANES


def line_of(z, y, x, c, lines):
    return [device(lax.rem(z + k, lines), y, x, c) for k in range(1, lines)]


def reduce_plan(lines, prepare, p_ref, o_ref, held, corner_a, corner_b, from_side, from_over, along, send, recv):
    z, y, x, c = coordinates()
    parts = lines
    rows, width = held.shape[2], held.shape[3]
    cut = column_cut(width)
    first, second = pl.ds(0, cut), pl.ds(cut, width - cut)
    side, over, sibling = device(z, y, 1 - x, c), device(z, 1 - y, x, c), device(z, y, x, 1 - c)
    def given(part, yy, xx, cc):
        member = yy * 4 + xx * 2 + cc
        return p_ref.at[lax.rem(z + part + 1, lines), member]

    def make(part, kind, src, dst, to):
        return remote(src, dst, send.at[part, kind], recv.at[part, kind], to)

    lane = lambda part, yy, xx: held.at[part, yy * 2 + xx]

    def over_core(part):
        return [
            make(part, yy * 2 + xx, given(part, yy, xx, 1 - c), lane(part, yy, xx), sibling)
            for yy in range(2)
            for xx in range(2)
        ]

    def to_corner(part):
        return (
            make(part, 4, lane(part, 1 - y, 1 - x).at[:, first], corner_a.at[part], over),
            make(part, 5, lane(part, 1 - y, 1 - x).at[:, second], corner_b.at[part], side),
        )

    def to_neighbour(part, way):
        columns = (first, second)[way % 2]
        if way < 2:
            return make(part, 6 + way, lane(part, y, 1 - x).at[:, columns], from_side.at[part, :, columns], side)
        return make(part, 6 + way, lane(part, 1 - y, x).at[:, columns], from_over.at[part, :, columns], over)

    def along_z(part):
        to = lax.rem(z + part + 1, lines)
        return make(part, 10, lane(part, y, x), along.at[part], device(to, y, x, c))

    step = 16

    def add_core(part):
        for copy in over_core(part):
            copy.wait_recv()
        for yy, xx in ((1 - y, 1 - x), (y, 1 - x), (1 - y, x), (y, x)):
            mine, other = given(part, yy, xx, c), lane(part, yy, xx)

            def body(i, carry):
                at = pl.ds(pl.multiple_of(i * step, step), step)
                total = mine[at, :].astype(jnp.float32) + other[at, :].astype(jnp.float32)
                other[at, :] = total.astype(other.dtype)
                return carry

            lax.fori_loop(0, rows // step, body, 0)
        for copy in to_corner(part):
            copy.start()
        to_neighbour(part, 1).start()
        to_neighbour(part, 2).start()

    def add_corner(part):
        copies = to_corner(part)
        pairs = (
            (copies[0], lane(part, y, 1 - x), corner_a.at[part], first),
            (copies[1], lane(part, 1 - y, x), corner_b.at[part], second),
        )
        for copy, mine, other, columns in pairs:
            copy.wait_recv()

            def body(i, carry):
                at = pl.ds(pl.multiple_of(i * step, step), step)
                total = mine[at, columns].astype(jnp.float32) + other[at, :].astype(jnp.float32)
                mine[at, columns] = total.astype(mine.dtype)
                return carry

            lax.fori_loop(0, rows // step, body, 0)
        to_neighbour(part, 0).start()
        to_neighbour(part, 3).start()

    def add_neighbours(part):
        for way in range(4):
            to_neighbour(part, way).wait_recv()
        last = part == parts - 1
        mine = lane(part, y, x)

        def body(i, carry):
            at = pl.ds(pl.multiple_of(i * step, step), step)
            total = mine[at, :].astype(jnp.float32) + from_side[part, at, :].astype(jnp.float32)
            total += from_over[part, at, :].astype(jnp.float32)
            if last:
                o_ref[at, :] = total
            else:
                mine[at, :] = total.astype(mine.dtype)
            return carry

        lax.fori_loop(0, rows // step, body, 0)
        if not last:
            along_z(part).start()

    def ready(part):
        prepare(lax.rem(z + part + 1, lines))
        for copy in over_core(part):
            copy.start()

    kinds = (ready, add_core, add_corner, add_neighbours)

    def run(number):
        for lag, kind in enumerate(kinds):
            if 0 <= number - lag < parts:
                kind(number - lag)

    def last():
        for part in range(parts - 1):
            along_z(part).wait_recv()

        def body(i, carry):
            at = pl.ds(pl.multiple_of(i * step, step), step)
            total = o_ref[at, :]
            for part in range(parts - 1):
                total += along[part, at, :].astype(jnp.float32)
            o_ref[at, :] = total
            return carry

        lax.fori_loop(0, rows // step, body, 0)
        for part in range(parts - 1):
            along_z(part).wait_send()
        for part in range(parts):
            for copy in (*over_core(part), *to_corner(part), *(to_neighbour(part, way) for way in range(4))):
                copy.wait_send()

    return [functools.partial(run, number) for number in range(parts + len(kinds) - 1)], last


def reduce_scratch(lines, share, columns, low):
    cut = column_cut(columns)
    return [
        pltpu.VMEM((lines, PLANE, share, columns), low),
        pltpu.VMEM((lines, 4, share, columns), low),
        pltpu.VMEM((lines, share, cut), low),
        pltpu.VMEM((lines, share, columns - cut), low),
        pltpu.VMEM((lines, share, columns), low),
        pltpu.VMEM((lines, share, columns), low),
        pltpu.VMEM((lines - 1, share, columns), low),
        pltpu.SemaphoreType.DMA((lines, 11)),
        pltpu.SemaphoreType.DMA((lines, 11)),
    ]


def store_terms(p, block, start, value):
    members, share = p.shape[1:3]
    width = value.shape[1]
    p[block, :, :, start : start + width] = value.astype(p.dtype).reshape(members, share, width)


def halves(width):
    cut = column_cut(width)
    return pl.ds(0, cut), pl.ds(cut, width - cut)


class PlaneGather:
    def __init__(self, place, at, width, send, recv):
        z, y, x, c = place
        side, over, sibling = device(z, y, 1 - x, c), device(z, 1 - y, x, c), device(z, y, x, 1 - c)
        self.send, self.recv = send, recv
        own, next_x, next_y, corner = at(y, x), at(y, 1 - x), at(1 - y, x), at(1 - y, 1 - x)
        first, second = [lambda ref, of=of: ref.at[..., of] for of in halves(width)]
        self.table = (
            (first(own), side),
            (second(own), side),
            (first(own), over),
            (second(own), over),
            (own, sibling),
            (first(next_x), over),
            (second(next_y), side),
            (first(next_x), sibling),
            (second(next_x), sibling),
            (first(next_y), sibling),
            (second(next_y), sibling),
            (first(corner), sibling),
            (second(corner), sibling),
        )

    def copy(self, kind):
        ref, to = self.table[kind]
        return remote(ref, ref, self.send.at[kind], self.recv.at[kind], to)

    def begin(self):
        for kind in (0, 3, 4, 1, 2):
            self.copy(kind).start()

    def came(self, *kinds):
        for kind in kinds:
            self.copy(kind).wait_recv()

    def forward_on(self):
        for kind, onward in ((0, (5, 7)), (3, (6, 10)), (1, (8,)), (2, (9,))):
            self.came(kind)
            for other in onward:
                self.copy(other).start()

    def corner_on(self):
        for kind, onward in ((5, 11), (6, 12)):
            self.came(kind)
            self.copy(onward).start()

    def rest(self):
        self.came(4, *range(7, GATHER_KINDS))

    def drain(self):
        for kind in range(GATHER_KINDS):
            self.copy(kind).wait_send()


GATHER_KINDS = 13
REDUCE_KINDS = 10


def reduce_steps(place, at_rows, partial, held, corner_a, corner_b, from_side, from_over, send, recv):
    z, y, x, c = place
    side, over, sibling = device(z, y, 1 - x, c), device(z, 1 - y, x, c), device(z, y, x, 1 - c)
    first, second = halves(held.shape[-1])
    lane = lambda yy, xx: held.at[yy * 2 + xx, at_rows]
    next_x, next_y, corner = lane(y, 1 - x), lane(1 - y, x), lane(1 - y, 1 - x)

    def to_core(yy, xx):
        kind = yy * 2 + xx
        src = partial.at[yy * 4 + xx * 2 + 1 - c, at_rows]
        return remote(src, lane(yy, xx), send.at[kind], recv.at[kind], sibling)

    table = (
        (corner.at[:, first], corner_a.at[at_rows], over),
        (corner.at[:, second], corner_b.at[at_rows], side),
        (next_x.at[:, first], from_side.at[at_rows, first], side),
        (next_x.at[:, second], from_side.at[at_rows, second], side),
        (next_y.at[:, first], from_over.at[at_rows, first], over),
        (next_y.at[:, second], from_over.at[at_rows, second], over),
    )

    def copy(kind):
        src, dst, to = table[kind]
        return remote(src, dst, send.at[4 + kind], recv.at[4 + kind], to)

    return to_core, copy


def add_rows(target, other, columns=None, step=32):
    def body(i, carry):
        at = pl.ds(pl.multiple_of(i * step, step), step)
        mine = target[at, :] if columns is None else target[at, columns]
        total = (mine.astype(jnp.float32) + other[at, :].astype(jnp.float32)).astype(target.dtype)
        if columns is None:
            target[at, :] = total
        else:
            target[at, columns] = total
        return carry

    lax.fori_loop(0, other.shape[0] // step, body, 0)


def feed_forward_kernel(
    out_rows, attended, tokens, teacher_rows, out_grad_rows, valid, gains, gate_up_rows, down_rows,
    result_out, square, norm, hidden_grad, branch, attended_grad, down_final, down_out, gate_out, up_out,
    result, down_rest, gate_grad, up_grad, store_sem, out_w, gate_up_w, teacher, out_grad, down_w, down_up, down_down, normed_all, kept, mixed, grads_all, partial, held, corner_a, corner_b, from_side, from_over, hidden, total_grad, scales, squares,
    load_sem, here, line_send, line_recv, down_send, down_recv, gather_send, gather_recv, reduce_send, reduce_recv,
):
    place = coordinates()
    z, y, x, c = place
    width = tokens.shape[1]
    pairs = ((out_rows, out_w), (gate_up_rows, gate_up_w), (teacher_rows, teacher), (out_grad_rows, out_grad))
    loads = [pltpu.make_async_copy(src, dst, load_sem.at[i]) for i, (src, dst) in enumerate(pairs)]
    for load in loads:
        load.start()
    lines, units = down_w.shape[:2]
    greet([device(z, y, 1 - x, c), device(z, 1 - y, x, c), device(z, y, x, 1 - c)] + line_of(z, y, x, c, lines))
    rows = tokens.shape[0]
    share = lines * units
    first, second = halves(width)
    down_lines = [
        line_gather(
            place, lines, down_rows.at[:, of], lambda zz, of=of: down_w.at[zz, :, of],
            line_send.at[i], line_recv.at[i], here.at[i],
        )
        for i, of in enumerate((first, second))
    ]
    (begin_one, pass_one, last_one), (begin_two, pass_two, last_two) = down_lines
    begin_one()
    begin_two()
    mine = y * 4 + x * 2 + c
    chips = ((y, x), (y, 1 - x), (1 - y, x), (1 - y, 1 - x))

    gain = gains[1:2, :]
    count = jnp.sum(gains[2:3, :], -1, keepdims=True) / (width // (lines * PLANE))
    norm[...] = 2.0 / (count * width)
    loads[0].wait()
    def hidden_rows(at):
        product = jnp.dot(attended[at, :], out_w[...], preferred_element_type=jnp.float32)
        hidden[at, :] = tokens[at, :].astype(jnp.float32) + product

    def norm_rows(at):
        values = hidden[at, :]
        scale = rms_scale(values)
        scales[at, :] = scale
        normed_all[mine, at, :] = (values * scale * gain[...]).astype(normed_all.dtype)

    parts = 2
    part_rows = rows // parts
    at_part = [pl.ds(part * part_rows, part_rows) for part in range(parts)]

    def of_part(part, body):
        by_rows(part_rows, lambda at: body(pl.ds(pl.multiple_of(part * part_rows + at.start, ROW_STEP), ROW_STEP)))

    class Phase(PlaneGather):
        def __init__(self, phase, part, whole):
            at_rows = at_part[part]
            self.part, self.at_rows = part, at_rows
            at = lambda yy, xx: whole.at[yy * 4 + xx * 2 + c, at_rows]
            super().__init__(place, at, width, gather_send.at[phase, part], gather_recv.at[phase, part])
            self.to_core, self.pass_on = reduce_steps(
                place, at_rows, partial, held, corner_a, corner_b, from_side, from_over,
                reduce_send.at[phase, part], reduce_recv.at[phase, part],
            )

        def join(self, yy, xx):
            self.to_core(yy, xx).wait_recv()
            add_rows(held.at[yy * 2 + xx, self.at_rows], partial.at[yy * 4 + xx * 2 + c, self.at_rows])

        def join_next(self, number):
            self.join(*chips[number])
            self.pass_on(2 + number).start()

        def join_corner(self):
            self.join(*chips[3])
            self.pass_on(0).start()
            self.pass_on(1).start()

        def add_corner(self):
            self.pass_on(0).wait_recv()
            add_rows(held.at[y * 2 + 1 - x, self.at_rows], corner_a.at[self.at_rows], first)
            self.pass_on(2).start()
            self.pass_on(1).wait_recv()
            add_rows(held.at[(1 - y) * 2 + x, self.at_rows], corner_b.at[self.at_rows], second)
            self.pass_on(5).start()

        def complete(self):
            for kind in (2, 3, 4, 5):
                self.pass_on(kind).wait_recv()
            for kind in range(6):
                self.pass_on(kind).wait_send()
            for yy, xx in chips:
                self.to_core(yy, xx).wait_send()

    def pair_of(number):
        yy, xx = chips[number]
        return pl.ds(yy * 4 + xx * 2, 2)

    one, two = [Phase(0, part, normed_all) for part in range(parts)]
    hidden_rows(at_part[0])
    of_part(0, norm_rows)
    one.begin()
    hidden_rows(at_part[1])
    of_part(1, norm_rows)

    def summed(at):
        total = held[y * 2 + x, at, :].astype(jnp.float32) + from_side[at, :].astype(jnp.float32)
        return total + from_over[at, :].astype(jnp.float32)

    def units_of(phase, number):
        where = (pair_of(number), phase.at_rows)
        both = jnp.dot(
            normed_all[where].reshape(rows, width), gate_up_w[...], preferred_element_type=jnp.float32
        )
        gate, up = both[:, :share], both[:, share:]
        sigmoid = 1.0 / (1.0 + jnp.exp(-gate))
        activated = gate * sigmoid
        slope = up * (sigmoid + activated * (1.0 - sigmoid))
        kept[(*where, slice(0, share))] = slope.astype(kept.dtype).reshape(2, part_rows, share)
        kept[(*where, slice(share, 2 * share))] = activated.astype(kept.dtype).reshape(2, part_rows, share)
        mixed[where] = (activated * up).astype(mixed.dtype).reshape(2, part_rows, share)

    def down_of(phase, number):
        where = (pair_of(number), phase.at_rows)
        out = jnp.dot(
            mixed[where].reshape(rows, share),
            down_w[...].reshape(share, width),
            preferred_element_type=jnp.float32,
        )
        partial[where] = out.astype(partial.dtype).reshape(2, part_rows, width)
        phase.to_core(*chips[number]).start()

    one.came(4)
    loads[1].wait()
    units_of(one, 0)
    pass_one(1)
    pass_two(1)
    one.forward_on()
    two.begin()
    for moment in range(2, lines - 1):
        pass_one(moment)
    one.came(7, 8)
    units_of(one, 1)
    for moment in range(2, lines - 1):
        pass_two(moment)
    one.came(9, 10)
    units_of(one, 2)
    pass_one(lines - 1)
    one.corner_on()
    two.came(4)
    units_of(two, 0)
    pass_two(lines - 1)
    last_one()
    last_two()
    two.forward_on()
    one.came(11, 12)
    units_of(one, 3)
    down_of(one, 1)
    two.came(7, 8)
    units_of(two, 1)
    down_of(one, 2)
    one.join_next(1)
    two.came(9, 10)
    units_of(two, 2)
    two.corner_on()
    down_of(one, 3)
    one.join_next(2)
    two.came(11, 12)
    units_of(two, 3)
    one.join_corner()
    down_of(two, 1)
    down_of(two, 2)
    two.join_next(1)
    down_of(one, 0)
    down_of(two, 3)
    two.join_next(2)
    one.join(*chips[0])
    one.add_corner()
    two.join_corner()
    down_of(two, 0)
    two.join(*chips[0])
    one.complete()
    loads[2].wait()
    loads[3].wait()

    def result_rows(at):
        values = hidden[at, :] + summed(at)
        result[at, :] = values.astype(result.dtype)
        differ = values - teacher[at, :].astype(jnp.float32)
        weighed = valid[at, :] * differ
        squares[at, :] = jnp.sum(weighed * differ, -1, keepdims=True)
        total = out_grad[at, :].astype(jnp.float32) + weighed * norm[...]
        total_grad[at, :] = total
        grads_all[mine, at, :] = total.astype(grads_all.dtype)

    def back_of(phase, number):
        where = (pair_of(number), phase.at_rows)
        mixed_grad = against(grads_all[where].reshape(rows, width), down_w[...].reshape(share, width))
        slope = kept[(*where, slice(0, share))].reshape(rows, share).astype(jnp.float32)
        activated = kept[(*where, slice(share, 2 * share))].reshape(rows, share).astype(jnp.float32)
        low_gate = (mixed_grad * slope).astype(kept.dtype)
        low_up = (mixed_grad * activated).astype(kept.dtype)
        kept[(*where, slice(0, share))] = low_gate.reshape(2, part_rows, share)
        kept[(*where, slice(share, 2 * share))] = low_up.reshape(2, part_rows, share)
        out = against(low_gate, gate_up_w[:, :share]) + against(low_up, gate_up_w[:, share:])
        partial[where] = out.astype(partial.dtype).reshape(2, part_rows, width)
        phase.to_core(*chips[number]).start()

    three, four = [Phase(1, part, grads_all) for part in range(parts)]
    of_part(0, result_rows)
    three.begin()
    two.add_corner()
    three.came(4)
    back_of(three, 0)
    two.complete()
    of_part(1, result_rows)
    square[...] = jnp.sum(squares[...], 0, keepdims=True)
    stores = transfers((result, down_rest, gate_grad, up_grad), (result_out, down_out, gate_out, up_out), store_sem)
    stores[0].start()
    three.forward_on()
    four.begin()
    three.came(7, 8)
    back_of(three, 1)
    three.came(9, 10)
    back_of(three, 2)
    three.join_next(1)
    four.came(4)
    back_of(four, 0)
    three.corner_on()
    three.join_next(2)
    three.came(11, 12)
    back_of(three, 3)
    four.forward_on()
    three.join_corner()
    four.came(7, 8)
    back_of(four, 1)
    three.join(*chips[0])
    four.came(9, 10)
    back_of(four, 2)
    four.join_next(1)
    four.corner_on()
    four.join_next(2)
    three.add_corner()
    four.came(11, 12)
    back_of(four, 3)
    four.join(*chips[0])
    four.join_corner()
    tokens_all = normed_all.shape[0] * rows
    block = 256

    def down_block(of, to):
        def run(i, carry):
            at = pl.ds(pl.multiple_of(i * block, block), block)
            left = mixed[:, :, at].reshape(tokens_all, block)
            grads = transposed(left, grads_all[:, :, of].reshape(tokens_all, of.size)).astype(to.dtype)
            per = block // units
            to[pl.ds(i * per, per)] = grads.reshape(per, units, of.size)
            return carry

        lax.fori_loop(0, share // block, run, 0)

    def both_block(i, carry):
        at = pl.ds(pl.multiple_of(i * block, block), block)
        left = normed_all[:, :, at].reshape(tokens_all, block)
        both = transposed(left, kept[...].reshape(tokens_all, 2 * share)).astype(gate_grad.dtype)
        gate_grad[at, :] = both[:, :share]
        up_grad[at, :] = both[:, share:]
        return carry

    down_parts = down_w.at[:, :, first]
    down_begin, down_hop, down_last = line_reduce(
        place, lines, down_parts, down_up, down_down, down_send, down_recv
    )
    down_block(first, down_parts)
    down_begin()
    down_block(second, down_rest)
    blocks = width // block
    third = blocks // 3
    lax.fori_loop(0, third, both_block, 0)
    three.complete()
    four.add_corner()
    down_hop(1)
    lax.fori_loop(third, 2 * third, both_block, 0)
    for moment in range(2, lines - 1):
        down_hop(moment)
    lax.fori_loop(2 * third, blocks, both_block, 0)
    for store in stores[1:]:
        store.start()

    def grad_rows(at):
        grads = summed(at)
        normed = hidden[at, :] * scales[at, :]
        scaled = grads * gain[...]
        values = total_grad[at, :] + scales[at, :] * (scaled - normed * jnp.mean(scaled * normed, -1, keepdims=True))
        hidden_grad[at, :] = values
        branch[at, :] = values.astype(branch.dtype)

    def attended_rows(at):
        attended_grad[at, :] = against(branch[at, :], out_w[...]).astype(attended_grad.dtype)

    of_part(0, grad_rows)
    attended_rows(at_part[0])
    four.complete()
    of_part(1, grad_rows)
    attended_rows(at_part[1])


    def keep_down(i, sums):
        down_final[pl.ds(pl.multiple_of(i * 32, 32), 32), :] = sums

    down_last(keep_down)
    for phase in (one, two, three, four):
        phase.drain()
    for store in stores:
        store.wait()


def feed_forward(lines, out_rows, attended, tokens, teacher, out_grad, valid, gains, gate_up_w, down_rows, identity):
    rows, width = tokens.shape
    units = down_rows.shape[0]
    share = lines * units
    low = tokens.dtype
    shape = jax.ShapeDtypeStruct
    vmem, anywhere = pl.BlockSpec(memory_space=pltpu.VMEM), pl.BlockSpec(memory_space=pl.ANY)
    cut = column_cut(width)
    return pl.pallas_call(
        feed_forward_kernel,
        out_shape=[
            shape((rows, width), low),
            shape((1, 1), jnp.float32),
            shape((1, 1), jnp.float32),
            shape((rows, width), jnp.float32),
            shape((rows, width), low),
            shape((rows, width), low),
            shape((units, cut), jnp.float32),
            shape((lines, units, width - cut), low),
            shape((width, share), low),
            shape((width, share), low),
        ],
        in_specs=[anywhere, vmem, vmem, anywhere, anywhere, vmem, vmem, anywhere, anywhere],
        out_specs=[anywhere] + [vmem] * 6 + [anywhere] * 3,
        scratch_shapes=[
            pltpu.VMEM((rows, width), low),
            pltpu.VMEM((lines, units, width - cut), low),
            pltpu.VMEM((width, share), low),
            pltpu.VMEM((width, share), low),
            pltpu.SemaphoreType.DMA((4,)),
            pltpu.VMEM((width, width), low),
            pltpu.VMEM((width, 2 * share), low),
            pltpu.VMEM((rows, width), low),
            pltpu.VMEM((rows, width), low),
            pltpu.VMEM((lines, units, width), low),
            pltpu.VMEM((lines, units, cut), low),
            pltpu.VMEM((lines, units, cut), low),
            pltpu.VMEM((PLANE, rows, width), low),
            pltpu.VMEM((PLANE, rows, 2 * share), low),
            pltpu.VMEM((PLANE, rows, share), low),
            pltpu.VMEM((PLANE, rows, width), low),
            pltpu.VMEM((PLANE, rows, width), low),
            pltpu.VMEM((4, rows, width), low),
            pltpu.VMEM((rows, cut), low),
            pltpu.VMEM((rows, width - cut), low),
            pltpu.VMEM((rows, width), low),
            pltpu.VMEM((rows, width), low),
            pltpu.VMEM((rows, width), jnp.float32),
            pltpu.VMEM((rows, width), jnp.float32),
            pltpu.VMEM((rows, 1), jnp.float32),
            pltpu.VMEM((rows, 1), jnp.float32),
            pltpu.SemaphoreType.DMA((4,)),
            pltpu.SemaphoreType.DMA((2,)),
            pltpu.SemaphoreType.DMA((2, 2, lines)),
            pltpu.SemaphoreType.DMA((2, 2, lines)),
            pltpu.SemaphoreType.DMA((2, lines)),
            pltpu.SemaphoreType.DMA((2, lines)),
            pltpu.SemaphoreType.DMA((2, 2, GATHER_KINDS)),
            pltpu.SemaphoreType.DMA((2, 2, GATHER_KINDS)),
            pltpu.SemaphoreType.DMA((2, 2, REDUCE_KINDS)),
            pltpu.SemaphoreType.DMA((2, 2, REDUCE_KINDS)),
        ],
        compiler_params=pltpu.CompilerParams(collective_id=identity, vmem_limit_bytes=VMEM_LIMIT),
        cost_estimate=pl.CostEstimate(flops=40 * PLANE * rows * width * share // 2, bytes_accessed=30 * 2**20, transcendentals=0),
        name="feed_forward",
    )(out_rows, attended, tokens, teacher, out_grad, valid, gains, gate_up_w, down_rows)


HEAD_TILES = 3
ROW_STEP = 64


def by_rows(rows, body, step=ROW_STEP):
    def run(i, carry):
        body(pl.ds(pl.multiple_of(i * step, step), step))
        return carry

    lax.fori_loop(0, rows // step, run, 0)


def lanes_of(values):
    return lax.broadcasted_iota(jnp.int32, values.shape, len(values.shape) - 1)


def turned(tile, cosine, sine):
    half = HD // 2
    partner = jnp.where(lanes_of(tile) < half, -pltpu.roll(tile, LANES - half, 1), pltpu.roll(tile, half, 1))
    return tile * cosine + partner * sine


def packed_pair(first, second, even):
    lane = lanes_of(first)
    moved = pltpu.roll(second, HD, 1)
    full_even = jnp.where(lane < HD, first, moved)
    full_odd = jnp.where(lane < 32, pltpu.roll(first, 64, 1), pltpu.roll(second, 32, 1))
    return jnp.where(even, full_even, full_odd), jnp.where(even, moved, first)


def unpacked_pair(full, part, even):
    lane = lanes_of(full)
    zero = jnp.zeros_like(full)
    first_even = jnp.where(lane < HD, full, zero)
    second_even = jnp.where(lane < 32, pltpu.roll(full, 32, 1), jnp.where(lane < HD, pltpu.roll(part, 32, 1), zero))
    first_odd = jnp.where(lane < 64, part, jnp.where(lane < HD, pltpu.roll(full, 64, 1), zero))
    second_odd = jnp.where(lane < HD, pltpu.roll(full, HD, 1), zero)
    return jnp.where(even, first_even, first_odd), jnp.where(even, second_even, second_odd)


def keys_and_values(qkv, keys, values, count, rows):
    def body(src, carry):
        block = qkv[src].astype(jnp.float32)
        tiles = [block[:, i * LANES : (i + 1) * LANES] for i in range(HEAD_TILES)]
        lane = lanes_of(tiles[0])
        key = jnp.where(lane < HD, tiles[2], 0.0)
        value = jnp.where(lane < 64, pltpu.roll(tiles[1], 64, 1), pltpu.roll(tiles[2], HD, 1))
        value = jnp.where(lane < 32, pltpu.roll(tiles[0], 32, 1), value)
        value = jnp.where(lane < HD, value, 0.0)
        at = pl.ds(pl.multiple_of(src * rows, rows), rows)
        for half in range(2):
            keys[half, at, :] = key[half * rows : (half + 1) * rows].astype(keys.dtype)
            values[half, at, :] = value[half * rows : (half + 1) * rows].astype(values.dtype)
        return carry

    lax.fori_loop(0, count, body, 0)


def segment_of(lengths, place):
    start, end = jnp.zeros_like(place), 0
    for length in [lengths[0, j] for j in range(NSEQ)]:
        end = end + length
        start = start + jnp.where(place >= end, length, 0)
    return start, end


def side_by_side(heads):
    full, part = packed_pair(heads[0], heads[1], True)
    full_odd, part_odd = packed_pair(heads[2], heads[3], False)
    middle = jnp.where(lanes_of(part) < 64, part, pltpu.roll(part_odd, 64, 1))
    return full, middle, full_odd


def apart(ref, group):
    start = group * HEAD_TILES * LANES
    tiles = [ref[:, start + i * LANES : start + (i + 1) * LANES].astype(jnp.float32) for i in range(HEAD_TILES)]
    return unpacked_pair(tiles[0], tiles[1], True) + unpacked_pair(tiles[2], pltpu.roll(tiles[1], 64, 1), False)


def arrange_rows(rows_in, w_query, w_key, w_value, gain_rows, count):
    share = rows_in.shape[0]
    groups = HEADS // KV
    queries = [head for group in range(HEADS // 4) for head in apart(w_query, group)]
    keys = [head for group in range(KV // 4) for head in apart(w_key, group)]
    values = [head for group in range(KV // 4) for head in apart(w_value, group)]
    lane = lanes_of(keys[0])
    for head in range(KV):
        for number, tile in enumerate(queries[head * groups : (head + 1) * groups] + [keys[head]]):
            third = pltpu.roll(values[head], HD - 32 * number, 1)
            start = (head * HEAD_TILES + number) * LANES
            rows_in[:, start : start + LANES] = jnp.where(lane < HD, tile, third).astype(rows_in.dtype)
    row = lax.broadcasted_iota(jnp.int32, (LANES, LANES), 0)
    columns = jnp.where(row == 0, gain_rows[0:1, :], jnp.where(row == 1, gain_rows[1:2, :], 0.0))
    columns = jnp.where(row == 2, count, columns)
    rows_in[:, KV * HEAD_TILES * LANES :] = jnp.transpose(columns)[:share, :].astype(rows_in.dtype)


def attend_kernel(
    scale, lines, w_query, w_key, w_value, w_gate, w_up, out_rows, gain_rows, freq, mask, deal, lengths, tokens,
    attended, normed, gains, cosine, sine, valid, weights, out_w, unit_w, qkv_out, probs,
    rows_in, unit_rows, w, place_row, sent, qkv, keys, values, prob_blocks, o_sent, o_came,
    send, recv, o_send, o_recv, p_sem, q_sem, w_sem, w_line_send, w_line_recv, w_send, w_recv, w_here, g_send, g_recv, g_here,
    o_line_send, o_line_recv,
    u_send, u_recv, u_here, l_send, l_recv,
):
    z, y, x, c = coordinates()
    count = sent.shape[0]
    me = z * 2 + y
    even = y == 0
    rows, width = tokens.shape
    half_rows = rows // 2
    head_cols = HEAD_TILES * LANES
    to_device = lambda i: (i, x * 2 + c)
    peer = lambda k: lax.rem(me + k, count)

    member = y * 4 + x * 2 + c
    in_plane = lambda i: (z * 2 + i // 4, i % 4)
    unit_peer = lambda k: lax.rem(member + k, PLANE)
    others = [device(z, yy, xx, cc) for yy, xx, cc in ((y, 1 - x, c), (y, x, 1 - c), (y, 1 - x, 1 - c))]
    others += [device(z, 1 - y, xx, cc) for xx, cc in ((1 - x, c), (x, 1 - c), (1 - x, 1 - c))]
    units = w_gate.shape[1] // (lines * PLANE)
    for i in range(PLANE):
        for zz in range(lines):
            start = (zz * PLANE + i) * units
            unit_rows[i, :, zz * units : (zz + 1) * units] = w_gate[:, start : start + units]
            unit_rows[i, :, (lines + zz) * units : (lines + zz + 1) * units] = w_up[:, start : start + units]
    greet([to_device(peer(k)) for k in range(1, count)] + others)

    def unit_out(k):
        i = unit_peer(k)
        return remote(unit_rows.at[i], unit_w.at[z, member], u_send.at[k], u_recv.at[k], in_plane(i))

    unit_own = pltpu.make_async_copy(unit_rows.at[member], unit_w.at[z, member], u_here)
    unit_own.start()
    columns = rows_in.shape[1]
    line_gathers, plane_gathers = [], []
    cut = 8 * LANES
    for part, of in enumerate((pl.ds(0, cut), pl.ds(cut, columns - cut))):
        line_gathers.append(
            line_gather(
                (z, y, x, c), lines, rows_in.at[:, of], lambda zz, of=of: w.at[zz, member, :, of],
                w_line_send.at[part], w_line_recv.at[part], w_here.at[part],
            )
        )
        plane_gathers.append(
            PlaneGather(
                (z, y, x, c), lambda yy, xx, of=of: w.at[:, yy * 4 + xx * 2 + c, :, of], of.size,
                w_send.at[part], w_recv.at[part],
            )
        )
    (one_begin, one_pass, one_last), (two_begin, two_pass, two_last) = line_gathers
    one, two = plane_gathers
    out_begin, out_pass, out_last = line_gather(
        (z, y, x, c), lines, out_rows, lambda zz: out_w.at[zz, member], o_line_send, o_line_recv, g_here
    )
    out_gather = PlaneGather(
        (z, y, x, c), lambda yy, xx: out_w.at[:, yy * 4 + xx * 2 + c], out_rows.shape[1], g_send, g_recv
    )
    line_begin, line_pass, line_last = line_gather(
        (z, y, x, c), lines, unit_w.at[z], lambda zz: unit_w.at[zz], l_send, l_recv
    )
    for k in range(1, PLANE):
        unit_out(k).start()
    first_block = deal[0, me]
    total = functools.reduce(lambda a, b: a + b, [lengths[0, j] for j in range(NSEQ)])
    token = lax.broadcasted_iota(jnp.int32, (1, rows), 1)
    in_pack = jnp.where(token < half_rows, first_block * half_rows, (2 * count - 2 - first_block) * half_rows) + token
    counted = jnp.where(in_pack < total, mask[...].astype(jnp.float32), 0.0)
    arrange_rows(rows_in, w_query, w_key, w_value, gain_rows, jnp.sum(counted, -1, keepdims=True))
    one_begin()
    valid[...] = jnp.transpose(jnp.broadcast_to(counted, (LANES, rows)))[:, :1]
    token = lax.broadcasted_iota(jnp.int32, (rows, 1), 0)
    in_pack = jnp.where(token < half_rows, first_block * half_rows, (2 * count - 2 - first_block) * half_rows) + token
    angle = (in_pack - segment_of(lengths, in_pack)[0]).astype(jnp.float32) * freq[...]
    cosine[...] = jnp.cos(angle)
    sine[...] = jnp.sin(angle)
    one_pass(1)
    two_begin()
    for moment in range(2, lines):
        one_pass(moment)
        two_pass(moment - 1)
    one_last()
    one.begin()
    two_pass(lines - 1)
    two_last()
    unit_own.wait()
    for k in range(1, PLANE):
        unit_out(k).wait_recv()
    line_begin()
    out_begin()
    one.forward_on()
    two.begin()
    for moment in range(1, lines - 1):
        out_pass(moment)
    one.corner_on()
    out_pass(lines - 1)
    out_last()
    two.forward_on()
    line_pass(1)
    one.rest()
    two.corner_on()
    two.rest()
    keep_weights = pltpu.make_async_copy(w, weights, w_sem)
    keep_weights.start()

    def columns_of(start, size):
        return w[:, :, :, pl.ds(start, size)].reshape(width, size)

    extras = columns_of(count * head_cols, LANES)
    gains[...] = jnp.transpose(extras.astype(jnp.float32))[: gains.shape[0], :]
    gain = gains[0:1, :]

    def norm_rows(at):
        values_at = tokens[at, :].astype(jnp.float32)
        normed[at, :] = (values_at * rms_scale(values_at) * gain).astype(normed.dtype)

    by_rows(rows, norm_rows)

    def out(k):
        return remote(sent.at[peer(k)], qkv.at[me], send.at[k], recv.at[k], to_device(peer(k)))

    def project(k, carry):
        i = peer(k)
        columns = columns_of(pl.multiple_of(i * head_cols, LANES), head_cols)
        both = jnp.dot(normed[...], columns, preferred_element_type=jnp.float32)
        for tile in range(HEAD_TILES):
            at = slice(tile * LANES, (tile + 1) * LANES)
            sent[i, :, at] = turned(both[:, at], cosine[...], sine[...]).astype(sent.dtype)

        @pl.when(k < count)
        def _():
            out(k).start()

        return carry

    lax.fori_loop(1, count + 1, project, 0)
    out_gather.begin()
    line_pass(2)
    qkv[me] = sent[me]
    for src in range(count):
        columns = slice(src * half_rows, (src + 1) * half_rows)
        steps = lax.broadcasted_iota(jnp.int32, (1, half_rows), 1)
        place_row[0, :, columns] = deal[0, src] * half_rows + steps
        place_row[1, :, columns] = (2 * count - 1 - deal[0, src]) * half_rows + steps

    def arrive(k, carry):
        out(k).wait_recv()
        return carry

    out_gather.forward_on()
    out_gather.corner_on()
    lax.fori_loop(1, count, arrive, 0)
    keep_qkv = pltpu.make_async_copy(qkv, qkv_out, q_sem)
    keep_qkv.start()
    keys_and_values(qkv, keys, values, count, half_rows)

    def back(k):
        return remote(o_sent.at[peer(k)], o_came.at[me], o_send.at[k], o_recv.at[k], to_device(peer(k)))

    def keep(src, half):
        return pltpu.make_async_copy(prob_blocks.at[src, half], probs.at[src, half], p_sem.at[src, half])

    def attend(k, carry):
        src = peer(k)
        halves_out = []
        for half in range(2):
            at = pl.ds(half * half_rows, half_rows)
            queries = jnp.concatenate([qkv[src, at, :LANES], qkv[src, at, LANES : 2 * LANES]], 0)
            score = against(queries, keys[half]) * scale
            first = deal[0, src]
            block = first if half == 0 else 2 * count - 1 - first
            own = block * half_rows + lax.broadcasted_iota(jnp.int32, (half_rows, 1), 0)
            start, end = segment_of(lengths, own)
            lowest = jnp.where(own < end, start, own)
            place = place_row[half]
            allowed = (place >= lowest) & (place <= own)
            bias = jnp.where(allowed, 0.0, masked_score)
            score = score + jnp.concatenate([bias, bias], 0)
            top = jnp.max(score, -1, keepdims=True)
            weight = jnp.exp(score - top)
            total = jnp.sum(weight, -1, keepdims=True)
            low = (weight * (1.0 / total)).astype(prob_blocks.dtype)
            prob_blocks[src, half] = low
            keep(src, half).start()
            summed = jnp.dot(low, values[half], preferred_element_type=jnp.float32)
            full, part = packed_pair(summed[:half_rows], summed[half_rows:], even)
            o_sent[src, at, :] = full.astype(o_sent.dtype)
            halves_out.append(part)
        lane = lanes_of(halves_out[0])
        part = jnp.where(lane < 64, halves_out[0], pltpu.roll(halves_out[1], 64, 1))
        o_sent[src, pl.ds(rows, half_rows), :] = part.astype(o_sent.dtype)

        @pl.when(k < count)
        def _():
            back(k).start()

        return carry

    lax.fori_loop(1, count + 1, attend, 0)
    o_came[me] = o_sent[me]

    def return_arrive(k, carry):
        back(k).wait_recv()
        return carry

    lax.fori_loop(1, count, return_arrive, 0)
    for pair in range(count // 2):
        at = pair * head_cols
        attended[:, at : at + LANES] = o_came[2 * pair, :rows, :]
        attended[:, at + 2 * LANES : at + 3 * LANES] = o_came[2 * pair + 1, :rows, :]
        one = o_came[2 * pair, rows:, :].astype(jnp.float32)
        two = o_came[2 * pair + 1, rows:, :].astype(jnp.float32)
        lane = lanes_of(one)
        middle = slice(at + LANES, at + 2 * LANES)
        attended[:half_rows, middle] = jnp.where(lane < 64, one, pltpu.roll(two, 64, 1)).astype(attended.dtype)
        attended[half_rows:, middle] = jnp.where(lane < 64, pltpu.roll(one, 64, 1), two).astype(attended.dtype)

    def drain(k, carry):
        out(k).wait_send()
        back(k).wait_send()
        return carry

    lax.fori_loop(1, count, drain, 0)

    def drain_probs(src, carry):
        keep(src, 0).wait()
        keep(src, 1).wait()
        return carry

    lax.fori_loop(0, count, drain_probs, 0)
    keep_qkv.wait()
    out_gather.rest()
    for gather in (out_gather, *plane_gathers):
        gather.drain()
    for moment in range(3, lines):
        line_pass(moment)
    line_last()
    for k in range(1, PLANE):
        unit_out(k).wait_send()
    keep_weights.wait()


def attend(scale, lines, w_query, w_key, w_value, w_gate, w_up, out_rows, gain_rows, freq, mask, deal, lengths, tokens, identity):
    rows, width = tokens.shape
    share, units = out_rows.shape[0], w_gate.shape[1] // PLANE
    count = KV
    columns = count * HEAD_TILES * LANES + LANES
    half_rows = rows // 2
    half = count * half_rows
    head_cols = HEAD_TILES * LANES
    low = tokens.dtype
    shape = jax.ShapeDtypeStruct
    vmem, anywhere = pl.BlockSpec(memory_space=pltpu.VMEM), pl.BlockSpec(memory_space=pl.ANY)
    smem = pl.BlockSpec(memory_space=pltpu.SMEM)
    dma = pltpu.SemaphoreType.DMA
    return pl.pallas_call(
        functools.partial(attend_kernel, scale, lines),
        out_shape=[
            shape((rows, width), low),
            shape((rows, width), low),
            shape((8, width), jnp.float32),
            shape((rows, LANES), jnp.float32),
            shape((rows, LANES), jnp.float32),
            shape((rows, 1), jnp.float32),
            shape((lines, PLANE, share, columns), low),
            shape((lines, PLANE) + out_rows.shape, low),
            shape((lines, PLANE, share, 2 * units), low),
            shape((count, rows, head_cols), low),
            shape((count, 2, rows, half), low),
        ],
        in_specs=[vmem] * 5 + [anywhere] + [vmem] * 3 + [smem, smem, vmem],
        out_specs=[vmem] * 6 + [anywhere] * 5,
        scratch_shapes=[
            pltpu.VMEM((share, columns), low),
            pltpu.VMEM((PLANE, share, 2 * units), low),
            pltpu.VMEM((lines, PLANE, share, columns), low),
            pltpu.VMEM((2, 1, half), jnp.int32),
            pltpu.VMEM((count, rows, head_cols), low),
            pltpu.VMEM((count, rows, head_cols), low),
            pltpu.VMEM((2, half, LANES), low),
            pltpu.VMEM((2, half, LANES), low),
            pltpu.VMEM((count, 2, rows, half), low),
            pltpu.VMEM((count, rows + half_rows, LANES), low),
            pltpu.VMEM((count, rows + half_rows, LANES), low),
            dma((count,)),
            dma((count,)),
            dma((count,)),
            dma((count,)),
            dma((count, 2)),
            dma,
            dma,
            dma((2, 2, lines)),
            dma((2, 2, lines)),
            dma((2, GATHER_KINDS)),
            dma((2, GATHER_KINDS)),
            dma((2,)),
            dma((GATHER_KINDS,)),
            dma((GATHER_KINDS,)),
            dma,
            dma((2, lines)),
            dma((2, lines)),
            dma((PLANE,)),
            dma((PLANE,)),
            dma,
            dma((2, lines)),
            dma((2, lines)),
        ],
        compiler_params=pltpu.CompilerParams(collective_id=identity, vmem_limit_bytes=VMEM_LIMIT),
        name="attend",
    )(w_query, w_key, w_value, w_gate, w_up, out_rows, gain_rows, freq, mask, deal, lengths, tokens)


def attend_back_kernel(
    scale, lines, attended_grad, probs, cosine, sine, qkv_in, attended_in, branch_in, gate_in, down_in,
    qkv_grad, out_final, gate_sums, down_final,
    qkv, attended, branch, gate_parts, down_parts, in_sem,
    sent, came, keys, values, prob_blocks, dk_sum, dv_sum, back_sent, back_came,
    send, recv, back_send, back_recv, p_sem, up, down, l_send, l_recv, down_up, down_down, d_send, d_recv, p, *reducing,
):
    z, y, x, c = coordinates()
    count = sent.shape[0]
    me = z * 2 + y
    even = y == 0
    rows, width = attended_grad.shape
    half_rows = rows // 2
    head_cols = HEAD_TILES * LANES
    to_device = lambda i: (i, x * 2 + c)
    peer = lambda k: lax.rem(me + k, count)
    source = lambda k: lax.rem(me + count - k, count)

    loads = transfers(
        (attended_in, branch_in, qkv_in, gate_in, down_in), (attended, branch, qkv, gate_parts, down_parts), in_sem
    )
    for load_in in loads:
        load_in.start()

    def load(src, half):
        return pltpu.make_async_copy(probs.at[src, half], prob_blocks.at[src, half], p_sem.at[src, half])

    def load_start(k, carry):
        load(source(k), 0).start()
        load(source(k), 1).start()
        return carry

    lax.fori_loop(0, count, load_start, 0)
    greet([to_device(peer(k)) for k in range(1, count)] + [device(z, y, 1 - x, c), device(z, y, x, 1 - c)])
    members, share = p.shape[1:3]

    def prepare(block):
        at = pl.ds(pl.multiple_of(block * members * share, LANES), members * share)
        store_terms(p, block, 0, transposed(attended[:, at], branch[...]))

    reduce_stages, reduce_last = reduce_plan(lines, prepare, p, out_final, *reducing)
    line_begin, line_hop, line_last = line_reduce((z, y, x, c), lines, gate_parts, up, down, l_send, l_recv)
    down_begin, down_hop, down_last = line_reduce((z, y, x, c), lines, down_parts, down_up, down_down, d_send, d_recv)
    for pair in range(count // 2):
        at = pair * head_cols
        sent[2 * pair, :rows, :] = attended_grad[:, at : at + LANES]
        sent[2 * pair + 1, :rows, :] = attended_grad[:, at + 2 * LANES : at + 3 * LANES]
        middle = attended_grad[:, at + LANES : at + 2 * LANES].astype(jnp.float32)
        one, two = middle[:half_rows], middle[half_rows:]
        lane = lanes_of(one)
        sent[2 * pair, rows:, :] = jnp.where(lane < 64, one, pltpu.roll(two, 64, 1)).astype(sent.dtype)
        sent[2 * pair + 1, rows:, :] = jnp.where(lane < 64, pltpu.roll(one, 64, 1), two).astype(sent.dtype)

    def out(k):
        return remote(sent.at[peer(k)], came.at[me], send.at[k], recv.at[k], to_device(peer(k)))

    def begin(k, carry):
        out(k).start()
        return carry

    lax.fori_loop(1, count, begin, 0)
    for load_in in loads[:2]:
        load_in.wait()
    reduce_stages[0]()
    came[me] = sent[me]
    for load_in in loads[2:]:
        load_in.wait()
    keys_and_values(qkv, keys, values, count, half_rows)
    dk_sum[...] = jnp.zeros_like(dk_sum)
    dv_sum[...] = jnp.zeros_like(dv_sum)

    def pack(src, kind, at, first, second):
        full, part = packed_pair(first, second, even)
        back_sent[src, kind, at, :] = full.astype(back_sent.dtype)
        return part

    def pack_parts(src, kind, parts):
        part = jnp.where(lanes_of(parts[0]) < 64, parts[0], pltpu.roll(parts[1], 64, 1))
        back_sent[src, kind, pl.ds(rows, half_rows), :] = part.astype(back_sent.dtype)

    def back(kind, k):
        to = source(k) if kind == 0 else peer(k)
        return remote(
            back_sent.at[to, kind], back_came.at[me, kind], back_send.at[kind, k], back_recv.at[kind, k], to_device(to)
        )

    def grads(k, carry):
        src = source(k)

        @pl.when(k > 0)
        def _():
            out(k).wait_recv()

        parts = []
        for half in range(2):
            at = pl.ds(half * half_rows, half_rows)
            full = came[src, at, :].astype(jnp.float32)
            part = came[src, pl.ds(rows, half_rows), :].astype(jnp.float32)
            if half:
                part = pltpu.roll(part, 64, 1)
            pair = jnp.concatenate(unpacked_pair(full, part, even), 0).astype(came.dtype)
            queries = jnp.concatenate([qkv[src, at, :LANES], qkv[src, at, LANES : 2 * LANES]], 0)
            load(src, half).wait()
            low = prob_blocks[src, half]
            prob = low.astype(jnp.float32)
            prob_grad = against(pair, values[half])
            delta = jnp.sum(prob * prob_grad, -1, keepdims=True)
            score_low = (prob * (prob_grad - delta)).astype(low.dtype)
            dq = jnp.dot(score_low, keys[half], preferred_element_type=jnp.float32) * scale
            parts.append(pack(src, 0, at, dq[:half_rows], dq[half_rows:]))
            dk_sum[half] += transposed(score_low, queries)
            dv_sum[half] += transposed(low, pair)
        pack_parts(src, 0, parts)

        @pl.when(k > 0)
        def _():
            back(0, k).start()

        pl.when(k == 2)(line_begin)
        pl.when(k == 5)(down_begin)
        for number in range(1, len(reduce_stages)):
            pl.when(k == number)(reduce_stages[number])
        return carry

    lax.fori_loop(0, count, grads, 0)

    def finish(k, carry):
        src = peer(k)
        in_half = pl.ds(pl.multiple_of(src * half_rows, half_rows), half_rows)
        parts = []
        for half in range(2):
            at = pl.ds(half * half_rows, half_rows)
            parts.append(pack(src, 1, at, dk_sum[half, in_half, :] * scale, dv_sum[half, in_half, :]))
        pack_parts(src, 1, parts)

        @pl.when(k < count)
        def _():
            back(1, k).start()

        return carry

    lax.fori_loop(1, count + 1, finish, 0)
    for moment in range(1, lines - 1):
        line_hop(moment)
        down_hop(moment)
    reduce_last()
    back_came[me] = back_sent[me]

    def turn_back(k, carry):
        src = source(k)
        src_even = lax.rem(src, 2) == 0

        @pl.when(k > 0)
        def _():
            back(0, count - k).wait_recv()
            back(1, k).wait_recv()

        for half in range(2):
            at = pl.ds(half * half_rows, half_rows)
            heads = []
            for kind in range(2):
                full = back_came[src, kind, at, :].astype(jnp.float32)
                part = back_came[src, kind, pl.ds(rows, half_rows), :].astype(jnp.float32)
                if half:
                    part = pltpu.roll(part, 64, 1)
                heads.extend(unpacked_pair(full, part, src_even))
            dv = heads.pop()
            lane = lanes_of(dv)
            for tile in range(HEAD_TILES):
                turned_at = turned(heads[tile], cosine[at, :], -sine[at, :])
                joined = jnp.where(lane < HD, turned_at, pltpu.roll(dv, HD - 32 * tile, 1))
                to = pl.ds(pl.multiple_of(src * head_cols + tile * LANES, LANES), LANES)
                qkv_grad[at, to] = joined.astype(qkv_grad.dtype)
        return carry

    lax.fori_loop(0, count, turn_back, 0)

    def keep_sums(i, sums):
        gate_sums[i] = sums.astype(gate_sums.dtype)

    line_last(keep_sums, gate_sums.shape[1])

    def keep_down(i, sums):
        down_final[pl.ds(pl.multiple_of(i * 32, 32), 32), :] = sums

    down_last(keep_down)

    def drain(k, carry):
        out(k).wait_send()
        back(0, k).wait_send()
        back(1, k).wait_send()
        return carry

    lax.fori_loop(1, count, drain, 0)


def attend_back(scale, lines, attended_grad, qkv, probs, tables, attended, branch, gate_parts, down_parts, identity):
    rows, width = attended_grad.shape
    count, _, head_cols = qkv.shape
    half = probs.shape[-1]
    half_rows = rows // 2
    share = width // (lines * PLANE)
    low = attended_grad.dtype
    vmem, anywhere = pl.BlockSpec(memory_space=pltpu.VMEM), pl.BlockSpec(memory_space=pl.ANY)
    dma = pltpu.SemaphoreType.DMA
    return pl.pallas_call(
        functools.partial(attend_back_kernel, scale, lines),
        out_shape=[
            jax.ShapeDtypeStruct((rows, count * head_cols), low),
            jax.ShapeDtypeStruct((share, width), jnp.float32),
            jax.ShapeDtypeStruct((PLANE, share, gate_parts.shape[2]), low),
            jax.ShapeDtypeStruct(down_parts.shape[1:], jnp.float32),
        ],
        in_specs=[vmem, anywhere, vmem, vmem] + [anywhere] * 5,
        out_specs=[vmem] * 4,
        scratch_shapes=[
            pltpu.VMEM(qkv.shape, low),
            pltpu.VMEM(attended.shape, low),
            pltpu.VMEM(branch.shape, low),
            pltpu.VMEM(gate_parts.shape, low),
            pltpu.VMEM(down_parts.shape, low),
            dma((5,)),
            pltpu.VMEM((count, rows + half_rows, LANES), low),
            pltpu.VMEM((count, rows + half_rows, LANES), low),
            pltpu.VMEM((2, half, LANES), low),
            pltpu.VMEM((2, half, LANES), low),
            pltpu.VMEM((count, 2, rows, half), low),
            pltpu.VMEM((2, half, LANES), jnp.float32),
            pltpu.VMEM((2, half, LANES), jnp.float32),
            pltpu.VMEM((count, 2, rows + half_rows, LANES), low),
            pltpu.VMEM((count, 2, rows + half_rows, LANES), low),
            dma((count,)),
            dma((count,)),
            dma((2, count)),
            dma((2, count)),
            dma((count, 2)),
            pltpu.VMEM(gate_parts.shape, low),
            pltpu.VMEM(gate_parts.shape, low),
            dma((2, lines)),
            dma((2, lines)),
            pltpu.VMEM(down_parts.shape, low),
            pltpu.VMEM(down_parts.shape, low),
            dma((2, lines)),
            dma((2, lines)),
            *reduce_scratch(lines, share, width, low),
        ],
        compiler_params=pltpu.CompilerParams(collective_id=identity, vmem_limit_bytes=VMEM_LIMIT),
        name="attend_back",
    )(attended_grad, probs, *tables, qkv, attended, branch, gate_parts, down_parts)


def finish_kernel(
    weights, normed, qkv_grad, gains, square, norm, up_parts, gate_sums, hidden_in, tokens_in, gate_in, up_in,
    input_grad, query_final, key_final, value_final, gate_final, up_final, gain_final, loss,
    hidden_grad, tokens, w_gate, w_up, in_sem, w, own_rows, normed_grad, final, up_sums, gate_came, up_came, line_up, line_down,
    w_sem, own_sem, gate_send, gate_recv, up_send, up_recv, here, l_send, l_recv, p, *reducing,
):
    z, y, x, c = coordinates()
    lines, members, share = p.shape[:3]
    rows, width = tokens.shape
    qkv_cols = qkv_grad.shape[1]
    low = normed.dtype
    load = pltpu.make_async_copy(weights.at[:, pl.ds(0, qkv_cols)], w, w_sem)
    load.start()
    loads = transfers((hidden_in, tokens_in, gate_in, up_in), (hidden_grad, tokens, w_gate, w_up), in_sem)
    for load_in in loads:
        load_in.start()
    number = (z * 2 + y) * 4 + x * 2 + c
    own_at = pl.ds(pl.multiple_of(number * share, 16), share)
    load_own = pltpu.make_async_copy(weights.at[own_at, :], own_rows, own_sem)
    load_own.start()
    me = y * 4 + x * 2 + c
    peer = lambda k: lax.rem(me + k, members)
    member = lambda i: (z * 2 + i // 4, i % 4)
    greet([member(peer(k)) for k in range(1, members)] + line_of(z, y, x, c, lines))

    def out(kind, k):
        src, came, send, recv = (
            (gate_sums, gate_came, gate_send, gate_recv),
            (up_sums, up_came, up_send, up_recv),
        )[kind]
        return remote(src.at[peer(k)], came.at[me], send.at[k], recv.at[k], member(peer(k)))

    gate_own = pltpu.make_async_copy(gate_sums.at[me], gate_came.at[me], here)
    gate_own.start()
    for k in range(1, members):
        out(0, k).start()
    line_begin, line_hop, line_last = line_reduce((z, y, x, c), lines, up_parts, line_up, line_down, l_send, l_recv)
    line_begin()

    def keep_up(i, sums):
        up_sums[i] = sums.astype(up_sums.dtype)

    devices = lines * PLANE
    place = lax.broadcasted_iota(jnp.int32, (1, LANES), 1) - number
    rest = square[...]
    loss_terms = jnp.zeros((1, LANES), jnp.float32)
    for term in range(3):
        top = rest.astype(low).astype(jnp.float32)
        loss_terms = loss_terms + jnp.where(place == term * devices, top, 0.0)
        rest = rest - top

    def prepare(block):
        at = pl.ds(pl.multiple_of(block * members * share, LANES), members * share)
        left = normed[:, at]
        chunk = qkv_cols // 2
        for start in range(0, qkv_cols, chunk):
            store_terms(p, block, start, transposed(left, qkv_grad[:, start : start + chunk]))
        store_terms(p, block, qkv_cols, jnp.broadcast_to(loss_terms, (members * share, LANES)))

    stages, last = reduce_plan(lines, prepare, p, final, *reducing)

    def grad_rows(at):
        values = tokens[at, :].astype(jnp.float32)
        scale = rms_scale(values)
        unit = values * scale
        scaled = normed_grad[at, :] * gains[0:1, :]
        input_grad[at, :] = hidden_grad[at, :] + scale * (
            scaled - unit * jnp.mean(scaled * unit, -1, keepdims=True)
        )

    block = rows // lines
    for index, stage in enumerate(stages):
        if index == 2:
            load.wait()
            for load_in in loads:
                load_in.wait()
        if 2 <= index < lines:
            line_hop(index - 1)
        if index == 1 + lines:
            line_last(keep_up, share)
            for k in range(1, members):
                out(1, k).start()
        stage()
        if 2 <= index < 2 + lines:
            at = slice((index - 2) * block, (index - 1) * block)
            normed_grad[at, :] = against(qkv_grad[at, :], w[...])
        if index == 2 + lines:
            by_rows(rows, grad_rows)
    up_came[me] = up_sums[me]
    gate_own.wait()
    for kind in range(2):
        for k in range(1, members):
            out(kind, k).wait_recv()
    units = gate_came.shape[2] // lines
    for i in range(members):
        for zz in range(lines):
            to = slice((zz * members + i) * units, (zz * members + i + 1) * units)
            of = slice(zz * units, (zz + 1) * units)
            gate_final[:, to] = gate_came[i, :, of].astype(jnp.float32)
            up_final[:, to] = up_came[i, :, of].astype(jnp.float32)
    last()

    def tile(head, number):
        start = (head * HEAD_TILES + number) * LANES
        return final[:, start : start + LANES]

    def put(ref, group, heads):
        for number, value in enumerate(side_by_side(heads)):
            start = (group * HEAD_TILES + number) * LANES
            ref[:, start : start + LANES] = value

    for pair in range(KV // 2):
        put(query_final, pair, [tile(2 * pair + i, j) for i in range(2) for j in range(2)])
    for group in range(KV // 4):
        heads = [4 * group + i for i in range(4)]
        put(key_final, group, [tile(head, 2) for head in heads])
        parts = []
        for head in heads:
            thirds = [pltpu.roll(tile(head, number), 32 * (number + 1), 1) for number in range(HEAD_TILES)]
            in_tile = lanes_of(thirds[0])
            parts.append(jnp.where(in_tile < 32, thirds[0], jnp.where(in_tile < 64, thirds[1], thirds[2])))
        put(value_final, group, parts)

    load_own.wait()
    own_gains = own_rows[:, qkv_cols:].astype(jnp.float32)

    def product(grads, weights_of, width_of):
        sums = jnp.zeros((share, 1), jnp.float32)
        for start in range(0, width_of, 4 * LANES):
            at = slice(start, start + 4 * LANES)
            sums += jnp.sum(grads[:, at] * weights_of[:, at].astype(jnp.float32), -1, keepdims=True)
        return sums

    units_all = w_gate.shape[1]
    first_gain = product(final, own_rows, qkv_cols) / own_gains[:, 0:1]
    second_gain = product(gate_final, w_gate, units_all) + product(up_final, w_up, units_all)
    second_gain = second_gain / own_gains[:, 1:2]
    columns = lax.broadcasted_iota(jnp.int32, (share, LANES), 1)
    both_gains = jnp.where(columns == 0, first_gain, jnp.where(columns == 1, second_gain, 0.0))
    both_gains = jnp.concatenate([both_gains, jnp.zeros((LANES - share, LANES), jnp.float32)], 0)
    gain_final[...] = jnp.transpose(both_gains)[:8, :]
    tail = final[:, qkv_cols:]
    of_loss = lax.broadcasted_iota(jnp.int32, (1, LANES), 1) < 3 * devices
    loss[...] = jnp.sum(jnp.where(of_loss, tail[:1, :], 0.0), -1, keepdims=True) * (0.5 * norm[...])
    for kind in range(2):
        for k in range(1, members):
            out(kind, k).wait_send()


def finish(
    lines, weights, normed, qkv_grad, hidden_grad, tokens, gains, square, norm, w_gate, w_up, gate_sums, up_parts, identity
):
    rows, width = tokens.shape
    qkv_cols = qkv_grad.shape[1]
    share = weights.shape[0] // (lines * PLANE)
    columns = weights.shape[1]
    units_all = w_gate.shape[1]
    low = tokens.dtype
    vmem, anywhere = pl.BlockSpec(memory_space=pltpu.VMEM), pl.BlockSpec(memory_space=pl.ANY)
    dma = pltpu.SemaphoreType.DMA
    shapes = [
        (rows, width),
        (share, width),
        (share, KV * HD),
        (share, KV * HD),
        (share, units_all),
        (share, units_all),
        (8, LANES),
        (1, 1),
    ]
    return pl.pallas_call(
        finish_kernel,
        out_shape=[jax.ShapeDtypeStruct(shape, jnp.float32) for shape in shapes],
        in_specs=[anywhere] + [vmem] * 6 + [anywhere] * 5,
        out_specs=[vmem] * len(shapes),
        scratch_shapes=[
            pltpu.VMEM(hidden_grad.shape, jnp.float32),
            pltpu.VMEM(tokens.shape, low),
            pltpu.VMEM(w_gate.shape, low),
            pltpu.VMEM(w_up.shape, low),
            dma((4,)),
            pltpu.VMEM((width, qkv_cols), low),
            pltpu.VMEM((share, columns), low),
            pltpu.VMEM((rows, width), jnp.float32),
            pltpu.VMEM((share, columns), jnp.float32),
            pltpu.VMEM(gate_sums.shape, low),
            pltpu.VMEM(gate_sums.shape, low),
            pltpu.VMEM(gate_sums.shape, low),
            pltpu.VMEM(up_parts.shape, low),
            pltpu.VMEM(up_parts.shape, low),
            dma,
            dma,
            dma((PLANE,)),
            dma((PLANE,)),
            dma((PLANE,)),
            dma((PLANE,)),
            dma,
            dma((2, lines)),
            dma((2, lines)),
            *reduce_scratch(lines, share, columns, low),
        ],
        compiler_params=pltpu.CompilerParams(collective_id=identity, vmem_limit_bytes=VMEM_LIMIT),
        name="finish",
    )(weights, normed, qkv_grad, gains, square, norm, up_parts, gate_sums, hidden_grad, tokens, w_gate, w_up)


def emit_kernel(joined, *refs):
    sem = refs[-1]
    count = (len(refs) - 2) // 2
    out = refs[count + 1 : -1]
    pairs = [(refs[i], out[i]) for i in range(count)]
    cut = refs[joined].shape[1]
    pairs[joined] = (refs[joined], out[joined].at[:, pl.ds(0, cut)])
    pairs.append((refs[count], out[joined].at[:, pl.ds(cut, refs[count].shape[1])]))
    copies = [pltpu.make_async_copy(src, dst, sem.at[i]) for i, (src, dst) in enumerate(pairs)]
    for copy in copies:
        copy.start()
    for copy in copies:
        copy.wait()


def emit(arrays, joined, rest):
    shapes = [array.shape for array in arrays]
    shapes[joined] = (shapes[joined][0], shapes[joined][1] + rest.shape[1])
    return pl.pallas_call(
        functools.partial(emit_kernel, joined),
        out_shape=[jax.ShapeDtypeStruct(shape, array.dtype) for shape, array in zip(shapes, arrays)],
        in_specs=[pl.BlockSpec(memory_space=pl.ANY)] * (len(arrays) + 1),
        out_specs=[pl.BlockSpec(memory_space=pltpu.VMEM)] * len(arrays),
        scratch_shapes=[pltpu.SemaphoreType.DMA((len(arrays) + 1,))],
        compiler_params=pltpu.CompilerParams(vmem_limit_bytes=VMEM_LIMIT),
        name="emit",
    )(*arrays, rest)


def plane_per_device(lines, *arrays):
    (
        tokens,
        lengths,
        deal,
        loss_mask,
        teacher,
        out_grad,
        attn_gain,
        w_query,
        w_key,
        w_value,
        w_out,
        ffn_gain,
        w_gate,
        w_up,
        w_down,
    ) = arrays
    devices = lines * PLANE
    width = tokens.shape[2]
    weight_rows = w_query.shape[0]
    scale = HD ** (-0.5)
    gain_rows = jnp.zeros((8, LANES), jnp.float32)
    gain_rows = gain_rows.at[0, :weight_rows].set(attn_gain.astype(jnp.float32))
    gain_rows = gain_rows.at[1, :weight_rows].set(ffn_gain.astype(jnp.float32))
    freq = rope_base ** (-(np.arange(HD // 2) * 2.0 / HD))
    freq = np.concatenate([freq, freq, np.zeros(LANES - HD)])[None].astype(np.float32)

    attended_low, normed_low, gains, cosine, sine, valid, attn_all, out_w, gate_up_w, qkv, probs = attend(
        scale,
        lines,
        w_query,
        w_key,
        w_value,
        w_gate,
        w_up,
        w_out,
        gain_rows,
        freq,
        loss_mask,
        deal,
        lengths,
        tokens[0],
        3,
    )
    attn_all = attn_all.reshape(devices * weight_rows, -1)
    gate_up_w = gate_up_w.reshape(devices * weight_rows, -1)

    result, square, norm, hidden_grad, branch_low, attended_grad, down_final, down_rest, gate_grad, up_grad = feed_forward(
        lines,
        out_w.reshape(width, width),
        attended_low,
        tokens[0],
        teacher[0],
        out_grad[0],
        valid,
        gains,
        gate_up_w,
        w_down,
        5,
    )
    gate_grad, up_grad = [grad.reshape(lines, PLANE * weight_rows, -1) for grad in (gate_grad, up_grad)]
    qkv_grad, out_final, gate_sums, down_more = attend_back(
        scale, lines, attended_grad, qkv, probs, (cosine, sine), attended_low, branch_low, gate_grad, down_rest, 9
    )

    input_grad, query_final, key_final, value_final, gate_final, up_final, gain_final, loss = finish(
        lines,
        attn_all,
        normed_low,
        qkv_grad,
        hidden_grad,
        tokens[0],
        gains,
        square,
        norm,
        w_gate,
        w_up,
        gate_sums,
        up_grad,
        11,
    )
    result, input_grad, query_final, key_final, value_final, out_final, gate_final, up_final, down_final = emit(
        (result, input_grad, query_final, key_final, value_final, out_final, gate_final, up_final, down_final),
        8,
        down_more,
    )
    return (
        result[None],
        loss.reshape(()),
        input_grad[None],
        gain_final[0, :weight_rows],
        query_final,
        key_final,
        value_final,
        out_final,
        gain_final[1, :weight_rows],
        gate_final,
        up_final,
        down_final,
    )


def suits_planes(mesh):
    sizes = dict(mesh.shape)
    return sizes["fsdp"] == 4 and sizes["ctx"] == KV


def solution(mesh):
    placed = (
        P("fsdp", "ctx", None),
        P("fsdp", None),
        P("fsdp", None),
        P("fsdp", "ctx"),
        P("fsdp", "ctx", None),
        P("fsdp", "ctx", None),
        P(("ctx", "fsdp")),
        P(("ctx", "fsdp"), None),
        P(("ctx", "fsdp"), None),
        P(("ctx", "fsdp"), None),
        P(("ctx", "fsdp"), None),
        P(("ctx", "fsdp")),
        P(("ctx", "fsdp"), None),
        P(("ctx", "fsdp"), None),
        P(("ctx", "fsdp"), None),
    )
    if suits_planes(mesh):
        per_device = functools.partial(plane_per_device, mesh.shape["ctx"] // ROWS_Y)
    else:
        per_device = ring_per_device
    return jax.shard_map(
        per_device,
        mesh=mesh,
        in_specs=placed,
        out_specs=(
            P("fsdp", "ctx", None),
            P(),
            P("fsdp", "ctx", None),
            P(("ctx", "fsdp")),
            P(("ctx", "fsdp"), None),
            P(("ctx", "fsdp"), None),
            P(("ctx", "fsdp"), None),
            P(("ctx", "fsdp"), None),
            P(("ctx", "fsdp")),
            P(("ctx", "fsdp"), None),
            P(("ctx", "fsdp"), None),
            P(("ctx", "fsdp"), None),
        ),
        check_vma=False,
    )
```
